32 devices in a mesh: gx: 8 (over z, x), trait: 4 (over y, core).
Axes of the slice: x: 2, y: 2, z: 4, core: 2. Of those that a mesh axis runs over, the one named last changes fastest.
Arguments:
- initial: float32 [64, 128, 1024], P('gx', None, 'trait'), may hold values from 0.2 to 2
- section_one: float32 [64, 128, 1024], P('gx', None, 'trait'), may hold values from 0.2 to 2
- section_two: float32 [64, 128, 1024], P('gx', None, 'trait'), may hold values from 0.2 to 2
- kernels: bfloat16 [2, 1024, 1024], P(None, None, 'trait'), may hold values from -0.1875 to 0.1875
- growth: float32 [1024], P('trait'), may hold values from -3 to 3
- death_rate: float32 [1024], P('trait'), may hold values from 0.5 to 8
Outputs:
- new_one: float32 [64, 128, 1024], P('gx', None, 'trait')
- new_two: float32 [64, 128, 1024], P('gx', None, 'trait')
The draws below stay inside these ranges and needn't reach their ends.
All inputs are finite; a program needn't handle non-finite values.
Results may differ from the reference program's by a relative error of at most 0.002.
Values may be sent and summed in bfloat16 or wider, within the bound.
No kernel may reach another device: no remote copies, remote signals or barrier semaphores. Data moves between devices by JAX's collectives and lax.ppermute only.
A program may use at most 64 MiB of HBM per device.

```python
import math
import jax
import jax.numpy as jnp
from jax import lax

M = 1024
NY = 128
NX = 64


def block_levels(rng, shape, split, low, top_value):
    loudness = 1.0
    for dim, parts in split:
        heights = jax.random.uniform(jax.random.fold_in(jax.random.fold_in(rng, 6), dim), (parts,), jnp.float32, low / len(split), top_value / len(split))
        loudness = loudness * jnp.repeat(jnp.exp(heights), shape[dim] // parts).reshape((-1,) + (1,) * (len(shape) - 1 - dim))
    return loudness


def normal_values(own_key, shape, scale, reach, pieces=(), dtype=jnp.bfloat16):
    array = scale * jax.random.normal(own_key, shape, jnp.float32)
    if pieces:
        array = array * block_levels(own_key, shape, pieces, -0.22, 0.18)
    return jnp.clip(array, -reach, reach).astype(dtype)


def setup_inputs(seed: int = 0) -> dict:
    splits = jax.random.split(jax.random.key(seed), 7)
    return {
        "initial": jnp.clip(jnp.exp(math.log(2.0) - 2.3025851 * jax.random.uniform(splits[0], (NX, NY, M), jnp.float32) ** block_levels(splits[0], (NX, NY, M), ((0, 8), (2, 4)), -0.2, 0.2)), 0.2, 2.0),
        "section_one": jnp.clip(jnp.exp(math.log(2.0) - 2.3025851 * jax.random.uniform(splits[1], (NX, NY, M), jnp.float32) ** block_levels(splits[1], (NX, NY, M), ((0, 8), (2, 4)), -0.2, 0.2)), 0.2, 2.0),
        "section_two": jnp.clip(jnp.exp(math.log(2.0) - 2.3025851 * jax.random.uniform(splits[2], (NX, NY, M), jnp.float32) ** block_levels(splits[2], (NX, NY, M), ((0, 8), (2, 4)), -0.2, 0.2)), 0.2, 2.0),
        "kernels": normal_values(splits[3], (2, M, M), M ** -0.5, 0.1875, ((2, 4),)),
        "growth": normal_values(splits[4], (M,), 1.0, 3.0, ((0, 4),), jnp.float32),
        "death_rate": jnp.clip(jnp.exp(math.log(8.0) - 2.7725887 * jax.random.uniform(splits[5], (M,), jnp.float32) ** block_levels(splits[5], (M,), ((0, 4),), -0.2, 0.2)), 0.5, 8.0),
    }


DIFFUSION = 0.25
STEP_SIZE = 0.5


def rounded(field):
    return lax.optimization_barrier(field.astype(jnp.bfloat16)).astype(jnp.float32)


def explicit(field, kernels, growth):
    lapl = (jnp.roll(field, 1, 0) + jnp.roll(field, -1, 0) + jnp.roll(field, 1, 1)
            + jnp.roll(field, -1, 1) - 4.0 * field)
    flat = rounded(field).reshape(-1, M)
    kern = kernels.astype(jnp.float32)
    compete = rounded(jnp.dot(flat, kern[0], preferred_element_type=jnp.float32)).reshape(field.shape)
    mutate = rounded(jnp.dot(flat, kern[1], preferred_element_type=jnp.float32)).reshape(field.shape)
    return DIFFUSION * lapl + field * (growth - compete) + mutate - field


def reference(initial, section_one, section_two, kernels, growth, death_rate):
    first_dt = STEP_SIZE / 3.0
    second_dt = 2.0 * STEP_SIZE / 3.0
    expl_one = explicit(section_one, kernels, growth)
    expl_two = explicit(section_two, kernels, growth)
    full_one = expl_one - death_rate * section_one
    full_two = expl_two - death_rate * section_two
    new_one = (initial + first_dt * death_rate * section_one
               + STEP_SIZE * (5.0 / 12.0 * full_one - 1.0 / 12.0 * full_two)) / (1.0 + first_dt * death_rate)
    expl_new = explicit(new_one, kernels, growth)
    new_two = (new_one + second_dt * (expl_new - expl_one) + second_dt * death_rate * section_two
               + STEP_SIZE / 3.0 * (full_one + full_two)) / (1.0 + second_dt * death_rate)
    return new_one, new_two
```

```python
import functools
import jax
import jax.numpy as jnp
from jax import lax
from jax.experimental import pallas as pl
from jax.experimental.pallas import tpu as pltpu
from jax.sharding import PartitionSpec as P

DIFFUSION = 0.25
STEP_SIZE = 0.5
FIRST = STEP_SIZE / 3.0
SECOND = 2.0 * STEP_SIZE / 3.0
F32 = jnp.float32
BF16 = jnp.bfloat16
VMEM_LIMIT = 24 * 1024 * 1024


def chunks_of(xcount):
    quarter = xcount // 4
    edge = list(range(quarter)) + list(range(xcount - quarter, xcount))
    middle = list(range(quarter, xcount - quarter))
    return edge, middle


def params():
    return pltpu.CompilerParams(vmem_limit_bytes=VMEM_LIMIT)


def vmem(count):
    return [pl.BlockSpec(memory_space=pltpu.VMEM)] * count


def round_chunk(fields, cells):
    _, ycount, owned = fields[0].shape
    count = len(fields)

    def body(*refs):
        out = refs[-1]
        for f in range(count):
            for i, x in enumerate(cells):
                out[f, i * ycount:(i + 1) * ycount, :] = refs[f][x].astype(BF16)

    return pl.pallas_call(
        body,
        out_shape=jax.ShapeDtypeStruct((count, len(cells) * ycount, owned), BF16),
        in_specs=vmem(count),
        out_specs=pl.BlockSpec(memory_space=pltpu.VMEM),
        compiler_params=params(),
        name="round_chunk",
    )(*fields)


def gathered_dot(parts, kernels_ref, k, me):
    depth = parts[0].shape[-1]
    lhs = jnp.concatenate(parts, axis=-1)
    rhs = jnp.concatenate(
        [kernels_ref[k, pl.ds(pl.multiple_of((me ^ j) * depth, depth), depth), :] for j in range(len(parts))], axis=0
    )
    return jnp.dot(lhs, rhs, preferred_element_type=F32).astype(BF16)


def neighbours(field_ref, lo_ref, hi_ref, f, x, xcount):
    before = field_ref[x - 1] if x > 0 else lo_ref[f].astype(F32)
    after = field_ref[x + 1] if x < xcount - 1 else hi_ref[f].astype(F32)
    return before + after


def expl(core, around, compete, mutate, growth):
    ycount = core.shape[0]
    lapl = around + pltpu.roll(core, 1, 0) + pltpu.roll(core, ycount - 1, 0)
    return DIFFUSION * lapl + core * (growth - compete - 2.0) + mutate


def first_node(me, own, sib, far, farsib, one, two, initial, faces_lo, faces_hi, kernels, growth, death, cells, previous, whole):
    xcount, ycount, owned = one.shape
    rows = len(cells) * ycount
    edge = {x: e for e, x in enumerate((0, xcount - 1)) if x in cells}
    n_prev = len(previous)

    def body(me_ref, own_ref, sib_ref, far_ref, farsib_ref, one_ref, two_ref, init_ref, lo_ref, hi_ref, k_ref, g_ref, d_ref, *refs):
        prev_refs = refs[:n_prev]
        new_ref, rounded_ref, rest_ref = refs[n_prev:n_prev + 3]
        scratch = refs[-1]
        me = me_ref[0]
        parts = [r[...].reshape(2 * rows, owned) for r in (own_ref, sib_ref, far_ref, farsib_ref)]
        for k in range(2):
            scratch[k] = gathered_dot(parts, k_ref, k, me)
        growth = g_ref[...]
        death = d_ref[...]
        inv_one = 1.0 / (1.0 + FIRST * death)
        inv_two = 1.0 / (1.0 + SECOND * death)
        for i, x in enumerate(cells):
            e = []
            cores = (one_ref[x], two_ref[x])
            for f, ref in enumerate((one_ref, two_ref)):
                at = pl.ds(f * rows + i * ycount, ycount)
                around = neighbours(ref, lo_ref, hi_ref, f, x, xcount)
                e.append(expl(cores[f], around, scratch[0, at, :].astype(F32), scratch[1, at, :].astype(F32), growth))
            full_one = e[0] - death * cores[0]
            full_two = e[1] - death * cores[1]
            new = (
                init_ref[x]
                + FIRST * death * cores[0]
                + STEP_SIZE * (5.0 / 12.0 * full_one - 1.0 / 12.0 * full_two)
            ) * inv_one
            rest = (new - SECOND * e[0] + SECOND * death * cores[1] + STEP_SIZE / 3.0 * (full_one + full_two)) * inv_two
            new_ref[x if whole else i] = new
            rounded_ref[0, i * ycount:(i + 1) * ycount, :] = new.astype(BF16)
            rest_ref[i] = rest
            if x in edge:
                refs[n_prev + 3][edge[x]] = new.astype(BF16)
        if whole:
            for ref, where in zip(prev_refs, previous):
                for i, x in enumerate(where[1]):
                    new_ref[x] = ref[i]

    out_shape = [
        jax.ShapeDtypeStruct((xcount if whole else len(cells), ycount, owned), F32),
        jax.ShapeDtypeStruct((1, rows, owned), BF16),
        jax.ShapeDtypeStruct((len(cells), ycount, owned), F32),
    ]
    if edge:
        out_shape.append(jax.ShapeDtypeStruct((2, ycount, owned), BF16))
    return pl.pallas_call(
        body,
        out_shape=out_shape,
        in_specs=[pl.BlockSpec(memory_space=pltpu.SMEM)] + vmem(12 + n_prev),
        out_specs=vmem(len(out_shape)),
        scratch_shapes=[pltpu.VMEM((2, 2 * rows, owned), BF16)],
        compiler_params=params(),
        name="first_node",
    )(me, own, sib, far, farsib, one, two, initial, faces_lo, faces_hi, kernels, growth, death, *[p[0] for p in previous])


def second_node(me, own, sib, far, farsib, new, rest, faces_lo, faces_hi, kernels, growth, death, cells, previous, whole):
    xcount, ycount, owned = new.shape
    rows = len(cells) * ycount
    n_prev = len(previous)

    def body(me_ref, own_ref, sib_ref, far_ref, farsib_ref, new_ref, rest_ref, lo_ref, hi_ref, k_ref, g_ref, d_ref, *refs):
        prev_refs = refs[:n_prev]
        out_ref, scratch = refs[n_prev:]
        me = me_ref[0]
        parts = [r[...].reshape(rows, owned) for r in (own_ref, sib_ref, far_ref, farsib_ref)]
        for k in range(2):
            scratch[k] = gathered_dot(parts, k_ref, k, me)
        growth = g_ref[...]
        factor = SECOND / (1.0 + SECOND * d_ref[...])
        for i, x in enumerate(cells):
            at = pl.ds(i * ycount, ycount)
            around = neighbours(new_ref, lo_ref, hi_ref, 0, x, xcount)
            e = expl(new_ref[x], around, scratch[0, at, :].astype(F32), scratch[1, at, :].astype(F32), growth)
            out_ref[x if whole else i] = rest_ref[i] + factor * e
        if whole:
            for ref, where in zip(prev_refs, previous):
                for i, x in enumerate(where[1]):
                    out_ref[x] = ref[i]

    return pl.pallas_call(
        body,
        out_shape=jax.ShapeDtypeStruct((xcount if whole else len(cells), ycount, owned), F32),
        in_specs=[pl.BlockSpec(memory_space=pltpu.SMEM)] + vmem(11 + n_prev),
        out_specs=pl.BlockSpec(memory_space=pltpu.VMEM),
        scratch_shapes=[pltpu.VMEM((2, rows, owned), BF16)],
        compiler_params=params(),
        name="second_node",
    )(me, own, sib, far, farsib, new, rest, faces_lo, faces_hi, kernels, growth, death, *[p[0] for p in previous])


def local(initial, section_one, section_two, kernels, growth, death_rate):
    xcount, ycount, owned = section_one.shape
    traits = lax.axis_size("trait")
    gcount = lax.axis_size("gx")
    me = lax.axis_index("trait").reshape(1)
    growth = growth.reshape(1, owned)
    death = death_rate.reshape(1, owned)
    chunks = chunks_of(xcount)

    def to_sibling(v):
        return lax.ppermute(v, "trait", [(i, i ^ 1) for i in range(traits)])

    def to_far(v):
        return lax.ppermute(v, "trait", [(i, i ^ 2) for i in range(traits)])

    def faces(head, tail):
        lo = lax.ppermute(tail, "gx", [(i, (i + 1) % gcount) for i in range(gcount)])
        hi = lax.ppermute(head, "gx", [((i + 1) % gcount, i) for i in range(gcount)])
        return lo, hi

    def gather(own):
        far = to_far(own)
        sib = to_sibling(own)
        farsib = to_sibling(far)
        return own, sib, far, farsib

    first = [gather(round_chunk((section_one, section_two), cells)) for cells in chunks]
    edge_rounded = first[0][0]
    lo, hi = faces(edge_rounded[:, :ycount], edge_rounded[:, -ycount:])

    previous = []
    second = []
    rests = []
    new_faces = None
    for c, cells in enumerate(chunks):
        last = c == len(chunks) - 1
        result = first_node(me, *first[c], section_one, section_two, initial, lo, hi, kernels, growth, death, cells, previous, last)
        new, rounded, rest = result[:3]
        if len(result) > 3:
            new_faces = faces(result[3][:1], result[3][1:])
        previous.append((new, cells))
        second.append(gather(rounded))
        rests.append(rest)
    new_one = previous[-1][0]
    previous = []
    for c, cells in enumerate(chunks):
        last = c == len(chunks) - 1
        out = second_node(me, *second[c], new_one, rests[c], *new_faces, kernels, growth, death, cells, previous, last)
        previous.append((out, cells))
    return new_one, previous[-1][0]


def solution(mesh):
    in_specs = (
        P("gx", None, "trait"),
        P("gx", None, "trait"),
        P("gx", None, "trait"),
        P(None, None, "trait"),
        P("trait"),
        P("trait"),
    )
    out_specs = (P("gx", None, "trait"), P("gx", None, "trait"))
    return jax.shard_map(local, mesh=mesh, in_specs=in_specs, out_specs=out_specs, check_vma=False)
```

```python
import jax
import jax.numpy as jnp
from jax import lax
from jax.experimental import pallas as pl
from jax.experimental.pallas import tpu as pltpu
from jax.sharding import PartitionSpec as P

DIFFUSION = 0.25
STEP_SIZE = 0.5
FIRST = STEP_SIZE / 3.0
SECOND = 2.0 * STEP_SIZE / 3.0
F32 = jnp.float32
BF16 = jnp.bfloat16
VMEM_LIMIT = 28 * 1024 * 1024
SPEC = pl.BlockSpec(memory_space=pltpu.VMEM)
ANYWHERE = pl.BlockSpec(memory_space=pl.ANY)
FROM_HBM = pl.BlockSpec(memory_space=pltpu.HBM)


def chunks_of(xcount):
    last = max(1, 3 * xcount // 8)
    start = (xcount - last + 1) // 2
    middle = list(range(start, start + last))
    return [x for x in range(xcount) if x not in middle], middle


def after(value, *others):
    return lax.optimization_barrier((value, *others))[0]


def call(body, name, args, outs, scratch=(), specs=None, out_specs=None, gflop=0.0):
    specs = specs or [SPEC] * len(args)
    space = {id(SPEC): pltpu.VMEM, id(FROM_HBM): pltpu.HBM}
    args = [
        pltpu.with_memory_space_constraint(a, space[id(s)]) if id(s) in space else a for a, s in zip(args, specs)
    ]
    return pl.pallas_call(
        body,
        out_shape=outs,
        in_specs=specs,
        out_specs=out_specs or [SPEC] * len(outs),
        scratch_shapes=list(scratch),
        compiler_params=pltpu.CompilerParams(vmem_limit_bytes=VMEM_LIMIT),
        cost_estimate=pl.CostEstimate(flops=int(gflop * 1e9), bytes_accessed=0, transcendentals=0),
        name=name,
    )(*args)


def rows_of(refs, owned):
    return jnp.concatenate([r[...].reshape(-1, owned) for r in refs], axis=0)


def round_chunk(fields, cells, with_faces):
    xcount, ycount, owned = fields[0].shape
    count = len(fields)

    def body(*refs):
        field_refs = refs[:count]
        out = refs[count]
        held, sems = refs[-2:]
        copies = []
        for f in range(count):
            for i, x in enumerate(cells):
                copies.append(pltpu.make_async_copy(field_refs[f].at[x], held.at[f, i], sems.at[f, i]))
                copies[-1].start()
        for f in range(count):
            for i, x in enumerate(cells):
                copies[f * len(cells) + i].wait()
                value = held[f, i].astype(BF16)
                out[f, i * ycount:(i + 1) * ycount, :] = value
                if with_faces and x == 0:
                    refs[count + 1][f] = value
                if with_faces and x == xcount - 1:
                    refs[count + 2][f] = value

    outs = [pltpu.VMEM((count, len(cells) * ycount, owned), BF16)]
    if with_faces:
        outs += [pltpu.VMEM((count, ycount, owned), BF16)] * 2
    return call(
        body, "round_chunk", fields, outs,
        scratch=[pltpu.VMEM((count, len(cells), ycount, owned), F32), pltpu.SemaphoreType.DMA((count, len(cells)))],
        specs=[FROM_HBM] * count, gflop=0.0,
    )


def half_dot(near, other, kernels_ref, k, first, second):
    depth = near.shape[-1]
    lhs = jnp.concatenate([near, other], axis=-1)
    rhs = jnp.concatenate(
        [kernels_ref[k, pl.ds(pl.multiple_of(b * depth, depth), depth), :] for b in (first, second)], axis=0
    )
    return jnp.dot(lhs, rhs, preferred_element_type=F32)


def stencil(get, faces, x, xcount):
    core = get(x)
    before = get(x - 1) if x > 0 else faces[0]().astype(F32)
    behind = get(x + 1) if x < xcount - 1 else faces[1]().astype(F32)
    around = before + behind + pltpu.roll(core, 1, 0) + pltpu.roll(core, core.shape[0] - 1, 0)
    return DIFFUSION * around - 2.0 * core, core


def before_first(me, owns, sibs, one, two, lo, hi, kernels, growth, chunks):
    xcount, ycount, owned = one.shape
    count = len(chunks)

    def body(me_ref, *refs):
        own_refs, sib_refs = refs[:count], refs[count:2 * count]
        one_ref, two_ref, lo_ref, hi_ref, k_ref, g_ref = refs[2 * count:2 * count + 6]
        outs = refs[2 * count + 6:]
        me = me_ref[0]
        growth = g_ref[...]
        for c, cells in enumerate(chunks):
            part_ref, base_ref = outs[2 * c:2 * c + 2]
            rows = len(cells) * ycount
            near = own_refs[c][...].reshape(2 * rows, owned)
            other = sib_refs[c][...].reshape(2 * rows, owned)
            for k in range(2):
                part_ref[k] = half_dot(near, other, k_ref, k, me, me ^ 1)
            for f, ref in enumerate((one_ref, two_ref)):
                for i, x in enumerate(cells):
                    base, core = stencil(lambda x: ref[x], (lambda: lo_ref[f], lambda: hi_ref[f]), x, xcount)
                    base_ref[f, i] = base + core * growth

    outs = []
    for cells in chunks:
        outs.append(pltpu.VMEM((2, 2 * len(cells) * ycount, owned), F32))
        outs.append(pltpu.VMEM((2, len(cells), ycount, owned), F32))
    args = [me, *owns, *sibs, one, two, lo, hi, kernels, growth]
    flat = call(body, "before_first", args, outs, specs=[pl.BlockSpec(memory_space=pltpu.SMEM)] + [SPEC] * (len(args) - 1), gflop=20.0)
    return [flat[2 * c:2 * c + 2] for c in range(count)]


def first_node(me, far, farsib, part, base, one, two, initial, kernels, death, cells, with_faces):
    xcount, ycount, owned = one.shape
    rows = len(cells) * ycount

    def body(me_ref, far_ref, farsib_ref, part_ref, base_ref, one_ref, two_ref, init_ref, k_ref, d_ref, *refs):
        new_ref, rounded_ref, rest_ref = refs[:3]
        sums = refs[-1]
        me = me_ref[0]
        near = far_ref[...].reshape(2 * rows, owned)
        other = farsib_ref[...].reshape(2 * rows, owned)
        for k in range(2):
            sums[k] = (part_ref[k] + half_dot(near, other, k_ref, k, me ^ 2, me ^ 3)).astype(BF16)
        death = d_ref[...]
        inv_one = 1.0 / (1.0 + FIRST * death)
        inv_two = 1.0 / (1.0 + SECOND * death)
        for i, x in enumerate(cells):
            cores = (one_ref[x], two_ref[x])
            e = []
            for f in range(2):
                at = pl.ds(f * rows + i * ycount, ycount)
                e.append(base_ref[f, i] - cores[f] * sums[0, at, :].astype(F32) + sums[1, at, :].astype(F32))
            full_one = e[0] - death * cores[0]
            full_two = e[1] - death * cores[1]
            new = (
                init_ref[x]
                + FIRST * death * cores[0]
                + STEP_SIZE * (5.0 / 12.0 * full_one - 1.0 / 12.0 * full_two)
            ) * inv_one
            new_ref[i] = new
            rounded = new.astype(BF16)
            rounded_ref[0, i * ycount:(i + 1) * ycount, :] = rounded
            if with_faces and x == 0:
                refs[3][0] = rounded
            if with_faces and x == xcount - 1:
                refs[4][0] = rounded
            rest_ref[i] = (
                new - SECOND * e[0] + SECOND * death * cores[1] + STEP_SIZE / 3.0 * (full_one + full_two)
            ) * inv_two

    outs = [
        pltpu.VMEM((len(cells), ycount, owned), F32),
        pltpu.VMEM((1, rows, owned), BF16),
        pltpu.VMEM((len(cells), ycount, owned), F32),
    ]
    if with_faces:
        outs += [pltpu.VMEM((1, ycount, owned), BF16)] * 2
    args = [me, far, farsib, part, base, one, two, initial, kernels, death]
    return call(
        body, "first_node", args, outs, scratch=[pltpu.VMEM((2, 2 * rows, owned), BF16)],
        specs=[pl.BlockSpec(memory_space=pltpu.SMEM)] + [SPEC] * (len(args) - 1), gflop=0.0,
    )


def near_part(me, own, sib, kernels):
    rows, owned = own.shape[1:]

    def body(me_ref, own_ref, sib_ref, k_ref, part_ref):
        me = me_ref[0]
        near, other = rows_of([own_ref], owned), rows_of([sib_ref], owned)
        for k in range(2):
            part_ref[k] = half_dot(near, other, k_ref, k, me, me ^ 1)

    return call(
        body, "near_part", [me, own, sib, kernels], [pltpu.VMEM((2, rows, owned), F32)],
        specs=[pl.BlockSpec(memory_space=pltpu.SMEM)] + [SPEC] * 3, gflop=20.0,
    )[0]


def before_second(me, own, sib, news, rests, lo, hi, kernels, growth, death, chunks):
    _, ycount, owned = news[0].shape
    xcount = sum(len(cells) for cells in chunks)
    count = len(chunks)
    rows = own.shape[1]
    place = {x: (c, i) for c, cells in enumerate(chunks) for i, x in enumerate(cells)}

    def body(me_ref, own_ref, sib_ref, *refs):
        new_refs, rest_refs = refs[:count], refs[count:2 * count]
        lo_ref, hi_ref, k_ref, g_ref, d_ref, whole_ref, part_ref = refs[2 * count:2 * count + 7]
        base_refs, sems = refs[2 * count + 7:-1], refs[-1]
        copies = [
            pltpu.make_async_copy(new_refs[c].at[i], whole_ref.at[x], sems.at[x]) for x, (c, i) in place.items()
        ]
        for copy in copies:
            copy.start()
        me = me_ref[0]
        growth = g_ref[...]
        factor = SECOND / (1.0 + SECOND * d_ref[...])

        def get(x):
            c, i = place[x]
            return new_refs[c][i]

        near, other = rows_of([own_ref], owned), rows_of([sib_ref], owned)
        for k in range(2):
            part_ref[k] = half_dot(near, other, k_ref, k, me, me ^ 1)
        for c, cells in enumerate(chunks):
            for i, x in enumerate(cells):
                base, core = stencil(get, (lambda: lo_ref[0], lambda: hi_ref[0]), x, xcount)
                base_refs[c][i] = rest_refs[c][i] + factor * (base + core * growth)
        for copy in copies:
            copy.wait()

    outs = [jax.ShapeDtypeStruct((xcount, ycount, owned), F32), pltpu.VMEM((2, rows, owned), F32)]
    outs += [pltpu.VMEM((len(cells), ycount, owned), F32) for cells in chunks]
    args = [me, own, sib, *news, *rests, lo, hi, kernels, growth, death]
    return call(
        body, "before_second", args, outs, scratch=[pltpu.SemaphoreType.DMA((xcount,))],
        specs=[pl.BlockSpec(memory_space=pltpu.SMEM)] + [SPEC] * (len(args) - 1),
        out_specs=[ANYWHERE] + [SPEC] * (len(outs) - 1), gflop=20.0,
    )


def second_node(me, far, farsib, part, base, new, kernels, death, cells, xcount, previous=None):
    _, ycount, owned = new.shape
    rows = len(cells) * ycount
    others = previous[1] if previous else []

    def body(me_ref, far_ref, farsib_ref, part_ref, base_ref, new_ref, k_ref, d_ref, *refs):
        if previous:
            prev_ref, out_ref, sums, held, sems = refs
            copies = [pltpu.make_async_copy(prev_ref.at[i], out_ref.at[x], sems.at[x]) for i, x in enumerate(others)]
            for copy in copies:
                copy.start()
        else:
            out_ref, sums = refs
        me = me_ref[0]
        near = far_ref[...].reshape(rows, owned)
        other = farsib_ref[...].reshape(rows, owned)
        for k in range(2):
            sums[k] = (part_ref[k] + half_dot(near, other, k_ref, k, me ^ 2, me ^ 3)).astype(BF16)
        factor = SECOND / (1.0 + SECOND * d_ref[...])
        for i, x in enumerate(cells):
            at = pl.ds(i * ycount, ycount)
            value = base_ref[i] + factor * (sums[1, at, :].astype(F32) - new_ref[i] * sums[0, at, :].astype(F32))
            if previous:
                held[i] = value
                copies.append(pltpu.make_async_copy(held.at[i], out_ref.at[x], sems.at[x]))
                copies[-1].start()
            else:
                out_ref[i] = value
        if previous:
            for copy in copies:
                copy.wait()

    args = [me, far, farsib, part, base, new, kernels, death]
    specs = [pl.BlockSpec(memory_space=pltpu.SMEM)] + [SPEC] * (len(args) - 1)
    scratch = [pltpu.VMEM((2, rows, owned), BF16)]
    if previous:
        args.append(previous[0])
        specs.append(SPEC)
        outs = [jax.ShapeDtypeStruct((xcount, ycount, owned), F32)]
        scratch += [pltpu.VMEM((len(cells), ycount, owned), F32), pltpu.SemaphoreType.DMA((xcount,))]
    else:
        outs = [pltpu.VMEM((len(cells), ycount, owned), F32)]
    return call(
        body, "second_node", args, outs, scratch=scratch, specs=specs,
        out_specs=[ANYWHERE] if previous else None, gflop=0.0,
    )[0]


def local(initial, section_one, section_two, kernels, growth, death_rate):
    xcount, ycount, owned = section_one.shape
    traits = lax.axis_size("trait")
    gcount = lax.axis_size("gx")
    me = lax.axis_index("trait").reshape(1)
    growth = growth.reshape(1, owned)
    death = death_rate.reshape(1, owned)
    chunks = chunks_of(xcount)

    def to_sibling(v):
        return lax.ppermute(v, "trait", [(i, i ^ 1) for i in range(traits)])

    def to_far(v):
        return lax.ppermute(v, "trait", [(i, i ^ 2) for i in range(traits)])

    def faces(head, tail):
        lo = lax.ppermute(tail, "gx", [(i, (i + 1) % gcount) for i in range(gcount)])
        hi = lax.ppermute(head, "gx", [((i + 1) % gcount, i) for i in range(gcount)])
        return lo, hi

    own_a, head, tail = round_chunk((section_one, section_two), chunks[0], True)
    far_a = to_far(own_a)
    own_b = round_chunk((after(section_one, own_a), section_two), chunks[1], False)[0]
    far_b = to_far(own_b)
    head, tail, near_a, near_b = lax.optimization_barrier((head, tail, own_a, own_b))
    lo, hi = faces(head, tail)
    sib_a = to_sibling(near_a)
    sib_b = to_sibling(after(near_b, lo))
    (part_a, base_a), (part_b, base_b) = before_first(
        me, (own_a, own_b), (sib_a, sib_b), section_one, section_two, lo, hi, kernels, growth, chunks
    )

    farsib_a = to_sibling(far_a)
    new_a, rounded_a, rest_a, new_head, new_tail = first_node(
        me, far_a, farsib_a, part_a, base_a, section_one, section_two, initial, kernels, death, chunks[0], True
    )
    nfar_a = to_far(rounded_a)
    new_lo, new_hi = faces(new_head, new_tail)
    nsib_a = to_sibling(rounded_a)
    npart_a = near_part(me, after(rounded_a, new_lo, new_hi), nsib_a, kernels)

    far_b = after(far_b, rounded_a)
    farsib_b = to_sibling(far_b)
    new_b, rounded_b, rest_b = first_node(
        me, far_b, farsib_b, after(part_b, npart_a), base_b, section_one, section_two, initial, kernels, death,
        chunks[1], False,
    )
    nfar_b = to_far(rounded_b)
    nsib_b = to_sibling(rounded_b)
    nfar_a = after(nfar_a, rounded_b)
    nfarsib_a = to_sibling(nfar_a)
    new_one, npart_b, nbase_a, nbase_b = before_second(
        me, rounded_b, nsib_b, (new_a, new_b), (rest_a, rest_b), new_lo, new_hi, kernels, growth, death, chunks
    )
    two_a = second_node(me, nfar_a, nfarsib_a, npart_a, nbase_a, new_a, kernels, death, chunks[0], xcount)
    nfar_b = after(nfar_b, two_a)
    nfarsib_b = to_sibling(nfar_b)
    new_two = second_node(
        me, nfar_b, nfarsib_b, npart_b, nbase_b, new_b, kernels, death, chunks[1], xcount, (two_a, chunks[0])
    )
    return new_one, new_two


def solution(mesh):
    in_specs = (
        P("gx", None, "trait"),
        P("gx", None, "trait"),
        P("gx", None, "trait"),
        P(None, None, "trait"),
        P("trait"),
        P("trait"),
    )
    out_specs = (P("gx", None, "trait"), P("gx", None, "trait"))
    return jax.shard_map(local, mesh=mesh, in_specs=in_specs, out_specs=out_specs, check_vma=False)
```

```python
import jax
import jax.numpy as jnp
from jax import lax
from jax.experimental import pallas as pl
from jax.experimental.pallas import tpu as pltpu
from jax.sharding import PartitionSpec as P

DIFFUSION = 0.25
STEP_SIZE = 0.5
FIRST = STEP_SIZE / 3.0
SECOND = 2.0 * STEP_SIZE / 3.0
F32 = jnp.float32
BF16 = jnp.bfloat16
VMEM_LIMIT = 20 * 1024 * 1024
SPEC = pl.BlockSpec(memory_space=pltpu.VMEM)
ANYWHERE = pl.BlockSpec(memory_space=pl.ANY)
FROM_HBM = pl.BlockSpec(memory_space=pltpu.HBM)


def chunks_of(xcount):
    last = max(1, 3 * xcount // 8)
    start = (xcount - last + 1) // 2
    middle = list(range(start, start + last))
    return [x for x in range(xcount) if x not in middle], middle


def after(value, *others):
    return lax.optimization_barrier((value, *others))[0]


def call(body, name, args, outs, scratch=(), specs=None, out_specs=None, gflop=0.0):
    specs = specs or [SPEC] * len(args)
    space = {id(SPEC): pltpu.VMEM, id(FROM_HBM): pltpu.HBM}
    args = [
        pltpu.with_memory_space_constraint(a, space[id(s)]) if id(s) in space else a for a, s in zip(args, specs)
    ]
    return pl.pallas_call(
        body,
        out_shape=outs,
        in_specs=specs,
        out_specs=out_specs or [SPEC] * len(outs),
        scratch_shapes=list(scratch),
        compiler_params=pltpu.CompilerParams(vmem_limit_bytes=VMEM_LIMIT),
        cost_estimate=pl.CostEstimate(flops=int(gflop * 1e9), bytes_accessed=0, transcendentals=0),
        name=name,
    )(*args)


def rows_of(refs, owned):
    return jnp.concatenate([r[...].reshape(-1, owned) for r in refs], axis=0)


def round_chunk(fields, cells, with_faces):
    xcount, ycount, owned = fields[0].shape
    count = len(fields)

    def body(*refs):
        field_refs = refs[:count]
        out = refs[count]
        held, sems = refs[-2:]
        copies = []
        for f in range(count):
            for i, x in enumerate(cells):
                copies.append(pltpu.make_async_copy(field_refs[f].at[x], held.at[f, i], sems.at[f, i]))
                copies[-1].start()
        for f in range(count):
            for i, x in enumerate(cells):
                copies[f * len(cells) + i].wait()
                value = held[f, i].astype(BF16)
                out[f, i * ycount:(i + 1) * ycount, :] = value
                if with_faces and x == 0:
                    refs[count + 1][f] = value
                if with_faces and x == xcount - 1:
                    refs[count + 2][f] = value

    outs = [pltpu.VMEM((count, len(cells) * ycount, owned), BF16)]
    if with_faces:
        outs += [pltpu.VMEM((count, ycount, owned), BF16)] * 2
    return call(
        body, "round_chunk", fields, outs,
        scratch=[pltpu.VMEM((count, len(cells), ycount, owned), F32), pltpu.SemaphoreType.DMA((count, len(cells)))],
        specs=[FROM_HBM] * count, gflop=0.0,
    )


def blocks_dot(blocks, kernels_ref, k, owners):
    depth = blocks[0].shape[-1]
    lhs = jnp.concatenate(blocks, axis=-1)
    rhs = jnp.concatenate(
        [kernels_ref[k, pl.ds(pl.multiple_of(o * depth, depth), depth), :] for o in owners], axis=0
    )
    return jnp.dot(lhs, rhs, preferred_element_type=F32)


def stencil(get, faces, x, xcount):
    core = get(x)
    before = get(x - 1) if x > 0 else faces[0]().astype(F32)
    behind = get(x + 1) if x < xcount - 1 else faces[1]().astype(F32)
    around = before + behind + pltpu.roll(core, 1, 0) + pltpu.roll(core, core.shape[0] - 1, 0)
    return DIFFUSION * around - 2.0 * core, core


def before_first(me, owns, one, two, lo, hi, kernels, growth, chunks):
    xcount, ycount, owned = one.shape
    count = len(chunks)

    def body(me_ref, *refs):
        own_refs = refs[:count]
        one_ref, two_ref, lo_ref, hi_ref, k_ref, g_ref = refs[count:count + 6]
        outs = refs[count + 6:]
        me = me_ref[0]
        growth = g_ref[...]
        for c, cells in enumerate(chunks):
            for k in range(2):
                outs[c][k] = blocks_dot([rows_of([own_refs[c]], owned)], k_ref, k, (me,))
            for f, ref in enumerate((one_ref, two_ref)):
                for i, x in enumerate(cells):
                    base, core = stencil(lambda x: ref[x], (lambda: lo_ref[f], lambda: hi_ref[f]), x, xcount)
                    outs[count + c][f, i] = base + core * growth

    outs = [pltpu.VMEM((2, 2 * len(cells) * ycount, owned), F32) for cells in chunks]
    outs += [pltpu.VMEM((2, len(cells), ycount, owned), F32) for cells in chunks]
    args = [me, *owns, one, two, lo, hi, kernels, growth]
    flat = call(
        body, "before_first", args, outs,
        specs=[pl.BlockSpec(memory_space=pltpu.SMEM)] + [SPEC] * (len(args) - 1), gflop=0.0,
    )
    return flat[:count], flat[count:]


def sibling_part(me, parts, sibs, kernels):
    owned = sibs[0].shape[-1]
    count = len(parts)

    def body(me_ref, *refs):
        part_refs, sib_refs, k_ref, outs = refs[:count], refs[count:2 * count], refs[2 * count], refs[2 * count + 1:]
        me = me_ref[0]
        for part_ref, sib_ref, out_ref in zip(part_refs, sib_refs, outs):
            for k in range(2):
                out_ref[k] = part_ref[k] + blocks_dot([rows_of([sib_ref], owned)], k_ref, k, (me ^ 1,))

    args = [me, *parts, *sibs, kernels]
    return call(
        body, "sibling_part", args, [pltpu.VMEM(p.shape, F32) for p in parts],
        specs=[pl.BlockSpec(memory_space=pltpu.SMEM)] + [SPEC] * (len(args) - 1), gflop=20.0,
    )


def first_node(me, far, farsib, part, base, one, two, initial, kernels, death, cells, with_faces):
    xcount, ycount, owned = one.shape
    rows = len(cells) * ycount

    count = len(far)

    def body(me_ref, *refs):
        far_refs, farsib_refs = refs[:count], refs[count:2 * count]
        part_ref, base_ref, one_ref, two_ref, init_ref, k_ref, d_ref = refs[2 * count:2 * count + 7]
        refs = refs[2 * count + 7:]
        new_ref, rounded_ref, rest_ref = refs[:3]
        sums = refs[-1]
        me = me_ref[0]
        blocks = [rows_of(far_refs, owned), rows_of(farsib_refs, owned)]
        for k in range(2):
            sums[k] = (part_ref[k] + blocks_dot(blocks, k_ref, k, (me ^ 2, me ^ 3))).astype(BF16)
        death = d_ref[...]
        inv_one = 1.0 / (1.0 + FIRST * death)
        inv_two = 1.0 / (1.0 + SECOND * death)
        for i, x in enumerate(cells):
            cores = (one_ref[x], two_ref[x])
            e = []
            for f in range(2):
                at = pl.ds(f * rows + i * ycount, ycount)
                e.append(base_ref[f, i] - cores[f] * sums[0, at, :].astype(F32) + sums[1, at, :].astype(F32))
            full_one = e[0] - death * cores[0]
            full_two = e[1] - death * cores[1]
            new = (
                init_ref[x]
                + FIRST * death * cores[0]
                + STEP_SIZE * (5.0 / 12.0 * full_one - 1.0 / 12.0 * full_two)
            ) * inv_one
            new_ref[i] = new
            rounded = new.astype(BF16)
            rounded_ref[0, i * ycount:(i + 1) * ycount, :] = rounded
            if with_faces and x == 0:
                refs[3][0] = rounded
            if with_faces and x == xcount - 1:
                refs[4][0] = rounded
            rest_ref[i] = (
                new - SECOND * e[0] + SECOND * death * cores[1] + STEP_SIZE / 3.0 * (full_one + full_two)
            ) * inv_two

    outs = [
        pltpu.VMEM((len(cells), ycount, owned), F32),
        pltpu.VMEM((1, rows, owned), BF16),
        pltpu.VMEM((len(cells), ycount, owned), F32),
    ]
    if with_faces:
        outs += [pltpu.VMEM((1, ycount, owned), BF16)] * 2
    args = [me, *far, *farsib, part, base, one, two, initial, kernels, death]
    return call(
        body, "first_node", args, outs, scratch=[pltpu.VMEM((2, 2 * rows, owned), BF16)],
        specs=[pl.BlockSpec(memory_space=pltpu.SMEM)] + [SPEC] * (len(args) - 1), gflop=0.0,
    )


def own_part(me, own, kernels):
    rows, owned = own.shape[1:]

    def body(me_ref, own_ref, k_ref, part_ref):
        me = me_ref[0]
        for k in range(2):
            part_ref[k] = blocks_dot([rows_of([own_ref], owned)], k_ref, k, (me,))

    return call(
        body, "own_part", [me, own, kernels], [pltpu.VMEM((2, rows, owned), F32)],
        specs=[pl.BlockSpec(memory_space=pltpu.SMEM)] + [SPEC] * 2, gflop=20.0,
    )[0]


def before_second(me, owned_a, sib_a, own, sib, news, rests, lo, hi, kernels, growth, death, chunks):
    _, ycount, owned = news[0].shape
    xcount = sum(len(cells) for cells in chunks)
    count = len(chunks)
    place = {x: (c, i) for c, cells in enumerate(chunks) for i, x in enumerate(cells)}

    def body(me_ref, owned_ref, sib_a_ref, own_ref, sib_ref, *refs):
        new_refs, rest_refs = refs[:count], refs[count:2 * count]
        lo_ref, hi_ref, k_ref, g_ref, d_ref, whole_ref, part_a_ref, part_b_ref = refs[2 * count:2 * count + 8]
        base_refs, sems = refs[2 * count + 8:-1], refs[-1]
        copies = [
            pltpu.make_async_copy(new_refs[c].at[i], whole_ref.at[x], sems.at[x]) for x, (c, i) in place.items()
        ]
        for copy in copies:
            copy.start()
        me = me_ref[0]
        growth = g_ref[...]
        factor = SECOND / (1.0 + SECOND * d_ref[...])

        def get(x):
            c, i = place[x]
            return new_refs[c][i]

        blocks = [rows_of([own_ref], owned), rows_of([sib_ref], owned)]
        for k in range(2):
            part_a_ref[k] = owned_ref[k] + blocks_dot([rows_of([sib_a_ref], owned)], k_ref, k, (me ^ 1,))
            part_b_ref[k] = blocks_dot(blocks, k_ref, k, (me, me ^ 1))
        for c, cells in enumerate(chunks):
            for i, x in enumerate(cells):
                base, core = stencil(get, (lambda: lo_ref[0], lambda: hi_ref[0]), x, xcount)
                base_refs[c][i] = rest_refs[c][i] + factor * (base + core * growth)
        for copy in copies:
            copy.wait()

    outs = [jax.ShapeDtypeStruct((xcount, ycount, owned), F32)]
    outs += [pltpu.VMEM((2, len(cells) * ycount, owned), F32) for cells in chunks]
    outs += [pltpu.VMEM((len(cells), ycount, owned), F32) for cells in chunks]
    args = [me, owned_a, sib_a, own, sib, *news, *rests, lo, hi, kernels, growth, death]
    return call(
        body, "before_second", args, outs, scratch=[pltpu.SemaphoreType.DMA((xcount,))],
        specs=[pl.BlockSpec(memory_space=pltpu.SMEM)] + [SPEC] * (len(args) - 1),
        out_specs=[ANYWHERE] + [SPEC] * (len(outs) - 1), gflop=20.0,
    )


def second_node(me, far, farsib, part, base, new, kernels, death, cells, xcount, previous=None):
    _, ycount, owned = new.shape
    rows = len(cells) * ycount
    others = previous[1] if previous else []

    def body(me_ref, far_ref, farsib_ref, part_ref, base_ref, new_ref, k_ref, d_ref, *refs):
        if previous:
            prev_ref, out_ref, sums, held, sems = refs
            copies = [pltpu.make_async_copy(prev_ref.at[i], out_ref.at[x], sems.at[x]) for i, x in enumerate(others)]
            for copy in copies:
                copy.start()
        else:
            out_ref, sums = refs
        me = me_ref[0]
        blocks = [rows_of([far_ref], owned), rows_of([farsib_ref], owned)]
        for k in range(2):
            sums[k] = (part_ref[k] + blocks_dot(blocks, k_ref, k, (me ^ 2, me ^ 3))).astype(BF16)
        factor = SECOND / (1.0 + SECOND * d_ref[...])
        for i, x in enumerate(cells):
            at = pl.ds(i * ycount, ycount)
            value = base_ref[i] + factor * (sums[1, at, :].astype(F32) - new_ref[i] * sums[0, at, :].astype(F32))
            if previous:
                held[i] = value
                copies.append(pltpu.make_async_copy(held.at[i], out_ref.at[x], sems.at[x]))
                copies[-1].start()
            else:
                out_ref[i] = value
        if previous:
            for copy in copies:
                copy.wait()

    args = [me, far, farsib, part, base, new, kernels, death]
    specs = [pl.BlockSpec(memory_space=pltpu.SMEM)] + [SPEC] * (len(args) - 1)
    scratch = [pltpu.VMEM((2, rows, owned), BF16)]
    if previous:
        args.append(previous[0])
        specs.append(SPEC)
        outs = [jax.ShapeDtypeStruct((xcount, ycount, owned), F32)]
        scratch += [pltpu.VMEM((len(cells), ycount, owned), F32), pltpu.SemaphoreType.DMA((xcount,))]
    else:
        outs = [pltpu.VMEM((len(cells), ycount, owned), F32)]
    return call(
        body, "second_node", args, outs, scratch=scratch, specs=specs,
        out_specs=[ANYWHERE] if previous else None, gflop=0.0,
    )[0]


def local(initial, section_one, section_two, kernels, growth, death_rate):
    xcount, ycount, owned = section_one.shape
    traits = lax.axis_size("trait")
    gcount = lax.axis_size("gx")
    me = lax.axis_index("trait").reshape(1)
    growth = growth.reshape(1, owned)
    death = death_rate.reshape(1, owned)
    chunks = chunks_of(xcount)

    def to_sibling(v):
        return lax.ppermute(v, "trait", [(i, i ^ 1) for i in range(traits)])

    def to_far(v):
        return lax.ppermute(v, "trait", [(i, i ^ 2) for i in range(traits)])

    def faces(head, tail):
        lo = lax.ppermute(tail, "gx", [(i, (i + 1) % gcount) for i in range(gcount)])
        hi = lax.ppermute(head, "gx", [((i + 1) % gcount, i) for i in range(gcount)])
        return lo, hi

    own_a, head, tail = round_chunk((section_one, section_two), chunks[0], True)
    far_a = to_far(own_a)
    own_b = round_chunk((after(section_one, own_a), section_two), chunks[1], False)[0]
    far_b = to_far(own_b)
    head, tail = lax.optimization_barrier((head, tail, own_b))[:2]
    lo, hi = faces(head, tail)
    (part_a, part_b), (base_a, base_b) = before_first(
        me, (own_a, own_b), section_one, section_two, lo, hi, kernels, growth, chunks
    )
    sib_a = to_sibling(after(own_a, own_b))
    sib_b = to_sibling(own_b)
    far_a = after(far_a, part_a)
    farsib_a = to_sibling(far_a)
    part_a, part_b = sibling_part(me, (part_a, part_b), (sib_a, sib_b), kernels)
    new_a, rounded_a, rest_a, new_head, new_tail = first_node(
        me, [far_a], [farsib_a], part_a, base_a, section_one, section_two, initial, kernels, death, chunks[0], True,
    )
    nfar_a = to_far(rounded_a)
    new_lo, new_hi = faces(new_head, new_tail)
    nsib_a = to_sibling(rounded_a)
    npart_a = own_part(me, rounded_a, kernels)

    far_b = after(far_b, rounded_a)
    farsib_b = to_sibling(far_b)
    new_b, rounded_b, rest_b = first_node(
        me, [far_b], [farsib_b], after(part_b, npart_a, new_lo, new_hi), base_b, section_one, section_two, initial, kernels, death,
        chunks[1], False,
    )
    nfar_b = to_far(rounded_b)
    nsib_b = to_sibling(rounded_b)
    nfar_a = after(nfar_a, rounded_b)
    nfarsib_a = to_sibling(nfar_a)
    new_one, npart_a, npart_b, nbase_a, nbase_b = before_second(
        me, npart_a, nsib_a, rounded_b, nsib_b, (new_a, new_b), (rest_a, rest_b), new_lo, new_hi, kernels, growth,
        death, chunks,
    )
    two_a = second_node(me, nfar_a, nfarsib_a, npart_a, nbase_a, new_a, kernels, death, chunks[0], xcount)
    nfar_b = after(nfar_b, two_a)
    nfarsib_b = to_sibling(nfar_b)
    new_two = second_node(
        me, nfar_b, nfarsib_b, npart_b, nbase_b, new_b, kernels, death, chunks[1], xcount, (two_a, chunks[0])
    )
    return new_one, new_two


def solution(mesh):
    in_specs = (
        P("gx", None, "trait"),
        P("gx", None, "trait"),
        P("gx", None, "trait"),
        P(None, None, "trait"),
        P("trait"),
        P("trait"),
    )
    out_specs = (P("gx", None, "trait"), P("gx", None, "trait"))
    return jax.shard_map(local, mesh=mesh, in_specs=in_specs, out_specs=out_specs, check_vma=False)
```

```python
import jax
import jax.numpy as jnp
from jax import lax
from jax.experimental import pallas as pl
from jax.experimental.pallas import tpu as pltpu
from jax.sharding import PartitionSpec as P

DIFFUSION = 0.25
STEP_SIZE = 0.5
FIRST = STEP_SIZE / 3.0
SECOND = 2.0 * STEP_SIZE / 3.0
F32 = jnp.float32
BF16 = jnp.bfloat16
VMEM_LIMIT = 20 * 1024 * 1024
SPEC = pl.BlockSpec(memory_space=pltpu.VMEM)
ANYWHERE = pl.BlockSpec(memory_space=pl.ANY)
FROM_HBM = pl.BlockSpec(memory_space=pltpu.HBM)


def chunks_of(xcount):
    last = max(1, 3 * xcount // 8)
    start = (xcount - last + 1) // 2
    middle = list(range(start, start + last))
    return [x for x in range(xcount) if x not in middle], middle


def after(value, *others):
    return lax.optimization_barrier((value, *others))[0]


def call(body, name, args, outs, scratch=(), specs=None, out_specs=None, gflop=0.0, alias=None):
    specs = specs or [SPEC] * len(args)
    space = {id(SPEC): pltpu.VMEM, id(FROM_HBM): pltpu.HBM}
    args = [
        pltpu.with_memory_space_constraint(a, space[id(s)]) if id(s) in space else a for a, s in zip(args, specs)
    ]
    return pl.pallas_call(
        body,
        out_shape=outs,
        in_specs=specs,
        out_specs=out_specs or [SPEC] * len(outs),
        scratch_shapes=list(scratch),
        compiler_params=pltpu.CompilerParams(vmem_limit_bytes=VMEM_LIMIT),
        cost_estimate=pl.CostEstimate(flops=int(gflop * 1e9), bytes_accessed=0, transcendentals=0),
        input_output_aliases=alias or {},
        name=name,
    )(*args)


def round_chunk(fields, cells, with_faces):
    xcount, ycount, owned = fields[0].shape
    count = len(fields)

    def body(*refs):
        field_refs = refs[:count]
        out = refs[count]
        held, sems = refs[-2:]
        copies = []
        for f in range(count):
            for i, x in enumerate(cells):
                copies.append(pltpu.make_async_copy(field_refs[f].at[x], held.at[f, i], sems.at[f, i]))
                copies[-1].start()
        for f in range(count):
            for i, x in enumerate(cells):
                copies[f * len(cells) + i].wait()
                value = held[f, i].astype(BF16)
                out[f, i * ycount:(i + 1) * ycount, :] = value
                if with_faces and x == 0:
                    refs[count + 1][f] = value
                if with_faces and x == xcount - 1:
                    refs[count + 2][f] = value

    outs = [pltpu.VMEM((count, len(cells) * ycount, owned), BF16)]
    if with_faces:
        outs += [pltpu.VMEM((count, ycount, owned), BF16)] * 2
    return call(
        body, "round_chunk", fields, outs,
        scratch=[pltpu.VMEM((count, len(cells), ycount, owned), F32), pltpu.SemaphoreType.DMA((count, len(cells)))],
        specs=[FROM_HBM] * count, gflop=0.0,
    )


def blocks_dot(blocks, kernels_ref, k, owners):
    depth = blocks[0].shape[-1]
    lhs = jnp.concatenate(blocks, axis=-1)
    rhs = jnp.concatenate(
        [kernels_ref[k, pl.ds(pl.multiple_of(o * depth, depth), depth), :] for o in owners], axis=0
    )
    return jnp.dot(lhs, rhs, preferred_element_type=F32)


def along_y(core):
    return DIFFUSION * (pltpu.roll(core, 1, 0) + pltpu.roll(core, core.shape[0] - 1, 0)) - 2.0 * core


def before_first(one, two, lo, hi, growth, cells, gflop):
    xcount, ycount, owned = one.shape
    ends = [] if lo is None else [lo, hi]

    def body(one_ref, two_ref, g_ref, *refs):
        end_refs, base_ref = refs[:-1], refs[-1]
        growth = g_ref[...]
        for f, ref in enumerate((one_ref, two_ref)):
            for i, x in enumerate(cells):
                core = ref[x]
                before = ref[x - 1] if x > 0 else end_refs[0][f].astype(F32)
                behind = ref[x + 1] if x < xcount - 1 else end_refs[1][f].astype(F32)
                base_ref[f, i] = DIFFUSION * (before + behind) + along_y(core) + core * growth

    args = [one, two, growth, *ends]
    return call(
        body, "before_first", args, [pltpu.VMEM((2, len(cells), ycount, owned), F32)], gflop=gflop
    )[0]


def first_node(me, blocks, base, one, two, initial, kernels, death, cells, with_faces):
    xcount, ycount, owned = one.shape
    rows = len(cells) * ycount
    count = len(blocks)

    def body(me_ref, *refs):
        block_refs = refs[:count]
        base_ref, one_ref, two_ref, init_ref, k_ref, d_ref = refs[count:count + 6]
        refs = refs[count + 6:]
        new_ref, rounded_ref, rest_ref = refs[:3]
        sums = refs[-1]
        me = me_ref[0]
        values = [r[...].reshape(2 * rows, owned) for r in block_refs]
        for k in range(2):
            sums[k] = blocks_dot(values, k_ref, k, [me ^ j for j in range(count)]).astype(BF16)
        death = d_ref[...]
        inv_one = 1.0 / (1.0 + FIRST * death)
        inv_two = 1.0 / (1.0 + SECOND * death)
        for i, x in enumerate(cells):
            cores = (one_ref[x], two_ref[x])
            e = []
            for f in range(2):
                at = pl.ds(f * rows + i * ycount, ycount)
                e.append(base_ref[f, i] - cores[f] * sums[0, at, :].astype(F32) + sums[1, at, :].astype(F32))
            full_one = e[0] - death * cores[0]
            full_two = e[1] - death * cores[1]
            new = (
                init_ref[x]
                + FIRST * death * cores[0]
                + STEP_SIZE * (5.0 / 12.0 * full_one - 1.0 / 12.0 * full_two)
            ) * inv_one
            new_ref[i] = new
            rounded = new.astype(BF16)
            rounded_ref[0, i * ycount:(i + 1) * ycount, :] = rounded
            if with_faces and x == 0:
                refs[3][0] = rounded
            if with_faces and x == xcount - 1:
                refs[4][0] = rounded
            rest_ref[i] = (
                new - SECOND * e[0] + SECOND * death * cores[1] + STEP_SIZE / 3.0 * (full_one + full_two)
            ) * inv_two

    outs = [
        pltpu.VMEM((len(cells), ycount, owned), F32),
        pltpu.VMEM((1, rows, owned), BF16),
        pltpu.VMEM((len(cells), ycount, owned), F32),
    ]
    if with_faces:
        outs += [pltpu.VMEM((1, ycount, owned), BF16)] * 2
    args = [me, *blocks, base, one, two, initial, kernels, death]
    return call(
        body, "first_node", args, outs, scratch=[pltpu.VMEM((2, 2 * rows, owned), BF16)],
        specs=[pl.BlockSpec(memory_space=pltpu.SMEM)] + [SPEC] * (len(args) - 1), gflop=0.0,
    )


def before_second(news, rests, growth, death, chunks, c, whole, gflop):
    _, ycount, owned = news[0].shape
    xcount = sum(len(cells) for cells in chunks)
    count = len(news)
    place = {x: (n, i) for n, cells in enumerate(chunks[:count]) for i, x in enumerate(cells)}

    def body(*refs):
        new_refs, rest_ref, g_ref, d_ref = refs[:count], refs[count], refs[count + 1], refs[count + 2]
        refs = refs[count + 3:]
        base_ref = refs[0]
        copies = []
        if whole:
            whole_ref, sems = refs[1:]
            copies = [
                pltpu.make_async_copy(new_refs[n].at[i], whole_ref.at[x], sems.at[x]) for x, (n, i) in place.items()
            ]
        for copy in copies:
            copy.start()
        growth = g_ref[...]
        factor = SECOND / (1.0 + SECOND * d_ref[...])
        for i, x in enumerate(chunks[c]):
            core = new_refs[c][i]
            e = along_y(core) + core * growth
            for near in (x - 1, x + 1):
                if near in place:
                    e = e + DIFFUSION * new_refs[place[near][0]][place[near][1]]
            base_ref[i] = rest_ref[i] + factor * e
        for copy in copies:
            copy.wait()

    outs = [pltpu.VMEM((len(chunks[c]), ycount, owned), F32)]
    out_specs = [SPEC]
    scratch = []
    if whole:
        outs.append(jax.ShapeDtypeStruct((xcount, ycount, owned), F32))
        out_specs.append(ANYWHERE)
        scratch.append(pltpu.SemaphoreType.DMA((xcount,)))
    return call(
        body, "before_second", [*news, rests[c], growth, death], outs, scratch=scratch, out_specs=out_specs, gflop=gflop
    )


def second_node(me, blocks, base, new, kernels, death, cells, xcount, around=(), begun=None):
    _, ycount, owned = new.shape
    rows = len(cells) * ycount
    count = len(blocks)

    def body(me_ref, *refs):
        block_refs = refs[:count]
        base_ref, new_ref, k_ref, d_ref = refs[count:count + 4]
        around_refs = refs[count + 4:count + 4 + len(around)]
        out_ref, sums, held, sems = refs[-4:]
        me = me_ref[0]
        values = [r[...].reshape(rows, owned) for r in block_refs]
        for k in range(2):
            sums[k] = blocks_dot(values, k_ref, k, [me ^ j for j in range(count)]).astype(BF16)
        factor = SECOND / (1.0 + SECOND * d_ref[...])
        copies = []
        for i, x in enumerate(cells):
            at = pl.ds(i * ycount, ycount)
            e = sums[1, at, :].astype(F32) - new_ref[i] * sums[0, at, :].astype(F32)
            for (cell, _, j), ref in zip(around, around_refs):
                if cell == x:
                    e = e + DIFFUSION * ref[j].astype(F32)
            held[i] = base_ref[i] + factor * e
            copies.append(pltpu.make_async_copy(held.at[i], out_ref.at[x], sems.at[i]))
            copies[-1].start()
        for copy in copies:
            copy.wait()

    args = [me, *blocks, base, new, kernels, death, *[a[1] for a in around]]
    specs = [pl.BlockSpec(memory_space=pltpu.SMEM)] + [SPEC] * (len(args) - 1)
    alias = {}
    if begun is not None:
        alias = {len(args): 0}
        args.append(begun)
        specs.append(FROM_HBM)
    return call(
        body, "second_node", args, [jax.ShapeDtypeStruct((xcount, ycount, owned), F32)],
        scratch=[
            pltpu.VMEM((2, rows, owned), BF16),
            pltpu.VMEM((len(cells), ycount, owned), F32),
            pltpu.SemaphoreType.DMA((len(cells),)),
        ],
        specs=specs, out_specs=[ANYWHERE], gflop=0.0, alias=alias,
    )[0]


def local(initial, section_one, section_two, kernels, growth, death_rate):
    xcount, ycount, owned = section_one.shape
    traits = lax.axis_size("trait")
    gcount = lax.axis_size("gx")
    me = lax.axis_index("trait").reshape(1)
    growth = growth.reshape(1, owned)
    death = death_rate.reshape(1, owned)
    chunks = chunks_of(xcount)

    def to_sibling(v):
        return lax.ppermute(v, "trait", [(i, i ^ 1) for i in range(traits)])

    def to_far(v):
        return lax.ppermute(v, "trait", [(i, i ^ 2) for i in range(traits)])

    def faces(head, tail):
        lo = lax.ppermute(tail, "gx", [(i, (i + 1) % gcount) for i in range(gcount)])
        hi = lax.ppermute(head, "gx", [((i + 1) % gcount, i) for i in range(gcount)])
        return lo, hi

    own_a, head, tail = round_chunk((section_one, section_two), chunks[0], True)
    far_a = to_far(own_a)
    own_b = round_chunk((after(section_one, own_a), section_two), chunks[1], False)[0]
    far_b = to_far(own_b)
    head, tail, kernels = lax.optimization_barrier((head, tail, kernels, own_b))[:3]
    lo, hi = faces(head, tail)
    base_a = before_first(section_one, section_two, lo, hi, growth, chunks[0], 0.0)
    base_b = before_first(section_one, section_two, None, None, growth, chunks[1], 20.0)
    sib_a = to_sibling(after(own_a, own_b))
    sib_b = to_sibling(own_b)
    far_a = after(far_a, base_a)
    farsib_a = to_sibling(far_a)
    new_a, rounded_a, rest_a, new_head, new_tail = first_node(
        me, [own_a, sib_a, far_a, farsib_a], after(base_a, base_b), section_one, section_two, initial, kernels, death,
        chunks[0], True,
    )
    nfar_a = to_far(rounded_a)
    nsib_a = to_sibling(rounded_a)
    nbase_a = before_second((new_a,), (rest_a,), growth, death, chunks, 0, False, 20.0)[0]

    far_b = after(far_b, rounded_a)
    farsib_b = to_sibling(far_b)
    new_b, rounded_b, rest_b = first_node(
        me, [own_b, sib_b, far_b, farsib_b], after(base_b, nbase_a), section_one, section_two, initial, kernels, death,
        chunks[1], False,
    )
    nfar_b = to_far(rounded_b)
    nsib_b = to_sibling(rounded_b)
    new_lo, new_hi = faces(*lax.optimization_barrier((new_head, new_tail, rounded_b))[:2])
    nfar_a = after(nfar_a, rounded_b)
    nfarsib_a = to_sibling(nfar_a)
    nbase_b, new_one = before_second((new_a, new_b), (rest_a, rest_b), growth, death, chunks, 1, True, 20.0)
    around = [(0, new_lo, 0), (xcount - 1, new_hi, 0)]
    around += [(x + d, new_b, i) for i, x in enumerate(chunks[1]) for d in (-1, 1) if x + d in chunks[0]]
    two_a = second_node(
        me, [rounded_a, nsib_a, nfar_a, nfarsib_a], after(nbase_a, nbase_b), new_a, kernels, death, chunks[0], xcount,
        around,
    )
    nfar_b = after(nfar_b, two_a)
    nfarsib_b = to_sibling(nfar_b)
    new_two = second_node(
        me, [rounded_b, nsib_b, nfar_b, nfarsib_b], nbase_b, new_b, kernels, death, chunks[1], xcount, begun=two_a
    )
    return new_one, new_two


def solution(mesh):
    in_specs = (
        P("gx", None, "trait"),
        P("gx", None, "trait"),
        P("gx", None, "trait"),
        P(None, None, "trait"),
        P("trait"),
        P("trait"),
    )
    out_specs = (P("gx", None, "trait"), P("gx", None, "trait"))
    return jax.shard_map(local, mesh=mesh, in_specs=in_specs, out_specs=out_specs, check_vma=False)
```

```python
import jax
import jax.numpy as jnp
from jax import lax
from jax.experimental import pallas as pl
from jax.experimental.pallas import tpu as pltpu
from jax.sharding import PartitionSpec as P

DIFFUSION = 0.25
STEP_SIZE = 0.5
FIRST = STEP_SIZE / 3.0
SECOND = 2.0 * STEP_SIZE / 3.0
F32 = jnp.float32
BF16 = jnp.bfloat16
VMEM_LIMIT = 20 * 1024 * 1024
SPEC = pl.BlockSpec(memory_space=pltpu.VMEM)
ANYWHERE = pl.BlockSpec(memory_space=pl.ANY)
FROM_HBM = pl.BlockSpec(memory_space=pltpu.HBM)


def chunks_of(xcount):
    last = max(1, 3 * xcount // 8)
    start = (xcount - last + 1) // 2
    middle = list(range(start, start + last))
    return [x for x in range(xcount) if x not in middle], middle


def after(value, *others):
    return lax.optimization_barrier((value, *others))[0]


def call(body, name, args, outs, scratch=(), specs=None, out_specs=None, gflop=0.0, alias=None):
    specs = specs or [SPEC] * len(args)
    space = {id(SPEC): pltpu.VMEM, id(FROM_HBM): pltpu.HBM}
    args = [
        pltpu.with_memory_space_constraint(a, space[id(s)]) if id(s) in space else a for a, s in zip(args, specs)
    ]
    return pl.pallas_call(
        body,
        out_shape=outs,
        in_specs=specs,
        out_specs=out_specs or [SPEC] * len(outs),
        scratch_shapes=list(scratch),
        compiler_params=pltpu.CompilerParams(vmem_limit_bytes=VMEM_LIMIT),
        cost_estimate=pl.CostEstimate(flops=int(gflop * 1e9), bytes_accessed=0, transcendentals=0),
        input_output_aliases=alias or {},
        name=name,
    )(*args)


def round_chunk(fields, cells, with_faces):
    xcount, ycount, owned = fields[0].shape
    count = len(fields)

    def body(*refs):
        field_refs = refs[:count]
        out = refs[count]
        held, sems = refs[-2:]
        copies = []
        for f in range(count):
            for i, x in enumerate(cells):
                copies.append(pltpu.make_async_copy(field_refs[f].at[x], held.at[f, i], sems.at[f, i]))
                copies[-1].start()
        for f in range(count):
            for i, x in enumerate(cells):
                copies[f * len(cells) + i].wait()
                value = held[f, i].astype(BF16)
                out[f, i * ycount:(i + 1) * ycount, :] = value
                if with_faces and x == 0:
                    refs[count + 1][f] = value
                if with_faces and x == xcount - 1:
                    refs[count + 2][f] = value

    outs = [pltpu.VMEM((count, len(cells) * ycount, owned), BF16)]
    if with_faces:
        outs += [pltpu.VMEM((count, ycount, owned), BF16)] * 2
    return call(
        body, "round_chunk", fields, outs,
        scratch=[pltpu.VMEM((count, len(cells), ycount, owned), F32), pltpu.SemaphoreType.DMA((count, len(cells)))],
        specs=[FROM_HBM] * count, gflop=0.0,
    )


def blocks_dot(blocks, kernels_ref, k, owners):
    depth = blocks[0].shape[-1]
    lhs = jnp.concatenate(blocks, axis=-1)
    rhs = jnp.concatenate(
        [kernels_ref[k, pl.ds(pl.multiple_of(o * depth, depth), depth), :] for o in owners], axis=0
    )
    return jnp.dot(lhs, rhs, preferred_element_type=F32)


def along_y(core):
    return DIFFUSION * (pltpu.roll(core, 1, 0) + pltpu.roll(core, core.shape[0] - 1, 0)) - 2.0 * core


def before_first(one, two, lo, hi, growth, cells, gflop):
    xcount, ycount, owned = one.shape
    ends = [] if lo is None else [lo, hi]

    def body(one_ref, two_ref, g_ref, *refs):
        end_refs, base_ref = refs[:-1], refs[-1]
        growth = g_ref[...]
        for f, ref in enumerate((one_ref, two_ref)):
            for i, x in enumerate(cells):
                core = ref[x]
                before = ref[x - 1] if x > 0 else end_refs[0][f].astype(F32)
                behind = ref[x + 1] if x < xcount - 1 else end_refs[1][f].astype(F32)
                base_ref[f, i] = DIFFUSION * (before + behind) + along_y(core) + core * growth

    args = [one, two, growth, *ends]
    return call(
        body, "before_first", args, [pltpu.VMEM((2, len(cells), ycount, owned), F32)], gflop=gflop
    )[0]


def first_node(blocks, base, one, two, initial, kernels, death, cells, with_faces):
    xcount, ycount, owned = one.shape
    rows = len(cells) * ycount
    count = len(blocks)

    def body(*refs):
        block_refs = refs[:count]
        base_ref, one_ref, two_ref, init_ref, k_ref, d_ref = refs[count:count + 6]
        refs = refs[count + 6:]
        new_ref, rounded_ref, rest_ref = refs[:3]
        sums = refs[-1]
        me = lax.axis_index("trait")
        values = [r[...].reshape(2 * rows, owned) for r in block_refs]
        for k in range(2):
            sums[k] = blocks_dot(values, k_ref, k, [me ^ j for j in range(count)]).astype(BF16)
        death = d_ref[...]
        inv_one = 1.0 / (1.0 + FIRST * death)
        inv_two = 1.0 / (1.0 + SECOND * death)
        for i, x in enumerate(cells):
            cores = (one_ref[x], two_ref[x])
            e = []
            for f in range(2):
                at = pl.ds(f * rows + i * ycount, ycount)
                e.append(base_ref[f, i] - cores[f] * sums[0, at, :].astype(F32) + sums[1, at, :].astype(F32))
            full_one = e[0] - death * cores[0]
            full_two = e[1] - death * cores[1]
            new = (
                init_ref[x]
                + FIRST * death * cores[0]
                + STEP_SIZE * (5.0 / 12.0 * full_one - 1.0 / 12.0 * full_two)
            ) * inv_one
            new_ref[i] = new
            rounded = new.astype(BF16)
            rounded_ref[0, i * ycount:(i + 1) * ycount, :] = rounded
            if with_faces and x == 0:
                refs[3][0] = rounded
            if with_faces and x == xcount - 1:
                refs[4][0] = rounded
            rest_ref[i] = (
                new - SECOND * e[0] + SECOND * death * cores[1] + STEP_SIZE / 3.0 * (full_one + full_two)
            ) * inv_two

    outs = [
        pltpu.VMEM((len(cells), ycount, owned), F32),
        pltpu.VMEM((1, rows, owned), BF16),
        pltpu.VMEM((len(cells), ycount, owned), F32),
    ]
    if with_faces:
        outs += [pltpu.VMEM((1, ycount, owned), BF16)] * 2
    args = [*blocks, base, one, two, initial, kernels, death]
    return call(
        body, "first_node", args, outs, scratch=[pltpu.VMEM((2, 2 * rows, owned), BF16)],
        gflop=0.0,
    )


def before_second(news, rests, growth, death, chunks, c, whole, gflop):
    _, ycount, owned = news[0].shape
    xcount = sum(len(cells) for cells in chunks)
    count = len(news)
    place = {x: (n, i) for n, cells in enumerate(chunks[:count]) for i, x in enumerate(cells)}

    def body(*refs):
        new_refs, rest_ref, g_ref, d_ref = refs[:count], refs[count], refs[count + 1], refs[count + 2]
        refs = refs[count + 3:]
        base_ref = refs[0]
        copies = []
        if whole:
            whole_ref, sems = refs[1:]
            copies = [
                pltpu.make_async_copy(new_refs[n].at[i], whole_ref.at[x], sems.at[x]) for x, (n, i) in place.items()
            ]
        for copy in copies:
            copy.start()
        growth = g_ref[...]
        factor = SECOND / (1.0 + SECOND * d_ref[...])
        for i, x in enumerate(chunks[c]):
            core = new_refs[c][i]
            e = along_y(core) + core * growth
            for near in (x - 1, x + 1):
                if near in place:
                    e = e + DIFFUSION * new_refs[place[near][0]][place[near][1]]
            base_ref[i] = rest_ref[i] + factor * e
        for copy in copies:
            copy.wait()

    outs = [pltpu.VMEM((len(chunks[c]), ycount, owned), F32)]
    out_specs = [SPEC]
    scratch = []
    if whole:
        outs.append(jax.ShapeDtypeStruct((xcount, ycount, owned), F32))
        out_specs.append(ANYWHERE)
        scratch.append(pltpu.SemaphoreType.DMA((xcount,)))
    return call(
        body, "before_second", [*news, rests[c], growth, death], outs, scratch=scratch, out_specs=out_specs, gflop=gflop
    )


def second_node(blocks, base, new, kernels, death, cells, xcount, around=(), begun=None):
    _, ycount, owned = new.shape
    rows = len(cells) * ycount
    count = len(blocks)

    def body(*refs):
        block_refs = refs[:count]
        base_ref, new_ref, k_ref, d_ref = refs[count:count + 4]
        around_refs = refs[count + 4:count + 4 + len(around)]
        out_ref, sums, held, sems = refs[-4:]
        me = lax.axis_index("trait")
        values = [r[...].reshape(rows, owned) for r in block_refs]
        for k in range(2):
            sums[k] = blocks_dot(values, k_ref, k, [me ^ j for j in range(count)]).astype(BF16)
        factor = SECOND / (1.0 + SECOND * d_ref[...])
        copies = []
        for i, x in enumerate(cells):
            at = pl.ds(i * ycount, ycount)
            e = sums[1, at, :].astype(F32) - new_ref[i] * sums[0, at, :].astype(F32)
            for (cell, _, j), ref in zip(around, around_refs):
                if cell == x:
                    e = e + DIFFUSION * ref[j].astype(F32)
            held[i] = base_ref[i] + factor * e
            copies.append(pltpu.make_async_copy(held.at[i], out_ref.at[x], sems.at[i]))
            copies[-1].start()
        for copy in copies:
            copy.wait()

    args = [*blocks, base, new, kernels, death, *[a[1] for a in around]]
    specs = [SPEC] * len(args)
    alias = {}
    if begun is not None:
        alias = {len(args): 0}
        args.append(begun)
        specs.append(FROM_HBM)
    return call(
        body, "second_node", args, [jax.ShapeDtypeStruct((xcount, ycount, owned), F32)],
        scratch=[
            pltpu.VMEM((2, rows, owned), BF16),
            pltpu.VMEM((len(cells), ycount, owned), F32),
            pltpu.SemaphoreType.DMA((len(cells),)),
        ],
        specs=specs, out_specs=[ANYWHERE], gflop=0.0, alias=alias,
    )[0]


def local(initial, section_one, section_two, kernels, growth, death_rate):
    xcount, ycount, owned = section_one.shape
    traits = lax.axis_size("trait")
    gcount = lax.axis_size("gx")
    growth = growth.reshape(1, owned)
    death = death_rate.reshape(1, owned)
    chunks = chunks_of(xcount)

    def to_sibling(v):
        return lax.ppermute(v, "trait", [(i, i ^ 1) for i in range(traits)])

    def to_far(v):
        return lax.ppermute(v, "trait", [(i, i ^ 2) for i in range(traits)])

    def faces(head, tail):
        lo = lax.ppermute(tail, "gx", [(i, (i + 1) % gcount) for i in range(gcount)])
        hi = lax.ppermute(head, "gx", [((i + 1) % gcount, i) for i in range(gcount)])
        return lo, hi

    own_a, head, tail = round_chunk((section_one, section_two), chunks[0], True)
    far_a = to_far(own_a)
    own_b = round_chunk((after(section_one, own_a), section_two), chunks[1], False)[0]
    far_b = to_far(own_b)
    head, tail, kernels = lax.optimization_barrier((head, tail, kernels, own_b))[:3]
    lo, hi = faces(head, tail)
    base_a = before_first(section_one, section_two, lo, hi, growth, chunks[0], 0.0)
    base_b = before_first(section_one, section_two, None, None, growth, chunks[1], 20.0)
    sib_a = to_sibling(after(own_a, own_b))
    sib_b = to_sibling(own_b)
    far_a = after(far_a, base_a)
    farsib_a = to_sibling(far_a)
    new_a, rounded_a, rest_a, new_head, new_tail = first_node(
        [own_a, sib_a, far_a, farsib_a], after(base_a, base_b), section_one, section_two, initial, kernels, death,
        chunks[0], True,
    )
    nfar_a = to_far(rounded_a)
    nsib_a = to_sibling(rounded_a)
    nbase_a = before_second((new_a,), (rest_a,), growth, death, chunks, 0, False, 20.0)[0]

    far_b = after(far_b, rounded_a)
    farsib_b = to_sibling(far_b)
    new_b, rounded_b, rest_b = first_node(
        [own_b, sib_b, far_b, farsib_b], after(base_b, nbase_a), section_one, section_two, initial, kernels, death,
        chunks[1], False,
    )
    nfar_b = to_far(rounded_b)
    nsib_b = to_sibling(rounded_b)
    new_lo, new_hi = faces(*lax.optimization_barrier((new_head, new_tail, rounded_b))[:2])
    nfar_a = after(nfar_a, rounded_b)
    nfarsib_a = to_sibling(nfar_a)
    nbase_b, new_one = before_second((new_a, new_b), (rest_a, rest_b), growth, death, chunks, 1, True, 20.0)
    around = [(0, new_lo, 0), (xcount - 1, new_hi, 0)]
    around += [(x + d, new_b, i) for i, x in enumerate(chunks[1]) for d in (-1, 1) if x + d in chunks[0]]
    two_a = second_node(
        [rounded_a, nsib_a, nfar_a, nfarsib_a], after(nbase_a, nbase_b), new_a, kernels, death, chunks[0], xcount,
        around,
    )
    nfar_b = after(nfar_b, two_a)
    nfarsib_b = to_sibling(nfar_b)
    new_two = second_node(
        [rounded_b, nsib_b, nfar_b, nfarsib_b], nbase_b, new_b, kernels, death, chunks[1], xcount, begun=two_a
    )
    return new_one, new_two


def solution(mesh):
    in_specs = (
        P("gx", None, "trait"),
        P("gx", None, "trait"),
        P("gx", None, "trait"),
        P(None, None, "trait"),
        P("trait"),
        P("trait"),
    )
    out_specs = (P("gx", None, "trait"), P("gx", None, "trait"))
    return jax.shard_map(local, mesh=mesh, in_specs=in_specs, out_specs=out_specs, check_vma=False)
```

```python
import jax
import jax.numpy as jnp
from jax import lax
from jax.experimental import pallas as pl
from jax.experimental.pallas import tpu as pltpu
from jax.sharding import PartitionSpec as P

DIFFUSION = 0.25
STEP_SIZE = 0.5
FIRST = STEP_SIZE / 3.0
SECOND = 2.0 * STEP_SIZE / 3.0
F32 = jnp.float32
BF16 = jnp.bfloat16
VMEM_LIMIT = 20 * 1024 * 1024
SPEC = pl.BlockSpec(memory_space=pltpu.VMEM)
ANYWHERE = pl.BlockSpec(memory_space=pl.ANY)
FROM_HBM = pl.BlockSpec(memory_space=pltpu.HBM)


def chunks_of(xcount):
    last = max(2, 3 * xcount // 8)
    below = last // 2
    inner = list(range(below, xcount - (last - below)))
    return inner, list(range(xcount - (last - below), xcount)) + list(range(below))


def after(value, *others):
    return lax.optimization_barrier((value, *others))[0]


def call(body, name, args, outs, scratch=(), specs=None, out_specs=None, gflop=0.0, alias=None):
    specs = specs or [SPEC] * len(args)
    space = {id(SPEC): pltpu.VMEM, id(FROM_HBM): pltpu.HBM}
    args = [
        pltpu.with_memory_space_constraint(a, space[id(s)]) if id(s) in space else a for a, s in zip(args, specs)
    ]
    return pl.pallas_call(
        body,
        out_shape=outs,
        in_specs=specs,
        out_specs=out_specs or [SPEC] * len(outs),
        scratch_shapes=list(scratch),
        compiler_params=pltpu.CompilerParams(vmem_limit_bytes=VMEM_LIMIT),
        cost_estimate=pl.CostEstimate(flops=int(gflop * 1e9), bytes_accessed=0, transcendentals=0),
        input_output_aliases=alias or {},
        name=name,
    )(*args)


def round_chunk(fields, cells, with_faces):
    xcount, ycount, owned = fields[0].shape
    count = len(fields)

    def body(*refs):
        field_refs = refs[:count]
        out = refs[count]
        held, sems = refs[-2:]
        copies = []
        for f in range(count):
            for i, x in enumerate(cells):
                copies.append(pltpu.make_async_copy(field_refs[f].at[x], held.at[f, i], sems.at[f, i]))
                copies[-1].start()
        for f in range(count):
            for i, x in enumerate(cells):
                copies[f * len(cells) + i].wait()
                value = held[f, i].astype(BF16)
                out[f, i * ycount:(i + 1) * ycount, :] = value
                if with_faces and x == 0:
                    refs[count + 1][f] = value
                if with_faces and x == xcount - 1:
                    refs[count + 2][f] = value

    outs = [pltpu.VMEM((count, len(cells) * ycount, owned), BF16)]
    if with_faces:
        outs += [pltpu.VMEM((count, ycount, owned), BF16)] * 2
    return call(
        body, "round_chunk", fields, outs,
        scratch=[pltpu.VMEM((count, len(cells), ycount, owned), F32), pltpu.SemaphoreType.DMA((count, len(cells)))],
        specs=[FROM_HBM] * count, gflop=0.0,
    )


def blocks_dot(blocks, kernels_ref, k, owners):
    depth = blocks[0].shape[-1]
    lhs = jnp.concatenate(blocks, axis=-1)
    rhs = jnp.concatenate(
        [kernels_ref[k, pl.ds(pl.multiple_of(o * depth, depth), depth), :] for o in owners], axis=0
    )
    return jnp.dot(lhs, rhs, preferred_element_type=F32)


def along_y(core):
    return DIFFUSION * (pltpu.roll(core, 1, 0) + pltpu.roll(core, core.shape[0] - 1, 0)) - 2.0 * core


def before_first(one, two, lo, hi, growth, chunks):
    xcount, ycount, owned = one.shape

    def body(one_ref, two_ref, lo_ref, hi_ref, g_ref, *outs):
        growth = g_ref[...]
        for cells, base_ref in zip(chunks, outs):
            for f, ref in enumerate((one_ref, two_ref)):
                for i, x in enumerate(cells):
                    core = ref[x]
                    before = ref[x - 1] if x > 0 else lo_ref[f].astype(F32)
                    behind = ref[x + 1] if x < xcount - 1 else hi_ref[f].astype(F32)
                    base_ref[f, i] = DIFFUSION * (before + behind) + along_y(core) + core * growth

    outs = [pltpu.VMEM((2, len(cells), ycount, owned), F32) for cells in chunks]
    return call(body, "before_first", [one, two, lo, hi, growth], outs)


def early_part(blocks, kernels):
    rows, owned = blocks[0].shape[0] * blocks[0].shape[1], blocks[0].shape[2]
    count = len(blocks)

    def body(*refs):
        block_refs, k_ref, part_ref = refs[:count], refs[count], refs[count + 1]
        me = lax.axis_index("trait")
        values = [r[...].reshape(rows, owned) for r in block_refs]
        for k in range(2):
            part_ref[k] = blocks_dot(values, k_ref, k, [me ^ j for j in range(count)])

    return call(body, "early_part", [*blocks, kernels], [pltpu.VMEM((2, rows, owned), F32)], gflop=20.0)[0]


def first_node(part, last, base, one, two, initial, kernels, death, cells, with_faces):
    xcount, ycount, owned = one.shape
    rows = len(cells) * ycount

    def body(part_ref, last_ref, base_ref, one_ref, two_ref, init_ref, k_ref, d_ref, *refs):
        new_ref, rounded_ref, rest_ref = refs[:3]
        sums = refs[-1]
        me = lax.axis_index("trait")
        for k in range(2):
            far_part = blocks_dot([last_ref[...].reshape(2 * rows, owned)], k_ref, k, [me ^ 3])
            sums[k] = (part_ref[k] + far_part).astype(BF16)
        death = d_ref[...]
        inv_one = 1.0 / (1.0 + FIRST * death)
        inv_two = 1.0 / (1.0 + SECOND * death)
        for i, x in enumerate(cells):
            cores = (one_ref[x], two_ref[x])
            e = []
            for f in range(2):
                at = pl.ds(f * rows + i * ycount, ycount)
                e.append(base_ref[f, i] - cores[f] * sums[0, at, :].astype(F32) + sums[1, at, :].astype(F32))
            full_one = e[0] - death * cores[0]
            full_two = e[1] - death * cores[1]
            new = (
                init_ref[x]
                + FIRST * death * cores[0]
                + STEP_SIZE * (5.0 / 12.0 * full_one - 1.0 / 12.0 * full_two)
            ) * inv_one
            new_ref[i] = new
            rounded = new.astype(BF16)
            rounded_ref[0, i * ycount:(i + 1) * ycount, :] = rounded
            if with_faces and x == 0:
                refs[3][0] = rounded
            if with_faces and x == xcount - 1:
                refs[4][0] = rounded
            rest_ref[i] = (
                new - SECOND * e[0] + SECOND * death * cores[1] + STEP_SIZE / 3.0 * (full_one + full_two)
            ) * inv_two

    outs = [
        pltpu.VMEM((len(cells), ycount, owned), F32),
        pltpu.VMEM((1, rows, owned), BF16),
        pltpu.VMEM((len(cells), ycount, owned), F32),
    ]
    if with_faces:
        outs += [pltpu.VMEM((1, ycount, owned), BF16)] * 2
    args = [part, last, base, one, two, initial, kernels, death]
    return call(
        body, "first_node", args, outs, scratch=[pltpu.VMEM((2, 2 * rows, owned), BF16)],
        gflop=0.0,
    )


def before_second(news, rests, growth, death, chunks):
    _, ycount, owned = news[0].shape
    xcount = sum(len(cells) for cells in chunks)
    count = len(chunks)
    place = {x: (c, i) for c, cells in enumerate(chunks) for i, x in enumerate(cells)}

    def body(*refs):
        new_refs, rest_refs = refs[:count], refs[count:2 * count]
        g_ref, d_ref, whole_ref = refs[2 * count:2 * count + 3]
        base_refs, sems = refs[2 * count + 3:-1], refs[-1]
        copies = [
            pltpu.make_async_copy(new_refs[c].at[i], whole_ref.at[x], sems.at[x]) for x, (c, i) in place.items()
        ]
        for copy in copies:
            copy.start()
        growth = g_ref[...]
        factor = SECOND / (1.0 + SECOND * d_ref[...])
        for x, (c, i) in place.items():
            core = new_refs[c][i]
            e = along_y(core) + core * growth
            for near in (x - 1, x + 1):
                if near in place:
                    e = e + DIFFUSION * new_refs[place[near][0]][place[near][1]]
            base_refs[c][i] = rest_refs[c][i] + factor * e
        for copy in copies:
            copy.wait()

    outs = [jax.ShapeDtypeStruct((xcount, ycount, owned), F32)]
    outs += [pltpu.VMEM((len(cells), ycount, owned), F32) for cells in chunks]
    return call(
        body, "before_second", [*news, *rests, growth, death], outs, scratch=[pltpu.SemaphoreType.DMA((xcount,))],
        out_specs=[ANYWHERE] + [SPEC] * count, gflop=20.0,
    )


def second_node(blocks, base, new, kernels, death, cells, xcount, part=None, faces=(), begun=None):
    _, ycount, owned = new.shape
    rows = len(cells) * ycount
    count = len(blocks)
    owners = range(4 - count, 4)

    def body(*refs):
        block_refs = refs[:count]
        base_ref, new_ref, k_ref, d_ref, *more = refs[count:-4]
        out_ref, sums, held, sems = refs[-4:]
        me = lax.axis_index("trait")
        values = [r[...].reshape(rows, owned) for r in block_refs]
        for k in range(2):
            total = blocks_dot(values, k_ref, k, [me ^ j for j in owners])
            sums[k] = (total if part is None else more[0][k] + total).astype(BF16)
        factor = SECOND / (1.0 + SECOND * d_ref[...])
        copies = []
        for i, x in enumerate(cells):
            at = pl.ds(i * ycount, ycount)
            e = sums[1, at, :].astype(F32) - new_ref[i] * sums[0, at, :].astype(F32)
            if faces and x == 0:
                e = e + DIFFUSION * more[1][0].astype(F32)
            if faces and x == xcount - 1:
                e = e + DIFFUSION * more[2][0].astype(F32)
            held[i] = base_ref[i] + factor * e
            copies.append(pltpu.make_async_copy(held.at[i], out_ref.at[x], sems.at[i]))
            copies[-1].start()
        for copy in copies:
            copy.wait()

    args = [*blocks, base, new, kernels, death]
    if part is not None:
        args += [part, *faces]
    specs = [SPEC] * len(args)
    alias = {}
    if begun is not None:
        alias = {len(args): 0}
        args.append(begun)
        specs.append(FROM_HBM)
    return call(
        body, "second_node", args, [jax.ShapeDtypeStruct((xcount, ycount, owned), F32)],
        scratch=[
            pltpu.VMEM((2, rows, owned), BF16),
            pltpu.VMEM((len(cells), ycount, owned), F32),
            pltpu.SemaphoreType.DMA((len(cells),)),
        ],
        specs=specs, out_specs=[ANYWHERE], alias=alias,
    )[0]


def local(initial, section_one, section_two, kernels, growth, death_rate):
    xcount, ycount, owned = section_one.shape
    traits = lax.axis_size("trait")
    gcount = lax.axis_size("gx")
    growth = growth.reshape(1, owned)
    death = death_rate.reshape(1, owned)
    chunks = chunks_of(xcount)

    def to_sibling(v):
        return lax.ppermute(v, "trait", [(i, i ^ 1) for i in range(traits)])

    def to_far(v):
        return lax.ppermute(v, "trait", [(i, i ^ 2) for i in range(traits)])

    def faces(head, tail):
        lo = lax.ppermute(tail, "gx", [(i, (i + 1) % gcount) for i in range(gcount)])
        hi = lax.ppermute(head, "gx", [((i + 1) % gcount, i) for i in range(gcount)])
        return lo, hi

    own_a = round_chunk((section_one, section_two), chunks[0], False)[0]
    far_a = to_far(own_a)
    own_b, head, tail = round_chunk((after(section_one, own_a), section_two), chunks[1], True)
    far_b = to_far(own_b)
    lo, hi = faces(head, tail)
    kernels = after(kernels, own_b)
    base_a, base_b = before_first(section_one, section_two, lo, hi, growth, chunks)
    sib_a = to_sibling(after(own_a, own_b))
    sib_b = to_sibling(own_b)
    far_a = after(far_a, base_a)
    farsib_a = to_sibling(far_a)
    part_a = early_part([own_a, sib_a, far_a], kernels)
    new_a, rounded_a, rest_a = first_node(
        part_a, farsib_a, base_a, section_one, section_two, initial, kernels, death, chunks[0], False
    )
    nfar_a = to_far(rounded_a)
    nsib_a = to_sibling(rounded_a)

    far_b = after(far_b, rounded_a)
    farsib_b = to_sibling(far_b)
    part_b = early_part([own_b, sib_b, far_b], kernels)
    new_b, rounded_b, rest_b, new_head, new_tail = first_node(
        part_b, farsib_b, base_b, section_one, section_two, initial, kernels, death, chunks[1], True
    )
    nfar_b = to_far(rounded_b)
    nsib_b = to_sibling(rounded_b)
    new_lo, new_hi = faces(new_head, new_tail)
    nfar_a = after(nfar_a, rounded_b)
    nfarsib_a = to_sibling(nfar_a)
    new_one, nbase_a, nbase_b = before_second((new_a, new_b), (rest_a, rest_b), growth, death, chunks)
    two_a = second_node([rounded_a, nsib_a, nfar_a, nfarsib_a], nbase_a, new_a, kernels, death, chunks[0], xcount)
    nfar_b = after(nfar_b, two_a, new_lo, new_hi)
    nfarsib_b = to_sibling(nfar_b)
    npart_b = early_part([rounded_b, nsib_b, nfar_b], kernels)
    new_two = second_node(
        [nfarsib_b], nbase_b, new_b, kernels, death, chunks[1], xcount, npart_b, (new_lo, new_hi), two_a
    )
    return new_one, new_two


def solution(mesh):
    in_specs = (
        P("gx", None, "trait"),
        P("gx", None, "trait"),
        P("gx", None, "trait"),
        P(None, None, "trait"),
        P("trait"),
        P("trait"),
    )
    out_specs = (P("gx", None, "trait"), P("gx", None, "trait"))
    return jax.shard_map(local, mesh=mesh, in_specs=in_specs, out_specs=out_specs, check_vma=False)
```

```python
import jax
import jax.numpy as jnp
from jax import lax
from jax.experimental import pallas as pl
from jax.experimental.pallas import tpu as pltpu
from jax.sharding import PartitionSpec as P

DIFFUSION = 0.25
STEP_SIZE = 0.5
FIRST = STEP_SIZE / 3.0
SECOND = 2.0 * STEP_SIZE / 3.0
F32 = jnp.float32
BF16 = jnp.bfloat16
VMEM_LIMIT = 20 * 1024 * 1024
SPEC = pl.BlockSpec(memory_space=pltpu.VMEM)
ANYWHERE = pl.BlockSpec(memory_space=pl.ANY)
FROM_HBM = pl.BlockSpec(memory_space=pltpu.HBM)


def chunks_of(xcount):
    last = max(1, 3 * xcount // 8)
    start = (xcount - last + 1) // 2
    middle = list(range(start, start + last))
    return [x for x in range(xcount) if x not in middle], middle


def after(value, *others):
    return lax.optimization_barrier((value, *others))[0]


def call(body, name, args, outs, scratch=(), specs=None, out_specs=None, gflop=0.0, alias=None):
    specs = specs or [SPEC] * len(args)
    space = {id(SPEC): pltpu.VMEM, id(FROM_HBM): pltpu.HBM}
    args = [
        pltpu.with_memory_space_constraint(a, space[id(s)]) if id(s) in space else a for a, s in zip(args, specs)
    ]
    return pl.pallas_call(
        body,
        out_shape=outs,
        in_specs=specs,
        out_specs=out_specs or [SPEC] * len(outs),
        scratch_shapes=list(scratch),
        compiler_params=pltpu.CompilerParams(vmem_limit_bytes=VMEM_LIMIT),
        cost_estimate=pl.CostEstimate(flops=int(gflop * 1e9), bytes_accessed=0, transcendentals=0),
        input_output_aliases=alias or {},
        name=name,
    )(*args)


def round_chunk(fields, cells, with_faces):
    xcount, ycount, owned = fields[0].shape
    count = len(fields)

    def body(*refs):
        field_refs = refs[:count]
        out = refs[count]
        held, sems = refs[-2:]
        copies = []
        for f in range(count):
            for i, x in enumerate(cells):
                copies.append(pltpu.make_async_copy(field_refs[f].at[x], held.at[f, i], sems.at[f, i]))
                copies[-1].start()
        for f in range(count):
            for i, x in enumerate(cells):
                copies[f * len(cells) + i].wait()
                value = held[f, i].astype(BF16)
                out[f, i * ycount:(i + 1) * ycount, :] = value
                if with_faces and x == 0:
                    refs[count + 1][f] = value
                if with_faces and x == xcount - 1:
                    refs[count + 2][f] = value

    outs = [pltpu.VMEM((count, len(cells) * ycount, owned), BF16)]
    if with_faces:
        outs += [pltpu.VMEM((count, ycount, owned), BF16)] * 2
    return call(
        body, "round_chunk", fields, outs,
        scratch=[pltpu.VMEM((count, len(cells), ycount, owned), F32), pltpu.SemaphoreType.DMA((count, len(cells)))],
        specs=[FROM_HBM] * count, gflop=0.0,
    )


def blocks_dot(blocks, kernels_ref, k, owners):
    depth = blocks[0].shape[-1]
    lhs = jnp.concatenate(blocks, axis=-1)
    rhs = jnp.concatenate(
        [kernels_ref[k, pl.ds(pl.multiple_of(o * depth, depth), depth), :] for o in owners], axis=0
    )
    return jnp.dot(lhs, rhs, preferred_element_type=F32)


def along_y(core):
    return DIFFUSION * (pltpu.roll(core, 1, 0) + pltpu.roll(core, core.shape[0] - 1, 0)) - 2.0 * core


def before_first(one, two, lo, hi, growth, chunks):
    xcount, ycount, owned = one.shape

    def body(one_ref, two_ref, lo_ref, hi_ref, g_ref, *outs):
        growth = g_ref[...]
        for cells, base_ref in zip(chunks, outs):
            for f, ref in enumerate((one_ref, two_ref)):
                for i, x in enumerate(cells):
                    core = ref[x]
                    before = ref[x - 1] if x > 0 else lo_ref[f].astype(F32)
                    behind = ref[x + 1] if x < xcount - 1 else hi_ref[f].astype(F32)
                    base_ref[f, i] = DIFFUSION * (before + behind) + along_y(core) + core * growth

    outs = [pltpu.VMEM((2, len(cells), ycount, owned), F32) for cells in chunks]
    return call(body, "before_first", [one, two, lo, hi, growth], outs)


def early_part(blocks, kernels):
    rows, owned = blocks[0].shape[0] * blocks[0].shape[1], blocks[0].shape[2]
    count = len(blocks)

    def body(*refs):
        block_refs, k_ref, part_ref = refs[:count], refs[count], refs[count + 1]
        me = lax.axis_index("trait")
        values = [r[...].reshape(rows, owned) for r in block_refs]
        for k in range(2):
            part_ref[k] = blocks_dot(values, k_ref, k, [me ^ j for j in range(count)])

    return call(body, "early_part", [*blocks, kernels], [pltpu.VMEM((2, rows, owned), F32)], gflop=20.0)[0]


def first_node(part, last, base, one, two, initial, kernels, death, cells, with_faces):
    xcount, ycount, owned = one.shape
    rows = len(cells) * ycount

    def body(part_ref, last_ref, base_ref, one_ref, two_ref, init_ref, k_ref, d_ref, *refs):
        new_ref, rounded_ref, rest_ref = refs[:3]
        sums = refs[-1]
        me = lax.axis_index("trait")
        for k in range(2):
            far_part = blocks_dot([last_ref[...].reshape(2 * rows, owned)], k_ref, k, [me ^ 3])
            sums[k] = (part_ref[k] + far_part).astype(BF16)
        death = d_ref[...]
        inv_one = 1.0 / (1.0 + FIRST * death)
        inv_two = 1.0 / (1.0 + SECOND * death)
        for i, x in enumerate(cells):
            cores = (one_ref[x], two_ref[x])
            e = []
            for f in range(2):
                at = pl.ds(f * rows + i * ycount, ycount)
                e.append(base_ref[f, i] - cores[f] * sums[0, at, :].astype(F32) + sums[1, at, :].astype(F32))
            full_one = e[0] - death * cores[0]
            full_two = e[1] - death * cores[1]
            new = (
                init_ref[x]
                + FIRST * death * cores[0]
                + STEP_SIZE * (5.0 / 12.0 * full_one - 1.0 / 12.0 * full_two)
            ) * inv_one
            new_ref[i] = new
            rounded = new.astype(BF16)
            rounded_ref[0, i * ycount:(i + 1) * ycount, :] = rounded
            if with_faces and x == 0:
                refs[3][0] = rounded
            if with_faces and x == xcount - 1:
                refs[4][0] = rounded
            rest_ref[i] = (
                new - SECOND * e[0] + SECOND * death * cores[1] + STEP_SIZE / 3.0 * (full_one + full_two)
            ) * inv_two

    outs = [
        pltpu.VMEM((len(cells), ycount, owned), F32),
        pltpu.VMEM((1, rows, owned), BF16),
        pltpu.VMEM((len(cells), ycount, owned), F32),
    ]
    if with_faces:
        outs += [pltpu.VMEM((1, ycount, owned), BF16)] * 2
    args = [part, last, base, one, two, initial, kernels, death]
    return call(
        body, "first_node", args, outs, scratch=[pltpu.VMEM((2, 2 * rows, owned), BF16)],
        gflop=0.0,
    )


def before_second(news, rests, growth, death, chunks):
    _, ycount, owned = news[0].shape
    xcount = sum(len(cells) for cells in chunks)
    count = len(chunks)
    place = {x: (c, i) for c, cells in enumerate(chunks) for i, x in enumerate(cells)}

    def body(*refs):
        new_refs, rest_refs = refs[:count], refs[count:2 * count]
        g_ref, d_ref, whole_ref = refs[2 * count:2 * count + 3]
        base_refs, sems = refs[2 * count + 3:-1], refs[-1]
        copies = [
            pltpu.make_async_copy(new_refs[c].at[i], whole_ref.at[x], sems.at[x]) for x, (c, i) in place.items()
        ]
        for copy in copies:
            copy.start()
        growth = g_ref[...]
        factor = SECOND / (1.0 + SECOND * d_ref[...])
        for x, (c, i) in place.items():
            core = new_refs[c][i]
            e = along_y(core) + core * growth
            for near in (x - 1, x + 1):
                if near in place:
                    e = e + DIFFUSION * new_refs[place[near][0]][place[near][1]]
            base_refs[c][i] = rest_refs[c][i] + factor * e
        for copy in copies:
            copy.wait()

    outs = [jax.ShapeDtypeStruct((xcount, ycount, owned), F32)]
    outs += [pltpu.VMEM((len(cells), ycount, owned), F32) for cells in chunks]
    return call(
        body, "before_second", [*news, *rests, growth, death], outs, scratch=[pltpu.SemaphoreType.DMA((xcount,))],
        out_specs=[ANYWHERE] + [SPEC] * count, gflop=20.0,
    )


def whole_sums(blocks, kernels):
    rows, owned = blocks[0].shape[1:]
    count = len(blocks)

    def body(*refs):
        block_refs, k_ref, sums_ref = refs[:count], refs[count], refs[count + 1]
        me = lax.axis_index("trait")
        values = [r[...].reshape(rows, owned) for r in block_refs]
        for k in range(2):
            sums_ref[k] = blocks_dot(values, k_ref, k, [me ^ j for j in range(count)]).astype(BF16)

    return call(body, "whole_sums", [*blocks, kernels], [pltpu.VMEM((2, rows, owned), BF16)])[0]


def finish(cells, ycount, sums, base_ref, new_ref, factor, faces, held, out_ref, sems):
    copies = []
    for i, x in enumerate(cells):
        at = pl.ds(i * ycount, ycount)
        e = sums[1, at, :].astype(F32) - new_ref[i] * sums[0, at, :].astype(F32)
        if x in faces:
            e = e + DIFFUSION * faces[x][0].astype(F32)
        held[i] = base_ref[i] + factor * e
        copies.append(pltpu.make_async_copy(held.at[i], out_ref.at[x], sems.at[i]))
        copies[-1].start()
    return copies


def second_first(sums, base, new, death, lo, hi, blocks, kernels, cells, xcount):
    _, ycount, owned = new.shape
    rows = blocks[0].shape[1]
    count = len(blocks)

    def body(sums_ref, base_ref, new_ref, d_ref, lo_ref, hi_ref, k_ref, *refs):
        block_refs = refs[:count]
        out_ref, part_ref, held, sems = refs[count:]
        factor = SECOND / (1.0 + SECOND * d_ref[...])
        faces = {0: lo_ref, xcount - 1: hi_ref}
        copies = finish(cells, ycount, sums_ref, base_ref, new_ref, factor, faces, held, out_ref, sems)
        me = lax.axis_index("trait")
        values = [r[...].reshape(rows, owned) for r in block_refs]
        for k in range(2):
            part_ref[k] = blocks_dot(values, k_ref, k, [me ^ j for j in range(count)])
        for copy in copies:
            copy.wait()

    return call(
        body, "second_first", [sums, base, new, death, lo, hi, kernels, *blocks],
        [jax.ShapeDtypeStruct((xcount, ycount, owned), F32), pltpu.VMEM((2, rows, owned), F32)],
        scratch=[pltpu.VMEM((len(cells), ycount, owned), F32), pltpu.SemaphoreType.DMA((len(cells),))],
        out_specs=[ANYWHERE, SPEC],
    )


def second_last(part, last, base, new, death, kernels, begun, cells, xcount):
    _, ycount, owned = new.shape
    rows = len(cells) * ycount

    def body(part_ref, last_ref, base_ref, new_ref, d_ref, k_ref, begun_ref, out_ref, sums, held, sems):
        me = lax.axis_index("trait")
        for k in range(2):
            sums[k] = (part_ref[k] + blocks_dot([last_ref[...].reshape(rows, owned)], k_ref, k, [me ^ 3])).astype(BF16)
        factor = SECOND / (1.0 + SECOND * d_ref[...])
        for copy in finish(cells, ycount, sums, base_ref, new_ref, factor, {}, held, out_ref, sems):
            copy.wait()

    return call(
        body, "second_last", [part, last, base, new, death, kernels, begun],
        [jax.ShapeDtypeStruct((xcount, ycount, owned), F32)],
        scratch=[
            pltpu.VMEM((2, rows, owned), BF16),
            pltpu.VMEM((len(cells), ycount, owned), F32),
            pltpu.SemaphoreType.DMA((len(cells),)),
        ],
        specs=[SPEC] * 6 + [FROM_HBM], out_specs=[ANYWHERE], alias={6: 0},
    )[0]


def local(initial, section_one, section_two, kernels, growth, death_rate):
    xcount, ycount, owned = section_one.shape
    traits = lax.axis_size("trait")
    gcount = lax.axis_size("gx")
    growth = growth.reshape(1, owned)
    death = death_rate.reshape(1, owned)
    chunks = chunks_of(xcount)

    def to_sibling(v):
        return lax.ppermute(v, "trait", [(i, i ^ 1) for i in range(traits)])

    def to_far(v):
        return lax.ppermute(v, "trait", [(i, i ^ 2) for i in range(traits)])

    def faces(head, tail):
        lo = lax.ppermute(tail, "gx", [(i, (i + 1) % gcount) for i in range(gcount)])
        hi = lax.ppermute(head, "gx", [((i + 1) % gcount, i) for i in range(gcount)])
        return lo, hi

    own_a, head, tail = round_chunk((section_one, section_two), chunks[0], True)
    far_a = to_far(own_a)
    own_b = round_chunk((after(section_one, own_a), section_two), chunks[1], False)[0]
    far_b = to_far(own_b)
    head, tail, kernels = lax.optimization_barrier((head, tail, kernels, own_b))[:3]
    lo, hi = faces(head, tail)
    base_a, base_b = before_first(section_one, section_two, lo, hi, growth, chunks)
    sib_a = to_sibling(after(own_a, own_b))
    sib_b = to_sibling(own_b)
    far_a = after(far_a, base_a)
    farsib_a = to_sibling(far_a)
    part_a = early_part([own_a, sib_a, far_a], kernels)
    new_a, rounded_a, rest_a, new_head, new_tail = first_node(
        part_a, farsib_a, base_a, section_one, section_two, initial, kernels, death, chunks[0], True
    )
    nfar_a = to_far(rounded_a)
    nsib_a = to_sibling(rounded_a)

    far_b = after(far_b, rounded_a)
    farsib_b = to_sibling(far_b)
    part_b = early_part([own_b, sib_b, far_b], kernels)
    new_b, rounded_b, rest_b = first_node(
        part_b, farsib_b, base_b, section_one, section_two, initial, kernels, death, chunks[1], False
    )
    nfar_b = to_far(rounded_b)
    nsib_b = to_sibling(rounded_b)
    new_lo, new_hi = faces(*lax.optimization_barrier((new_head, new_tail, rounded_b))[:2])
    nfar_a = after(nfar_a, rounded_b)
    nfarsib_a = to_sibling(nfar_a)
    new_one, nbase_a, nbase_b = before_second((new_a, new_b), (rest_a, rest_b), growth, death, chunks)
    sums_a = whole_sums([rounded_a, nsib_a, nfar_a, nfarsib_a], after(kernels, nbase_a))
    nfar_b = after(nfar_b, sums_a, new_lo, new_hi)
    nfarsib_b = to_sibling(nfar_b)
    begun, npart_b = second_first(
        sums_a, nbase_a, new_a, death, new_lo, new_hi, [rounded_b, nsib_b, nfar_b], kernels, chunks[0], xcount
    )
    new_two = second_last(npart_b, nfarsib_b, nbase_b, new_b, death, kernels, begun, chunks[1], xcount)
    return new_one, new_two


def solution(mesh):
    in_specs = (
        P("gx", None, "trait"),
        P("gx", None, "trait"),
        P("gx", None, "trait"),
        P(None, None, "trait"),
        P("trait"),
        P("trait"),
    )
    out_specs = (P("gx", None, "trait"), P("gx", None, "trait"))
    return jax.shard_map(local, mesh=mesh, in_specs=in_specs, out_specs=out_specs, check_vma=False)
```

```python
import jax
import jax.numpy as jnp
from jax import lax
from jax.experimental import pallas as pl
from jax.experimental.pallas import tpu as pltpu
from jax.sharding import PartitionSpec as P

DIFFUSION = 0.25
STEP_SIZE = 0.5
FIRST = STEP_SIZE / 3.0
SECOND = 2.0 * STEP_SIZE / 3.0
F32 = jnp.float32
BF16 = jnp.bfloat16
VMEM_LIMIT = 20 * 1024 * 1024
SPEC = pl.BlockSpec(memory_space=pltpu.VMEM)
ANYWHERE = pl.BlockSpec(memory_space=pl.ANY)
FROM_HBM = pl.BlockSpec(memory_space=pltpu.HBM)


def chunks_of(xcount):
    last = max(1, xcount // 4)
    start = (xcount - last + 1) // 2
    middle = list(range(start, start + last))
    return [x for x in range(xcount) if x not in middle], middle


def after(value, *others):
    return lax.optimization_barrier((value, *others))[0]


def call(body, name, args, outs, scratch=(), specs=None, out_specs=None, gflop=0.0, alias=None):
    specs = specs or [SPEC] * len(args)
    space = {id(SPEC): pltpu.VMEM, id(FROM_HBM): pltpu.HBM}
    args = [
        pltpu.with_memory_space_constraint(a, space[id(s)]) if id(s) in space else a for a, s in zip(args, specs)
    ]
    return pl.pallas_call(
        body,
        out_shape=outs,
        in_specs=specs,
        out_specs=out_specs or [SPEC] * len(outs),
        scratch_shapes=list(scratch),
        compiler_params=pltpu.CompilerParams(vmem_limit_bytes=VMEM_LIMIT),
        cost_estimate=pl.CostEstimate(flops=int(gflop * 1e9), bytes_accessed=0, transcendentals=0),
        input_output_aliases=alias or {},
        name=name,
    )(*args)


def side_of(low_value, high_value):
    return jnp.where(lax.axis_index("gx") % 2 == 0, low_value, high_value)


def round_chunk(fields, cells, with_faces):
    xcount, ycount, owned = fields[0].shape
    count = len(fields)

    def body(*refs):
        field_refs = refs[:count]
        out = refs[count]
        held, sems = refs[-2:]
        copies = []
        ends = {}
        for f in range(count):
            for i, x in enumerate(cells):
                copies.append(pltpu.make_async_copy(field_refs[f].at[x], held.at[f, i], sems.at[f, i]))
                copies[-1].start()
        for f in range(count):
            for i, x in enumerate(cells):
                copies[f * len(cells) + i].wait()
                value = held[f, i].astype(BF16)
                out[f, i * ycount:(i + 1) * ycount, :] = value
                ends[x, f] = value
        if with_faces:
            for f in range(count):
                refs[count + 1][f] = side_of(ends[xcount - 1, f], ends[0, f])
                refs[count + 2][f] = side_of(ends[0, f], ends[xcount - 1, f])

    outs = [pltpu.VMEM((count, len(cells) * ycount, owned), BF16)]
    if with_faces:
        outs += [pltpu.VMEM((count, ycount, owned), BF16)] * 2
    return call(
        body, "round_chunk", fields, outs,
        scratch=[pltpu.VMEM((count, len(cells), ycount, owned), F32), pltpu.SemaphoreType.DMA((count, len(cells)))],
        specs=[FROM_HBM] * count, gflop=0.0,
    )


def blocks_dot(blocks, kernels_ref, k, owners):
    depth = blocks[0].shape[-1]
    lhs = jnp.concatenate(blocks, axis=-1)
    rhs = jnp.concatenate(
        [kernels_ref[k, pl.ds(pl.multiple_of(o * depth, depth), depth), :] for o in owners], axis=0
    )
    return jnp.dot(lhs, rhs, preferred_element_type=F32)


def along_y(core):
    return DIFFUSION * (pltpu.roll(core, 1, 0) + pltpu.roll(core, core.shape[0] - 1, 0)) - 2.0 * core


def before_first(one, two, near, beyond, growth, chunks):
    xcount, ycount, owned = one.shape

    def body(one_ref, two_ref, near_ref, beyond_ref, g_ref, *outs):
        growth = g_ref[...]
        for cells, base_ref in zip(chunks, outs):
            for f, ref in enumerate((one_ref, two_ref)):
                for i, x in enumerate(cells):
                    core = ref[x]
                    before = ref[x - 1] if x > 0 else side_of(beyond_ref[f], near_ref[f]).astype(F32)
                    behind = ref[x + 1] if x < xcount - 1 else side_of(near_ref[f], beyond_ref[f]).astype(F32)
                    base_ref[f, i] = DIFFUSION * (before + behind) + along_y(core) + core * growth

    outs = [pltpu.VMEM((2, len(cells), ycount, owned), F32) for cells in chunks]
    return call(body, "before_first", [one, two, near, beyond, growth], outs)


def early_part(blocks, kernels, new=None, cells=(), xcount=0):
    rows, owned = blocks[0].shape[0] * blocks[0].shape[1], blocks[0].shape[2]
    count = len(blocks)

    def body(*refs):
        block_refs, k_ref = refs[:count], refs[count]
        copies = []
        if new is None:
            part_ref = refs[-1]
        else:
            new_ref, part_ref, whole_ref, sems = refs[count + 1:]
            copies = [pltpu.make_async_copy(new_ref.at[i], whole_ref.at[x], sems.at[i]) for i, x in enumerate(cells)]
        for copy in copies:
            copy.start()
        me = lax.axis_index("trait")
        values = [r[...].reshape(rows, owned) for r in block_refs]
        for k in range(2):
            part_ref[k] = blocks_dot(values, k_ref, k, [me ^ j for j in range(count)])
        for copy in copies:
            copy.wait()

    args = [*blocks, kernels]
    outs = [pltpu.VMEM((2, rows, owned), F32)]
    if new is None:
        return call(body, "early_part", args, outs, gflop=20.0)[0]
    outs.append(jax.ShapeDtypeStruct((xcount, *new.shape[1:]), F32))
    return call(
        body, "early_part", [*args, new], outs, scratch=[pltpu.SemaphoreType.DMA((len(cells),))],
        out_specs=[SPEC, ANYWHERE], gflop=20.0,
    )


def first_node(part, last, base, one, two, initial, kernels, death, cells, with_faces):
    xcount, ycount, owned = one.shape
    rows = len(cells) * ycount

    def body(part_ref, last_ref, base_ref, one_ref, two_ref, init_ref, k_ref, d_ref, *refs):
        new_ref, rounded_ref, rest_ref = refs[:3]
        sums = refs[-1]
        me = lax.axis_index("trait")
        for k in range(2):
            far_part = blocks_dot([last_ref[...].reshape(2 * rows, owned)], k_ref, k, [me ^ 3])
            sums[k] = (part_ref[k] + far_part).astype(BF16)
        death = d_ref[...]
        inv_one = 1.0 / (1.0 + FIRST * death)
        inv_two = 1.0 / (1.0 + SECOND * death)
        ends = {}
        for i, x in enumerate(cells):
            cores = (one_ref[x], two_ref[x])
            e = []
            for f in range(2):
                at = pl.ds(f * rows + i * ycount, ycount)
                e.append(base_ref[f, i] - cores[f] * sums[0, at, :].astype(F32) + sums[1, at, :].astype(F32))
            full_one = e[0] - death * cores[0]
            full_two = e[1] - death * cores[1]
            new = (
                init_ref[x]
                + FIRST * death * cores[0]
                + STEP_SIZE * (5.0 / 12.0 * full_one - 1.0 / 12.0 * full_two)
            ) * inv_one
            new_ref[i] = new
            rounded = new.astype(BF16)
            rounded_ref[0, i * ycount:(i + 1) * ycount, :] = rounded
            ends[x] = rounded
            rest_ref[i] = (
                new - SECOND * e[0] + SECOND * death * cores[1] + STEP_SIZE / 3.0 * (full_one + full_two)
            ) * inv_two
        if with_faces:
            refs[3][0] = side_of(ends[xcount - 1], ends[0])
            refs[4][0] = side_of(ends[0], ends[xcount - 1])

    outs = [
        pltpu.VMEM((len(cells), ycount, owned), F32),
        pltpu.VMEM((1, rows, owned), BF16),
        pltpu.VMEM((len(cells), ycount, owned), F32),
    ]
    if with_faces:
        outs += [pltpu.VMEM((1, ycount, owned), BF16)] * 2
    args = [part, last, base, one, two, initial, kernels, death]
    return call(
        body, "first_node", args, outs, scratch=[pltpu.VMEM((2, 2 * rows, owned), BF16)],
        gflop=0.0,
    )


def before_second(news, rests, growth, death, begun, chunks):
    _, ycount, owned = news[0].shape
    xcount = sum(len(cells) for cells in chunks)
    count = len(chunks)
    place = {x: (c, i) for c, cells in enumerate(chunks) for i, x in enumerate(cells)}

    def body(*refs):
        new_refs, rest_refs = refs[:count], refs[count:2 * count]
        g_ref, d_ref, _, whole_ref = refs[2 * count:2 * count + 4]
        base_refs, sems = refs[2 * count + 4:-1], refs[-1]
        copies = [
            pltpu.make_async_copy(new_refs[-1].at[i], whole_ref.at[x], sems.at[i]) for i, x in enumerate(chunks[-1])
        ]
        for copy in copies:
            copy.start()
        growth = g_ref[...]
        factor = SECOND / (1.0 + SECOND * d_ref[...])
        for x, (c, i) in place.items():
            core = new_refs[c][i]
            e = along_y(core) + core * growth
            for near in (x - 1, x + 1):
                if near in place:
                    e = e + DIFFUSION * new_refs[place[near][0]][place[near][1]]
            base_refs[c][i] = rest_refs[c][i] + factor * e
        for copy in copies:
            copy.wait()

    outs = [jax.ShapeDtypeStruct((xcount, ycount, owned), F32)]
    outs += [pltpu.VMEM((len(cells), ycount, owned), F32) for cells in chunks]
    args = [*news, *rests, growth, death, begun]
    return call(
        body, "before_second", args, outs, scratch=[pltpu.SemaphoreType.DMA((len(chunks[-1]),))],
        specs=[SPEC] * (len(args) - 1) + [FROM_HBM], out_specs=[ANYWHERE] + [SPEC] * count, gflop=20.0,
        alias={len(args) - 1: 0},
    )


def finish(cells, sums_at, base_ref, new_ref, factor, faces, held, out_ref, sems):
    copies = []
    for j, (i, x) in enumerate(cells):
        e = sums_at(1, j) - new_ref[i] * sums_at(0, j)
        if x in faces:
            e = e + DIFFUSION * faces[x].astype(F32)
        held[j] = base_ref[i] + factor * e
        copies.append(pltpu.make_async_copy(held.at[j], out_ref.at[x], sems.at[j]))
        copies[-1].start()
    return copies


def split_cells(cells, xcount):
    placed = list(enumerate(cells))
    return [p for p in placed if p[1] in (0, xcount - 1)], [p for p in placed if p[1] not in (0, xcount - 1)]


def second_inner(blocks, base, new, death, kernels, cells, xcount):
    _, ycount, owned = new.shape
    rows = blocks[0].shape[1]
    count = len(blocks)
    outer, inner = split_cells(cells, xcount)

    def body(*refs):
        block_refs = refs[:count]
        base_ref, new_ref, d_ref, k_ref, out_ref, sums_ref, sums, held, sems = refs[count:]
        me = lax.axis_index("trait")
        values = [r[...].reshape(rows, owned) for r in block_refs]
        for k in range(2):
            sums[k] = blocks_dot(values, k_ref, k, [me ^ j for j in range(count)]).astype(BF16)
        factor = SECOND / (1.0 + SECOND * d_ref[...])

        def sums_at(k, j):
            return sums[k, pl.ds(inner[j][0] * ycount, ycount), :].astype(F32)

        copies = finish(inner, sums_at, base_ref, new_ref, factor, {}, held, out_ref, sems)
        for j, (i, _) in enumerate(outer):
            for k in range(2):
                sums_ref[k, j] = sums[k, pl.ds(i * ycount, ycount), :]
        for copy in copies:
            copy.wait()

    return call(
        body, "second_inner", [*blocks, base, new, death, kernels],
        [jax.ShapeDtypeStruct((xcount, ycount, owned), F32), pltpu.VMEM((2, len(outer), ycount, owned), BF16)],
        scratch=[
            pltpu.VMEM((2, rows, owned), BF16),
            pltpu.VMEM((len(inner), ycount, owned), F32),
            pltpu.SemaphoreType.DMA((len(inner),)),
        ],
        out_specs=[ANYWHERE, SPEC],
    )


def second_outer(sums, base, new, death, near, beyond, kernels, blocks, begun, cells, xcount):
    _, ycount, owned = new.shape
    rows = blocks[0].shape[1]
    count = len(blocks)
    outer, _ = split_cells(cells, xcount)

    def body(sums_ref, base_ref, new_ref, d_ref, near_ref, beyond_ref, k_ref, *refs):
        block_refs = refs[:count]
        _, out_ref, part_ref, held, sems = refs[count:]
        factor = SECOND / (1.0 + SECOND * d_ref[...])
        faces = {
            0: side_of(beyond_ref[0], near_ref[0]),
            xcount - 1: side_of(near_ref[0], beyond_ref[0]),
        }
        copies = finish(
            outer, lambda k, j: sums_ref[k, j].astype(F32), base_ref, new_ref, factor, faces, held, out_ref, sems
        )
        me = lax.axis_index("trait")
        values = [r[...].reshape(rows, owned) for r in block_refs]
        for k in range(2):
            part_ref[k] = blocks_dot(values, k_ref, k, [me ^ j for j in range(count)])
        for copy in copies:
            copy.wait()

    args = [sums, base, new, death, near, beyond, kernels, *blocks, begun]
    return call(
        body, "second_outer", args,
        [jax.ShapeDtypeStruct((xcount, ycount, owned), F32), pltpu.VMEM((2, rows, owned), F32)],
        scratch=[pltpu.VMEM((len(outer), ycount, owned), F32), pltpu.SemaphoreType.DMA((len(outer),))],
        specs=[SPEC] * (len(args) - 1) + [FROM_HBM], out_specs=[ANYWHERE, SPEC], alias={len(args) - 1: 0},
    )


def second_last(part, last, base, new, death, kernels, begun, cells, xcount):
    _, ycount, owned = new.shape
    rows = len(cells) * ycount

    def body(part_ref, last_ref, base_ref, new_ref, d_ref, k_ref, begun_ref, out_ref, sums, held, sems):
        me = lax.axis_index("trait")
        for k in range(2):
            sums[k] = (part_ref[k] + blocks_dot([last_ref[...].reshape(rows, owned)], k_ref, k, [me ^ 3])).astype(BF16)
        factor = SECOND / (1.0 + SECOND * d_ref[...])

        def sums_at(k, j):
            return sums[k, pl.ds(j * ycount, ycount), :].astype(F32)

        for copy in finish(list(enumerate(cells)), sums_at, base_ref, new_ref, factor, {}, held, out_ref, sems):
            copy.wait()

    return call(
        body, "second_last", [part, last, base, new, death, kernels, begun],
        [jax.ShapeDtypeStruct((xcount, ycount, owned), F32)],
        scratch=[
            pltpu.VMEM((2, rows, owned), BF16),
            pltpu.VMEM((len(cells), ycount, owned), F32),
            pltpu.SemaphoreType.DMA((len(cells),)),
        ],
        specs=[SPEC] * 6 + [FROM_HBM], out_specs=[ANYWHERE], alias={6: 0},
    )[0]


def local(initial, section_one, section_two, kernels, growth, death_rate):
    xcount, ycount, owned = section_one.shape
    traits = lax.axis_size("trait")
    gcount = lax.axis_size("gx")
    growth = growth.reshape(1, owned)
    death = death_rate.reshape(1, owned)
    chunks = chunks_of(xcount)

    def to_sibling(v):
        return lax.ppermute(v, "trait", [(i, i ^ 1) for i in range(traits)])

    def to_far(v):
        return lax.ppermute(v, "trait", [(i, i ^ 2) for i in range(traits)])

    def to_near(v):
        return lax.ppermute(v, "gx", [(i, i ^ 1) for i in range(gcount)])

    def to_beyond(v):
        return lax.ppermute(v, "gx", [(i, (i + 1 - 2 * (i % 2 == 0)) % gcount) for i in range(gcount)])

    own_a, near, beyond = round_chunk((section_one, section_two), chunks[0], True)
    far_a = to_far(own_a)
    own_b = round_chunk((after(section_one, own_a), section_two), chunks[1], False)[0]
    far_b = to_far(own_b)
    near, beyond, kernels = lax.optimization_barrier((near, beyond, kernels, own_b))[:3]
    near, beyond = to_near(near), to_beyond(beyond)
    base_a, base_b = before_first(section_one, section_two, near, beyond, growth, chunks)
    sib_a = to_sibling(after(own_a, own_b))
    sib_b = to_sibling(own_b)
    far_a = after(far_a, base_a)
    farsib_a = to_sibling(far_a)
    part_a = early_part([own_a, sib_a, far_a], kernels)
    new_a, rounded_a, rest_a, new_near, new_beyond = first_node(
        part_a, farsib_a, base_a, section_one, section_two, initial, kernels, death, chunks[0], True
    )
    nfar_a = to_far(rounded_a)
    nsib_a = to_sibling(rounded_a)

    far_b = after(far_b, rounded_a)
    farsib_b = to_sibling(far_b)
    part_b, new_one = early_part([own_b, sib_b, far_b], kernels, new_a, chunks[0], xcount)
    new_b, rounded_b, rest_b = first_node(
        part_b, farsib_b, base_b, section_one, section_two, initial, kernels, death, chunks[1], False
    )
    nfar_b = to_far(rounded_b)
    nsib_b = to_sibling(rounded_b)
    new_near, new_beyond = lax.optimization_barrier((new_near, new_beyond, rounded_b))[:2]
    new_near, new_beyond = to_near(new_near), to_beyond(new_beyond)
    nfar_a = after(nfar_a, rounded_b)
    nfarsib_a = to_sibling(nfar_a)
    new_one, nbase_a, nbase_b = before_second((new_a, new_b), (rest_a, rest_b), growth, death, new_one, chunks)
    begun, sums_a = second_inner(
        [rounded_a, nsib_a, nfar_a, nfarsib_a], nbase_a, new_a, death, kernels, chunks[0], xcount
    )
    nfar_b = after(nfar_b, sums_a, new_near, new_beyond)
    nfarsib_b = to_sibling(nfar_b)
    begun, npart_b = second_outer(
        sums_a, nbase_a, new_a, death, new_near, new_beyond, kernels, [rounded_b, nsib_b, nfar_b], begun, chunks[0],
        xcount,
    )
    new_two = second_last(npart_b, nfarsib_b, nbase_b, new_b, death, kernels, begun, chunks[1], xcount)
    return new_one, new_two


def solution(mesh):
    in_specs = (
        P("gx", None, "trait"),
        P("gx", None, "trait"),
        P("gx", None, "trait"),
        P(None, None, "trait"),
        P("trait"),
        P("trait"),
    )
    out_specs = (P("gx", None, "trait"), P("gx", None, "trait"))
    return jax.shard_map(local, mesh=mesh, in_specs=in_specs, out_specs=out_specs, check_vma=False)
```

```python
import jax
import jax.numpy as jnp
from jax import lax
from jax.experimental import pallas as pl
from jax.experimental.pallas import tpu as pltpu
from jax.sharding import PartitionSpec as P

DIFFUSION = 0.25
STEP_SIZE = 0.5
FIRST = STEP_SIZE / 3.0
SECOND = 2.0 * STEP_SIZE / 3.0
F32 = jnp.float32
BF16 = jnp.bfloat16
VMEM_LIMIT = 20 * 1024 * 1024
SPEC = pl.BlockSpec(memory_space=pltpu.VMEM)
ANYWHERE = pl.BlockSpec(memory_space=pl.ANY)
FROM_HBM = pl.BlockSpec(memory_space=pltpu.HBM)


def chunks_of(xcount):
    last = max(1, 3 * xcount // 8)
    start = (xcount - last + 1) // 2
    middle = list(range(start, start + last))
    return [x for x in range(xcount) if x not in middle], middle


def after(value, *others):
    return lax.optimization_barrier((value, *others))[0]


def call(body, name, args, outs, scratch=(), specs=None, out_specs=None, gflop=0.0, alias=None):
    specs = specs or [SPEC] * len(args)
    space = {id(SPEC): pltpu.VMEM, id(FROM_HBM): pltpu.HBM}
    args = [
        pltpu.with_memory_space_constraint(a, space[id(s)]) if id(s) in space else a for a, s in zip(args, specs)
    ]
    return pl.pallas_call(
        body,
        out_shape=outs,
        in_specs=specs,
        out_specs=out_specs or [SPEC] * len(outs),
        scratch_shapes=list(scratch),
        compiler_params=pltpu.CompilerParams(vmem_limit_bytes=VMEM_LIMIT),
        cost_estimate=pl.CostEstimate(flops=int(gflop * 1e9), bytes_accessed=0, transcendentals=0),
        input_output_aliases=alias or {},
        name=name,
    )(*args)


def round_field(field, cells):
    _, ycount, owned = field.shape

    def body(field_ref, out_ref, held, sems):
        copies = [pltpu.make_async_copy(field_ref.at[x], held.at[i], sems.at[i]) for i, x in enumerate(cells)]
        for copy in copies:
            copy.start()
        for i, copy in enumerate(copies):
            copy.wait()
            out_ref[0, pl.ds(i * ycount, ycount), :] = held[i].astype(BF16)

    return call(
        body, "round_field", [field], [pltpu.VMEM((1, len(cells) * ycount, owned), BF16)],
        scratch=[pltpu.VMEM((len(cells), ycount, owned), F32), pltpu.SemaphoreType.DMA((len(cells),))],
        specs=[FROM_HBM],
    )[0]


def round_rest(fields, chunks):
    xcount, ycount, owned = fields[0].shape
    count = len(fields)
    cells = chunks[-1]
    ends = (0, xcount - 1)
    wanted = [(f, x) for f in range(count) for x in (*cells, *ends)]

    def body(*refs):
        field_refs = refs[:count]
        out_ref, head_ref, tail_ref, held, sems = refs[count:]
        copies = [
            pltpu.make_async_copy(field_refs[f].at[x], held.at[j], sems.at[j]) for j, (f, x) in enumerate(wanted)
        ]
        for copy in copies:
            copy.start()
        for j, (f, x) in enumerate(wanted):
            copies[j].wait()
            value = held[j].astype(BF16)
            if x in cells:
                i = cells.index(x)
                out_ref[f, pl.ds(i * ycount, ycount), :] = value
            else:
                (head_ref if x == 0 else tail_ref)[f] = value

    outs = [
        pltpu.VMEM((count, len(cells) * ycount, owned), BF16),
        pltpu.VMEM((count, ycount, owned), BF16),
        pltpu.VMEM((count, ycount, owned), BF16),
    ]
    return call(
        body, "round_rest", fields, outs,
        scratch=[pltpu.VMEM((len(wanted), ycount, owned), F32), pltpu.SemaphoreType.DMA((len(wanted),))],
        specs=[FROM_HBM] * count,
    )


def rows_of(refs):
    return jnp.concatenate([r[...].reshape(-1, r.shape[-1]) for r in refs], axis=0)


def blocks_dot(blocks, kernels_ref, k, owners):
    depth = blocks[0].shape[-1]
    lhs = jnp.concatenate(blocks, axis=-1)
    rhs = jnp.concatenate(
        [kernels_ref[k, pl.ds(pl.multiple_of(o * depth, depth), depth), :] for o in owners], axis=0
    )
    return jnp.dot(lhs, rhs, preferred_element_type=F32)


def along_y(core):
    return DIFFUSION * (pltpu.roll(core, 1, 0) + pltpu.roll(core, core.shape[0] - 1, 0)) - 2.0 * core


def before_first(one, two, lo, hi, growth, chunks):
    xcount, ycount, owned = one.shape

    def body(one_ref, two_ref, lo_ref, hi_ref, g_ref, *outs):
        growth = g_ref[...]
        for cells, base_ref in zip(chunks, outs):
            for f, ref in enumerate((one_ref, two_ref)):
                for i, x in enumerate(cells):
                    core = ref[x]
                    before = ref[x - 1] if x > 0 else lo_ref[f].astype(F32)
                    behind = ref[x + 1] if x < xcount - 1 else hi_ref[f].astype(F32)
                    base_ref[f, i] = DIFFUSION * (before + behind) + along_y(core) + core * growth

    outs = [pltpu.VMEM((2, len(cells), ycount, owned), F32) for cells in chunks]
    return call(body, "before_first", [one, two, lo, hi, growth], outs)


def early_part(own, sib, far, kernels, new=None, cells=(), xcount=0):
    owned = own[0].shape[-1]
    rows = len(own) * own[0].shape[0] * own[0].shape[1]
    count = len(own)

    def body(*refs):
        blocks = [refs[j * count:(j + 1) * count] for j in range(3)]
        k_ref = refs[3 * count]
        copies = []
        if new is None:
            part_ref = refs[-1]
        else:
            new_ref, part_ref, whole_ref, sems = refs[3 * count + 1:]
            copies = [pltpu.make_async_copy(new_ref.at[i], whole_ref.at[x], sems.at[i]) for i, x in enumerate(cells)]
        for copy in copies:
            copy.start()
        me = lax.axis_index("trait")
        values = [rows_of(block) for block in blocks]
        for k in range(2):
            part_ref[k] = blocks_dot(values, k_ref, k, [me, me ^ 1, me ^ 2])
        for copy in copies:
            copy.wait()

    args = [*own, *sib, *far, kernels]
    outs = [pltpu.VMEM((2, rows, owned), F32)]
    if new is None:
        return call(body, "early_part", args, outs, gflop=20.0)[0]
    outs.append(jax.ShapeDtypeStruct((xcount, *new.shape[1:]), F32))
    return call(
        body, "early_part", [*args, new], outs, scratch=[pltpu.SemaphoreType.DMA((len(cells),))],
        out_specs=[SPEC, ANYWHERE], gflop=20.0,
    )


def first_node(part, last, base, one, two, initial, kernels, death, cells, with_faces):
    xcount, ycount, owned = one.shape
    rows = len(cells) * ycount
    count = len(last)

    def body(*refs):
        last_refs = refs[:count]
        part_ref, base_ref, one_ref, two_ref, init_ref, k_ref, d_ref = refs[count:count + 7]
        refs = refs[count + 7:]
        new_ref, rounded_ref, rest_ref = refs[:3]
        sums = refs[-1]
        me = lax.axis_index("trait")
        for k in range(2):
            far_part = blocks_dot([rows_of(last_refs)], k_ref, k, [me ^ 3])
            sums[k] = (part_ref[k] + far_part).astype(BF16)
        death = d_ref[...]
        inv_one = 1.0 / (1.0 + FIRST * death)
        inv_two = 1.0 / (1.0 + SECOND * death)
        for i, x in enumerate(cells):
            cores = (one_ref[x], two_ref[x])
            e = []
            for f in range(2):
                at = pl.ds(f * rows + i * ycount, ycount)
                e.append(base_ref[f, i] - cores[f] * sums[0, at, :].astype(F32) + sums[1, at, :].astype(F32))
            full_one = e[0] - death * cores[0]
            full_two = e[1] - death * cores[1]
            new = (
                init_ref[x]
                + FIRST * death * cores[0]
                + STEP_SIZE * (5.0 / 12.0 * full_one - 1.0 / 12.0 * full_two)
            ) * inv_one
            new_ref[i] = new
            rounded = new.astype(BF16)
            rounded_ref[0, i * ycount:(i + 1) * ycount, :] = rounded
            if with_faces and x == 0:
                refs[3][0] = rounded
            if with_faces and x == xcount - 1:
                refs[4][0] = rounded
            rest_ref[i] = (
                new - SECOND * e[0] + SECOND * death * cores[1] + STEP_SIZE / 3.0 * (full_one + full_two)
            ) * inv_two

    outs = [
        pltpu.VMEM((len(cells), ycount, owned), F32),
        pltpu.VMEM((1, rows, owned), BF16),
        pltpu.VMEM((len(cells), ycount, owned), F32),
    ]
    if with_faces:
        outs += [pltpu.VMEM((1, ycount, owned), BF16)] * 2
    args = [*last, part, base, one, two, initial, kernels, death]
    return call(
        body, "first_node", args, outs, scratch=[pltpu.VMEM((2, 2 * rows, owned), BF16)],
        gflop=0.0,
    )


def before_second(news, rests, growth, death, begun, blocks, kernels, chunks):
    _, ycount, owned = news[0].shape
    rows = blocks[0].shape[1]
    xcount = sum(len(cells) for cells in chunks)
    count = len(chunks)
    size = len(blocks)
    place = {x: (c, i) for c, cells in enumerate(chunks) for i, x in enumerate(cells)}

    def body(*refs):
        new_refs, rest_refs, block_refs = refs[:count], refs[count:2 * count], refs[2 * count:2 * count + size]
        k_ref, g_ref, d_ref, _, whole_ref, part_ref = refs[2 * count + size:2 * count + size + 6]
        base_refs, sems = refs[2 * count + size + 6:-1], refs[-1]
        copies = [
            pltpu.make_async_copy(new_refs[-1].at[i], whole_ref.at[x], sems.at[i]) for i, x in enumerate(chunks[-1])
        ]
        for copy in copies:
            copy.start()
        me = lax.axis_index("trait")
        values = [r[...].reshape(rows, owned) for r in block_refs]
        for k in range(2):
            part_ref[k] = blocks_dot(values, k_ref, k, [me ^ j for j in range(size)])
        growth = g_ref[...]
        factor = SECOND / (1.0 + SECOND * d_ref[...])
        for x, (c, i) in place.items():
            core = new_refs[c][i]
            e = along_y(core) + core * growth
            for near in (x - 1, x + 1):
                if near in place:
                    e = e + DIFFUSION * new_refs[place[near][0]][place[near][1]]
            base_refs[c][i] = rest_refs[c][i] + factor * e
        for copy in copies:
            copy.wait()

    outs = [jax.ShapeDtypeStruct((xcount, ycount, owned), F32), pltpu.VMEM((2, rows, owned), F32)]
    outs += [pltpu.VMEM((len(cells), ycount, owned), F32) for cells in chunks]
    args = [*news, *rests, *blocks, kernels, growth, death, begun]
    return call(
        body, "before_second", args, outs, scratch=[pltpu.SemaphoreType.DMA((len(chunks[-1]),))],
        specs=[SPEC] * (len(args) - 1) + [FROM_HBM], out_specs=[ANYWHERE] + [SPEC] * (len(outs) - 1), gflop=20.0,
        alias={len(args) - 1: 0},
    )


def whole_sums(part, blocks, kernels):
    rows, owned = blocks[0].shape[1:]

    def body(part_ref, sib_ref, far_ref, farsib_ref, k_ref, sums_ref):
        me = lax.axis_index("trait")
        values = [r[...].reshape(rows, owned) for r in (sib_ref, far_ref, farsib_ref)]
        for k in range(2):
            sums_ref[k] = (part_ref[k] + blocks_dot(values, k_ref, k, [me ^ 1, me ^ 2, me ^ 3])).astype(BF16)

    return call(body, "whole_sums", [part, *blocks, kernels], [pltpu.VMEM((2, rows, owned), BF16)])[0]


def finish(cells, ycount, sums, base_ref, new_ref, factor, faces, held, out_ref, sems):
    copies = []
    for i, x in enumerate(cells):
        at = pl.ds(i * ycount, ycount)
        e = sums[1, at, :].astype(F32) - new_ref[i] * sums[0, at, :].astype(F32)
        if x in faces:
            e = e + DIFFUSION * faces[x][0].astype(F32)
        held[i] = base_ref[i] + factor * e
        copies.append(pltpu.make_async_copy(held.at[i], out_ref.at[x], sems.at[i]))
        copies[-1].start()
    return copies


def second_first(sums, base, new, death, lo, hi, blocks, kernels, cells, xcount):
    _, ycount, owned = new.shape
    rows = blocks[0].shape[1]
    count = len(blocks)

    def body(sums_ref, base_ref, new_ref, d_ref, lo_ref, hi_ref, k_ref, *refs):
        block_refs = refs[:count]
        out_ref, part_ref, held, sems = refs[count:]
        factor = SECOND / (1.0 + SECOND * d_ref[...])
        faces = {0: lo_ref, xcount - 1: hi_ref}
        copies = finish(cells, ycount, sums_ref, base_ref, new_ref, factor, faces, held, out_ref, sems)
        me = lax.axis_index("trait")
        values = [r[...].reshape(rows, owned) for r in block_refs]
        for k in range(2):
            part_ref[k] = blocks_dot(values, k_ref, k, [me ^ j for j in range(count)])
        for copy in copies:
            copy.wait()

    return call(
        body, "second_first", [sums, base, new, death, lo, hi, kernels, *blocks],
        [jax.ShapeDtypeStruct((xcount, ycount, owned), F32), pltpu.VMEM((2, rows, owned), F32)],
        scratch=[pltpu.VMEM((len(cells), ycount, owned), F32), pltpu.SemaphoreType.DMA((len(cells),))],
        out_specs=[ANYWHERE, SPEC],
    )


def second_last(part, last, base, new, death, kernels, begun, cells, xcount):
    _, ycount, owned = new.shape
    rows = len(cells) * ycount

    def body(part_ref, last_ref, base_ref, new_ref, d_ref, k_ref, begun_ref, out_ref, sums, held, sems):
        me = lax.axis_index("trait")
        for k in range(2):
            sums[k] = (part_ref[k] + blocks_dot([last_ref[...].reshape(rows, owned)], k_ref, k, [me ^ 3])).astype(BF16)
        factor = SECOND / (1.0 + SECOND * d_ref[...])
        for copy in finish(cells, ycount, sums, base_ref, new_ref, factor, {}, held, out_ref, sems):
            copy.wait()

    return call(
        body, "second_last", [part, last, base, new, death, kernels, begun],
        [jax.ShapeDtypeStruct((xcount, ycount, owned), F32)],
        scratch=[
            pltpu.VMEM((2, rows, owned), BF16),
            pltpu.VMEM((len(cells), ycount, owned), F32),
            pltpu.SemaphoreType.DMA((len(cells),)),
        ],
        specs=[SPEC] * 6 + [FROM_HBM], out_specs=[ANYWHERE], alias={6: 0},
    )[0]


def local(initial, section_one, section_two, kernels, growth, death_rate):
    xcount, ycount, owned = section_one.shape
    traits = lax.axis_size("trait")
    gcount = lax.axis_size("gx")
    growth = growth.reshape(1, owned)
    death = death_rate.reshape(1, owned)
    chunks = chunks_of(xcount)

    def to_sibling(v):
        return lax.ppermute(v, "trait", [(i, i ^ 1) for i in range(traits)])

    def to_far(v):
        return lax.ppermute(v, "trait", [(i, i ^ 2) for i in range(traits)])

    def faces(head, tail):
        lo = lax.ppermute(tail, "gx", [(i, (i + 1) % gcount) for i in range(gcount)])
        hi = lax.ppermute(head, "gx", [((i + 1) % gcount, i) for i in range(gcount)])
        return lo, hi

    own_a = [round_field(section_one, chunks[0])]
    far_a = [to_far(own_a[0])]
    own_a.append(round_field(after(section_two, own_a[0]), chunks[0]))
    far_a.append(to_far(own_a[1]))
    own_b, head, tail = round_rest((after(section_one, own_a[1]), section_two), chunks)
    far_b = to_far(own_b)
    kernels = after(kernels, own_b)
    lo, hi = faces(head, tail)
    base_a, base_b = before_first(section_one, section_two, lo, hi, growth, chunks)
    sib_a = [to_sibling(v) for v in lax.optimization_barrier((*own_a, own_b))[:-1]]
    sib_b = to_sibling(own_b)
    far_a = list(lax.optimization_barrier((*far_a, base_a))[:-1])
    farsib_a = [to_sibling(v) for v in far_a]
    part_a = early_part(own_a, sib_a, far_a, kernels)
    new_a, rounded_a, rest_a, new_head, new_tail = first_node(
        part_a, farsib_a, base_a, section_one, section_two, initial, kernels, death, chunks[0], True
    )
    nfar_a = to_far(rounded_a)
    nsib_a = to_sibling(rounded_a)

    far_b = after(far_b, rounded_a)
    farsib_b = to_sibling(far_b)
    part_b, new_one = early_part([own_b], [sib_b], [far_b], kernels, new_a, chunks[0], xcount)
    new_b, rounded_b, rest_b = first_node(
        part_b, [farsib_b], base_b, section_one, section_two, initial, kernels, death, chunks[1], False
    )
    nfar_b = to_far(rounded_b)
    nsib_b = to_sibling(rounded_b)
    new_lo, new_hi = faces(*lax.optimization_barrier((new_head, new_tail, rounded_b))[:2])
    nfar_a = after(nfar_a, rounded_b)
    nfarsib_a = to_sibling(nfar_a)
    new_one, npart_a, nbase_a, nbase_b = before_second(
        (new_a, new_b), (rest_a, rest_b), growth, death, new_one, [rounded_a], kernels, chunks
    )
    sums_a = whole_sums(npart_a, [nsib_a, nfar_a, nfarsib_a], after(kernels, nbase_a))
    nfar_b = after(nfar_b, sums_a, new_lo, new_hi)
    nfarsib_b = to_sibling(nfar_b)
    begun, npart_b = second_first(
        sums_a, nbase_a, new_a, death, new_lo, new_hi, [rounded_b, nsib_b, nfar_b], kernels, chunks[0], xcount
    )
    new_two = second_last(npart_b, nfarsib_b, nbase_b, new_b, death, kernels, begun, chunks[1], xcount)
    return new_one, new_two


def solution(mesh):
    in_specs = (
        P("gx", None, "trait"),
        P("gx", None, "trait"),
        P("gx", None, "trait"),
        P(None, None, "trait"),
        P("trait"),
        P("trait"),
    )
    out_specs = (P("gx", None, "trait"), P("gx", None, "trait"))
    return jax.shard_map(local, mesh=mesh, in_specs=in_specs, out_specs=out_specs, check_vma=False)
```

```python
import jax
import jax.numpy as jnp
from jax import lax
from jax.experimental import pallas as pl
from jax.experimental.pallas import tpu as pltpu
from jax.sharding import PartitionSpec as P

DIFFUSION = 0.25
STEP_SIZE = 0.5
FIRST = STEP_SIZE / 3.0
SECOND = 2.0 * STEP_SIZE / 3.0
F32 = jnp.float32
BF16 = jnp.bfloat16
VMEM_LIMIT = 20 * 1024 * 1024
SPEC = pl.BlockSpec(memory_space=pltpu.VMEM)
ANYWHERE = pl.BlockSpec(memory_space=pl.ANY)
FROM_HBM = pl.BlockSpec(memory_space=pltpu.HBM)


def chunks_of(xcount):
    last = max(1, 3 * xcount // 8)
    start = (xcount - last + 1) // 2
    middle = list(range(start, start + last))
    return [x for x in range(xcount) if x not in middle], middle


def after(value, *others):
    return lax.optimization_barrier((value, *others))[0]


def call(body, name, args, outs, scratch=(), specs=None, out_specs=None, gflop=0.0, alias=None):
    specs = specs or [SPEC] * len(args)
    space = {id(SPEC): pltpu.VMEM, id(FROM_HBM): pltpu.HBM}
    args = [
        pltpu.with_memory_space_constraint(a, space[id(s)]) if id(s) in space else a for a, s in zip(args, specs)
    ]
    return pl.pallas_call(
        body,
        out_shape=outs,
        in_specs=specs,
        out_specs=out_specs or [SPEC] * len(outs),
        scratch_shapes=list(scratch),
        compiler_params=pltpu.CompilerParams(vmem_limit_bytes=VMEM_LIMIT),
        cost_estimate=pl.CostEstimate(flops=int(gflop * 1e9), bytes_accessed=0, transcendentals=0),
        input_output_aliases=alias or {},
        name=name,
    )(*args)


def load_chunk(fields, cells, with_faces):
    xcount, ycount, owned = fields[0].shape
    count = len(fields)

    def body(*refs):
        field_refs, held_refs, out_ref = refs[:count], refs[count:2 * count], refs[2 * count]
        sems = refs[-1]
        copies = []
        for f in range(count):
            for i, x in enumerate(cells):
                copies.append(pltpu.make_async_copy(field_refs[f].at[x], held_refs[f].at[i], sems.at[f, i]))
                copies[-1].start()
        for f in range(count):
            for i, x in enumerate(cells):
                copies[f * len(cells) + i].wait()
                value = held_refs[f][i].astype(BF16)
                out_ref[f, i * ycount:(i + 1) * ycount, :] = value
                if with_faces and x == 0:
                    refs[2 * count + 1][f] = value
                if with_faces and x == xcount - 1:
                    refs[2 * count + 2][f] = value

    outs = [pltpu.VMEM((len(cells), ycount, owned), F32)] * count
    outs.append(pltpu.VMEM((count, len(cells) * ycount, owned), BF16))
    if with_faces:
        outs += [pltpu.VMEM((count, ycount, owned), BF16)] * 2
    return call(
        body, "load_chunk", fields, outs, scratch=[pltpu.SemaphoreType.DMA((count, len(cells)))],
        specs=[FROM_HBM] * count,
    )


def blocks_dot(blocks, kernels_ref, k, owners):
    depth = blocks[0].shape[-1]
    lhs = jnp.concatenate(blocks, axis=-1)
    rhs = jnp.concatenate(
        [kernels_ref[k, pl.ds(pl.multiple_of(o * depth, depth), depth), :] for o in owners], axis=0
    )
    return jnp.dot(lhs, rhs, preferred_element_type=F32)


def along_y(core):
    return DIFFUSION * (pltpu.roll(core, 1, 0) + pltpu.roll(core, core.shape[0] - 1, 0)) - 2.0 * core


def before_first(ones, twos, lo, hi, growth, chunks):
    _, ycount, owned = ones[0].shape
    xcount = sum(len(cells) for cells in chunks)
    count = len(chunks)
    place = {x: (c, i) for c, cells in enumerate(chunks) for i, x in enumerate(cells)}

    def body(*refs):
        lo_ref, hi_ref, g_ref, *outs = refs[2 * count:]
        growth = g_ref[...]
        for f in range(2):

            def get(x):
                c, i = place[x]
                return refs[f * count + c][i]

            for x, (c, i) in place.items():
                core = get(x)
                before = get(x - 1) if x > 0 else lo_ref[f].astype(F32)
                behind = get(x + 1) if x < xcount - 1 else hi_ref[f].astype(F32)
                outs[c][f, i] = DIFFUSION * (before + behind) + along_y(core) + core * growth

    outs = [pltpu.VMEM((2, len(cells), ycount, owned), F32) for cells in chunks]
    return call(body, "before_first", [*ones, *twos, lo, hi, growth], outs)


def early_part(blocks, kernels, new=None, cells=(), xcount=0):
    rows, owned = blocks[0].shape[0] * blocks[0].shape[1], blocks[0].shape[2]
    count = len(blocks)

    def body(*refs):
        block_refs, k_ref = refs[:count], refs[count]
        copies = []
        if new is None:
            part_ref = refs[-1]
        else:
            new_ref, part_ref, whole_ref, sems = refs[count + 1:]
            copies = [pltpu.make_async_copy(new_ref.at[i], whole_ref.at[x], sems.at[i]) for i, x in enumerate(cells)]
        for copy in copies:
            copy.start()
        me = lax.axis_index("trait")
        values = [r[...].reshape(rows, owned) for r in block_refs]
        for k in range(2):
            part_ref[k] = blocks_dot(values, k_ref, k, [me ^ j for j in range(count)])
        for copy in copies:
            copy.wait()

    args = [*blocks, kernels]
    outs = [pltpu.VMEM((2, rows, owned), F32)]
    if new is None:
        return call(body, "early_part", args, outs, gflop=20.0)[0]
    outs.append(jax.ShapeDtypeStruct((xcount, *new.shape[1:]), F32))
    return call(
        body, "early_part", [*args, new], outs, scratch=[pltpu.SemaphoreType.DMA((len(cells),))],
        out_specs=[SPEC, ANYWHERE], gflop=20.0,
    )


def first_node(part, last, base, one, two, initial, kernels, death, cells, with_faces):
    xcount, ycount, owned = initial.shape
    rows = len(cells) * ycount

    def body(part_ref, last_ref, base_ref, one_ref, two_ref, init_ref, k_ref, d_ref, *refs):
        new_ref, rounded_ref, rest_ref = refs[:3]
        sums = refs[-1]
        me = lax.axis_index("trait")
        for k in range(2):
            far_part = blocks_dot([last_ref[...].reshape(2 * rows, owned)], k_ref, k, [me ^ 3])
            sums[k] = (part_ref[k] + far_part).astype(BF16)
        death = d_ref[...]
        inv_one = 1.0 / (1.0 + FIRST * death)
        inv_two = 1.0 / (1.0 + SECOND * death)
        for i, x in enumerate(cells):
            cores = (one_ref[i], two_ref[i])
            e = []
            for f in range(2):
                at = pl.ds(f * rows + i * ycount, ycount)
                e.append(base_ref[f, i] - cores[f] * sums[0, at, :].astype(F32) + sums[1, at, :].astype(F32))
            full_one = e[0] - death * cores[0]
            full_two = e[1] - death * cores[1]
            new = (
                init_ref[x]
                + FIRST * death * cores[0]
                + STEP_SIZE * (5.0 / 12.0 * full_one - 1.0 / 12.0 * full_two)
            ) * inv_one
            new_ref[i] = new
            rounded = new.astype(BF16)
            rounded_ref[0, i * ycount:(i + 1) * ycount, :] = rounded
            if with_faces and x == 0:
                refs[3][0] = rounded
            if with_faces and x == xcount - 1:
                refs[4][0] = rounded
            rest_ref[i] = (
                new - SECOND * e[0] + SECOND * death * cores[1] + STEP_SIZE / 3.0 * (full_one + full_two)
            ) * inv_two

    outs = [
        pltpu.VMEM((len(cells), ycount, owned), F32),
        pltpu.VMEM((1, rows, owned), BF16),
        pltpu.VMEM((len(cells), ycount, owned), F32),
    ]
    if with_faces:
        outs += [pltpu.VMEM((1, ycount, owned), BF16)] * 2
    args = [part, last, base, one, two, initial, kernels, death]
    return call(
        body, "first_node", args, outs, scratch=[pltpu.VMEM((2, 2 * rows, owned), BF16)],
        gflop=0.0,
    )


def before_second(news, rests, growth, death, begun, blocks, kernels, chunks):
    _, ycount, owned = news[0].shape
    rows = blocks[0].shape[1]
    xcount = sum(len(cells) for cells in chunks)
    count = len(chunks)
    size = len(blocks)
    place = {x: (c, i) for c, cells in enumerate(chunks) for i, x in enumerate(cells)}

    def body(*refs):
        new_refs, rest_refs, block_refs = refs[:count], refs[count:2 * count], refs[2 * count:2 * count + size]
        k_ref, g_ref, d_ref, _, whole_ref, part_ref = refs[2 * count + size:2 * count + size + 6]
        base_refs, sems = refs[2 * count + size + 6:-1], refs[-1]
        copies = [
            pltpu.make_async_copy(new_refs[-1].at[i], whole_ref.at[x], sems.at[i]) for i, x in enumerate(chunks[-1])
        ]
        for copy in copies:
            copy.start()
        me = lax.axis_index("trait")
        values = [r[...].reshape(rows, owned) for r in block_refs]
        for k in range(2):
            part_ref[k] = blocks_dot(values, k_ref, k, [me ^ j for j in range(size)])
        growth = g_ref[...]
        factor = SECOND / (1.0 + SECOND * d_ref[...])
        for x, (c, i) in place.items():
            core = new_refs[c][i]
            e = along_y(core) + core * growth
            for near in (x - 1, x + 1):
                if near in place:
                    e = e + DIFFUSION * new_refs[place[near][0]][place[near][1]]
            base_refs[c][i] = rest_refs[c][i] + factor * e
        for copy in copies:
            copy.wait()

    outs = [jax.ShapeDtypeStruct((xcount, ycount, owned), F32), pltpu.VMEM((2, rows, owned), F32)]
    outs += [pltpu.VMEM((len(cells), ycount, owned), F32) for cells in chunks]
    args = [*news, *rests, *blocks, kernels, growth, death, begun]
    return call(
        body, "before_second", args, outs, scratch=[pltpu.SemaphoreType.DMA((len(chunks[-1]),))],
        specs=[SPEC] * (len(args) - 1) + [FROM_HBM], out_specs=[ANYWHERE] + [SPEC] * (len(outs) - 1), gflop=20.0,
        alias={len(args) - 1: 0},
    )


def whole_sums(part, blocks, kernels):
    rows, owned = blocks[0].shape[1:]

    def body(part_ref, sib_ref, far_ref, farsib_ref, k_ref, sums_ref):
        me = lax.axis_index("trait")
        values = [r[...].reshape(rows, owned) for r in (sib_ref, far_ref, farsib_ref)]
        for k in range(2):
            sums_ref[k] = (part_ref[k] + blocks_dot(values, k_ref, k, [me ^ 1, me ^ 2, me ^ 3])).astype(BF16)

    return call(body, "whole_sums", [part, *blocks, kernels], [pltpu.VMEM((2, rows, owned), BF16)])[0]


def finish(cells, ycount, sums, base_ref, new_ref, factor, faces, held, out_ref, sems):
    copies = []
    for i, x in enumerate(cells):
        at = pl.ds(i * ycount, ycount)
        e = sums[1, at, :].astype(F32) - new_ref[i] * sums[0, at, :].astype(F32)
        if x in faces:
            e = e + DIFFUSION * faces[x][0].astype(F32)
        held[i] = base_ref[i] + factor * e
        copies.append(pltpu.make_async_copy(held.at[i], out_ref.at[x], sems.at[i]))
        copies[-1].start()
    return copies


def second_first(sums, base, new, death, lo, hi, blocks, kernels, cells, xcount):
    _, ycount, owned = new.shape
    rows = blocks[0].shape[1]
    count = len(blocks)

    def body(sums_ref, base_ref, new_ref, d_ref, lo_ref, hi_ref, k_ref, *refs):
        block_refs = refs[:count]
        out_ref, part_ref, held, sems = refs[count:]
        factor = SECOND / (1.0 + SECOND * d_ref[...])
        faces = {0: lo_ref, xcount - 1: hi_ref}
        copies = finish(cells, ycount, sums_ref, base_ref, new_ref, factor, faces, held, out_ref, sems)
        me = lax.axis_index("trait")
        values = [r[...].reshape(rows, owned) for r in block_refs]
        for k in range(2):
            part_ref[k] = blocks_dot(values, k_ref, k, [me ^ j for j in range(count)])
        for copy in copies:
            copy.wait()

    return call(
        body, "second_first", [sums, base, new, death, lo, hi, kernels, *blocks],
        [jax.ShapeDtypeStruct((xcount, ycount, owned), F32), pltpu.VMEM((2, rows, owned), F32)],
        scratch=[pltpu.VMEM((len(cells), ycount, owned), F32), pltpu.SemaphoreType.DMA((len(cells),))],
        out_specs=[ANYWHERE, SPEC],
    )


def second_last(part, last, base, new, death, kernels, begun, cells, xcount):
    _, ycount, owned = new.shape
    rows = len(cells) * ycount

    def body(part_ref, last_ref, base_ref, new_ref, d_ref, k_ref, begun_ref, out_ref, sums, held, sems):
        me = lax.axis_index("trait")
        for k in range(2):
            sums[k] = (part_ref[k] + blocks_dot([last_ref[...].reshape(rows, owned)], k_ref, k, [me ^ 3])).astype(BF16)
        factor = SECOND / (1.0 + SECOND * d_ref[...])
        for copy in finish(cells, ycount, sums, base_ref, new_ref, factor, {}, held, out_ref, sems):
            copy.wait()

    return call(
        body, "second_last", [part, last, base, new, death, kernels, begun],
        [jax.ShapeDtypeStruct((xcount, ycount, owned), F32)],
        scratch=[
            pltpu.VMEM((2, rows, owned), BF16),
            pltpu.VMEM((len(cells), ycount, owned), F32),
            pltpu.SemaphoreType.DMA((len(cells),)),
        ],
        specs=[SPEC] * 6 + [FROM_HBM], out_specs=[ANYWHERE], alias={6: 0},
    )[0]


def local(initial, section_one, section_two, kernels, growth, death_rate):
    xcount, ycount, owned = section_one.shape
    traits = lax.axis_size("trait")
    gcount = lax.axis_size("gx")
    growth = growth.reshape(1, owned)
    death = death_rate.reshape(1, owned)
    chunks = chunks_of(xcount)

    def to_sibling(v):
        return lax.ppermute(v, "trait", [(i, i ^ 1) for i in range(traits)])

    def to_far(v):
        return lax.ppermute(v, "trait", [(i, i ^ 2) for i in range(traits)])

    def faces(head, tail):
        lo = lax.ppermute(tail, "gx", [(i, (i + 1) % gcount) for i in range(gcount)])
        hi = lax.ppermute(head, "gx", [((i + 1) % gcount, i) for i in range(gcount)])
        return lo, hi

    one_a, two_a, own_a, head, tail = load_chunk((section_one, section_two), chunks[0], True)
    far_a = to_far(own_a)
    one_b, two_b, own_b = load_chunk((after(section_one, own_a), section_two), chunks[1], False)
    far_b = to_far(own_b)
    head, tail, kernels = lax.optimization_barrier((head, tail, kernels, own_b))[:3]
    lo, hi = faces(head, tail)
    base_a, base_b = before_first((one_a, one_b), (two_a, two_b), lo, hi, growth, chunks)
    sib_a = to_sibling(after(own_a, own_b))
    sib_b = to_sibling(own_b)
    far_a = after(far_a, base_a)
    farsib_a = to_sibling(far_a)
    part_a = early_part([own_a, sib_a, far_a], kernels)
    new_a, rounded_a, rest_a, new_head, new_tail = first_node(
        part_a, farsib_a, base_a, one_a, two_a, initial, kernels, death, chunks[0], True
    )
    nfar_a = to_far(rounded_a)
    nsib_a = to_sibling(rounded_a)

    far_b = after(far_b, rounded_a)
    farsib_b = to_sibling(far_b)
    part_b, new_one = early_part([own_b, sib_b, far_b], kernels, new_a, chunks[0], xcount)
    new_b, rounded_b, rest_b = first_node(
        part_b, farsib_b, base_b, one_b, two_b, initial, kernels, death, chunks[1], False
    )
    nfar_b = to_far(rounded_b)
    nsib_b = to_sibling(rounded_b)
    new_lo, new_hi = faces(*lax.optimization_barrier((new_head, new_tail, rounded_b))[:2])
    nfar_a = after(nfar_a, rounded_b)
    nfarsib_a = to_sibling(nfar_a)
    new_one, npart_a, nbase_a, nbase_b = before_second(
        (new_a, new_b), (rest_a, rest_b), growth, death, new_one, [rounded_a], kernels, chunks
    )
    sums_a = whole_sums(npart_a, [nsib_a, nfar_a, nfarsib_a], after(kernels, nbase_a))
    nfar_b = after(nfar_b, sums_a, new_lo, new_hi)
    nfarsib_b = to_sibling(nfar_b)
    begun, npart_b = second_first(
        sums_a, nbase_a, new_a, death, new_lo, new_hi, [rounded_b, nsib_b, nfar_b], kernels, chunks[0], xcount
    )
    new_two = second_last(npart_b, nfarsib_b, nbase_b, new_b, death, kernels, begun, chunks[1], xcount)
    return new_one, new_two


def solution(mesh):
    in_specs = (
        P("gx", None, "trait"),
        P("gx", None, "trait"),
        P("gx", None, "trait"),
        P(None, None, "trait"),
        P("trait"),
        P("trait"),
    )
    out_specs = (P("gx", None, "trait"), P("gx", None, "trait"))
    return jax.shard_map(local, mesh=mesh, in_specs=in_specs, out_specs=out_specs, check_vma=False)
```

```python
import jax
import jax.numpy as jnp
from jax import lax
from jax.experimental import pallas as pl
from jax.experimental.pallas import tpu as pltpu
from jax.sharding import PartitionSpec as P

DIFFUSION = 0.25
STEP_SIZE = 0.5
FIRST = STEP_SIZE / 3.0
SECOND = 2.0 * STEP_SIZE / 3.0
F32 = jnp.float32
BF16 = jnp.bfloat16
VMEM_LIMIT = 20 * 1024 * 1024
SPEC = pl.BlockSpec(memory_space=pltpu.VMEM)
ANYWHERE = pl.BlockSpec(memory_space=pl.ANY)
FROM_HBM = pl.BlockSpec(memory_space=pltpu.HBM)


def chunks_of(xcount):
    last = max(1, 3 * xcount // 8)
    inner = list(range(1, xcount - 1))
    return [0, xcount - 1], inner[:-last], inner[-last:]


def after(value, *others):
    return lax.optimization_barrier((value, *others))[0]


def call(body, name, args, outs, scratch=(), specs=None, out_specs=None, gflop=0.0, alias=None):
    specs = specs or [SPEC] * len(args)
    space = {id(SPEC): pltpu.VMEM, id(FROM_HBM): pltpu.HBM}
    args = [
        pltpu.with_memory_space_constraint(a, space[id(s)]) if id(s) in space else a for a, s in zip(args, specs)
    ]
    return pl.pallas_call(
        body,
        out_shape=outs,
        in_specs=specs,
        out_specs=out_specs or [SPEC] * len(outs),
        scratch_shapes=list(scratch),
        compiler_params=pltpu.CompilerParams(vmem_limit_bytes=VMEM_LIMIT),
        cost_estimate=pl.CostEstimate(flops=int(gflop * 1e9), bytes_accessed=0, transcendentals=0),
        input_output_aliases=alias or {},
        name=name,
    )(*args)


def load_cells(fields, groups, with_faces):
    xcount, ycount, owned = fields[0].shape
    count = len(fields)
    size = count + 1

    def body(*refs):
        field_refs, outs, sems = refs[:count], refs[count:-1], refs[-1]
        copies = {}
        for g, cells in enumerate(groups):
            for f in range(count):
                for i, x in enumerate(cells):
                    copies[f, x] = pltpu.make_async_copy(field_refs[f].at[x], outs[size * g + f].at[i], sems.at[f, x])
                    copies[f, x].start()
        for g, cells in enumerate(groups):
            for f in range(count):
                for i, x in enumerate(cells):
                    copies[f, x].wait()
                    value = outs[size * g + f][i].astype(BF16)
                    outs[size * g + count][f, pl.ds(i * ycount, ycount), :] = value
                    if with_faces and x in (0, xcount - 1):
                        outs[-2 if x == 0 else -1][f] = value

    outs = []
    for cells in groups:
        outs += [pltpu.VMEM((len(cells), ycount, owned), F32)] * count
        outs.append(pltpu.VMEM((count, len(cells) * ycount, owned), BF16))
    if with_faces:
        outs += [pltpu.VMEM((count, ycount, owned), BF16)] * 2
    return call(
        body, "load_cells", fields, outs, scratch=[pltpu.SemaphoreType.DMA((count, xcount))],
        specs=[FROM_HBM] * count,
    )


def blocks_dot(blocks, kernels_ref, k, owners):
    depth = blocks[0].shape[-1]
    lhs = jnp.concatenate(blocks, axis=-1)
    rhs = jnp.concatenate(
        [kernels_ref[k, pl.ds(pl.multiple_of(o * depth, depth), depth), :] for o in owners], axis=0
    )
    return jnp.dot(lhs, rhs, preferred_element_type=F32)


def along_y(core):
    return DIFFUSION * (pltpu.roll(core, 1, 0) + pltpu.roll(core, core.shape[0] - 1, 0)) - 2.0 * core


def before_first(ones, twos, lo, hi, growth, chunks):
    _, ycount, owned = ones[0].shape
    xcount = sum(len(cells) for cells in chunks)
    count = len(chunks)
    place = {x: (c, i) for c, cells in enumerate(chunks) for i, x in enumerate(cells)}

    def body(*refs):
        lo_ref, hi_ref, g_ref, *outs = refs[2 * count:]
        growth = g_ref[...]
        for f in range(2):

            def get(x):
                c, i = place[x]
                return refs[f * count + c][i]

            for x, (c, i) in place.items():
                core = get(x)
                before = get(x - 1) if x > 0 else lo_ref[f].astype(F32)
                behind = get(x + 1) if x < xcount - 1 else hi_ref[f].astype(F32)
                outs[c][f, i] = DIFFUSION * (before + behind) + along_y(core) + core * growth

    outs = [pltpu.VMEM((2, len(cells), ycount, owned), F32) for cells in chunks]
    return call(body, "before_first", [*ones, *twos, lo, hi, growth], outs)


def early_part(own, sib, far, kernels, new=None, cells=(), xcount=0):
    fields, size, owned = own.shape
    rows = fields * size

    def body(own_ref, sib_ref, far_ref, k_ref, *refs):
        copies = []
        if new is None:
            (part_ref,) = refs
        else:
            new_ref, part_ref, whole_ref, sems = refs
            copies = [pltpu.make_async_copy(new_ref.at[i], whole_ref.at[x], sems.at[i]) for i, x in enumerate(cells)]
        for copy in copies:
            copy.start()
        me = lax.axis_index("trait")
        values = [r[...].reshape(rows, owned) for r in (own_ref, sib_ref, far_ref)]
        for k in range(2):
            part_ref[k] = blocks_dot(values, k_ref, k, [me, me ^ 1, me ^ 2])
        for copy in copies:
            copy.wait()

    args = [own, sib, far, kernels]
    outs = [pltpu.VMEM((2, rows, owned), F32)]
    if new is None:
        return call(body, "early_part", args, outs, gflop=20.0)[0]
    outs.append(jax.ShapeDtypeStruct((xcount, *new.shape[1:]), F32))
    return call(
        body, "early_part", [*args, new], outs, scratch=[pltpu.SemaphoreType.DMA((len(cells),))],
        out_specs=[SPEC, ANYWHERE], gflop=20.0,
    )


def first_node(part, last, base, one, two, initial, kernels, death, cells, with_faces, begun=()):
    xcount, ycount, owned = initial.shape
    rows = len(cells) * ycount
    count = len(begun)
    ahead = begun[0].shape[0] if begun else 0

    def body(part_ref, last_ref, base_ref, one_ref, two_ref, init_ref, k_ref, d_ref, *refs):
        begun_refs, (new_ref, rounded_ref, rest_ref, *face_refs, sums) = refs[:count], refs[count:]
        me = lax.axis_index("trait")
        for k in range(2):
            far_part = blocks_dot([last_ref[...].reshape(2 * rows, owned)], k_ref, k, [me ^ 3])
            sums[k] = (part_ref[k] + far_part).astype(BF16)
        if begun:
            new_ref[pl.ds(0, ahead)] = begun_refs[0][...]
            rounded_ref[:, pl.ds(0, ahead * ycount), :] = begun_refs[1][...]
            rest_ref[pl.ds(0, ahead)] = begun_refs[2][...]
        death = d_ref[...]
        inv_one = 1.0 / (1.0 + FIRST * death)
        inv_two = 1.0 / (1.0 + SECOND * death)
        for i, x in enumerate(cells):
            cores = (one_ref[i], two_ref[i])
            e = []
            for f in range(2):
                at = pl.ds(f * rows + i * ycount, ycount)
                e.append(base_ref[f, i] - cores[f] * sums[0, at, :].astype(F32) + sums[1, at, :].astype(F32))
            full_one = e[0] - death * cores[0]
            full_two = e[1] - death * cores[1]
            new = (
                init_ref[x]
                + FIRST * death * cores[0]
                + STEP_SIZE * (5.0 / 12.0 * full_one - 1.0 / 12.0 * full_two)
            ) * inv_one
            new_ref[ahead + i] = new
            rounded = new.astype(BF16)
            rounded_ref[0, pl.ds((ahead + i) * ycount, ycount), :] = rounded
            if with_faces and x in (0, xcount - 1):
                face_refs[x != 0][0] = rounded
            rest_ref[ahead + i] = (
                new - SECOND * e[0] + SECOND * death * cores[1] + STEP_SIZE / 3.0 * (full_one + full_two)
            ) * inv_two

    size = ahead + len(cells)
    outs = [
        pltpu.VMEM((size, ycount, owned), F32),
        pltpu.VMEM((1, size * ycount, owned), BF16),
        pltpu.VMEM((size, ycount, owned), F32),
    ]
    if with_faces:
        outs += [pltpu.VMEM((1, ycount, owned), BF16)] * 2
    return call(
        body, "first_node", [part, last, base, one, two, initial, kernels, death, *begun], outs,
        scratch=[pltpu.VMEM((2, 2 * rows, owned), BF16)],
    )


def before_second(news, rests, growth, death, begun, blocks, kernels, chunks):
    _, ycount, owned = news[0].shape
    rows = blocks[0].shape[1]
    xcount = sum(len(cells) for cells in chunks)
    count = len(chunks)
    size = len(blocks)
    place = {x: (c, i) for c, cells in enumerate(chunks) for i, x in enumerate(cells)}

    def body(*refs):
        new_refs, rest_refs, block_refs = refs[:count], refs[count:2 * count], refs[2 * count:2 * count + size]
        k_ref, g_ref, d_ref, _, whole_ref, part_ref = refs[2 * count + size:2 * count + size + 6]
        base_refs, sems = refs[2 * count + size + 6:-1], refs[-1]
        copies = [
            pltpu.make_async_copy(new_refs[-1].at[i], whole_ref.at[x], sems.at[i]) for i, x in enumerate(chunks[-1])
        ]
        for copy in copies:
            copy.start()
        me = lax.axis_index("trait")
        values = [r[...].reshape(rows, owned) for r in block_refs]
        for k in range(2):
            part_ref[k] = blocks_dot(values, k_ref, k, [me ^ j for j in range(size)])
        growth = g_ref[...]
        factor = SECOND / (1.0 + SECOND * d_ref[...])
        for x, (c, i) in place.items():
            core = new_refs[c][i]
            e = along_y(core) + core * growth
            for near in (x - 1, x + 1):
                if near in place:
                    e = e + DIFFUSION * new_refs[place[near][0]][place[near][1]]
            base_refs[c][i] = rest_refs[c][i] + factor * e
        for copy in copies:
            copy.wait()

    outs = [jax.ShapeDtypeStruct((xcount, ycount, owned), F32), pltpu.VMEM((2, rows, owned), F32)]
    outs += [pltpu.VMEM((len(cells), ycount, owned), F32) for cells in chunks]
    args = [*news, *rests, *blocks, kernels, growth, death, begun]
    return call(
        body, "before_second", args, outs, scratch=[pltpu.SemaphoreType.DMA((len(chunks[-1]),))],
        specs=[SPEC] * (len(args) - 1) + [FROM_HBM], out_specs=[ANYWHERE] + [SPEC] * (len(outs) - 1), gflop=20.0,
        alias={len(args) - 1: 0},
    )


def whole_sums(part, blocks, kernels):
    rows, owned = blocks[0].shape[1:]

    def body(part_ref, sib_ref, far_ref, farsib_ref, k_ref, sums_ref):
        me = lax.axis_index("trait")
        values = [r[...].reshape(rows, owned) for r in (sib_ref, far_ref, farsib_ref)]
        for k in range(2):
            sums_ref[k] = (part_ref[k] + blocks_dot(values, k_ref, k, [me ^ 1, me ^ 2, me ^ 3])).astype(BF16)

    return call(body, "whole_sums", [part, *blocks, kernels], [pltpu.VMEM((2, rows, owned), BF16)])[0]


def finish(cells, ycount, sums, base_ref, new_ref, factor, faces, held, out_ref, sems):
    copies = []
    for i, x in enumerate(cells):
        at = pl.ds(i * ycount, ycount)
        e = sums[1, at, :].astype(F32) - new_ref[i] * sums[0, at, :].astype(F32)
        if x in faces:
            e = e + DIFFUSION * faces[x][0].astype(F32)
        held[i] = base_ref[i] + factor * e
        copies.append(pltpu.make_async_copy(held.at[i], out_ref.at[x], sems.at[i]))
        copies[-1].start()
    return copies


def second_first(sums, base, new, death, lo, hi, blocks, kernels, cells, xcount):
    _, ycount, owned = new.shape
    rows = blocks[0].shape[1]
    count = len(blocks)

    def body(sums_ref, base_ref, new_ref, d_ref, lo_ref, hi_ref, k_ref, *refs):
        block_refs = refs[:count]
        out_ref, part_ref, held, sems = refs[count:]
        factor = SECOND / (1.0 + SECOND * d_ref[...])
        faces = {0: lo_ref, xcount - 1: hi_ref}
        copies = finish(cells, ycount, sums_ref, base_ref, new_ref, factor, faces, held, out_ref, sems)
        me = lax.axis_index("trait")
        values = [r[...].reshape(rows, owned) for r in block_refs]
        for k in range(2):
            part_ref[k] = blocks_dot(values, k_ref, k, [me ^ j for j in range(count)])
        for copy in copies:
            copy.wait()

    return call(
        body, "second_first", [sums, base, new, death, lo, hi, kernels, *blocks],
        [jax.ShapeDtypeStruct((xcount, ycount, owned), F32), pltpu.VMEM((2, rows, owned), F32)],
        scratch=[pltpu.VMEM((len(cells), ycount, owned), F32), pltpu.SemaphoreType.DMA((len(cells),))],
        out_specs=[ANYWHERE, SPEC],
    )


def second_last(part, last, base, new, death, kernels, begun, cells, xcount):
    _, ycount, owned = new.shape
    rows = len(cells) * ycount

    def body(part_ref, last_ref, base_ref, new_ref, d_ref, k_ref, begun_ref, out_ref, sums, held, sems):
        me = lax.axis_index("trait")
        for k in range(2):
            sums[k] = (part_ref[k] + blocks_dot([last_ref[...].reshape(rows, owned)], k_ref, k, [me ^ 3])).astype(BF16)
        factor = SECOND / (1.0 + SECOND * d_ref[...])
        for copy in finish(cells, ycount, sums, base_ref, new_ref, factor, {}, held, out_ref, sems):
            copy.wait()

    return call(
        body, "second_last", [part, last, base, new, death, kernels, begun],
        [jax.ShapeDtypeStruct((xcount, ycount, owned), F32)],
        scratch=[
            pltpu.VMEM((2, rows, owned), BF16),
            pltpu.VMEM((len(cells), ycount, owned), F32),
            pltpu.SemaphoreType.DMA((len(cells),)),
        ],
        specs=[SPEC] * 6 + [FROM_HBM], out_specs=[ANYWHERE], alias={6: 0},
    )[0]


def local(initial, section_one, section_two, kernels, growth, death_rate):
    xcount, ycount, owned = section_one.shape
    traits = lax.axis_size("trait")
    gcount = lax.axis_size("gx")
    growth = growth.reshape(1, owned)
    death = death_rate.reshape(1, owned)
    chunks = chunks_of(xcount)

    def to_sibling(v):
        return lax.ppermute(v, "trait", [(i, i ^ 1) for i in range(traits)])

    def to_far(v):
        return lax.ppermute(v, "trait", [(i, i ^ 2) for i in range(traits)])

    def faces(head, tail):
        lo = lax.ppermute(tail, "gx", [(i, (i + 1) % gcount) for i in range(gcount)])
        hi = lax.ppermute(head, "gx", [((i + 1) % gcount, i) for i in range(gcount)])
        return lo, hi

    inputs = (section_one, section_two)
    outer, inner, ending = chunks
    one_e, two_e, own_e, head, tail = load_cells(inputs, [outer], True)
    far_e = to_far(own_e)
    one_a, two_a, own_a, one_b, two_b, own_b = load_cells((after(section_one, own_e), section_two), [inner, ending], False)
    far_a = to_far(own_a)
    far_b = to_far(own_b)
    head, tail, kernels = lax.optimization_barrier((head, tail, kernels, own_b))[:3]
    lo, hi = faces(head, tail)
    sib_e = to_sibling(after(own_e, own_b))
    sib_a = to_sibling(own_a)
    sib_b = to_sibling(own_b)
    base_e, base_a, base_b = before_first((one_e, one_a, one_b), (two_e, two_a, two_b), lo, hi, growth, chunks)

    far_e = after(far_e, base_e)
    farsib_e = to_sibling(far_e)
    part_e = early_part(own_e, sib_e, far_e, kernels)
    *begun, new_head, new_tail = first_node(
        part_e, farsib_e, base_e, one_e, two_e, initial, kernels, death, outer, True
    )
    new_lo, new_hi = faces(new_head, new_tail)

    far_a = after(far_a, new_lo, new_hi)
    farsib_a = to_sibling(far_a)
    part_a = early_part(own_a, sib_a, far_a, kernels)
    new_a, rounded_a, rest_a = first_node(
        part_a, farsib_a, base_a, one_a, two_a, initial, kernels, death, inner, False, begun
    )
    chunks = (outer + inner, ending)
    nfar_a = to_far(rounded_a)
    nsib_a = to_sibling(rounded_a)

    far_b = after(far_b, rounded_a)
    farsib_b = to_sibling(far_b)
    part_b, new_one = early_part(own_b, sib_b, far_b, kernels, new_a, chunks[0], xcount)
    new_b, rounded_b, rest_b = first_node(
        part_b, farsib_b, base_b, one_b, two_b, initial, kernels, death, chunks[1], False
    )
    nfar_b = to_far(rounded_b)
    nsib_b = to_sibling(rounded_b)
    nfar_a = after(nfar_a, rounded_b)
    nfarsib_a = to_sibling(nfar_a)
    new_one, npart_a, nbase_a, nbase_b = before_second(
        (new_a, new_b), (rest_a, rest_b), growth, death, new_one, [rounded_a], kernels, chunks
    )
    sums_a = whole_sums(npart_a, [nsib_a, nfar_a, nfarsib_a], after(kernels, nbase_a))
    nfar_b = after(nfar_b, sums_a)
    nfarsib_b = to_sibling(nfar_b)
    begun, npart_b = second_first(
        sums_a, nbase_a, new_a, death, new_lo, new_hi, [rounded_b, nsib_b, nfar_b], kernels, chunks[0], xcount
    )
    new_two = second_last(npart_b, nfarsib_b, nbase_b, new_b, death, kernels, begun, chunks[1], xcount)
    return new_one, new_two


def solution(mesh):
    in_specs = (
        P("gx", None, "trait"),
        P("gx", None, "trait"),
        P("gx", None, "trait"),
        P(None, None, "trait"),
        P("trait"),
        P("trait"),
    )
    out_specs = (P("gx", None, "trait"), P("gx", None, "trait"))
    return jax.shard_map(local, mesh=mesh, in_specs=in_specs, out_specs=out_specs, check_vma=False)
```

```python
import jax
import jax.numpy as jnp
from jax import lax
from jax.experimental import pallas as pl
from jax.experimental.pallas import tpu as pltpu
from jax.sharding import PartitionSpec as P

DIFFUSION = 0.25
STEP_SIZE = 0.5
FIRST = STEP_SIZE / 3.0
SECOND = 2.0 * STEP_SIZE / 3.0
F32 = jnp.float32
BF16 = jnp.bfloat16
VMEM_LIMIT = 20 * 1024 * 1024
SPEC = pl.BlockSpec(memory_space=pltpu.VMEM)
ANYWHERE = pl.BlockSpec(memory_space=pl.ANY)
FROM_HBM = pl.BlockSpec(memory_space=pltpu.HBM)


def chunks_of(xcount):
    last = max(1, 3 * xcount // 8)
    start = (xcount - last + 1) // 2
    middle = list(range(start, start + last))
    return [x for x in range(xcount) if x not in middle], middle


def after(value, *others):
    return lax.optimization_barrier((value, *others))[0]


def call(body, name, args, outs, scratch=(), specs=None, out_specs=None, gflop=0.0, alias=None):
    specs = specs or [SPEC] * len(args)
    space = {id(SPEC): pltpu.VMEM, id(FROM_HBM): pltpu.HBM}
    args = [
        pltpu.with_memory_space_constraint(a, space[id(s)]) if id(s) in space else a for a, s in zip(args, specs)
    ]
    return pl.pallas_call(
        body,
        out_shape=outs,
        in_specs=specs,
        out_specs=out_specs or [SPEC] * len(outs),
        scratch_shapes=list(scratch),
        compiler_params=pltpu.CompilerParams(vmem_limit_bytes=VMEM_LIMIT),
        cost_estimate=pl.CostEstimate(flops=int(gflop * 1e9), bytes_accessed=0, transcendentals=0),
        input_output_aliases=alias or {},
        name=name,
    )(*args)


def load_chunk(fields, cells, with_faces):
    xcount, ycount, owned = fields[0].shape
    count = len(fields)

    def body(*refs):
        field_refs, held_refs, out_ref = refs[:count], refs[count:2 * count], refs[2 * count]
        sems = refs[-1]
        copies = []
        for f in range(count):
            for i, x in enumerate(cells):
                copies.append(pltpu.make_async_copy(field_refs[f].at[x], held_refs[f].at[i], sems.at[f, i]))
                copies[-1].start()
        for f in range(count):
            for i, x in enumerate(cells):
                copies[f * len(cells) + i].wait()
                value = held_refs[f][i].astype(BF16)
                out_ref[f, i * ycount:(i + 1) * ycount, :] = value
                if with_faces and x == 0:
                    refs[2 * count + 1][f] = value
                if with_faces and x == xcount - 1:
                    refs[2 * count + 2][f] = value

    outs = [pltpu.VMEM((len(cells), ycount, owned), F32)] * count
    outs.append(pltpu.VMEM((count, len(cells) * ycount, owned), BF16))
    if with_faces:
        outs += [pltpu.VMEM((count, ycount, owned), BF16)] * 2
    return call(
        body, "load_chunk", fields, outs, scratch=[pltpu.SemaphoreType.DMA((count, len(cells)))],
        specs=[FROM_HBM] * count,
    )


def blocks_dot(blocks, kernels_ref, k, owners):
    depth = blocks[0].shape[-1]
    lhs = jnp.concatenate(blocks, axis=-1)
    rhs = jnp.concatenate(
        [kernels_ref[k, pl.ds(pl.multiple_of(o * depth, depth), depth), :] for o in owners], axis=0
    )
    return jnp.dot(lhs, rhs, preferred_element_type=F32)


def along_y(core):
    return DIFFUSION * (pltpu.roll(core, 1, 0) + pltpu.roll(core, core.shape[0] - 1, 0)) - 2.0 * core


def before_first(ones, twos, lo, hi, growth, chunks):
    _, ycount, owned = ones[0].shape
    xcount = sum(len(cells) for cells in chunks)
    count = len(chunks)
    place = {x: (c, i) for c, cells in enumerate(chunks) for i, x in enumerate(cells)}

    def body(*refs):
        lo_ref, hi_ref, g_ref, *outs = refs[2 * count:]
        growth = g_ref[...]
        for f in range(2):

            def get(x):
                c, i = place[x]
                return refs[f * count + c][i]

            for x, (c, i) in place.items():
                core = get(x)
                before = get(x - 1) if x > 0 else lo_ref[f].astype(F32)
                behind = get(x + 1) if x < xcount - 1 else hi_ref[f].astype(F32)
                outs[c][f, i] = DIFFUSION * (before + behind) + along_y(core) + core * growth

    outs = [pltpu.VMEM((2, len(cells), ycount, owned), F32) for cells in chunks]
    return call(body, "before_first", [*ones, *twos, lo, hi, growth], outs)


def early_part(blocks, kernels, new=None, cells=(), xcount=0):
    rows, owned = blocks[0].shape[0] * blocks[0].shape[1], blocks[0].shape[2]
    count = len(blocks)

    def body(*refs):
        block_refs, k_ref = refs[:count], refs[count]
        copies = []
        if new is None:
            part_ref = refs[-1]
        else:
            new_ref, part_ref, whole_ref, sems = refs[count + 1:]
            copies = [pltpu.make_async_copy(new_ref.at[i], whole_ref.at[x], sems.at[i]) for i, x in enumerate(cells)]
        for copy in copies:
            copy.start()
        me = lax.axis_index("trait")
        values = [r[...].reshape(rows, owned) for r in block_refs]
        for k in range(2):
            part_ref[k] = blocks_dot(values, k_ref, k, [me ^ j for j in range(count)])
        for copy in copies:
            copy.wait()

    args = [*blocks, kernels]
    outs = [pltpu.VMEM((2, rows, owned), F32)]
    if new is None:
        return call(body, "early_part", args, outs, gflop=20.0)[0]
    outs.append(jax.ShapeDtypeStruct((xcount, *new.shape[1:]), F32))
    return call(
        body, "early_part", [*args, new], outs, scratch=[pltpu.SemaphoreType.DMA((len(cells),))],
        out_specs=[SPEC, ANYWHERE], gflop=20.0,
    )


def first_node(part, last, base, one, two, initial, kernels, death, cells, with_faces):
    xcount, ycount, owned = initial.shape
    rows = len(cells) * ycount

    def body(part_ref, last_ref, base_ref, one_ref, two_ref, init_ref, k_ref, d_ref, *refs):
        new_ref, rounded_ref, rest_ref = refs[:3]
        sums = refs[-1]
        me = lax.axis_index("trait")
        for k in range(2):
            far_part = blocks_dot([last_ref[...].reshape(2 * rows, owned)], k_ref, k, [me ^ 3])
            sums[k] = (part_ref[k] + far_part).astype(BF16)
        death = d_ref[...]
        inv_one = 1.0 / (1.0 + FIRST * death)
        inv_two = 1.0 / (1.0 + SECOND * death)
        for i, x in enumerate(cells):
            cores = (one_ref[i], two_ref[i])
            e = []
            for f in range(2):
                at = pl.ds(f * rows + i * ycount, ycount)
                e.append(base_ref[f, i] - cores[f] * sums[0, at, :].astype(F32) + sums[1, at, :].astype(F32))
            full_one = e[0] - death * cores[0]
            full_two = e[1] - death * cores[1]
            new = (
                init_ref[x]
                + FIRST * death * cores[0]
                + STEP_SIZE * (5.0 / 12.0 * full_one - 1.0 / 12.0 * full_two)
            ) * inv_one
            new_ref[i] = new
            rounded = new.astype(BF16)
            rounded_ref[0, i * ycount:(i + 1) * ycount, :] = rounded
            if with_faces and x == 0:
                refs[3][0] = rounded
            if with_faces and x == xcount - 1:
                refs[4][0] = rounded
            rest_ref[i] = (
                new - SECOND * e[0] + SECOND * death * cores[1] + STEP_SIZE / 3.0 * (full_one + full_two)
            ) * inv_two

    outs = [
        pltpu.VMEM((len(cells), ycount, owned), F32),
        pltpu.VMEM((1, rows, owned), BF16),
        pltpu.VMEM((len(cells), ycount, owned), F32),
    ]
    if with_faces:
        outs += [pltpu.VMEM((1, ycount, owned), BF16)] * 2
    args = [part, last, base, one, two, initial, kernels, death]
    return call(
        body, "first_node", args, outs, scratch=[pltpu.VMEM((2, 2 * rows, owned), BF16)],
        gflop=0.0,
    )


def before_second(news, rests, growth, death, begun, blocks, kernels, chunks):
    _, ycount, owned = news[0].shape
    rows = blocks[0].shape[1]
    xcount = sum(len(cells) for cells in chunks)
    count = len(chunks)
    size = len(blocks)
    place = {x: (c, i) for c, cells in enumerate(chunks) for i, x in enumerate(cells)}

    def body(*refs):
        new_refs, rest_refs, block_refs = refs[:count], refs[count:2 * count], refs[2 * count:2 * count + size]
        k_ref, g_ref, d_ref, _, whole_ref, part_ref = refs[2 * count + size:2 * count + size + 6]
        base_refs, sems = refs[2 * count + size + 6:-1], refs[-1]
        copies = [
            pltpu.make_async_copy(new_refs[-1].at[i], whole_ref.at[x], sems.at[i]) for i, x in enumerate(chunks[-1])
        ]
        for copy in copies:
            copy.start()
        me = lax.axis_index("trait")
        values = [r[...].reshape(rows, owned) for r in block_refs]
        for k in range(2):
            part_ref[k] = blocks_dot(values, k_ref, k, [me ^ j for j in range(size)])
        growth = g_ref[...]
        factor = SECOND / (1.0 + SECOND * d_ref[...])
        for x, (c, i) in place.items():
            core = new_refs[c][i]
            e = along_y(core) + core * growth
            for near in (x - 1, x + 1):
                if near in place:
                    e = e + DIFFUSION * new_refs[place[near][0]][place[near][1]]
            base_refs[c][i] = rest_refs[c][i] + factor * e
        for copy in copies:
            copy.wait()

    outs = [jax.ShapeDtypeStruct((xcount, ycount, owned), F32), pltpu.VMEM((2, rows, owned), F32)]
    outs += [pltpu.VMEM((len(cells), ycount, owned), F32) for cells in chunks]
    args = [*news, *rests, *blocks, kernels, growth, death, begun]
    return call(
        body, "before_second", args, outs, scratch=[pltpu.SemaphoreType.DMA((len(chunks[-1]),))],
        specs=[SPEC] * (len(args) - 1) + [FROM_HBM], out_specs=[ANYWHERE] + [SPEC] * (len(outs) - 1), gflop=20.0,
        alias={len(args) - 1: 0},
    )


def whole_sums(part, blocks, kernels):
    rows, owned = blocks[0].shape[1:]

    def body(part_ref, sib_ref, far_ref, farsib_ref, k_ref, sums_ref):
        me = lax.axis_index("trait")
        values = [r[...].reshape(rows, owned) for r in (sib_ref, far_ref, farsib_ref)]
        for k in range(2):
            sums_ref[k] = (part_ref[k] + blocks_dot(values, k_ref, k, [me ^ 1, me ^ 2, me ^ 3])).astype(BF16)

    return call(body, "whole_sums", [part, *blocks, kernels], [pltpu.VMEM((2, rows, owned), BF16)])[0]


def finish(cells, ycount, sums, base_ref, new_ref, factor, faces, held, out_ref, sems):
    copies = []
    for i, x in enumerate(cells):
        at = pl.ds(i * ycount, ycount)
        e = sums[1, at, :].astype(F32) - new_ref[i] * sums[0, at, :].astype(F32)
        if x in faces:
            e = e + DIFFUSION * faces[x][0].astype(F32)
        held[i] = base_ref[i] + factor * e
        copies.append(pltpu.make_async_copy(held.at[i], out_ref.at[x], sems.at[i]))
        copies[-1].start()
    return copies


def second_first(sums, base, new, death, lo, hi, blocks, kernels, cells, xcount):
    _, ycount, owned = new.shape
    rows = blocks[0].shape[1]
    count = len(blocks)

    def body(sums_ref, base_ref, new_ref, d_ref, lo_ref, hi_ref, k_ref, *refs):
        block_refs = refs[:count]
        out_ref, part_ref, held, sems = refs[count:]
        factor = SECOND / (1.0 + SECOND * d_ref[...])
        faces = {0: lo_ref, xcount - 1: hi_ref}
        copies = finish(cells, ycount, sums_ref, base_ref, new_ref, factor, faces, held, out_ref, sems)
        me = lax.axis_index("trait")
        values = [r[...].reshape(rows, owned) for r in block_refs]
        for k in range(2):
            part_ref[k] = blocks_dot(values, k_ref, k, [me ^ j for j in range(count)])
        for copy in copies:
            copy.wait()

    return call(
        body, "second_first", [sums, base, new, death, lo, hi, kernels, *blocks],
        [jax.ShapeDtypeStruct((xcount, ycount, owned), F32), pltpu.VMEM((2, rows, owned), F32)],
        scratch=[pltpu.VMEM((len(cells), ycount, owned), F32), pltpu.SemaphoreType.DMA((len(cells),))],
        out_specs=[ANYWHERE, SPEC],
    )


def second_last(part, last, base, new, death, kernels, begun, cells, xcount):
    _, ycount, owned = new.shape
    rows = len(cells) * ycount

    def body(part_ref, last_ref, base_ref, new_ref, d_ref, k_ref, begun_ref, out_ref, sums, held, sems):
        me = lax.axis_index("trait")
        for k in range(2):
            sums[k] = (part_ref[k] + blocks_dot([last_ref[...].reshape(rows, owned)], k_ref, k, [me ^ 3])).astype(BF16)
        factor = SECOND / (1.0 + SECOND * d_ref[...])
        for copy in finish(cells, ycount, sums, base_ref, new_ref, factor, {}, held, out_ref, sems):
            copy.wait()

    return call(
        body, "second_last", [part, last, base, new, death, kernels, begun],
        [jax.ShapeDtypeStruct((xcount, ycount, owned), F32)],
        scratch=[
            pltpu.VMEM((2, rows, owned), BF16),
            pltpu.VMEM((len(cells), ycount, owned), F32),
            pltpu.SemaphoreType.DMA((len(cells),)),
        ],
        specs=[SPEC] * 6 + [FROM_HBM], out_specs=[ANYWHERE], alias={6: 0},
    )[0]


def local(initial, section_one, section_two, kernels, growth, death_rate):
    xcount, ycount, owned = section_one.shape
    traits = lax.axis_size("trait")
    gcount = lax.axis_size("gx")
    growth = growth.reshape(1, owned)
    death = death_rate.reshape(1, owned)
    chunks = chunks_of(xcount)

    def to_sibling(v):
        return lax.ppermute(v, "trait", [(i, i ^ 1) for i in range(traits)])

    def to_far(v):
        return lax.ppermute(v, "trait", [(i, i ^ 2) for i in range(traits)])

    def from_below(tail):
        return lax.ppermute(tail, "gx", [(i, (i + 1) % gcount) for i in range(gcount)])

    def from_above(head):
        return lax.ppermute(head, "gx", [((i + 1) % gcount, i) for i in range(gcount)])

    one_a, two_a, own_a, head, tail = load_chunk((section_one, section_two), chunks[0], True)
    far_a = to_far(own_a)
    one_b, two_b, own_b = load_chunk((after(section_one, own_a), section_two), chunks[1], False)
    far_b = to_far(own_b)
    head, tail, kernels = lax.optimization_barrier((head, tail, kernels, own_b))[:3]
    lo, hi = from_below(tail), from_above(head)
    base_a, base_b = before_first((one_a, one_b), (two_a, two_b), lo, hi, growth, chunks)
    sib_a = to_sibling(after(own_a, own_b))
    sib_b = to_sibling(own_b)
    far_a = after(far_a, base_a)
    farsib_a = to_sibling(far_a)
    part_a = early_part([own_a, sib_a, far_a], kernels)
    new_a, rounded_a, rest_a, new_head, new_tail = first_node(
        part_a, farsib_a, base_a, one_a, two_a, initial, kernels, death, chunks[0], True
    )
    nfar_a = to_far(rounded_a)
    nsib_a = to_sibling(rounded_a)

    new_hi = from_above(new_head)
    far_b = after(far_b, rounded_a, new_hi)
    farsib_b = to_sibling(far_b)
    part_b, new_one = early_part([own_b, sib_b, far_b], kernels, new_a, chunks[0], xcount)
    new_b, rounded_b, rest_b = first_node(
        part_b, farsib_b, base_b, one_b, two_b, initial, kernels, death, chunks[1], False
    )
    nfar_b = to_far(rounded_b)
    nsib_b = to_sibling(rounded_b)
    new_lo = from_below(after(new_tail, rounded_b))
    nfar_a = after(nfar_a, rounded_b)
    nfarsib_a = to_sibling(nfar_a)
    new_one, npart_a, nbase_a, nbase_b = before_second(
        (new_a, new_b), (rest_a, rest_b), growth, death, new_one, [rounded_a], kernels, chunks
    )
    sums_a = whole_sums(npart_a, [nsib_a, nfar_a, nfarsib_a], after(kernels, nbase_a))
    nfar_b = after(nfar_b, sums_a, new_lo)
    nfarsib_b = to_sibling(nfar_b)
    begun, npart_b = second_first(
        sums_a, nbase_a, new_a, death, new_lo, new_hi, [rounded_b, nsib_b, nfar_b], kernels, chunks[0], xcount
    )
    new_two = second_last(npart_b, nfarsib_b, nbase_b, new_b, death, kernels, begun, chunks[1], xcount)
    return new_one, new_two


def solution(mesh):
    in_specs = (
        P("gx", None, "trait"),
        P("gx", None, "trait"),
        P("gx", None, "trait"),
        P(None, None, "trait"),
        P("trait"),
        P("trait"),
    )
    out_specs = (P("gx", None, "trait"), P("gx", None, "trait"))
    return jax.shard_map(local, mesh=mesh, in_specs=in_specs, out_specs=out_specs, check_vma=False)
```

```python
import jax
import jax.numpy as jnp
from jax import lax
from jax.experimental import pallas as pl
from jax.experimental.pallas import tpu as pltpu
from jax.sharding import PartitionSpec as P

DIFFUSION = 0.25
STEP_SIZE = 0.5
FIRST = STEP_SIZE / 3.0
SECOND = 2.0 * STEP_SIZE / 3.0
F32 = jnp.float32
BF16 = jnp.bfloat16
VMEM_LIMIT = 20 * 1024 * 1024
SPEC = pl.BlockSpec(memory_space=pltpu.VMEM)
ANYWHERE = pl.BlockSpec(memory_space=pl.ANY)
FROM_HBM = pl.BlockSpec(memory_space=pltpu.HBM)


def chunks_of(xcount):
    last = max(1, 3 * xcount // 8)
    start = (xcount - last + 1) // 2
    middle = list(range(start, start + last))
    return [x for x in range(xcount) if x not in middle], middle


def after(value, *others):
    return lax.optimization_barrier((value, *others))[0]


def call(body, name, args, outs, scratch=(), specs=None, out_specs=None, gflop=0.0, alias=None):
    specs = specs or [SPEC] * len(args)
    space = {id(SPEC): pltpu.VMEM, id(FROM_HBM): pltpu.HBM}
    args = [
        pltpu.with_memory_space_constraint(a, space[id(s)]) if id(s) in space else a for a, s in zip(args, specs)
    ]
    return pl.pallas_call(
        body,
        out_shape=outs,
        in_specs=specs,
        out_specs=out_specs or [SPEC] * len(outs),
        scratch_shapes=list(scratch),
        compiler_params=pltpu.CompilerParams(vmem_limit_bytes=VMEM_LIMIT),
        cost_estimate=pl.CostEstimate(flops=int(gflop * 1e9), bytes_accessed=0, transcendentals=0),
        input_output_aliases=alias or {},
        name=name,
    )(*args)


def load_chunk(fields, cells, with_faces):
    xcount, ycount, owned = fields[0].shape
    count = len(fields)

    def body(*refs):
        field_refs, held_refs, out_ref = refs[:count], refs[count:2 * count], refs[2 * count]
        sems = refs[-1]
        copies = []
        for f in range(count):
            for i, x in enumerate(cells):
                copies.append(pltpu.make_async_copy(field_refs[f].at[x], held_refs[f].at[i], sems.at[f, i]))
                copies[-1].start()
        for f in range(count):
            for i, x in enumerate(cells):
                copies[f * len(cells) + i].wait()
                value = held_refs[f][i].astype(BF16)
                out_ref[f, i * ycount:(i + 1) * ycount, :] = value
                if with_faces and x == 0:
                    refs[2 * count + 1][f] = value
                if with_faces and x == xcount - 1:
                    refs[2 * count + 2][f] = value

    outs = [pltpu.VMEM((len(cells), ycount, owned), F32)] * count
    outs.append(pltpu.VMEM((count, len(cells) * ycount, owned), BF16))
    if with_faces:
        outs += [pltpu.VMEM((count, ycount, owned), BF16)] * 2
    return call(
        body, "load_chunk", fields, outs, scratch=[pltpu.SemaphoreType.DMA((count, len(cells)))],
        specs=[FROM_HBM] * count,
    )


def blocks_dot(blocks, kernels_ref, k, owners):
    depth = blocks[0].shape[-1]
    lhs = jnp.concatenate(blocks, axis=-1)
    rhs = jnp.concatenate(
        [kernels_ref[k, pl.ds(pl.multiple_of(o * depth, depth), depth), :] for o in owners], axis=0
    )
    return jnp.dot(lhs, rhs, preferred_element_type=F32)


def along_y(core):
    return DIFFUSION * (pltpu.roll(core, 1, 0) + pltpu.roll(core, core.shape[0] - 1, 0)) - 2.0 * core


def before_first(ones, twos, lo, hi, growth, chunks):
    _, ycount, owned = ones[0].shape
    xcount = sum(len(cells) for cells in chunks)
    count = len(chunks)
    place = {x: (c, i) for c, cells in enumerate(chunks) for i, x in enumerate(cells)}

    def body(*refs):
        lo_ref, hi_ref, g_ref, *outs = refs[2 * count:]
        growth = g_ref[...]
        for f in range(2):

            def get(x):
                c, i = place[x]
                return refs[f * count + c][i]

            for x, (c, i) in place.items():
                core = get(x)
                before = get(x - 1) if x > 0 else lo_ref[f].astype(F32)
                behind = get(x + 1) if x < xcount - 1 else hi_ref[f].astype(F32)
                outs[c][f, i] = DIFFUSION * (before + behind) + along_y(core) + core * growth

    outs = [pltpu.VMEM((2, len(cells), ycount, owned), F32) for cells in chunks]
    return call(body, "before_first", [*ones, *twos, lo, hi, growth], outs)


def early_part(blocks, kernels, new=None, cells=(), xcount=0):
    rows, owned = blocks[0].shape[0] * blocks[0].shape[1], blocks[0].shape[2]
    count = len(blocks)

    def body(*refs):
        block_refs, k_ref = refs[:count], refs[count]
        copies = []
        if new is None:
            part_ref = refs[-1]
        else:
            new_ref, part_ref, whole_ref, sems = refs[count + 1:]
            copies = [pltpu.make_async_copy(new_ref.at[i], whole_ref.at[x], sems.at[i]) for i, x in enumerate(cells)]
        for copy in copies:
            copy.start()
        me = lax.axis_index("trait")
        values = [r[...].reshape(rows, owned) for r in block_refs]
        for k in range(2):
            part_ref[k] = blocks_dot(values, k_ref, k, [me ^ j for j in range(count)])
        for copy in copies:
            copy.wait()

    args = [*blocks, kernels]
    outs = [pltpu.VMEM((2, rows, owned), F32)]
    if new is None:
        return call(body, "early_part", args, outs, gflop=20.0)[0]
    outs.append(jax.ShapeDtypeStruct((xcount, *new.shape[1:]), F32))
    return call(
        body, "early_part", [*args, new], outs, scratch=[pltpu.SemaphoreType.DMA((len(cells),))],
        out_specs=[SPEC, ANYWHERE], gflop=20.0,
    )


def first_node(part, last, base, one, two, initial, kernels, death, cells, with_faces):
    xcount, ycount, owned = initial.shape
    rows = len(cells) * ycount

    def body(part_ref, last_ref, base_ref, one_ref, two_ref, init_ref, k_ref, d_ref, *refs):
        new_ref, rounded_ref, rest_ref = refs[:3]
        sums = refs[-1]
        me = lax.axis_index("trait")
        for k in range(2):
            far_part = blocks_dot([last_ref[...].reshape(2 * rows, owned)], k_ref, k, [me ^ 3])
            sums[k] = (part_ref[k] + far_part).astype(BF16)
        death = d_ref[...]
        inv_one = 1.0 / (1.0 + FIRST * death)
        inv_two = 1.0 / (1.0 + SECOND * death)
        for i, x in enumerate(cells):
            cores = (one_ref[i], two_ref[i])
            e = []
            for f in range(2):
                at = pl.ds(f * rows + i * ycount, ycount)
                e.append(base_ref[f, i] - cores[f] * sums[0, at, :].astype(F32) + sums[1, at, :].astype(F32))
            full_one = e[0] - death * cores[0]
            full_two = e[1] - death * cores[1]
            new = (
                init_ref[x]
                + FIRST * death * cores[0]
                + STEP_SIZE * (5.0 / 12.0 * full_one - 1.0 / 12.0 * full_two)
            ) * inv_one
            new_ref[i] = new
            rounded = new.astype(BF16)
            rounded_ref[0, i * ycount:(i + 1) * ycount, :] = rounded
            if with_faces and x == 0:
                refs[3][0] = rounded
            if with_faces and x == xcount - 1:
                refs[4][0] = rounded
            rest_ref[i] = (
                new - SECOND * e[0] + SECOND * death * cores[1] + STEP_SIZE / 3.0 * (full_one + full_two)
            ) * inv_two

    outs = [
        pltpu.VMEM((len(cells), ycount, owned), F32),
        pltpu.VMEM((1, rows, owned), BF16),
        pltpu.VMEM((len(cells), ycount, owned), F32),
    ]
    if with_faces:
        outs += [pltpu.VMEM((1, ycount, owned), BF16)] * 2
    args = [part, last, base, one, two, initial, kernels, death]
    return call(
        body, "first_node", args, outs, scratch=[pltpu.VMEM((2, 2 * rows, owned), BF16)],
        gflop=0.0,
    )


def before_second(news, rests, growth, death, begun, blocks, kernels, chunks):
    _, ycount, owned = news[0].shape
    rows = blocks[0].shape[1]
    xcount = sum(len(cells) for cells in chunks)
    count = len(chunks)
    size = len(blocks)
    place = {x: (c, i) for c, cells in enumerate(chunks) for i, x in enumerate(cells)}

    def body(*refs):
        new_refs, rest_refs, block_refs = refs[:count], refs[count:2 * count], refs[2 * count:2 * count + size]
        k_ref, g_ref, d_ref, _, whole_ref, part_ref = refs[2 * count + size:2 * count + size + 6]
        base_refs, sems = refs[2 * count + size + 6:-1], refs[-1]
        copies = [
            pltpu.make_async_copy(new_refs[-1].at[i], whole_ref.at[x], sems.at[i]) for i, x in enumerate(chunks[-1])
        ]
        for copy in copies:
            copy.start()
        me = lax.axis_index("trait")
        values = [r[...].reshape(rows, owned) for r in block_refs]
        for k in range(2):
            part_ref[k] = blocks_dot(values, k_ref, k, [me ^ j for j in range(size)])
        growth = g_ref[...]
        factor = SECOND / (1.0 + SECOND * d_ref[...])
        for x, (c, i) in place.items():
            core = new_refs[c][i]
            e = along_y(core) + core * growth
            for near in (x - 1, x + 1):
                if near in place:
                    e = e + DIFFUSION * new_refs[place[near][0]][place[near][1]]
            base_refs[c][i] = rest_refs[c][i] + factor * e
        for copy in copies:
            copy.wait()

    outs = [jax.ShapeDtypeStruct((xcount, ycount, owned), F32), pltpu.VMEM((2, rows, owned), F32)]
    outs += [pltpu.VMEM((len(cells), ycount, owned), F32) for cells in chunks]
    args = [*news, *rests, *blocks, kernels, growth, death, begun]
    return call(
        body, "before_second", args, outs, scratch=[pltpu.SemaphoreType.DMA((len(chunks[-1]),))],
        specs=[SPEC] * (len(args) - 1) + [FROM_HBM], out_specs=[ANYWHERE] + [SPEC] * (len(outs) - 1), gflop=20.0,
        alias={len(args) - 1: 0},
    )


def whole_sums(part, blocks, kernels):
    rows, owned = blocks[0].shape[1:]

    def body(part_ref, sib_ref, far_ref, farsib_ref, k_ref, sums_ref):
        me = lax.axis_index("trait")
        values = [r[...].reshape(rows, owned) for r in (sib_ref, far_ref, farsib_ref)]
        for k in range(2):
            sums_ref[k] = (part_ref[k] + blocks_dot(values, k_ref, k, [me ^ 1, me ^ 2, me ^ 3])).astype(BF16)

    return call(body, "whole_sums", [part, *blocks, kernels], [pltpu.VMEM((2, rows, owned), BF16)])[0]


def finish(cells, ycount, sums, base_ref, new_ref, factor, faces, held, out_ref, sems):
    copies = []
    for i, x in enumerate(cells):
        at = pl.ds(i * ycount, ycount)
        e = sums[1, at, :].astype(F32) - new_ref[i] * sums[0, at, :].astype(F32)
        if x in faces:
            e = e + DIFFUSION * faces[x][0].astype(F32)
        held[i] = base_ref[i] + factor * e
        copies.append(pltpu.make_async_copy(held.at[i], out_ref.at[x], sems.at[i]))
        copies[-1].start()
    return copies


def second_first(sums, base, new, death, lo, hi, blocks, kernels, cells, xcount):
    _, ycount, owned = new.shape
    rows = blocks[0].shape[1]
    count = len(blocks)

    def body(sums_ref, base_ref, new_ref, d_ref, lo_ref, hi_ref, k_ref, *refs):
        block_refs = refs[:count]
        out_ref, part_ref, held, sems = refs[count:]
        factor = SECOND / (1.0 + SECOND * d_ref[...])
        faces = {0: lo_ref, xcount - 1: hi_ref}
        copies = finish(cells, ycount, sums_ref, base_ref, new_ref, factor, faces, held, out_ref, sems)
        me = lax.axis_index("trait")
        values = [r[...].reshape(rows, owned) for r in block_refs]
        for k in range(2):
            part_ref[k] = blocks_dot(values, k_ref, k, [me ^ j for j in range(count)])
        for copy in copies:
            copy.wait()

    return call(
        body, "second_first", [sums, base, new, death, lo, hi, kernels, *blocks],
        [jax.ShapeDtypeStruct((xcount, ycount, owned), F32), pltpu.VMEM((2, rows, owned), F32)],
        scratch=[pltpu.VMEM((len(cells), ycount, owned), F32), pltpu.SemaphoreType.DMA((len(cells),))],
        out_specs=[ANYWHERE, SPEC],
    )


def second_last(part, last, base, new, death, kernels, begun, cells, xcount):
    _, ycount, owned = new.shape
    rows = len(cells) * ycount

    def body(part_ref, last_ref, base_ref, new_ref, d_ref, k_ref, begun_ref, out_ref, sums, held, sems):
        me = lax.axis_index("trait")
        for k in range(2):
            sums[k] = (part_ref[k] + blocks_dot([last_ref[...].reshape(rows, owned)], k_ref, k, [me ^ 3])).astype(BF16)
        factor = SECOND / (1.0 + SECOND * d_ref[...])
        for copy in finish(cells, ycount, sums, base_ref, new_ref, factor, {}, held, out_ref, sems):
            copy.wait()

    return call(
        body, "second_last", [part, last, base, new, death, kernels, begun],
        [jax.ShapeDtypeStruct((xcount, ycount, owned), F32)],
        scratch=[
            pltpu.VMEM((2, rows, owned), BF16),
            pltpu.VMEM((len(cells), ycount, owned), F32),
            pltpu.SemaphoreType.DMA((len(cells),)),
        ],
        specs=[SPEC] * 6 + [FROM_HBM], out_specs=[ANYWHERE], alias={6: 0},
    )[0]


def local(initial, section_one, section_two, kernels, growth, death_rate):
    xcount, ycount, owned = section_one.shape
    traits = lax.axis_size("trait")
    gcount = lax.axis_size("gx")
    growth = growth.reshape(1, owned)
    death = death_rate.reshape(1, owned)
    chunks = chunks_of(xcount)

    def to_sibling(v):
        return lax.ppermute(v, "trait", [(i, i ^ 1) for i in range(traits)])

    def to_far(v):
        return lax.ppermute(v, "trait", [(i, i ^ 2) for i in range(traits)])

    def from_below(tail):
        return lax.ppermute(tail, "gx", [(i, (i + 1) % gcount) for i in range(gcount)])

    def from_above(head):
        return lax.ppermute(head, "gx", [((i + 1) % gcount, i) for i in range(gcount)])

    one_a, two_a, own_a, head, tail = load_chunk((section_one, section_two), chunks[0], True)
    far_a = to_far(own_a)
    one_b, two_b, own_b = load_chunk((after(section_one, own_a), section_two), chunks[1], False)
    far_b = to_far(own_b)
    head, tail, kernels = lax.optimization_barrier((head, tail, kernels, own_b))[:3]
    lo, hi = from_below(tail), from_above(head)
    base_a, base_b = before_first((one_a, one_b), (two_a, two_b), lo, hi, growth, chunks)
    sib_a = to_sibling(after(own_a, own_b))
    sib_b = to_sibling(own_b)
    far_a = after(far_a, base_a)
    farsib_a = to_sibling(far_a)
    part_a = early_part([own_a, sib_a, far_a], kernels)
    new_a, rounded_a, rest_a, new_head, new_tail = first_node(
        part_a, farsib_a, base_a, one_a, two_a, initial, kernels, death, chunks[0], True
    )
    nfar_a = to_far(rounded_a)
    nsib_a = to_sibling(rounded_a)

    new_lo = from_below(new_tail)
    far_b = after(far_b, rounded_a, new_lo)
    farsib_b = to_sibling(far_b)
    part_b, new_one = early_part([own_b, sib_b, far_b], kernels, new_a, chunks[0], xcount)
    new_b, rounded_b, rest_b = first_node(
        part_b, farsib_b, base_b, one_b, two_b, initial, kernels, death, chunks[1], False
    )
    nfar_b = to_far(rounded_b)
    nsib_b = to_sibling(rounded_b)
    new_hi = from_above(after(new_head, rounded_b))
    nfar_a = after(nfar_a, rounded_b)
    nfarsib_a = to_sibling(nfar_a)
    new_one, npart_a, nbase_a, nbase_b = before_second(
        (new_a, new_b), (rest_a, rest_b), growth, death, new_one, [rounded_a], kernels, chunks
    )
    sums_a = whole_sums(npart_a, [nsib_a, nfar_a, nfarsib_a], after(kernels, nbase_a))
    nfar_b = after(nfar_b, sums_a, new_hi)
    nfarsib_b = to_sibling(nfar_b)
    begun, npart_b = second_first(
        sums_a, nbase_a, new_a, death, new_lo, new_hi, [rounded_b, nsib_b, nfar_b], kernels, chunks[0], xcount
    )
    new_two = second_last(npart_b, nfarsib_b, nbase_b, new_b, death, kernels, begun, chunks[1], xcount)
    return new_one, new_two


def solution(mesh):
    in_specs = (
        P("gx", None, "trait"),
        P("gx", None, "trait"),
        P("gx", None, "trait"),
        P(None, None, "trait"),
        P("trait"),
        P("trait"),
    )
    out_specs = (P("gx", None, "trait"), P("gx", None, "trait"))
    return jax.shard_map(local, mesh=mesh, in_specs=in_specs, out_specs=out_specs, check_vma=False)
```

```python
import jax
import jax.numpy as jnp
from jax import lax
from jax.experimental import pallas as pl
from jax.experimental.pallas import tpu as pltpu
from jax.sharding import PartitionSpec as P

DIFFUSION = 0.25
STEP_SIZE = 0.5
FIRST = STEP_SIZE / 3.0
SECOND = 2.0 * STEP_SIZE / 3.0
F32 = jnp.float32
BF16 = jnp.bfloat16
VMEM_LIMIT = 20 * 1024 * 1024
SPEC = pl.BlockSpec(memory_space=pltpu.VMEM)
ANYWHERE = pl.BlockSpec(memory_space=pl.ANY)
FROM_HBM = pl.BlockSpec(memory_space=pltpu.HBM)


def chunks_of(xcount):
    last = max(1, 3 * xcount // 8)
    start = (xcount - last + 1) // 2
    middle = list(range(start, start + last))
    return [x for x in range(xcount) if x not in middle], middle


def after(value, *others):
    return lax.optimization_barrier((value, *others))[0]


def call(body, name, args, outs, scratch=(), specs=None, out_specs=None, gflop=0.0, alias=None):
    specs = specs or [SPEC] * len(args)
    space = {id(SPEC): pltpu.VMEM, id(FROM_HBM): pltpu.HBM}
    args = [
        pltpu.with_memory_space_constraint(a, space[id(s)]) if id(s) in space else a for a, s in zip(args, specs)
    ]
    return pl.pallas_call(
        body,
        out_shape=outs,
        in_specs=specs,
        out_specs=out_specs or [SPEC] * len(outs),
        scratch_shapes=list(scratch),
        compiler_params=pltpu.CompilerParams(vmem_limit_bytes=VMEM_LIMIT),
        cost_estimate=pl.CostEstimate(flops=int(gflop * 1e9), bytes_accessed=0, transcendentals=0),
        input_output_aliases=alias or {},
        name=name,
    )(*args)


def load_chunk(fields, cells, with_faces):
    xcount, ycount, owned = fields[0].shape
    count = len(fields)

    def body(*refs):
        field_refs, held_refs, out_ref = refs[:count], refs[count:2 * count], refs[2 * count]
        sems = refs[-1]
        copies = []
        for f in range(count):
            for i, x in enumerate(cells):
                copies.append(pltpu.make_async_copy(field_refs[f].at[x], held_refs[f].at[i], sems.at[f, i]))
                copies[-1].start()
        for f in range(count):
            for i, x in enumerate(cells):
                copies[f * len(cells) + i].wait()
                value = held_refs[f][i].astype(BF16)
                out_ref[f, i * ycount:(i + 1) * ycount, :] = value
                if with_faces and x == 0:
                    refs[2 * count + 1][f] = value
                if with_faces and x == xcount - 1:
                    refs[2 * count + 2][f] = value

    outs = [pltpu.VMEM((len(cells), ycount, owned), F32)] * count
    outs.append(pltpu.VMEM((count, len(cells) * ycount, owned), BF16))
    if with_faces:
        outs += [pltpu.VMEM((count, ycount, owned), BF16)] * 2
    return call(
        body, "load_chunk", fields, outs, scratch=[pltpu.SemaphoreType.DMA((count, len(cells)))],
        specs=[FROM_HBM] * count,
    )


def blocks_dot(blocks, kernels_ref, k, owners):
    depth = blocks[0].shape[-1]
    lhs = jnp.concatenate(blocks, axis=-1)
    rhs = jnp.concatenate(
        [kernels_ref[k, pl.ds(pl.multiple_of(o * depth, depth), depth), :] for o in owners], axis=0
    )
    return jnp.dot(lhs, rhs, preferred_element_type=F32)


def along_y(core):
    return DIFFUSION * (pltpu.roll(core, 1, 0) + pltpu.roll(core, core.shape[0] - 1, 0)) - 2.0 * core


def before_first(ones, twos, lo, hi, growth, chunks):
    _, ycount, owned = ones[0].shape
    xcount = sum(len(cells) for cells in chunks)
    count = len(chunks)
    place = {x: (c, i) for c, cells in enumerate(chunks) for i, x in enumerate(cells)}

    def body(*refs):
        lo_ref, hi_ref, g_ref, *outs = refs[2 * count:]
        growth = g_ref[...]
        for f in range(2):

            def get(x):
                c, i = place[x]
                return refs[f * count + c][i]

            for x, (c, i) in place.items():
                core = get(x)
                before = get(x - 1) if x > 0 else lo_ref[f].astype(F32)
                behind = get(x + 1) if x < xcount - 1 else hi_ref[f].astype(F32)
                outs[c][f, i] = DIFFUSION * (before + behind) + along_y(core) + core * growth

    outs = [pltpu.VMEM((2, len(cells), ycount, owned), F32) for cells in chunks]
    return call(body, "before_first", [*ones, *twos, lo, hi, growth], outs)


def early_part(blocks, kernels, new=None, cells=(), xcount=0):
    rows, owned = blocks[0].shape[0] * blocks[0].shape[1], blocks[0].shape[2]
    count = len(blocks)

    def body(*refs):
        block_refs, k_ref = refs[:count], refs[count]
        copies = []
        if new is None:
            part_ref = refs[-1]
        else:
            new_ref, part_ref, whole_ref, sems = refs[count + 1:]
            copies = [pltpu.make_async_copy(new_ref.at[i], whole_ref.at[x], sems.at[i]) for i, x in enumerate(cells)]
        for copy in copies:
            copy.start()
        me = lax.axis_index("trait")
        values = [r[...].reshape(rows, owned) for r in block_refs]
        for k in range(2):
            part_ref[k] = blocks_dot(values, k_ref, k, [me ^ j for j in range(count)])
        for copy in copies:
            copy.wait()

    args = [*blocks, kernels]
    outs = [pltpu.VMEM((2, rows, owned), F32)]
    if new is None:
        return call(body, "early_part", args, outs, gflop=20.0)[0]
    outs.append(jax.ShapeDtypeStruct((xcount, *new.shape[1:]), F32))
    return call(
        body, "early_part", [*args, new], outs, scratch=[pltpu.SemaphoreType.DMA((len(cells),))],
        out_specs=[SPEC, ANYWHERE], gflop=20.0,
    )


def first_node(part, last, base, one, two, initial, kernels, death, cells, with_faces):
    xcount, ycount, owned = initial.shape
    rows = len(cells) * ycount

    def body(part_ref, last_ref, base_ref, one_ref, two_ref, init_ref, k_ref, d_ref, *refs):
        new_ref, rounded_ref, rest_ref = refs[:3]
        sums = refs[-1]
        me = lax.axis_index("trait")
        for k in range(2):
            far_part = blocks_dot([last_ref[...].reshape(2 * rows, owned)], k_ref, k, [me ^ 3])
            sums[k] = (part_ref[k] + far_part).astype(BF16)
        death = d_ref[...]
        inv_one = 1.0 / (1.0 + FIRST * death)
        inv_two = 1.0 / (1.0 + SECOND * death)
        for i, x in enumerate(cells):
            cores = (one_ref[i], two_ref[i])
            e = []
            for f in range(2):
                at = pl.ds(f * rows + i * ycount, ycount)
                e.append(base_ref[f, i] - cores[f] * sums[0, at, :].astype(F32) + sums[1, at, :].astype(F32))
            full_one = e[0] - death * cores[0]
            full_two = e[1] - death * cores[1]
            new = (
                init_ref[x]
                + FIRST * death * cores[0]
                + STEP_SIZE * (5.0 / 12.0 * full_one - 1.0 / 12.0 * full_two)
            ) * inv_one
            new_ref[i] = new
            rounded = new.astype(BF16)
            rounded_ref[0, i * ycount:(i + 1) * ycount, :] = rounded
            if with_faces and x in (0, xcount - 1):
                refs[3 if x == 0 else 4][0] = rounded

                @pl.when(lax.axis_index("gx") == (0 if x == 0 else lax.axis_size("gx") - 1))
                def _():
                    refs[5][0] = rounded

            rest_ref[i] = (
                new - SECOND * e[0] + SECOND * death * cores[1] + STEP_SIZE / 3.0 * (full_one + full_two)
            ) * inv_two

    outs = [
        pltpu.VMEM((len(cells), ycount, owned), F32),
        pltpu.VMEM((1, rows, owned), BF16),
        pltpu.VMEM((len(cells), ycount, owned), F32),
    ]
    if with_faces:
        outs += [pltpu.VMEM((1, ycount, owned), BF16)] * 3
    args = [part, last, base, one, two, initial, kernels, death]
    return call(
        body, "first_node", args, outs, scratch=[pltpu.VMEM((2, 2 * rows, owned), BF16)],
        gflop=0.0,
    )


def before_second(news, rests, growth, death, begun, blocks, kernels, chunks):
    _, ycount, owned = news[0].shape
    rows = blocks[0].shape[1]
    xcount = sum(len(cells) for cells in chunks)
    count = len(chunks)
    size = len(blocks)
    place = {x: (c, i) for c, cells in enumerate(chunks) for i, x in enumerate(cells)}

    def body(*refs):
        new_refs, rest_refs, block_refs = refs[:count], refs[count:2 * count], refs[2 * count:2 * count + size]
        k_ref, g_ref, d_ref, _, whole_ref, part_ref = refs[2 * count + size:2 * count + size + 6]
        base_refs, sems = refs[2 * count + size + 6:-1], refs[-1]
        copies = [
            pltpu.make_async_copy(new_refs[-1].at[i], whole_ref.at[x], sems.at[i]) for i, x in enumerate(chunks[-1])
        ]
        for copy in copies:
            copy.start()
        me = lax.axis_index("trait")
        values = [r[...].reshape(rows, owned) for r in block_refs]
        for k in range(2):
            part_ref[k] = blocks_dot(values, k_ref, k, [me ^ j for j in range(size)])
        growth = g_ref[...]
        factor = SECOND / (1.0 + SECOND * d_ref[...])
        for x, (c, i) in place.items():
            core = new_refs[c][i]
            e = along_y(core) + core * growth
            for near in (x - 1, x + 1):
                if near in place:
                    e = e + DIFFUSION * new_refs[place[near][0]][place[near][1]]
            base_refs[c][i] = rest_refs[c][i] + factor * e
        for copy in copies:
            copy.wait()

    outs = [jax.ShapeDtypeStruct((xcount, ycount, owned), F32), pltpu.VMEM((2, rows, owned), F32)]
    outs += [pltpu.VMEM((len(cells), ycount, owned), F32) for cells in chunks]
    args = [*news, *rests, *blocks, kernels, growth, death, begun]
    return call(
        body, "before_second", args, outs, scratch=[pltpu.SemaphoreType.DMA((len(chunks[-1]),))],
        specs=[SPEC] * (len(args) - 1) + [FROM_HBM], out_specs=[ANYWHERE] + [SPEC] * (len(outs) - 1), gflop=20.0,
        alias={len(args) - 1: 0},
    )


def whole_sums(part, blocks, kernels):
    rows, owned = blocks[0].shape[1:]

    def body(part_ref, sib_ref, far_ref, farsib_ref, k_ref, sums_ref):
        me = lax.axis_index("trait")
        values = [r[...].reshape(rows, owned) for r in (sib_ref, far_ref, farsib_ref)]
        for k in range(2):
            sums_ref[k] = (part_ref[k] + blocks_dot(values, k_ref, k, [me ^ 1, me ^ 2, me ^ 3])).astype(BF16)

    return call(body, "whole_sums", [part, *blocks, kernels], [pltpu.VMEM((2, rows, owned), BF16)])[0]


def finish(cells, ycount, sums, base_ref, new_ref, factor, faces, held, out_ref, sems):
    copies = []
    for i, x in enumerate(cells):
        at = pl.ds(i * ycount, ycount)
        e = sums[1, at, :].astype(F32) - new_ref[i] * sums[0, at, :].astype(F32)
        if x in faces:
            e = e + DIFFUSION * faces[x][0].astype(F32)
        held[i] = base_ref[i] + factor * e
        copies.append(pltpu.make_async_copy(held.at[i], out_ref.at[x], sems.at[i]))
        copies[-1].start()
    return copies


def second_first(sums, base, new, death, lo, hi, around, blocks, kernels, cells, xcount):
    _, ycount, owned = new.shape
    rows = blocks[0].shape[1]
    count = len(blocks)

    def body(sums_ref, base_ref, new_ref, d_ref, lo_ref, hi_ref, around_ref, k_ref, *refs):
        block_refs = refs[:count]
        out_ref, part_ref, held, sems = refs[count:]
        factor = SECOND / (1.0 + SECOND * d_ref[...])
        place = lax.axis_index("gx")
        faces = {
            0: jnp.where(place == 0, around_ref[...], lo_ref[...]),
            xcount - 1: jnp.where(place == lax.axis_size("gx") - 1, around_ref[...], hi_ref[...]),
        }
        copies = finish(cells, ycount, sums_ref, base_ref, new_ref, factor, faces, held, out_ref, sems)
        me = lax.axis_index("trait")
        values = [r[...].reshape(rows, owned) for r in block_refs]
        for k in range(2):
            part_ref[k] = blocks_dot(values, k_ref, k, [me ^ j for j in range(count)])
        for copy in copies:
            copy.wait()

    return call(
        body, "second_first", [sums, base, new, death, lo, hi, around, kernels, *blocks],
        [jax.ShapeDtypeStruct((xcount, ycount, owned), F32), pltpu.VMEM((2, rows, owned), F32)],
        scratch=[pltpu.VMEM((len(cells), ycount, owned), F32), pltpu.SemaphoreType.DMA((len(cells),))],
        out_specs=[ANYWHERE, SPEC],
    )


def second_last(part, last, base, new, death, kernels, begun, cells, xcount):
    _, ycount, owned = new.shape
    rows = len(cells) * ycount

    def body(part_ref, last_ref, base_ref, new_ref, d_ref, k_ref, begun_ref, out_ref, sums, held, sems):
        me = lax.axis_index("trait")
        for k in range(2):
            sums[k] = (part_ref[k] + blocks_dot([last_ref[...].reshape(rows, owned)], k_ref, k, [me ^ 3])).astype(BF16)
        factor = SECOND / (1.0 + SECOND * d_ref[...])
        for copy in finish(cells, ycount, sums, base_ref, new_ref, factor, {}, held, out_ref, sems):
            copy.wait()

    return call(
        body, "second_last", [part, last, base, new, death, kernels, begun],
        [jax.ShapeDtypeStruct((xcount, ycount, owned), F32)],
        scratch=[
            pltpu.VMEM((2, rows, owned), BF16),
            pltpu.VMEM((len(cells), ycount, owned), F32),
            pltpu.SemaphoreType.DMA((len(cells),)),
        ],
        specs=[SPEC] * 6 + [FROM_HBM], out_specs=[ANYWHERE], alias={6: 0},
    )[0]


def local(initial, section_one, section_two, kernels, growth, death_rate):
    xcount, ycount, owned = section_one.shape
    traits = lax.axis_size("trait")
    gcount = lax.axis_size("gx")
    growth = growth.reshape(1, owned)
    death = death_rate.reshape(1, owned)
    chunks = chunks_of(xcount)

    def to_sibling(v):
        return lax.ppermute(v, "trait", [(i, i ^ 1) for i in range(traits)])

    def to_far(v):
        return lax.ppermute(v, "trait", [(i, i ^ 2) for i in range(traits)])

    def from_below(tail, pairs):
        return lax.ppermute(tail, "gx", [(i, (i + 1) % gcount) for i in range(pairs)])

    def from_above(head, pairs):
        return lax.ppermute(head, "gx", [((i + 1) % gcount, i) for i in range(pairs)])

    def round_the_boundary(face):
        return lax.ppermute(face, "gx", [(0, gcount - 1), (gcount - 1, 0)])

    one_a, two_a, own_a, head, tail = load_chunk((section_one, section_two), chunks[0], True)
    far_a = to_far(own_a)
    one_b, two_b, own_b = load_chunk((after(section_one, own_a), section_two), chunks[1], False)
    far_b = to_far(own_b)
    head, tail, kernels = lax.optimization_barrier((head, tail, kernels, own_b))[:3]
    lo, hi = from_below(tail, gcount), from_above(head, gcount)
    base_a, base_b = before_first((one_a, one_b), (two_a, two_b), lo, hi, growth, chunks)
    sib_a = to_sibling(after(own_a, own_b))
    sib_b = to_sibling(own_b)
    far_a = after(far_a, base_a)
    farsib_a = to_sibling(far_a)
    part_a = early_part([own_a, sib_a, far_a], kernels)
    new_a, rounded_a, rest_a, new_head, new_tail, new_outer = first_node(
        part_a, farsib_a, base_a, one_a, two_a, initial, kernels, death, chunks[0], True
    )
    nfar_a = to_far(rounded_a)
    nsib_a = to_sibling(rounded_a)

    new_lo, new_hi = from_below(new_tail, gcount - 1), from_above(new_head, gcount - 1)
    far_b = after(far_b, rounded_a, new_lo, new_hi)
    farsib_b = to_sibling(far_b)
    part_b, new_one = early_part([own_b, sib_b, far_b], kernels, new_a, chunks[0], xcount)
    new_b, rounded_b, rest_b = first_node(
        part_b, farsib_b, base_b, one_b, two_b, initial, kernels, death, chunks[1], False
    )
    nfar_b = to_far(rounded_b)
    nsib_b = to_sibling(rounded_b)
    new_round = round_the_boundary(after(new_outer, rounded_b))
    nfar_a = after(nfar_a, rounded_b)
    nfarsib_a = to_sibling(nfar_a)
    new_one, npart_a, nbase_a, nbase_b = before_second(
        (new_a, new_b), (rest_a, rest_b), growth, death, new_one, [rounded_a], kernels, chunks
    )
    sums_a = whole_sums(npart_a, [nsib_a, nfar_a, nfarsib_a], after(kernels, nbase_a))
    nfar_b = after(nfar_b, sums_a, new_round)
    nfarsib_b = to_sibling(nfar_b)
    begun, npart_b = second_first(
        sums_a, nbase_a, new_a, death, new_lo, new_hi, new_round, [rounded_b, nsib_b, nfar_b], kernels, chunks[0], xcount
    )
    new_two = second_last(npart_b, nfarsib_b, nbase_b, new_b, death, kernels, begun, chunks[1], xcount)
    return new_one, new_two


def solution(mesh):
    in_specs = (
        P("gx", None, "trait"),
        P("gx", None, "trait"),
        P("gx", None, "trait"),
        P(None, None, "trait"),
        P("trait"),
        P("trait"),
    )
    out_specs = (P("gx", None, "trait"), P("gx", None, "trait"))
    return jax.shard_map(local, mesh=mesh, in_specs=in_specs, out_specs=out_specs, check_vma=False)
```

```python
import jax
import jax.numpy as jnp
from jax import lax
from jax.experimental import pallas as pl
from jax.experimental.pallas import tpu as pltpu
from jax.sharding import PartitionSpec as P

DIFFUSION = 0.25
STEP_SIZE = 0.5
FIRST = STEP_SIZE / 3.0
SECOND = 2.0 * STEP_SIZE / 3.0
F32 = jnp.float32
BF16 = jnp.bfloat16
VMEM_LIMIT = 20 * 1024 * 1024
SPEC = pl.BlockSpec(memory_space=pltpu.VMEM)
ANYWHERE = pl.BlockSpec(memory_space=pl.ANY)
FROM_HBM = pl.BlockSpec(memory_space=pltpu.HBM)


def chunks_of(xcount):
    last = max(1, 3 * xcount // 8)
    start = (xcount - last + 1) // 2
    middle = list(range(start, start + last))
    return [x for x in range(xcount) if x not in middle], middle


def after(value, *others):
    return lax.optimization_barrier((value, *others))[0]


def call(body, name, args, outs, scratch=(), specs=None, out_specs=None, gflop=0.0, alias=None):
    specs = specs or [SPEC] * len(args)
    space = {id(SPEC): pltpu.VMEM, id(FROM_HBM): pltpu.HBM}
    args = [
        pltpu.with_memory_space_constraint(a, space[id(s)]) if id(s) in space else a for a, s in zip(args, specs)
    ]
    return pl.pallas_call(
        body,
        out_shape=outs,
        in_specs=specs,
        out_specs=out_specs or [SPEC] * len(outs),
        scratch_shapes=list(scratch),
        compiler_params=pltpu.CompilerParams(vmem_limit_bytes=VMEM_LIMIT),
        cost_estimate=pl.CostEstimate(flops=int(gflop * 1e9), bytes_accessed=0, transcendentals=0),
        input_output_aliases=alias or {},
        name=name,
    )(*args)


def runs_of(cells):
    runs = []
    for i, x in enumerate(cells):
        if runs and x == sum(runs[-1][1:]):
            runs[-1][2] += 1
        else:
            runs.append([i, x, 1])
    return runs


def load_chunk(fields, cells, with_faces):
    xcount, ycount, owned = fields[0].shape
    count = len(fields)
    runs = runs_of(cells)

    def body(*refs):
        field_refs, held_refs, out_ref = refs[:count], refs[count:2 * count], refs[2 * count]
        sems = refs[-1]
        copies = {}
        for f in range(count):
            for r, (i, x, size) in enumerate(runs):
                copies[f, r] = pltpu.make_async_copy(
                    field_refs[f].at[pl.ds(x, size)], held_refs[f].at[pl.ds(i, size)], sems.at[f, r]
                )
                copies[f, r].start()
        for f in range(count):
            for r, (start, _, size) in enumerate(runs):
                copies[f, r].wait()
                for i in range(start, start + size):
                    value = held_refs[f][i].astype(BF16)
                    out_ref[f, i * ycount:(i + 1) * ycount, :] = value
                    if with_faces and cells[i] == 0:
                        refs[2 * count + 1][f] = value
                    if with_faces and cells[i] == xcount - 1:
                        refs[2 * count + 2][f] = value

    outs = [pltpu.VMEM((len(cells), ycount, owned), F32)] * count
    outs.append(pltpu.VMEM((count, len(cells) * ycount, owned), BF16))
    if with_faces:
        outs += [pltpu.VMEM((count, ycount, owned), BF16)] * 2
    return call(
        body, "load_chunk", fields, outs, scratch=[pltpu.SemaphoreType.DMA((count, len(runs)))],
        specs=[FROM_HBM] * count,
    )


def blocks_dot(blocks, kernels_ref, k, owners):
    depth = blocks[0].shape[-1]
    lhs = jnp.concatenate(blocks, axis=-1)
    rhs = jnp.concatenate(
        [kernels_ref[k, pl.ds(pl.multiple_of(o * depth, depth), depth), :] for o in owners], axis=0
    )
    return jnp.dot(lhs, rhs, preferred_element_type=F32)


def along_y(core):
    return DIFFUSION * (pltpu.roll(core, 1, 0) + pltpu.roll(core, core.shape[0] - 1, 0)) - 2.0 * core


def before_first(ones, twos, lo, hi, growth, chunks):
    _, ycount, owned = ones[0].shape
    xcount = sum(len(cells) for cells in chunks)
    count = len(chunks)
    place = {x: (c, i) for c, cells in enumerate(chunks) for i, x in enumerate(cells)}

    def body(*refs):
        lo_ref, hi_ref, g_ref, *outs = refs[2 * count:]
        growth = g_ref[...]
        for f in range(2):

            def get(x):
                c, i = place[x]
                return refs[f * count + c][i]

            for x, (c, i) in place.items():
                core = get(x)
                before = get(x - 1) if x > 0 else lo_ref[f].astype(F32)
                behind = get(x + 1) if x < xcount - 1 else hi_ref[f].astype(F32)
                outs[c][f, i] = DIFFUSION * (before + behind) + along_y(core) + core * growth

    outs = [pltpu.VMEM((2, len(cells), ycount, owned), F32) for cells in chunks]
    return call(body, "before_first", [*ones, *twos, lo, hi, growth], outs)


def early_part(blocks, kernels, new=None, cells=(), xcount=0):
    rows, owned = blocks[0].shape[0] * blocks[0].shape[1], blocks[0].shape[2]
    count = len(blocks)

    def body(*refs):
        block_refs, k_ref = refs[:count], refs[count]
        copies = []
        if new is None:
            part_ref = refs[-1]
        else:
            new_ref, part_ref, whole_ref, sems = refs[count + 1:]
            copies = [pltpu.make_async_copy(new_ref.at[i], whole_ref.at[x], sems.at[i]) for i, x in enumerate(cells)]
        for copy in copies:
            copy.start()
        me = lax.axis_index("trait")
        values = [r[...].reshape(rows, owned) for r in block_refs]
        for k in range(2):
            part_ref[k] = blocks_dot(values, k_ref, k, [me ^ j for j in range(count)])
        for copy in copies:
            copy.wait()

    args = [*blocks, kernels]
    outs = [pltpu.VMEM((2, rows, owned), F32)]
    if new is None:
        return call(body, "early_part", args, outs, gflop=20.0)[0]
    outs.append(jax.ShapeDtypeStruct((xcount, *new.shape[1:]), F32))
    return call(
        body, "early_part", [*args, new], outs, scratch=[pltpu.SemaphoreType.DMA((len(cells),))],
        out_specs=[SPEC, ANYWHERE], gflop=20.0,
    )


def first_node(part, last, base, one, two, initial, kernels, death, cells, with_faces):
    xcount, ycount, owned = initial.shape
    rows = len(cells) * ycount

    def body(part_ref, last_ref, base_ref, one_ref, two_ref, init_ref, k_ref, d_ref, *refs):
        new_ref, rounded_ref, rest_ref = refs[:3]
        sums = refs[-1]
        me = lax.axis_index("trait")
        for k in range(2):
            far_part = blocks_dot([last_ref[...].reshape(2 * rows, owned)], k_ref, k, [me ^ 3])
            sums[k] = (part_ref[k] + far_part).astype(BF16)
        death = d_ref[...]
        inv_one = 1.0 / (1.0 + FIRST * death)
        inv_two = 1.0 / (1.0 + SECOND * death)
        for i, x in enumerate(cells):
            cores = (one_ref[i], two_ref[i])
            e = []
            for f in range(2):
                at = pl.ds(f * rows + i * ycount, ycount)
                e.append(base_ref[f, i] - cores[f] * sums[0, at, :].astype(F32) + sums[1, at, :].astype(F32))
            full_one = e[0] - death * cores[0]
            full_two = e[1] - death * cores[1]
            new = (
                init_ref[x]
                + FIRST * death * cores[0]
                + STEP_SIZE * (5.0 / 12.0 * full_one - 1.0 / 12.0 * full_two)
            ) * inv_one
            new_ref[i] = new
            rounded = new.astype(BF16)
            rounded_ref[0, i * ycount:(i + 1) * ycount, :] = rounded
            if with_faces and x == 0:
                refs[3][0] = rounded
            if with_faces and x == xcount - 1:
                refs[4][0] = rounded
            rest_ref[i] = (
                new - SECOND * e[0] + SECOND * death * cores[1] + STEP_SIZE / 3.0 * (full_one + full_two)
            ) * inv_two

    outs = [
        pltpu.VMEM((len(cells), ycount, owned), F32),
        pltpu.VMEM((1, rows, owned), BF16),
        pltpu.VMEM((len(cells), ycount, owned), F32),
    ]
    if with_faces:
        outs += [pltpu.VMEM((1, ycount, owned), BF16)] * 2
    args = [part, last, base, one, two, initial, kernels, death]
    return call(
        body, "first_node", args, outs, scratch=[pltpu.VMEM((2, 2 * rows, owned), BF16)],
        gflop=0.0,
    )


def before_second(news, rests, growth, death, begun, blocks, kernels, chunks):
    _, ycount, owned = news[0].shape
    rows = blocks[0].shape[1]
    xcount = sum(len(cells) for cells in chunks)
    count = len(chunks)
    size = len(blocks)
    place = {x: (c, i) for c, cells in enumerate(chunks) for i, x in enumerate(cells)}

    def body(*refs):
        new_refs, rest_refs, block_refs = refs[:count], refs[count:2 * count], refs[2 * count:2 * count + size]
        k_ref, g_ref, d_ref, _, whole_ref, part_ref = refs[2 * count + size:2 * count + size + 6]
        base_refs, sems = refs[2 * count + size + 6:-1], refs[-1]
        copies = [
            pltpu.make_async_copy(new_refs[-1].at[i], whole_ref.at[x], sems.at[i]) for i, x in enumerate(chunks[-1])
        ]
        for copy in copies:
            copy.start()
        me = lax.axis_index("trait")
        values = [r[...].reshape(rows, owned) for r in block_refs]
        for k in range(2):
            part_ref[k] = blocks_dot(values, k_ref, k, [me ^ j for j in range(size)])
        growth = g_ref[...]
        factor = SECOND / (1.0 + SECOND * d_ref[...])
        for x, (c, i) in place.items():
            core = new_refs[c][i]
            e = along_y(core) + core * growth
            for near in (x - 1, x + 1):
                if near in place:
                    e = e + DIFFUSION * new_refs[place[near][0]][place[near][1]]
            base_refs[c][i] = rest_refs[c][i] + factor * e
        for copy in copies:
            copy.wait()

    outs = [jax.ShapeDtypeStruct((xcount, ycount, owned), F32), pltpu.VMEM((2, rows, owned), F32)]
    outs += [pltpu.VMEM((len(cells), ycount, owned), F32) for cells in chunks]
    args = [*news, *rests, *blocks, kernels, growth, death, begun]
    return call(
        body, "before_second", args, outs, scratch=[pltpu.SemaphoreType.DMA((len(chunks[-1]),))],
        specs=[SPEC] * (len(args) - 1) + [FROM_HBM], out_specs=[ANYWHERE] + [SPEC] * (len(outs) - 1), gflop=20.0,
        alias={len(args) - 1: 0},
    )


def whole_sums(part, blocks, kernels):
    rows, owned = blocks[0].shape[1:]

    def body(part_ref, sib_ref, far_ref, farsib_ref, k_ref, sums_ref):
        me = lax.axis_index("trait")
        values = [r[...].reshape(rows, owned) for r in (sib_ref, far_ref, farsib_ref)]
        for k in range(2):
            sums_ref[k] = (part_ref[k] + blocks_dot(values, k_ref, k, [me ^ 1, me ^ 2, me ^ 3])).astype(BF16)

    return call(body, "whole_sums", [part, *blocks, kernels], [pltpu.VMEM((2, rows, owned), BF16)])[0]


def finish(cells, ycount, sums, base_ref, new_ref, factor, faces, held, out_ref, sems):
    copies = []
    for i, x in enumerate(cells):
        at = pl.ds(i * ycount, ycount)
        e = sums[1, at, :].astype(F32) - new_ref[i] * sums[0, at, :].astype(F32)
        if x in faces:
            e = e + DIFFUSION * faces[x][0].astype(F32)
        held[i] = base_ref[i] + factor * e
        copies.append(pltpu.make_async_copy(held.at[i], out_ref.at[x], sems.at[i]))
        copies[-1].start()
    return copies


def second_first(sums, base, new, death, lo, hi, blocks, kernels, cells, xcount):
    _, ycount, owned = new.shape
    rows = blocks[0].shape[1]
    count = len(blocks)

    def body(sums_ref, base_ref, new_ref, d_ref, lo_ref, hi_ref, k_ref, *refs):
        block_refs = refs[:count]
        out_ref, part_ref, held, sems = refs[count:]
        factor = SECOND / (1.0 + SECOND * d_ref[...])
        faces = {0: lo_ref, xcount - 1: hi_ref}
        copies = finish(cells, ycount, sums_ref, base_ref, new_ref, factor, faces, held, out_ref, sems)
        me = lax.axis_index("trait")
        values = [r[...].reshape(rows, owned) for r in block_refs]
        for k in range(2):
            part_ref[k] = blocks_dot(values, k_ref, k, [me ^ j for j in range(count)])
        for copy in copies:
            copy.wait()

    return call(
        body, "second_first", [sums, base, new, death, lo, hi, kernels, *blocks],
        [jax.ShapeDtypeStruct((xcount, ycount, owned), F32), pltpu.VMEM((2, rows, owned), F32)],
        scratch=[pltpu.VMEM((len(cells), ycount, owned), F32), pltpu.SemaphoreType.DMA((len(cells),))],
        out_specs=[ANYWHERE, SPEC],
    )


def second_last(part, last, base, new, death, kernels, begun, cells, xcount):
    _, ycount, owned = new.shape
    rows = len(cells) * ycount

    def body(part_ref, last_ref, base_ref, new_ref, d_ref, k_ref, begun_ref, out_ref, sums, held, sems):
        me = lax.axis_index("trait")
        for k in range(2):
            sums[k] = (part_ref[k] + blocks_dot([last_ref[...].reshape(rows, owned)], k_ref, k, [me ^ 3])).astype(BF16)
        factor = SECOND / (1.0 + SECOND * d_ref[...])
        for copy in finish(cells, ycount, sums, base_ref, new_ref, factor, {}, held, out_ref, sems):
            copy.wait()

    return call(
        body, "second_last", [part, last, base, new, death, kernels, begun],
        [jax.ShapeDtypeStruct((xcount, ycount, owned), F32)],
        scratch=[
            pltpu.VMEM((2, rows, owned), BF16),
            pltpu.VMEM((len(cells), ycount, owned), F32),
            pltpu.SemaphoreType.DMA((len(cells),)),
        ],
        specs=[SPEC] * 6 + [FROM_HBM], out_specs=[ANYWHERE], alias={6: 0},
    )[0]


def local(initial, section_one, section_two, kernels, growth, death_rate):
    xcount, ycount, owned = section_one.shape
    traits = lax.axis_size("trait")
    gcount = lax.axis_size("gx")
    growth = growth.reshape(1, owned)
    death = death_rate.reshape(1, owned)
    chunks = chunks_of(xcount)

    def to_sibling(v):
        return lax.ppermute(v, "trait", [(i, i ^ 1) for i in range(traits)])

    def to_far(v):
        return lax.ppermute(v, "trait", [(i, i ^ 2) for i in range(traits)])

    def from_below(tail):
        return lax.ppermute(tail, "gx", [(i, (i + 1) % gcount) for i in range(gcount)])

    def from_above(head):
        return lax.ppermute(head, "gx", [((i + 1) % gcount, i) for i in range(gcount)])

    one_a, two_a, own_a, head, tail = load_chunk((section_one, section_two), chunks[0], True)
    far_a = to_far(own_a)
    one_b, two_b, own_b = load_chunk((after(section_one, own_a), section_two), chunks[1], False)
    far_b = to_far(own_b)
    head, tail, kernels = lax.optimization_barrier((head, tail, kernels, own_b))[:3]
    lo, hi = from_below(tail), from_above(head)
    base_a, base_b = before_first((one_a, one_b), (two_a, two_b), lo, hi, growth, chunks)
    sib_a = to_sibling(after(own_a, own_b))
    sib_b = to_sibling(own_b)
    far_a = after(far_a, base_a)
    farsib_a = to_sibling(far_a)
    part_a = early_part([own_a, sib_a, far_a], kernels)
    new_a, rounded_a, rest_a, new_head, new_tail = first_node(
        part_a, farsib_a, base_a, one_a, two_a, initial, kernels, death, chunks[0], True
    )
    nfar_a = to_far(rounded_a)
    nsib_a = to_sibling(rounded_a)

    new_lo = from_below(new_tail)
    far_b = after(far_b, rounded_a, new_lo)
    farsib_b = to_sibling(far_b)
    part_b, new_one = early_part([own_b, sib_b, far_b], kernels, new_a, chunks[0], xcount)
    new_b, rounded_b, rest_b = first_node(
        part_b, farsib_b, base_b, one_b, two_b, initial, kernels, death, chunks[1], False
    )
    nfar_b = to_far(rounded_b)
    nsib_b = to_sibling(rounded_b)
    new_hi = from_above(after(new_head, rounded_b))
    nfar_a = after(nfar_a, rounded_b)
    nfarsib_a = to_sibling(nfar_a)
    new_one, npart_a, nbase_a, nbase_b = before_second(
        (new_a, new_b), (rest_a, rest_b), growth, death, new_one, [rounded_a], kernels, chunks
    )
    sums_a = whole_sums(npart_a, [nsib_a, nfar_a, nfarsib_a], after(kernels, nbase_a))
    nfar_b = after(nfar_b, sums_a, new_hi)
    nfarsib_b = to_sibling(nfar_b)
    begun, npart_b = second_first(
        sums_a, nbase_a, new_a, death, new_lo, new_hi, [rounded_b, nsib_b, nfar_b], kernels, chunks[0], xcount
    )
    new_two = second_last(npart_b, nfarsib_b, nbase_b, new_b, death, kernels, begun, chunks[1], xcount)
    return new_one, new_two


def solution(mesh):
    in_specs = (
        P("gx", None, "trait"),
        P("gx", None, "trait"),
        P("gx", None, "trait"),
        P(None, None, "trait"),
        P("trait"),
        P("trait"),
    )
    out_specs = (P("gx", None, "trait"), P("gx", None, "trait"))
    return jax.shard_map(local, mesh=mesh, in_specs=in_specs, out_specs=out_specs, check_vma=False)
```

```python
import jax
import jax.numpy as jnp
from jax import lax
from jax.experimental import pallas as pl
from jax.experimental.pallas import tpu as pltpu
from jax.sharding import PartitionSpec as P

DIFFUSION = 0.25
STEP_SIZE = 0.5
FIRST = STEP_SIZE / 3.0
SECOND = 2.0 * STEP_SIZE / 3.0
F32 = jnp.float32
BF16 = jnp.bfloat16
VMEM_LIMIT = 20 * 1024 * 1024
SPEC = pl.BlockSpec(memory_space=pltpu.VMEM)
ANYWHERE = pl.BlockSpec(memory_space=pl.ANY)
FROM_HBM = pl.BlockSpec(memory_space=pltpu.HBM)


def chunks_of(xcount):
    last = max(1, 3 * xcount // 8)
    start = (xcount - last + 1) // 2
    middle = list(range(start, start + last))
    return [x for x in range(xcount) if x not in middle], middle


def after(value, *others):
    return lax.optimization_barrier((value, *others))[0]


def call(body, name, args, outs, scratch=(), specs=None, out_specs=None, gflop=0.0, alias=None):
    specs = specs or [SPEC] * len(args)
    space = {id(SPEC): pltpu.VMEM, id(FROM_HBM): pltpu.HBM}
    args = [
        pltpu.with_memory_space_constraint(a, space[id(s)]) if id(s) in space else a for a, s in zip(args, specs)
    ]
    return pl.pallas_call(
        body,
        out_shape=outs,
        in_specs=specs,
        out_specs=out_specs or [SPEC] * len(outs),
        scratch_shapes=list(scratch),
        compiler_params=pltpu.CompilerParams(vmem_limit_bytes=VMEM_LIMIT),
        cost_estimate=pl.CostEstimate(flops=int(gflop * 1e9), bytes_accessed=0, transcendentals=0),
        input_output_aliases=alias or {},
        name=name,
    )(*args)


def runs_of(cells):
    runs = []
    for i, x in enumerate(cells):
        if runs and x == sum(runs[-1][1:]):
            runs[-1][2] += 1
        else:
            runs.append([i, x, 1])
    return runs


def load_chunk(fields, cells, with_faces):
    xcount, ycount, owned = fields[0].shape
    count = len(fields)
    runs = runs_of(cells)

    def body(*refs):
        field_refs, held_refs, out_ref = refs[:count], refs[count:2 * count], refs[2 * count]
        sems = refs[-1]
        copies = {}
        for f in range(count):
            for r, (i, x, size) in enumerate(runs):
                copies[f, r] = pltpu.make_async_copy(
                    field_refs[f].at[pl.ds(x, size)], held_refs[f].at[pl.ds(i, size)], sems.at[f, r]
                )
                copies[f, r].start()
        for f in range(count):
            for r, (start, _, size) in enumerate(runs):
                copies[f, r].wait()
                for i in range(start, start + size):
                    value = held_refs[f][i].astype(BF16)
                    out_ref[f, i * ycount:(i + 1) * ycount, :] = value
                    if with_faces and cells[i] == 0:
                        refs[2 * count + 1][f] = value
                    if with_faces and cells[i] == xcount - 1:
                        refs[2 * count + 2][f] = value

    outs = [pltpu.VMEM((len(cells), ycount, owned), F32)] * count
    outs.append(pltpu.VMEM((count, len(cells) * ycount, owned), BF16))
    if with_faces:
        outs += [pltpu.VMEM((count, ycount, owned), BF16)] * 2
    return call(
        body, "load_chunk", fields, outs, scratch=[pltpu.SemaphoreType.DMA((count, len(runs)))],
        specs=[FROM_HBM] * count,
    )


def blocks_dot(blocks, kernels_ref, k, owners):
    depth = blocks[0].shape[-1]
    lhs = jnp.concatenate(blocks, axis=-1)
    rhs = jnp.concatenate(
        [kernels_ref[k, pl.ds(pl.multiple_of(o * depth, depth), depth), :] for o in owners], axis=0
    )
    return jnp.dot(lhs, rhs, preferred_element_type=F32)


def along_y(core):
    return DIFFUSION * (pltpu.roll(core, 1, 0) + pltpu.roll(core, core.shape[0] - 1, 0)) - 2.0 * core


def before_first(ones, twos, lo, hi, growth, chunks):
    _, ycount, owned = ones[0].shape
    xcount = sum(len(cells) for cells in chunks)
    count = len(chunks)
    place = {x: (c, i) for c, cells in enumerate(chunks) for i, x in enumerate(cells)}

    def body(*refs):
        lo_ref, hi_ref, g_ref, *outs = refs[2 * count:]
        growth = g_ref[...]
        for f in range(2):

            def get(x):
                c, i = place[x]
                return refs[f * count + c][i]

            for x, (c, i) in place.items():
                core = get(x)
                before = get(x - 1) if x > 0 else lo_ref[f].astype(F32)
                behind = get(x + 1) if x < xcount - 1 else hi_ref[f].astype(F32)
                outs[c][f, i] = DIFFUSION * (before + behind) + along_y(core) + core * growth

    outs = [pltpu.VMEM((2, len(cells), ycount, owned), F32) for cells in chunks]
    return call(body, "before_first", [*ones, *twos, lo, hi, growth], outs)


def early_part(blocks, kernels, new=None, cells=(), xcount=0):
    rows, owned = blocks[0].shape[0] * blocks[0].shape[1], blocks[0].shape[2]
    count = len(blocks)

    def body(*refs):
        block_refs, k_ref = refs[:count], refs[count]
        copies = []
        if new is None:
            part_ref = refs[-1]
        else:
            new_ref, part_ref, whole_ref, sems = refs[count + 1:]
            copies = [pltpu.make_async_copy(new_ref.at[i], whole_ref.at[x], sems.at[i]) for i, x in enumerate(cells)]
        for copy in copies:
            copy.start()
        me = lax.axis_index("trait")
        values = [r[...].reshape(rows, owned) for r in block_refs]
        for k in range(2):
            part_ref[k] = blocks_dot(values, k_ref, k, [me ^ j for j in range(count)])
        for copy in copies:
            copy.wait()

    args = [*blocks, kernels]
    outs = [pltpu.VMEM((2, rows, owned), F32)]
    if new is None:
        return call(body, "early_part", args, outs, gflop=20.0)[0]
    outs.append(jax.ShapeDtypeStruct((xcount, *new.shape[1:]), F32))
    return call(
        body, "early_part", [*args, new], outs, scratch=[pltpu.SemaphoreType.DMA((len(cells),))],
        out_specs=[SPEC, ANYWHERE], gflop=20.0,
    )


def first_node(part, last, base, one, two, initial, kernels, death, cells, with_faces):
    xcount, ycount, owned = initial.shape
    rows = len(cells) * ycount

    def body(part_ref, last_ref, base_ref, one_ref, two_ref, init_ref, k_ref, d_ref, *refs):
        new_ref, rounded_ref, rest_ref = refs[:3]
        sums = refs[-1]
        me = lax.axis_index("trait")
        for k in range(2):
            far_part = blocks_dot([last_ref[...].reshape(2 * rows, owned)], k_ref, k, [me ^ 3])
            sums[k] = (part_ref[k] + far_part).astype(BF16)
        death = d_ref[...]
        inv_one = 1.0 / (1.0 + FIRST * death)
        inv_two = 1.0 / (1.0 + SECOND * death)
        for i, x in enumerate(cells):
            cores = (one_ref[i], two_ref[i])
            e = []
            for f in range(2):
                at = pl.ds(f * rows + i * ycount, ycount)
                e.append(base_ref[f, i] - cores[f] * sums[0, at, :].astype(F32) + sums[1, at, :].astype(F32))
            full_one = e[0] - death * cores[0]
            full_two = e[1] - death * cores[1]
            new = (
                init_ref[x]
                + FIRST * death * cores[0]
                + STEP_SIZE * (5.0 / 12.0 * full_one - 1.0 / 12.0 * full_two)
            ) * inv_one
            new_ref[i] = new
            rounded = new.astype(BF16)
            rounded_ref[0, i * ycount:(i + 1) * ycount, :] = rounded
            if with_faces and x == 0:
                refs[3][0] = rounded
            if with_faces and x == xcount - 1:
                refs[4][0] = rounded
            rest_ref[i] = (
                new - SECOND * e[0] + SECOND * death * cores[1] + STEP_SIZE / 3.0 * (full_one + full_two)
            ) * inv_two

    outs = [
        pltpu.VMEM((len(cells), ycount, owned), F32),
        pltpu.VMEM((1, rows, owned), BF16),
        pltpu.VMEM((len(cells), ycount, owned), F32),
    ]
    if with_faces:
        outs += [pltpu.VMEM((1, ycount, owned), BF16)] * 2
    args = [part, last, base, one, two, initial, kernels, death]
    return call(
        body, "first_node", args, outs, scratch=[pltpu.VMEM((2, 2 * rows, owned), BF16)],
        gflop=0.0,
    )


def before_second(news, rests, growth, death, begun, owns, kernels, chunks):
    _, ycount, owned = news[0].shape
    xcount = sum(len(cells) for cells in chunks)
    count = len(chunks)
    place = {x: (c, i) for c, cells in enumerate(chunks) for i, x in enumerate(cells)}

    def body(*refs):
        new_refs, rest_refs = refs[:count], refs[count:2 * count]
        own_refs, (k_ref, g_ref, d_ref, _, whole_ref) = refs[2 * count:3 * count], refs[3 * count:3 * count + 5]
        part_refs, base_refs, sems = refs[3 * count + 5:4 * count + 5], refs[4 * count + 5:-1], refs[-1]
        copies = [
            pltpu.make_async_copy(new_refs[-1].at[i], whole_ref.at[x], sems.at[i]) for i, x in enumerate(chunks[-1])
        ]
        for copy in copies:
            copy.start()
        me = lax.axis_index("trait")
        for part_ref, own_ref in zip(part_refs, own_refs):
            for k in range(2):
                part_ref[k] = blocks_dot([own_ref[...].reshape(-1, owned)], k_ref, k, [me])
        growth = g_ref[...]
        factor = SECOND / (1.0 + SECOND * d_ref[...])
        for x, (c, i) in place.items():
            core = new_refs[c][i]
            e = along_y(core) + core * growth
            for near in (x - 1, x + 1):
                if near in place:
                    e = e + DIFFUSION * new_refs[place[near][0]][place[near][1]]
            base_refs[c][i] = rest_refs[c][i] + factor * e
        for copy in copies:
            copy.wait()

    outs = [jax.ShapeDtypeStruct((xcount, ycount, owned), F32)]
    outs += [pltpu.VMEM((2, len(cells) * ycount, owned), F32) for cells in chunks]
    outs += [pltpu.VMEM((len(cells), ycount, owned), F32) for cells in chunks]
    args = [*news, *rests, *owns, kernels, growth, death, begun]
    return call(
        body, "before_second", args, outs, scratch=[pltpu.SemaphoreType.DMA((len(chunks[-1]),))],
        specs=[SPEC] * (len(args) - 1) + [FROM_HBM], out_specs=[ANYWHERE] + [SPEC] * (len(outs) - 1), gflop=20.0,
        alias={len(args) - 1: 0},
    )


def whole_sums(part, blocks, kernels):
    rows, owned = blocks[0].shape[1:]

    def body(part_ref, sib_ref, far_ref, farsib_ref, k_ref, sums_ref):
        me = lax.axis_index("trait")
        values = [r[...].reshape(rows, owned) for r in (sib_ref, far_ref, farsib_ref)]
        for k in range(2):
            sums_ref[k] = (part_ref[k] + blocks_dot(values, k_ref, k, [me ^ 1, me ^ 2, me ^ 3])).astype(BF16)

    return call(body, "whole_sums", [part, *blocks, kernels], [pltpu.VMEM((2, rows, owned), BF16)])[0]


def second_first(sums, base, new, death, lo, hi, cells, part, sib, far, base_b, new_b, kernels, xcount):
    _, ycount, owned = new.shape
    rows = far.shape[1]

    def body(sums_ref, base_ref, new_ref, d_ref, lo_ref, hi_ref, part_ref, sib_ref, far_ref, base_b_ref, new_b_ref, *refs):
        k_ref, out_ref, base_out_ref, held, sems = refs
        factor = SECOND / (1.0 + SECOND * d_ref[...])
        faces = {0: lo_ref, xcount - 1: hi_ref}
        copies = []
        for i, x in enumerate(cells):
            at = pl.ds(i * ycount, ycount)
            e = sums_ref[1, at, :].astype(F32) - new_ref[i] * sums_ref[0, at, :].astype(F32)
            if x in faces:
                e = e + DIFFUSION * faces[x][0].astype(F32)
            held[i] = base_ref[i] + factor * e
            copies.append(pltpu.make_async_copy(held.at[i], out_ref.at[x], sems.at[i]))
            copies[-1].start()
        me = lax.axis_index("trait")
        values = [r[...].reshape(rows, owned) for r in (sib_ref, far_ref)]
        compete, mutate = (part_ref[k] + blocks_dot(values, k_ref, k, [me ^ 1, me ^ 2]) for k in range(2))
        for i in range(rows // ycount):
            at = slice(i * ycount, (i + 1) * ycount)
            base_out_ref[i] = base_b_ref[i] + factor * (mutate[at] - new_b_ref[i] * compete[at])
        for copy in copies:
            copy.wait()

    return call(
        body, "second_first", [sums, base, new, death, lo, hi, part, sib, far, base_b, new_b, kernels],
        [jax.ShapeDtypeStruct((xcount, ycount, owned), F32), pltpu.VMEM(base_b.shape, F32)],
        scratch=[pltpu.VMEM((len(cells), ycount, owned), F32), pltpu.SemaphoreType.DMA((len(cells),))],
        out_specs=[ANYWHERE, SPEC],
    )


def second_last(last, base, new, death, kernels, begun, cells, xcount):
    _, ycount, owned = new.shape
    rows = len(cells) * ycount

    def body(last_ref, base_ref, new_ref, d_ref, k_ref, begun_ref, out_ref, held, sems):
        me = lax.axis_index("trait")
        compete, mutate = (
            blocks_dot([last_ref[...].reshape(rows, owned)], k_ref, k, [me ^ 3]) for k in range(2)
        )
        factor = SECOND / (1.0 + SECOND * d_ref[...])
        copies = []
        for i, x in enumerate(cells):
            at = slice(i * ycount, (i + 1) * ycount)
            held[i] = base_ref[i] + factor * (mutate[at] - new_ref[i] * compete[at])
            copies.append(pltpu.make_async_copy(held.at[i], out_ref.at[x], sems.at[i]))
            copies[-1].start()
        for copy in copies:
            copy.wait()

    return call(
        body, "second_last", [last, base, new, death, kernels, begun],
        [jax.ShapeDtypeStruct((xcount, ycount, owned), F32)],
        scratch=[pltpu.VMEM((len(cells), ycount, owned), F32), pltpu.SemaphoreType.DMA((len(cells),))],
        specs=[SPEC] * 5 + [FROM_HBM], out_specs=[ANYWHERE], alias={5: 0},
    )[0]


def local(initial, section_one, section_two, kernels, growth, death_rate):
    xcount, ycount, owned = section_one.shape
    traits = lax.axis_size("trait")
    gcount = lax.axis_size("gx")
    growth = growth.reshape(1, owned)
    death = death_rate.reshape(1, owned)
    chunks = chunks_of(xcount)

    def to_sibling(v):
        return lax.ppermute(v, "trait", [(i, i ^ 1) for i in range(traits)])

    def to_far(v):
        return lax.ppermute(v, "trait", [(i, i ^ 2) for i in range(traits)])

    def from_below(tail):
        return lax.ppermute(tail, "gx", [(i, (i + 1) % gcount) for i in range(gcount)])

    def from_above(head):
        return lax.ppermute(head, "gx", [((i + 1) % gcount, i) for i in range(gcount)])

    one_a, two_a, own_a, head, tail = load_chunk((section_one, section_two), chunks[0], True)
    far_a = to_far(own_a)
    one_b, two_b, own_b = load_chunk((after(section_one, own_a), section_two), chunks[1], False)
    far_b = to_far(own_b)
    head, tail, kernels = lax.optimization_barrier((head, tail, kernels, own_b))[:3]
    lo, hi = from_below(tail), from_above(head)
    base_a, base_b = before_first((one_a, one_b), (two_a, two_b), lo, hi, growth, chunks)
    sib_a = to_sibling(after(own_a, own_b))
    sib_b = to_sibling(own_b)
    far_a = after(far_a, base_a)
    farsib_a = to_sibling(far_a)
    part_a = early_part([own_a, sib_a, far_a], kernels)
    new_a, rounded_a, rest_a, new_head, new_tail = first_node(
        part_a, farsib_a, base_a, one_a, two_a, initial, kernels, death, chunks[0], True
    )
    nfar_a = to_far(rounded_a)
    nsib_a = to_sibling(rounded_a)

    new_lo = from_below(new_tail)
    far_b = after(far_b, rounded_a, new_lo)
    farsib_b = to_sibling(far_b)
    part_b, new_one = early_part([own_b, sib_b, far_b], kernels, new_a, chunks[0], xcount)
    new_b, rounded_b, rest_b = first_node(
        part_b, farsib_b, base_b, one_b, two_b, initial, kernels, death, chunks[1], False
    )
    nfar_b = to_far(rounded_b)
    nsib_b = to_sibling(rounded_b)
    new_hi = from_above(after(new_head, rounded_b))
    nfar_a = after(nfar_a, rounded_b)
    nfarsib_a = to_sibling(nfar_a)
    new_one, npart_a, npart_b, nbase_a, nbase_b = before_second(
        (new_a, new_b), (rest_a, rest_b), growth, death, new_one, (rounded_a, rounded_b), kernels, chunks
    )
    sums_a = whole_sums(npart_a, [nsib_a, nfar_a, nfarsib_a], after(kernels, nbase_a))
    nfar_b = after(nfar_b, sums_a, new_hi)
    nfarsib_b = to_sibling(nfar_b)
    begun, nbase_b = second_first(
        sums_a, nbase_a, new_a, death, new_lo, new_hi, chunks[0], npart_b, nsib_b, nfar_b, nbase_b, new_b,
        kernels, xcount,
    )
    new_two = second_last(nfarsib_b, nbase_b, new_b, death, kernels, begun, chunks[1], xcount)
    return new_one, new_two


def solution(mesh):
    in_specs = (
        P("gx", None, "trait"),
        P("gx", None, "trait"),
        P("gx", None, "trait"),
        P(None, None, "trait"),
        P("trait"),
        P("trait"),
    )
    out_specs = (P("gx", None, "trait"), P("gx", None, "trait"))
    return jax.shard_map(local, mesh=mesh, in_specs=in_specs, out_specs=out_specs, check_vma=False)
```

```python
import jax
import jax.numpy as jnp
from jax import lax
from jax.experimental import pallas as pl
from jax.experimental.pallas import tpu as pltpu
from jax.sharding import PartitionSpec as P

DIFFUSION = 0.25
STEP_SIZE = 0.5
FIRST = STEP_SIZE / 3.0
SECOND = 2.0 * STEP_SIZE / 3.0
F32 = jnp.float32
BF16 = jnp.bfloat16
VMEM_LIMIT = 20 * 1024 * 1024
SPEC = pl.BlockSpec(memory_space=pltpu.VMEM)
ANYWHERE = pl.BlockSpec(memory_space=pl.ANY)
FROM_HBM = pl.BlockSpec(memory_space=pltpu.HBM)


def chunks_of(xcount):
    last = max(1, 3 * xcount // 8)
    start = (xcount - last + 1) // 2
    middle = list(range(start, start + last))
    return [x for x in range(xcount) if x not in middle], middle


def after(value, *others):
    return lax.optimization_barrier((value, *others))[0]


def call(body, name, args, outs, scratch=(), specs=None, out_specs=None, gflop=0.0, alias=None):
    specs = specs or [SPEC] * len(args)
    space = {id(SPEC): pltpu.VMEM, id(FROM_HBM): pltpu.HBM}
    args = [
        pltpu.with_memory_space_constraint(a, space[id(s)]) if id(s) in space else a for a, s in zip(args, specs)
    ]
    return pl.pallas_call(
        body,
        out_shape=outs,
        in_specs=specs,
        out_specs=out_specs or [SPEC] * len(outs),
        scratch_shapes=list(scratch),
        compiler_params=pltpu.CompilerParams(vmem_limit_bytes=VMEM_LIMIT),
        cost_estimate=pl.CostEstimate(flops=int(gflop * 1e9), bytes_accessed=0, transcendentals=0),
        input_output_aliases=alias or {},
        name=name,
    )(*args)


def runs_of(cells):
    runs = []
    for i, x in enumerate(cells):
        if runs and x == sum(runs[-1][1:]):
            runs[-1][2] += 1
        else:
            runs.append([i, x, 1])
    return runs


def load_chunk(fields, cells, with_faces):
    xcount, ycount, owned = fields[0].shape
    count = len(fields)
    runs = runs_of(cells)

    def body(*refs):
        field_refs, held_refs, out_ref = refs[:count], refs[count:2 * count], refs[2 * count]
        sems = refs[-1]
        copies = {}
        for f in range(count):
            for r, (i, x, size) in enumerate(runs):
                copies[f, r] = pltpu.make_async_copy(
                    field_refs[f].at[pl.ds(x, size)], held_refs[f].at[pl.ds(i, size)], sems.at[f, r]
                )
                copies[f, r].start()
        for f in range(count):
            for r, (start, _, size) in enumerate(runs):
                copies[f, r].wait()
                for i in range(start, start + size):
                    value = held_refs[f][i].astype(BF16)
                    out_ref[f, i * ycount:(i + 1) * ycount, :] = value
                    if with_faces and cells[i] == 0:
                        refs[2 * count + 1][f] = value
                    if with_faces and cells[i] == xcount - 1:
                        refs[2 * count + 2][f] = value

    outs = [pltpu.VMEM((len(cells), ycount, owned), F32)] * count
    outs.append(pltpu.VMEM((count, len(cells) * ycount, owned), BF16))
    if with_faces:
        outs += [pltpu.VMEM((count, ycount, owned), BF16)] * 2
    return call(
        body, "load_chunk", fields, outs, scratch=[pltpu.SemaphoreType.DMA((count, len(runs)))],
        specs=[FROM_HBM] * count,
    )


def blocks_dot(blocks, kernels_ref, k, owners):
    depth = blocks[0].shape[-1]
    lhs = jnp.concatenate(blocks, axis=-1)
    rhs = jnp.concatenate(
        [kernels_ref[k, pl.ds(pl.multiple_of(o * depth, depth), depth), :] for o in owners], axis=0
    )
    return jnp.dot(lhs, rhs, preferred_element_type=F32)


def along_y(core):
    return DIFFUSION * (pltpu.roll(core, 1, 0) + pltpu.roll(core, core.shape[0] - 1, 0)) - 2.0 * core


def before_first(ones, twos, lo, hi, growth, chunks):
    _, ycount, owned = ones[0].shape
    xcount = sum(len(cells) for cells in chunks)
    count = len(chunks)
    place = {x: (c, i) for c, cells in enumerate(chunks) for i, x in enumerate(cells)}

    def body(*refs):
        lo_ref, hi_ref, g_ref, *outs = refs[2 * count:]
        growth = g_ref[...]
        for f in range(2):

            def get(x):
                c, i = place[x]
                return refs[f * count + c][i]

            for x, (c, i) in place.items():
                core = get(x)
                before = get(x - 1) if x > 0 else lo_ref[f].astype(F32)
                behind = get(x + 1) if x < xcount - 1 else hi_ref[f].astype(F32)
                outs[c][f, i] = DIFFUSION * (before + behind) + along_y(core) + core * growth

    outs = [pltpu.VMEM((2, len(cells), ycount, owned), F32) for cells in chunks]
    return call(body, "before_first", [*ones, *twos, lo, hi, growth], outs)


def early_part(blocks, kernels, new=None, cells=(), xcount=0):
    rows, owned = blocks[0].shape[0] * blocks[0].shape[1], blocks[0].shape[2]
    count = len(blocks)

    def body(*refs):
        block_refs, k_ref = refs[:count], refs[count]
        copies = []
        if new is None:
            part_ref = refs[-1]
        else:
            new_ref, part_ref, whole_ref, sems = refs[count + 1:]
            copies = [
                pltpu.make_async_copy(new_ref.at[pl.ds(i, size)], whole_ref.at[pl.ds(x, size)], sems.at[r])
                for r, (i, x, size) in enumerate(runs_of(cells))
            ]
        for copy in copies:
            copy.start()
        me = lax.axis_index("trait")
        values = [r[...].reshape(rows, owned) for r in block_refs]
        for k in range(2):
            part_ref[k] = blocks_dot(values, k_ref, k, [me ^ j for j in range(count)])
        for copy in copies:
            copy.wait()

    args = [*blocks, kernels]
    outs = [pltpu.VMEM((2, rows, owned), F32)]
    if new is None:
        return call(body, "early_part", args, outs, gflop=20.0)[0]
    outs.append(jax.ShapeDtypeStruct((xcount, *new.shape[1:]), F32))
    return call(
        body, "early_part", [*args, new], outs, scratch=[pltpu.SemaphoreType.DMA((len(runs_of(cells)),))],
        out_specs=[SPEC, ANYWHERE], gflop=20.0,
    )


def first_node(part, last, base, one, two, initial, kernels, death, cells, with_faces):
    xcount, ycount, owned = initial.shape
    rows = len(cells) * ycount

    def body(part_ref, last_ref, base_ref, one_ref, two_ref, init_ref, k_ref, d_ref, *refs):
        new_ref, rounded_ref, rest_ref = refs[:3]
        sums = refs[-1]
        me = lax.axis_index("trait")
        for k in range(2):
            far_part = blocks_dot([last_ref[...].reshape(2 * rows, owned)], k_ref, k, [me ^ 3])
            sums[k] = (part_ref[k] + far_part).astype(BF16)
        death = d_ref[...]
        inv_one = 1.0 / (1.0 + FIRST * death)
        inv_two = 1.0 / (1.0 + SECOND * death)
        for i, x in enumerate(cells):
            cores = (one_ref[i], two_ref[i])
            e = []
            for f in range(2):
                at = pl.ds(f * rows + i * ycount, ycount)
                e.append(base_ref[f, i] - cores[f] * sums[0, at, :].astype(F32) + sums[1, at, :].astype(F32))
            full_one = e[0] - death * cores[0]
            full_two = e[1] - death * cores[1]
            new = (
                init_ref[x]
                + FIRST * death * cores[0]
                + STEP_SIZE * (5.0 / 12.0 * full_one - 1.0 / 12.0 * full_two)
            ) * inv_one
            new_ref[i] = new
            rounded = new.astype(BF16)
            rounded_ref[0, i * ycount:(i + 1) * ycount, :] = rounded
            if with_faces and x == 0:
                refs[3][0] = rounded
            if with_faces and x == xcount - 1:
                refs[4][0] = rounded
            rest_ref[i] = (
                new - SECOND * e[0] + SECOND * death * cores[1] + STEP_SIZE / 3.0 * (full_one + full_two)
            ) * inv_two

    outs = [
        pltpu.VMEM((len(cells), ycount, owned), F32),
        pltpu.VMEM((1, rows, owned), BF16),
        pltpu.VMEM((len(cells), ycount, owned), F32),
    ]
    if with_faces:
        outs += [pltpu.VMEM((1, ycount, owned), BF16)] * 2
    args = [part, last, base, one, two, initial, kernels, death]
    return call(
        body, "first_node", args, outs, scratch=[pltpu.VMEM((2, 2 * rows, owned), BF16)],
        gflop=0.0,
    )


def before_second(news, rests, growth, death, begun, blocks, kernels, chunks):
    _, ycount, owned = news[0].shape
    rows = blocks[0].shape[1]
    xcount = sum(len(cells) for cells in chunks)
    count = len(chunks)
    size = len(blocks)
    place = {x: (c, i) for c, cells in enumerate(chunks) for i, x in enumerate(cells)}

    def body(*refs):
        new_refs, rest_refs, block_refs = refs[:count], refs[count:2 * count], refs[2 * count:2 * count + size]
        k_ref, g_ref, d_ref, _, whole_ref, part_ref = refs[2 * count + size:2 * count + size + 6]
        base_refs, sems = refs[2 * count + size + 6:-1], refs[-1]
        copies = [
            pltpu.make_async_copy(new_refs[-1].at[pl.ds(i, size)], whole_ref.at[pl.ds(x, size)], sems.at[r])
            for r, (i, x, size) in enumerate(runs_of(chunks[-1]))
        ]
        for copy in copies:
            copy.start()
        me = lax.axis_index("trait")
        values = [r[...].reshape(rows, owned) for r in block_refs]
        for k in range(2):
            part_ref[k] = blocks_dot(values, k_ref, k, [me ^ j for j in range(size)])
        growth = g_ref[...]
        factor = SECOND / (1.0 + SECOND * d_ref[...])
        for x, (c, i) in place.items():
            core = new_refs[c][i]
            e = along_y(core) + core * growth
            for near in (x - 1, x + 1):
                if near in place:
                    e = e + DIFFUSION * new_refs[place[near][0]][place[near][1]]
            base_refs[c][i] = rest_refs[c][i] + factor * e
        for copy in copies:
            copy.wait()

    outs = [jax.ShapeDtypeStruct((xcount, ycount, owned), F32), pltpu.VMEM((2, rows, owned), F32)]
    outs += [pltpu.VMEM((len(cells), ycount, owned), F32) for cells in chunks]
    args = [*news, *rests, *blocks, kernels, growth, death, begun]
    return call(
        body, "before_second", args, outs, scratch=[pltpu.SemaphoreType.DMA((len(runs_of(chunks[-1])),))],
        specs=[SPEC] * (len(args) - 1) + [FROM_HBM], out_specs=[ANYWHERE] + [SPEC] * (len(outs) - 1), gflop=20.0,
        alias={len(args) - 1: 0},
    )


def whole_sums(part, blocks, kernels):
    rows, owned = blocks[0].shape[1:]

    def body(part_ref, sib_ref, far_ref, farsib_ref, k_ref, sums_ref):
        me = lax.axis_index("trait")
        values = [r[...].reshape(rows, owned) for r in (sib_ref, far_ref, farsib_ref)]
        for k in range(2):
            sums_ref[k] = (part_ref[k] + blocks_dot(values, k_ref, k, [me ^ 1, me ^ 2, me ^ 3])).astype(BF16)

    return call(body, "whole_sums", [part, *blocks, kernels], [pltpu.VMEM((2, rows, owned), BF16)])[0]


def finish(cells, runs, ycount, sums, base_ref, new_ref, factor, faces, held, out_ref, sems):
    copies = []
    for r, (start, place, size) in enumerate(runs):
        for i in range(start, start + size):
            at = pl.ds(i * ycount, ycount)
            e = sums[1, at, :].astype(F32) - new_ref[i] * sums[0, at, :].astype(F32)
            if cells[i] in faces:
                e = e + DIFFUSION * faces[cells[i]][0].astype(F32)
            held[i] = base_ref[i] + factor * e
        copies.append(
            pltpu.make_async_copy(held.at[pl.ds(start, size)], out_ref.at[pl.ds(place, size)], sems.at[r])
        )
        copies[-1].start()
    return copies


def second_first(sums, base, new, death, lo, hi, blocks, kernels, cells, xcount):
    _, ycount, owned = new.shape
    rows = blocks[0].shape[1]
    count = len(blocks)

    def body(sums_ref, base_ref, new_ref, d_ref, lo_ref, hi_ref, k_ref, *refs):
        block_refs = refs[:count]
        out_ref, part_ref, held, sems = refs[count:]
        factor = SECOND / (1.0 + SECOND * d_ref[...])
        faces = {0: lo_ref, xcount - 1: hi_ref}
        copies = finish(cells, runs_of(cells), ycount, sums_ref, base_ref, new_ref, factor, faces, held, out_ref, sems)
        me = lax.axis_index("trait")
        values = [r[...].reshape(rows, owned) for r in block_refs]
        for k in range(2):
            part_ref[k] = blocks_dot(values, k_ref, k, [me ^ j for j in range(count)])
        for copy in copies:
            copy.wait()

    return call(
        body, "second_first", [sums, base, new, death, lo, hi, kernels, *blocks],
        [jax.ShapeDtypeStruct((xcount, ycount, owned), F32), pltpu.VMEM((2, rows, owned), F32)],
        scratch=[pltpu.VMEM((len(cells), ycount, owned), F32), pltpu.SemaphoreType.DMA((len(runs_of(cells)),))],
        out_specs=[ANYWHERE, SPEC],
    )


def second_last(part, last, base, new, death, kernels, begun, cells, xcount):
    _, ycount, owned = new.shape
    rows = len(cells) * ycount
    runs = runs_of(cells[:-1]) + [[len(cells) - 1, cells[-1], 1]]

    def body(part_ref, last_ref, base_ref, new_ref, d_ref, k_ref, begun_ref, out_ref, sums, held, sems):
        me = lax.axis_index("trait")
        for k in range(2):
            sums[k] = (part_ref[k] + blocks_dot([last_ref[...].reshape(rows, owned)], k_ref, k, [me ^ 3])).astype(BF16)
        factor = SECOND / (1.0 + SECOND * d_ref[...])
        for copy in finish(cells, runs, ycount, sums, base_ref, new_ref, factor, {}, held, out_ref, sems):
            copy.wait()

    return call(
        body, "second_last", [part, last, base, new, death, kernels, begun],
        [jax.ShapeDtypeStruct((xcount, ycount, owned), F32)],
        scratch=[
            pltpu.VMEM((2, rows, owned), BF16),
            pltpu.VMEM((len(cells), ycount, owned), F32),
            pltpu.SemaphoreType.DMA((len(runs),)),
        ],
        specs=[SPEC] * 6 + [FROM_HBM], out_specs=[ANYWHERE], alias={6: 0},
    )[0]


def local(initial, section_one, section_two, kernels, growth, death_rate):
    xcount, ycount, owned = section_one.shape
    traits = lax.axis_size("trait")
    gcount = lax.axis_size("gx")
    growth = growth.reshape(1, owned)
    death = death_rate.reshape(1, owned)
    chunks = chunks_of(xcount)

    def to_sibling(v):
        return lax.ppermute(v, "trait", [(i, i ^ 1) for i in range(traits)])

    def to_far(v):
        return lax.ppermute(v, "trait", [(i, i ^ 2) for i in range(traits)])

    def from_below(tail):
        return lax.ppermute(tail, "gx", [(i, (i + 1) % gcount) for i in range(gcount)])

    def from_above(head):
        return lax.ppermute(head, "gx", [((i + 1) % gcount, i) for i in range(gcount)])

    one_a, two_a, own_a, head, tail = load_chunk((section_one, section_two), chunks[0], True)
    far_a = to_far(own_a)
    one_b, two_b, own_b = load_chunk((after(section_one, own_a), section_two), chunks[1], False)
    far_b = to_far(own_b)
    head, tail, kernels = lax.optimization_barrier((head, tail, kernels, own_b))[:3]
    lo, hi = from_below(tail), from_above(head)
    base_a, base_b = before_first((one_a, one_b), (two_a, two_b), lo, hi, growth, chunks)
    sib_a = to_sibling(after(own_a, own_b))
    sib_b = to_sibling(own_b)
    far_a = after(far_a, base_a)
    farsib_a = to_sibling(far_a)
    part_a = early_part([own_a, sib_a, far_a], kernels)
    new_a, rounded_a, rest_a, new_head, new_tail = first_node(
        part_a, farsib_a, base_a, one_a, two_a, initial, kernels, death, chunks[0], True
    )
    nfar_a = to_far(rounded_a)
    nsib_a = to_sibling(rounded_a)

    new_lo = from_below(new_tail)
    far_b = after(far_b, rounded_a, new_lo)
    farsib_b = to_sibling(far_b)
    part_b, new_one = early_part([own_b, sib_b, far_b], kernels, new_a, chunks[0], xcount)
    new_b, rounded_b, rest_b = first_node(
        part_b, farsib_b, base_b, one_b, two_b, initial, kernels, death, chunks[1], False
    )
    nfar_b = to_far(rounded_b)
    nsib_b = to_sibling(rounded_b)
    new_hi = from_above(after(new_head, rounded_b))
    nfar_a = after(nfar_a, rounded_b)
    nfarsib_a = to_sibling(nfar_a)
    new_one, npart_a, nbase_a, nbase_b = before_second(
        (new_a, new_b), (rest_a, rest_b), growth, death, new_one, [rounded_a], kernels, chunks
    )
    sums_a = whole_sums(npart_a, [nsib_a, nfar_a, nfarsib_a], after(kernels, nbase_a))
    nfar_b = after(nfar_b, sums_a, new_hi)
    nfarsib_b = to_sibling(nfar_b)
    begun, npart_b = second_first(
        sums_a, nbase_a, new_a, death, new_lo, new_hi, [rounded_b, nsib_b, nfar_b], kernels, chunks[0], xcount
    )
    new_two = second_last(npart_b, nfarsib_b, nbase_b, new_b, death, kernels, begun, chunks[1], xcount)
    return new_one, new_two


def solution(mesh):
    in_specs = (
        P("gx", None, "trait"),
        P("gx", None, "trait"),
        P("gx", None, "trait"),
        P(None, None, "trait"),
        P("trait"),
        P("trait"),
    )
    out_specs = (P("gx", None, "trait"), P("gx", None, "trait"))
    return jax.shard_map(local, mesh=mesh, in_specs=in_specs, out_specs=out_specs, check_vma=False)
```

```python
import jax
import jax.numpy as jnp
from jax import lax
from jax.experimental import pallas as pl
from jax.experimental.pallas import tpu as pltpu
from jax.sharding import PartitionSpec as P

DIFFUSION = 0.25
STEP_SIZE = 0.5
FIRST = STEP_SIZE / 3.0
SECOND = 2.0 * STEP_SIZE / 3.0
F32 = jnp.float32
BF16 = jnp.bfloat16
VMEM_LIMIT = 20 * 1024 * 1024
SPEC = pl.BlockSpec(memory_space=pltpu.VMEM)
ANYWHERE = pl.BlockSpec(memory_space=pl.ANY)
FROM_HBM = pl.BlockSpec(memory_space=pltpu.HBM)


def chunks_of(xcount):
    last = max(1, 3 * xcount // 8)
    start = (xcount - last + 1) // 2
    middle = list(range(start, start + last))
    return [x for x in range(xcount) if x not in middle], middle


def after(value, *others):
    return lax.optimization_barrier((value, *others))[0]


def call(body, name, args, outs, scratch=(), specs=None, out_specs=None, gflop=0.0, alias=None):
    specs = specs or [SPEC] * len(args)
    space = {id(SPEC): pltpu.VMEM, id(FROM_HBM): pltpu.HBM}
    args = [
        pltpu.with_memory_space_constraint(a, space[id(s)]) if id(s) in space else a for a, s in zip(args, specs)
    ]
    return pl.pallas_call(
        body,
        out_shape=outs,
        in_specs=specs,
        out_specs=out_specs or [SPEC] * len(outs),
        scratch_shapes=list(scratch),
        compiler_params=pltpu.CompilerParams(vmem_limit_bytes=VMEM_LIMIT),
        cost_estimate=pl.CostEstimate(flops=int(gflop * 1e9), bytes_accessed=0, transcendentals=0),
        input_output_aliases=alias or {},
        name=name,
    )(*args)


def runs_of(cells):
    runs = []
    for i, x in enumerate(cells):
        if runs and x == sum(runs[-1][1:]):
            runs[-1][2] += 1
        else:
            runs.append([i, x, 1])
    return runs


def load_chunk(fields, cells, with_faces):
    xcount, ycount, owned = fields[0].shape
    count = len(fields)
    runs = runs_of(cells)

    def body(*refs):
        field_refs, held_refs, out_ref = refs[:count], refs[count:2 * count], refs[2 * count]
        sems = refs[-1]
        copies = {}
        for f in range(count):
            for r, (i, x, size) in enumerate(runs):
                copies[f, r] = pltpu.make_async_copy(
                    field_refs[f].at[pl.ds(x, size)], held_refs[f].at[pl.ds(i, size)], sems.at[f, r]
                )
                copies[f, r].start()
        for f in range(count):
            for r, (start, _, size) in enumerate(runs):
                copies[f, r].wait()
                for i in range(start, start + size):
                    value = held_refs[f][i].astype(BF16)
                    out_ref[f, i * ycount:(i + 1) * ycount, :] = value
                    if with_faces and cells[i] == 0:
                        refs[2 * count + 1][f] = value
                    if with_faces and cells[i] == xcount - 1:
                        refs[2 * count + 2][f] = value

    outs = [pltpu.VMEM((len(cells), ycount, owned), F32)] * count
    outs.append(pltpu.VMEM((count, len(cells) * ycount, owned), BF16))
    if with_faces:
        outs += [pltpu.VMEM((count, ycount, owned), BF16)] * 2
    return call(
        body, "load_chunk", fields, outs, scratch=[pltpu.SemaphoreType.DMA((count, len(runs)))],
        specs=[FROM_HBM] * count,
    )


def blocks_dot(blocks, kernels_ref, k, owners):
    depth = blocks[0].shape[-1]
    lhs = jnp.concatenate(blocks, axis=-1)
    rhs = jnp.concatenate(
        [kernels_ref[k, pl.ds(pl.multiple_of(o * depth, depth), depth), :] for o in owners], axis=0
    )
    return jnp.dot(lhs, rhs, preferred_element_type=F32)


def along_y(core):
    return DIFFUSION * (pltpu.roll(core, 1, 0) + pltpu.roll(core, core.shape[0] - 1, 0)) - 2.0 * core


def before_first(ones, twos, lo, hi, growth, chunks):
    _, ycount, owned = ones[0].shape
    xcount = sum(len(cells) for cells in chunks)
    count = len(chunks)
    place = {x: (c, i) for c, cells in enumerate(chunks) for i, x in enumerate(cells)}

    def body(*refs):
        lo_ref, hi_ref, g_ref, *outs = refs[2 * count:]
        growth = g_ref[...]
        for f in range(2):

            def get(x):
                c, i = place[x]
                return refs[f * count + c][i]

            for x, (c, i) in place.items():
                core = get(x)
                before = get(x - 1) if x > 0 else lo_ref[f].astype(F32)
                behind = get(x + 1) if x < xcount - 1 else hi_ref[f].astype(F32)
                outs[c][f, i] = DIFFUSION * (before + behind) + along_y(core) + core * growth

    outs = [pltpu.VMEM((2, len(cells), ycount, owned), F32) for cells in chunks]
    return call(body, "before_first", [*ones, *twos, lo, hi, growth], outs)


def early_part(blocks, kernels, new=None, cells=(), xcount=0):
    rows, owned = blocks[0].shape[0] * blocks[0].shape[1], blocks[0].shape[2]
    count = len(blocks)

    def body(*refs):
        block_refs, k_ref = refs[:count], refs[count]
        copies = []
        if new is None:
            part_ref = refs[-1]
        else:
            new_ref, part_ref, whole_ref, sems = refs[count + 1:]
            copies = [
                pltpu.make_async_copy(new_ref.at[pl.ds(i, size)], whole_ref.at[pl.ds(x, size)], sems.at[r])
                for r, (i, x, size) in enumerate(runs_of(cells))
            ]
        for copy in copies:
            copy.start()
        me = lax.axis_index("trait")
        values = [r[...].reshape(rows, owned) for r in block_refs]
        for k in range(2):
            part_ref[k] = blocks_dot(values, k_ref, k, [me ^ j for j in range(count)])
        for copy in copies:
            copy.wait()

    args = [*blocks, kernels]
    outs = [pltpu.VMEM((2, rows, owned), F32)]
    if new is None:
        return call(body, "early_part", args, outs, gflop=20.0)[0]
    outs.append(jax.ShapeDtypeStruct((xcount, *new.shape[1:]), F32))
    return call(
        body, "early_part", [*args, new], outs, scratch=[pltpu.SemaphoreType.DMA((len(runs_of(cells)),))],
        out_specs=[SPEC, ANYWHERE], gflop=20.0,
    )


def first_node(part, last, base, one, two, initial, kernels, death, cells, with_faces):
    xcount, ycount, owned = initial.shape
    rows = len(cells) * ycount

    def body(part_ref, last_ref, base_ref, one_ref, two_ref, init_ref, k_ref, d_ref, *refs):
        new_ref, rounded_ref, rest_ref = refs[:3]
        sums = refs[-1]
        me = lax.axis_index("trait")
        for k in range(2):
            far_part = blocks_dot([last_ref[...].reshape(2 * rows, owned)], k_ref, k, [me ^ 3])
            sums[k] = (part_ref[k] + far_part).astype(BF16)
        death = d_ref[...]
        inv_one = 1.0 / (1.0 + FIRST * death)
        inv_two = 1.0 / (1.0 + SECOND * death)
        for i, x in enumerate(cells):
            cores = (one_ref[i], two_ref[i])
            e = []
            for f in range(2):
                at = pl.ds(f * rows + i * ycount, ycount)
                e.append(base_ref[f, i] - cores[f] * sums[0, at, :].astype(F32) + sums[1, at, :].astype(F32))
            full_one = e[0] - death * cores[0]
            full_two = e[1] - death * cores[1]
            new = (
                init_ref[x]
                + FIRST * death * cores[0]
                + STEP_SIZE * (5.0 / 12.0 * full_one - 1.0 / 12.0 * full_two)
            ) * inv_one
            new_ref[i] = new
            rounded = new.astype(BF16)
            rounded_ref[0, i * ycount:(i + 1) * ycount, :] = rounded
            if with_faces and x == 0:
                refs[3][0] = rounded
            if with_faces and x == xcount - 1:
                refs[4][0] = rounded
            rest_ref[i] = (
                new - SECOND * e[0] + SECOND * death * cores[1] + STEP_SIZE / 3.0 * (full_one + full_two)
            ) * inv_two

    outs = [
        pltpu.VMEM((len(cells), ycount, owned), F32),
        pltpu.VMEM((1, rows, owned), BF16),
        pltpu.VMEM((len(cells), ycount, owned), F32),
    ]
    if with_faces:
        outs += [pltpu.VMEM((1, ycount, owned), BF16)] * 2
    args = [part, last, base, one, two, initial, kernels, death]
    return call(
        body, "first_node", args, outs, scratch=[pltpu.VMEM((2, 2 * rows, owned), BF16)],
        gflop=0.0,
    )


def before_second(news, rests, growth, death, begun, blocks, kernels, chunks):
    _, ycount, owned = news[0].shape
    rows = blocks[0].shape[1]
    xcount = sum(len(cells) for cells in chunks)
    count = len(chunks)
    size = len(blocks)
    place = {x: (c, i) for c, cells in enumerate(chunks) for i, x in enumerate(cells)}

    def body(*refs):
        new_refs, rest_refs, block_refs = refs[:count], refs[count:2 * count], refs[2 * count:2 * count + size]
        k_ref, g_ref, d_ref, _, whole_ref, part_ref = refs[2 * count + size:2 * count + size + 6]
        base_refs, sems = refs[2 * count + size + 6:-1], refs[-1]
        copies = [
            pltpu.make_async_copy(new_refs[-1].at[pl.ds(i, size)], whole_ref.at[pl.ds(x, size)], sems.at[r])
            for r, (i, x, size) in enumerate(runs_of(chunks[-1]))
        ]
        for copy in copies:
            copy.start()
        me = lax.axis_index("trait")
        values = [r[...].reshape(rows, owned) for r in block_refs]
        for k in range(2):
            part_ref[k] = blocks_dot(values, k_ref, k, [me ^ j for j in range(size)])
        growth = g_ref[...]
        factor = SECOND / (1.0 + SECOND * d_ref[...])
        for x, (c, i) in place.items():
            core = new_refs[c][i]
            e = along_y(core) + core * growth
            for near in (x - 1, x + 1):
                if near in place:
                    e = e + DIFFUSION * new_refs[place[near][0]][place[near][1]]
            base_refs[c][i] = rest_refs[c][i] + factor * e
        for copy in copies:
            copy.wait()

    outs = [jax.ShapeDtypeStruct((xcount, ycount, owned), F32), pltpu.VMEM((2, rows, owned), F32)]
    outs += [pltpu.VMEM((len(cells), ycount, owned), F32) for cells in chunks]
    args = [*news, *rests, *blocks, kernels, growth, death, begun]
    return call(
        body, "before_second", args, outs, scratch=[pltpu.SemaphoreType.DMA((len(runs_of(chunks[-1])),))],
        specs=[SPEC] * (len(args) - 1) + [FROM_HBM], out_specs=[ANYWHERE] + [SPEC] * (len(outs) - 1), gflop=20.0,
        alias={len(args) - 1: 0},
    )


def whole_sums(part, blocks, kernels):
    rows, owned = blocks[0].shape[1:]

    def body(part_ref, sib_ref, far_ref, farsib_ref, k_ref, sums_ref):
        me = lax.axis_index("trait")
        values = [r[...].reshape(rows, owned) for r in (sib_ref, far_ref, farsib_ref)]
        for k in range(2):
            sums_ref[k] = (part_ref[k] + blocks_dot(values, k_ref, k, [me ^ 1, me ^ 2, me ^ 3])).astype(BF16)

    return call(body, "whole_sums", [part, *blocks, kernels], [pltpu.VMEM((2, rows, owned), BF16)])[0]


def finish(cells, pieces, ycount, sums, base_ref, new_ref, factor, faces, held, out_ref, sems):
    copies = []
    size = ycount // pieces
    for i, x in enumerate(cells):
        for p in range(pieces):
            rows = pl.ds(p * size, size)
            at = pl.ds(i * ycount + p * size, size)
            e = sums[1, at, :].astype(F32) - new_ref[i, rows, :] * sums[0, at, :].astype(F32)
            if x in faces:
                e = e + DIFFUSION * faces[x][0, rows, :].astype(F32)
            held[i, rows, :] = base_ref[i, rows, :] + factor * e
            copies.append(
                pltpu.make_async_copy(held.at[i, rows], out_ref.at[x, rows], sems.at[i * pieces + p])
            )
            copies[-1].start()
    return copies


def second_first(sums, base, new, death, lo, hi, blocks, kernels, cells, xcount):
    _, ycount, owned = new.shape
    rows = blocks[0].shape[1]
    count = len(blocks)

    def body(sums_ref, base_ref, new_ref, d_ref, lo_ref, hi_ref, k_ref, *refs):
        block_refs = refs[:count]
        out_ref, part_ref, held, sems = refs[count:]
        factor = SECOND / (1.0 + SECOND * d_ref[...])
        faces = {0: lo_ref, xcount - 1: hi_ref}
        copies = finish(cells, 1, ycount, sums_ref, base_ref, new_ref, factor, faces, held, out_ref, sems)
        me = lax.axis_index("trait")
        values = [r[...].reshape(rows, owned) for r in block_refs]
        for k in range(2):
            part_ref[k] = blocks_dot(values, k_ref, k, [me ^ j for j in range(count)])
        for copy in copies:
            copy.wait()

    return call(
        body, "second_first", [sums, base, new, death, lo, hi, kernels, *blocks],
        [jax.ShapeDtypeStruct((xcount, ycount, owned), F32), pltpu.VMEM((2, rows, owned), F32)],
        scratch=[pltpu.VMEM((len(cells), ycount, owned), F32), pltpu.SemaphoreType.DMA((len(cells),))],
        out_specs=[ANYWHERE, SPEC],
    )


def second_last(part, last, base, new, death, kernels, begun, cells, xcount):
    _, ycount, owned = new.shape
    rows = len(cells) * ycount

    def body(part_ref, last_ref, base_ref, new_ref, d_ref, k_ref, begun_ref, out_ref, sums, held, sems):
        me = lax.axis_index("trait")
        for k in range(2):
            sums[k] = (part_ref[k] + blocks_dot([last_ref[...].reshape(rows, owned)], k_ref, k, [me ^ 3])).astype(BF16)
        factor = SECOND / (1.0 + SECOND * d_ref[...])
        for copy in finish(cells, 2, ycount, sums, base_ref, new_ref, factor, {}, held, out_ref, sems):
            copy.wait()

    return call(
        body, "second_last", [part, last, base, new, death, kernels, begun],
        [jax.ShapeDtypeStruct((xcount, ycount, owned), F32)],
        scratch=[
            pltpu.VMEM((2, rows, owned), BF16),
            pltpu.VMEM((len(cells), ycount, owned), F32),
            pltpu.SemaphoreType.DMA((2 * len(cells),)),
        ],
        specs=[SPEC] * 6 + [FROM_HBM], out_specs=[ANYWHERE], alias={6: 0},
    )[0]


def local(initial, section_one, section_two, kernels, growth, death_rate):
    xcount, ycount, owned = section_one.shape
    traits = lax.axis_size("trait")
    gcount = lax.axis_size("gx")
    growth = growth.reshape(1, owned)
    death = death_rate.reshape(1, owned)
    chunks = chunks_of(xcount)

    def to_sibling(v):
        return lax.ppermute(v, "trait", [(i, i ^ 1) for i in range(traits)])

    def to_far(v):
        return lax.ppermute(v, "trait", [(i, i ^ 2) for i in range(traits)])

    def from_below(tail):
        return lax.ppermute(tail, "gx", [(i, (i + 1) % gcount) for i in range(gcount)])

    def from_above(head):
        return lax.ppermute(head, "gx", [((i + 1) % gcount, i) for i in range(gcount)])

    one_a, two_a, own_a, head, tail = load_chunk((section_one, section_two), chunks[0], True)
    far_a = to_far(own_a)
    one_b, two_b, own_b = load_chunk((after(section_one, own_a), section_two), chunks[1], False)
    far_b = to_far(own_b)
    head, tail, kernels = lax.optimization_barrier((head, tail, kernels, own_b))[:3]
    lo, hi = from_below(tail), from_above(head)
    base_a, base_b = before_first((one_a, one_b), (two_a, two_b), lo, hi, growth, chunks)
    sib_a = to_sibling(after(own_a, own_b))
    sib_b = to_sibling(own_b)
    far_a = after(far_a, base_a)
    farsib_a = to_sibling(far_a)
    part_a = early_part([own_a, sib_a, far_a], kernels)
    new_a, rounded_a, rest_a, new_head, new_tail = first_node(
        part_a, farsib_a, base_a, one_a, two_a, initial, kernels, death, chunks[0], True
    )
    nfar_a = to_far(rounded_a)
    nsib_a = to_sibling(rounded_a)

    new_lo = from_below(new_tail)
    far_b = after(far_b, rounded_a, new_lo)
    farsib_b = to_sibling(far_b)
    part_b, new_one = early_part([own_b, sib_b, far_b], kernels, new_a, chunks[0], xcount)
    new_b, rounded_b, rest_b = first_node(
        part_b, farsib_b, base_b, one_b, two_b, initial, kernels, death, chunks[1], False
    )
    nfar_b = to_far(rounded_b)
    nsib_b = to_sibling(rounded_b)
    new_hi = from_above(after(new_head, rounded_b))
    nfar_a = after(nfar_a, rounded_b)
    nfarsib_a = to_sibling(nfar_a)
    new_one, npart_a, nbase_a, nbase_b = before_second(
        (new_a, new_b), (rest_a, rest_b), growth, death, new_one, [rounded_a], kernels, chunks
    )
    sums_a = whole_sums(npart_a, [nsib_a, nfar_a, nfarsib_a], after(kernels, nbase_a))
    nfar_b = after(nfar_b, sums_a, new_hi)
    nfarsib_b = to_sibling(nfar_b)
    begun, npart_b = second_first(
        sums_a, nbase_a, new_a, death, new_lo, new_hi, [rounded_b, nsib_b, nfar_b], kernels, chunks[0], xcount
    )
    new_two = second_last(npart_b, nfarsib_b, nbase_b, new_b, death, kernels, begun, chunks[1], xcount)
    return new_one, new_two


def solution(mesh):
    in_specs = (
        P("gx", None, "trait"),
        P("gx", None, "trait"),
        P("gx", None, "trait"),
        P(None, None, "trait"),
        P("trait"),
        P("trait"),
    )
    out_specs = (P("gx", None, "trait"), P("gx", None, "trait"))
    return jax.shard_map(local, mesh=mesh, in_specs=in_specs, out_specs=out_specs, check_vma=False)
```

```python
import jax
import jax.numpy as jnp
from jax import lax
from jax.experimental import pallas as pl
from jax.experimental.pallas import tpu as pltpu
from jax.sharding import PartitionSpec as P

DIFFUSION = 0.25
STEP_SIZE = 0.5
FIRST = STEP_SIZE / 3.0
SECOND = 2.0 * STEP_SIZE / 3.0
F32 = jnp.float32
BF16 = jnp.bfloat16
VMEM_LIMIT = 20 * 1024 * 1024
SPEC = pl.BlockSpec(memory_space=pltpu.VMEM)
ANYWHERE = pl.BlockSpec(memory_space=pl.ANY)
FROM_HBM = pl.BlockSpec(memory_space=pltpu.HBM)


def chunks_of(xcount):
    last = max(1, 3 * xcount // 8)
    start = (xcount - last + 1) // 2
    middle = list(range(start, start + last))
    return [x for x in range(xcount) if x not in middle], middle


def after(value, *others):
    return lax.optimization_barrier((value, *others))[0]


def call(body, name, args, outs, scratch=(), specs=None, out_specs=None, gflop=0.0, alias=None):
    specs = specs or [SPEC] * len(args)
    space = {id(SPEC): pltpu.VMEM, id(FROM_HBM): pltpu.HBM}
    args = [
        pltpu.with_memory_space_constraint(a, space[id(s)]) if id(s) in space else a for a, s in zip(args, specs)
    ]
    return pl.pallas_call(
        body,
        out_shape=outs,
        in_specs=specs,
        out_specs=out_specs or [SPEC] * len(outs),
        scratch_shapes=list(scratch),
        compiler_params=pltpu.CompilerParams(vmem_limit_bytes=VMEM_LIMIT),
        cost_estimate=pl.CostEstimate(flops=int(gflop * 1e9), bytes_accessed=0, transcendentals=0),
        input_output_aliases=alias or {},
        name=name,
    )(*args)


def runs_of(cells):
    runs = []
    for i, x in enumerate(cells):
        if runs and x == sum(runs[-1][1:]):
            runs[-1][2] += 1
        else:
            runs.append([i, x, 1])
    return runs


def load_chunk(fields, cells, with_faces):
    xcount, ycount, owned = fields[0].shape
    count = len(fields)
    runs = runs_of(cells)

    def body(*refs):
        field_refs, held_refs, out_ref = refs[:count], refs[count:2 * count], refs[2 * count]
        sems = refs[-1]
        copies = {}
        for f in range(count):
            for r, (i, x, size) in enumerate(runs):
                copies[f, r] = pltpu.make_async_copy(
                    field_refs[f].at[pl.ds(x, size)], held_refs[f].at[pl.ds(i, size)], sems.at[f, r]
                )
                copies[f, r].start()
        for f in range(count):
            for r, (start, _, size) in enumerate(runs):
                copies[f, r].wait()
                for i in range(start, start + size):
                    value = held_refs[f][i].astype(BF16)
                    out_ref[f, i * ycount:(i + 1) * ycount, :] = value
                    if with_faces and cells[i] == 0:
                        refs[2 * count + 1][f] = value
                    if with_faces and cells[i] == xcount - 1:
                        refs[2 * count + 2][f] = value

    outs = [pltpu.VMEM((len(cells), ycount, owned), F32)] * count
    outs.append(pltpu.VMEM((count, len(cells) * ycount, owned), BF16))
    if with_faces:
        outs += [pltpu.VMEM((count, ycount, owned), BF16)] * 2
    return call(
        body, "load_chunk", fields, outs, scratch=[pltpu.SemaphoreType.DMA((count, len(runs)))],
        specs=[FROM_HBM] * count,
    )


def blocks_dot(blocks, kernels_ref, k, owners):
    depth = blocks[0].shape[-1]
    lhs = jnp.concatenate(blocks, axis=-1)
    rhs = jnp.concatenate(
        [kernels_ref[k, pl.ds(pl.multiple_of(o * depth, depth), depth), :] for o in owners], axis=0
    )
    return jnp.dot(lhs, rhs, preferred_element_type=F32)


def along_y(core):
    return DIFFUSION * (pltpu.roll(core, 1, 0) + pltpu.roll(core, core.shape[0] - 1, 0)) - 2.0 * core


def before_first(ones, twos, lo, hi, growth, chunks):
    _, ycount, owned = ones[0].shape
    xcount = sum(len(cells) for cells in chunks)
    count = len(chunks)
    place = {x: (c, i) for c, cells in enumerate(chunks) for i, x in enumerate(cells)}

    def body(*refs):
        lo_ref, hi_ref, g_ref, *outs = refs[2 * count:]
        growth = g_ref[...]
        for f in range(2):

            def get(x):
                c, i = place[x]
                return refs[f * count + c][i]

            for x, (c, i) in place.items():
                core = get(x)
                before = get(x - 1) if x > 0 else lo_ref[f].astype(F32)
                behind = get(x + 1) if x < xcount - 1 else hi_ref[f].astype(F32)
                outs[c][f, i] = DIFFUSION * (before + behind) + along_y(core) + core * growth

    outs = [pltpu.VMEM((2, len(cells), ycount, owned), F32) for cells in chunks]
    return call(body, "before_first", [*ones, *twos, lo, hi, growth], outs)


def early_part(blocks, kernels, new=None, cells=(), xcount=0):
    rows, owned = blocks[0].shape[0] * blocks[0].shape[1], blocks[0].shape[2]
    count = len(blocks)

    def body(*refs):
        block_refs, k_ref = refs[:count], refs[count]
        copies = []
        if new is None:
            part_ref = refs[-1]
        else:
            new_ref, part_ref, whole_ref, sems = refs[count + 1:]
            copies = [
                pltpu.make_async_copy(new_ref.at[pl.ds(i, size)], whole_ref.at[pl.ds(x, size)], sems.at[r])
                for r, (i, x, size) in enumerate(runs_of(cells))
            ]
        for copy in copies:
            copy.start()
        me = lax.axis_index("trait")
        values = [r[...].reshape(rows, owned) for r in block_refs]
        for k in range(2):
            part_ref[k] = blocks_dot(values, k_ref, k, [me ^ j for j in range(count)])
        for copy in copies:
            copy.wait()

    args = [*blocks, kernels]
    outs = [pltpu.VMEM((2, rows, owned), F32)]
    if new is None:
        return call(body, "early_part", args, outs, gflop=20.0)[0]
    outs.append(jax.ShapeDtypeStruct((xcount, *new.shape[1:]), F32))
    return call(
        body, "early_part", [*args, new], outs, scratch=[pltpu.SemaphoreType.DMA((len(runs_of(cells)),))],
        out_specs=[SPEC, ANYWHERE], gflop=20.0,
    )


def first_node(part, last, base, one, two, initial, kernels, death, cells, with_faces):
    xcount, ycount, owned = initial.shape
    rows = len(cells) * ycount

    def body(part_ref, last_ref, base_ref, one_ref, two_ref, init_ref, k_ref, d_ref, *refs):
        new_ref, rounded_ref, rest_ref = refs[:3]
        sums = refs[-1]
        me = lax.axis_index("trait")
        for k in range(2):
            far_part = blocks_dot([last_ref[...].reshape(2 * rows, owned)], k_ref, k, [me ^ 3])
            sums[k] = (part_ref[k] + far_part).astype(BF16)
        death = d_ref[...]
        inv_one = 1.0 / (1.0 + FIRST * death)
        inv_two = 1.0 / (1.0 + SECOND * death)
        for i, x in enumerate(cells):
            cores = (one_ref[i], two_ref[i])
            e = []
            for f in range(2):
                at = pl.ds(f * rows + i * ycount, ycount)
                e.append(base_ref[f, i] - cores[f] * sums[0, at, :].astype(F32) + sums[1, at, :].astype(F32))
            full_one = e[0] - death * cores[0]
            full_two = e[1] - death * cores[1]
            new = (
                init_ref[x]
                + FIRST * death * cores[0]
                + STEP_SIZE * (5.0 / 12.0 * full_one - 1.0 / 12.0 * full_two)
            ) * inv_one
            new_ref[i] = new
            rounded = new.astype(BF16)
            rounded_ref[0, i * ycount:(i + 1) * ycount, :] = rounded
            if with_faces and x == 0:
                refs[3][0] = rounded
            if with_faces and x == xcount - 1:
                refs[4][0] = rounded
            rest_ref[i] = (
                new - SECOND * e[0] + SECOND * death * cores[1] + STEP_SIZE / 3.0 * (full_one + full_two)
            ) * inv_two

    outs = [
        pltpu.VMEM((len(cells), ycount, owned), F32),
        pltpu.VMEM((1, rows, owned), BF16),
        pltpu.VMEM((len(cells), ycount, owned), F32),
    ]
    if with_faces:
        outs += [pltpu.VMEM((1, ycount, owned), BF16)] * 2
    args = [part, last, base, one, two, initial, kernels, death]
    return call(
        body, "first_node", args, outs, scratch=[pltpu.VMEM((2, 2 * rows, owned), BF16)],
        gflop=0.0,
    )


def before_second(news, rests, growth, death, begun, blocks, kernels, chunks):
    _, ycount, owned = news[0].shape
    rows = blocks[0].shape[1]
    xcount = sum(len(cells) for cells in chunks)
    count = len(chunks)
    size = len(blocks)
    place = {x: (c, i) for c, cells in enumerate(chunks) for i, x in enumerate(cells)}

    def body(*refs):
        new_refs, rest_refs, block_refs = refs[:count], refs[count:2 * count], refs[2 * count:2 * count + size]
        k_ref, g_ref, d_ref, _, whole_ref, part_ref = refs[2 * count + size:2 * count + size + 6]
        base_refs, sems = refs[2 * count + size + 6:-1], refs[-1]
        copies = [
            pltpu.make_async_copy(new_refs[-1].at[pl.ds(i, size)], whole_ref.at[pl.ds(x, size)], sems.at[r])
            for r, (i, x, size) in enumerate(runs_of(chunks[-1]))
        ]
        for copy in copies:
            copy.start()
        me = lax.axis_index("trait")
        values = [r[...].reshape(rows, owned) for r in block_refs]
        for k in range(2):
            part_ref[k] = blocks_dot(values, k_ref, k, [me ^ j for j in range(size)])
        growth = g_ref[...]
        factor = SECOND / (1.0 + SECOND * d_ref[...])
        for x, (c, i) in place.items():
            core = new_refs[c][i]
            e = along_y(core) + core * growth
            for near in (x - 1, x + 1):
                if near in place:
                    e = e + DIFFUSION * new_refs[place[near][0]][place[near][1]]
            base_refs[c][i] = rest_refs[c][i] + factor * e
        for copy in copies:
            copy.wait()

    outs = [jax.ShapeDtypeStruct((xcount, ycount, owned), F32), pltpu.VMEM((2, rows, owned), F32)]
    outs += [pltpu.VMEM((len(cells), ycount, owned), F32) for cells in chunks]
    args = [*news, *rests, *blocks, kernels, growth, death, begun]
    return call(
        body, "before_second", args, outs, scratch=[pltpu.SemaphoreType.DMA((len(runs_of(chunks[-1])),))],
        specs=[SPEC] * (len(args) - 1) + [FROM_HBM], out_specs=[ANYWHERE] + [SPEC] * (len(outs) - 1), gflop=20.0,
        alias={len(args) - 1: 0},
    )


def whole_sums(part, blocks, kernels):
    rows, owned = blocks[0].shape[1:]

    def body(part_ref, sib_ref, far_ref, farsib_ref, k_ref, sums_ref):
        me = lax.axis_index("trait")
        values = [r[...].reshape(rows, owned) for r in (sib_ref, far_ref, farsib_ref)]
        for k in range(2):
            sums_ref[k] = (part_ref[k] + blocks_dot(values, k_ref, k, [me ^ 1, me ^ 2, me ^ 3])).astype(BF16)

    return call(body, "whole_sums", [part, *blocks, kernels], [pltpu.VMEM((2, rows, owned), BF16)])[0]


def finish(cells, pieces, ycount, sums, base_ref, new_ref, factor, faces, held, out_ref, sems):
    copies = []
    size = ycount // pieces
    for i, x in enumerate(cells):
        for p in range(pieces):
            rows = pl.ds(p * size, size)
            at = pl.ds(i * ycount + p * size, size)
            e = sums[1, at, :].astype(F32) - new_ref[i, rows, :] * sums[0, at, :].astype(F32)
            if x in faces:
                e = e + DIFFUSION * faces[x][0, rows, :].astype(F32)
            held[i, rows, :] = base_ref[i, rows, :] + factor * e
            copies.append(
                pltpu.make_async_copy(held.at[i, rows], out_ref.at[x, rows], sems.at[i * pieces + p])
            )
            copies[-1].start()
    return copies


def second_first(sums, base, new, death, lo, hi, blocks, kernels, cells, xcount):
    _, ycount, owned = new.shape
    rows = blocks[0].shape[1]
    count = len(blocks)

    def body(sums_ref, base_ref, new_ref, d_ref, lo_ref, hi_ref, k_ref, *refs):
        block_refs = refs[:count]
        out_ref, part_ref, held, sems = refs[count:]
        factor = SECOND / (1.0 + SECOND * d_ref[...])
        faces = {0: lo_ref, xcount - 1: hi_ref}
        copies = finish(cells, 1, ycount, sums_ref, base_ref, new_ref, factor, faces, held, out_ref, sems)
        me = lax.axis_index("trait")
        values = [r[...].reshape(rows, owned) for r in block_refs]
        for k in range(2):
            part_ref[k] = blocks_dot(values, k_ref, k, [me ^ j for j in range(count)])
        for copy in copies:
            copy.wait()

    return call(
        body, "second_first", [sums, base, new, death, lo, hi, kernels, *blocks],
        [jax.ShapeDtypeStruct((xcount, ycount, owned), F32), pltpu.VMEM((2, rows, owned), F32)],
        scratch=[pltpu.VMEM((len(cells), ycount, owned), F32), pltpu.SemaphoreType.DMA((len(cells),))],
        out_specs=[ANYWHERE, SPEC],
    )


def second_last(part, last, base, new, death, kernels, begun, cells, xcount):
    _, ycount, owned = new.shape
    rows = len(cells) * ycount

    def body(part_ref, last_ref, base_ref, new_ref, d_ref, k_ref, begun_ref, out_ref, sums, held, sems):
        me = lax.axis_index("trait")
        for k in range(2):
            sums[k] = (part_ref[k] + blocks_dot([last_ref[...].reshape(rows, owned)], k_ref, k, [me ^ 3])).astype(BF16)
        factor = SECOND / (1.0 + SECOND * d_ref[...])
        for copy in finish(cells, 2, ycount, sums, base_ref, new_ref, factor, {}, held, out_ref, sems):
            copy.wait()

    return call(
        body, "second_last", [part, last, base, new, death, kernels, begun],
        [jax.ShapeDtypeStruct((xcount, ycount, owned), F32)],
        scratch=[
            pltpu.VMEM((2, rows, owned), BF16),
            pltpu.VMEM((len(cells), ycount, owned), F32),
            pltpu.SemaphoreType.DMA((2 * len(cells),)),
        ],
        specs=[SPEC] * 6 + [FROM_HBM], out_specs=[ANYWHERE], alias={6: 0},
    )[0]


def local(initial, section_one, section_two, kernels, growth, death_rate):
    xcount, ycount, owned = section_one.shape
    traits = lax.axis_size("trait")
    gcount = lax.axis_size("gx")
    growth = growth.reshape(1, owned)
    death = death_rate.reshape(1, owned)
    chunks = chunks_of(xcount)

    def to_sibling(v):
        return lax.ppermute(v, "trait", [(i, i ^ 1) for i in range(traits)])

    def to_far(v):
        return lax.ppermute(v, "trait", [(i, i ^ 2) for i in range(traits)])

    def from_below(tail):
        return lax.ppermute(tail, "gx", [(i, (i + 1) % gcount) for i in range(gcount)])

    def from_above(head):
        return lax.ppermute(head, "gx", [((i + 1) % gcount, i) for i in range(gcount)])

    one_a, two_a, own_a, head, tail = load_chunk((section_one, section_two), chunks[0], True)
    far_a = to_far(own_a)
    one_b, two_b, own_b = load_chunk((after(section_one, own_a), section_two), chunks[1], False)
    far_b = to_far(own_b)
    head, tail, kernels = lax.optimization_barrier((head, tail, kernels, own_b))[:3]
    lo, hi = from_below(tail), from_above(head)
    base_a, base_b = before_first((one_a, one_b), (two_a, two_b), lo, hi, growth, chunks)
    sib_a = to_sibling(after(own_a, own_b))
    sib_b = to_sibling(own_b)
    far_a = after(far_a, base_a)
    farsib_a = to_sibling(far_a)
    part_a = early_part([own_a, sib_a, far_a], kernels)
    new_a, rounded_a, rest_a, new_head, new_tail = first_node(
        part_a, farsib_a, base_a, one_a, two_a, initial, kernels, death, chunks[0], True
    )
    nfar_a = to_far(rounded_a)
    nsib_a = to_sibling(rounded_a)

    new_lo = from_below(new_tail)
    far_b = after(far_b, rounded_a)
    farsib_b = to_sibling(far_b)
    part_b, new_one = early_part([own_b, sib_b, far_b], after(kernels, new_lo), new_a, chunks[0], xcount)
    new_b, rounded_b, rest_b = first_node(
        part_b, farsib_b, base_b, one_b, two_b, initial, kernels, death, chunks[1], False
    )
    nfar_b = to_far(rounded_b)
    nsib_b = to_sibling(rounded_b)
    new_hi = from_above(after(new_head, rounded_b))
    nfar_a = after(nfar_a, rounded_b)
    nfarsib_a = to_sibling(nfar_a)
    new_one, npart_a, nbase_a, nbase_b = before_second(
        (new_a, new_b), (rest_a, rest_b), growth, death, new_one, [rounded_a], kernels, chunks
    )
    sums_a = whole_sums(npart_a, [nsib_a, nfar_a, nfarsib_a], after(kernels, nbase_a))
    nfar_b = after(nfar_b, sums_a, new_hi)
    nfarsib_b = to_sibling(nfar_b)
    begun, npart_b = second_first(
        sums_a, nbase_a, new_a, death, new_lo, new_hi, [rounded_b, nsib_b, nfar_b], kernels, chunks[0], xcount
    )
    new_two = second_last(npart_b, nfarsib_b, nbase_b, new_b, death, kernels, begun, chunks[1], xcount)
    return new_one, new_two


def solution(mesh):
    in_specs = (
        P("gx", None, "trait"),
        P("gx", None, "trait"),
        P("gx", None, "trait"),
        P(None, None, "trait"),
        P("trait"),
        P("trait"),
    )
    out_specs = (P("gx", None, "trait"), P("gx", None, "trait"))
    return jax.shard_map(local, mesh=mesh, in_specs=in_specs, out_specs=out_specs, check_vma=False)
```

```python
import jax
import jax.numpy as jnp
from jax import lax
from jax.experimental import pallas as pl
from jax.experimental.pallas import tpu as pltpu
from jax.sharding import PartitionSpec as P

DIFFUSION = 0.25
STEP_SIZE = 0.5
FIRST = STEP_SIZE / 3.0
SECOND = 2.0 * STEP_SIZE / 3.0
F32 = jnp.float32
BF16 = jnp.bfloat16
VMEM_LIMIT = 20 * 1024 * 1024
SPEC = pl.BlockSpec(memory_space=pltpu.VMEM)
ANYWHERE = pl.BlockSpec(memory_space=pl.ANY)
FROM_HBM = pl.BlockSpec(memory_space=pltpu.HBM)


def chunks_of(xcount):
    last = max(1, 3 * xcount // 8)
    start = (xcount - last + 1) // 2
    middle = list(range(start, start + last))
    return [x for x in range(xcount) if x not in middle], middle


def after(value, *others):
    return lax.optimization_barrier((value, *others))[0]


def call(body, name, args, outs, scratch=(), specs=None, out_specs=None, gflop=0.0, alias=None):
    specs = specs or [SPEC] * len(args)
    space = {id(SPEC): pltpu.VMEM, id(FROM_HBM): pltpu.HBM}
    args = [
        pltpu.with_memory_space_constraint(a, space[id(s)]) if id(s) in space else a for a, s in zip(args, specs)
    ]
    return pl.pallas_call(
        body,
        out_shape=outs,
        in_specs=specs,
        out_specs=out_specs or [SPEC] * len(outs),
        scratch_shapes=list(scratch),
        compiler_params=pltpu.CompilerParams(vmem_limit_bytes=VMEM_LIMIT),
        cost_estimate=pl.CostEstimate(flops=int(gflop * 1e9), bytes_accessed=0, transcendentals=0),
        input_output_aliases=alias or {},
        name=name,
    )(*args)


def runs_of(cells):
    runs = []
    for i, x in enumerate(cells):
        if runs and x == sum(runs[-1][1:]):
            runs[-1][2] += 1
        else:
            runs.append([i, x, 1])
    return runs


def load_chunk(fields, cells, with_faces):
    xcount, ycount, owned = fields[0].shape
    count = len(fields)
    runs = runs_of(cells)

    def body(*refs):
        field_refs, held_refs, out_ref = refs[:count], refs[count:2 * count], refs[2 * count]
        sems = refs[-1]
        copies = {}
        for f in range(count):
            for r, (i, x, size) in enumerate(runs):
                copies[f, r] = pltpu.make_async_copy(
                    field_refs[f].at[pl.ds(x, size)], held_refs[f].at[pl.ds(i, size)], sems.at[f, r]
                )
                copies[f, r].start()
        for f in range(count):
            for r, (start, _, size) in enumerate(runs):
                copies[f, r].wait()
                for i in range(start, start + size):
                    value = held_refs[f][i].astype(BF16)
                    out_ref[f, i * ycount:(i + 1) * ycount, :] = value
                    if with_faces and cells[i] == 0:
                        refs[2 * count + 1][f] = value
                    if with_faces and cells[i] == xcount - 1:
                        refs[2 * count + 2][f] = value

    outs = [pltpu.VMEM((len(cells), ycount, owned), F32)] * count
    outs.append(pltpu.VMEM((count, len(cells) * ycount, owned), BF16))
    if with_faces:
        outs += [pltpu.VMEM((count, ycount, owned), BF16)] * 2
    return call(
        body, "load_chunk", fields, outs, scratch=[pltpu.SemaphoreType.DMA((count, len(runs)))],
        specs=[FROM_HBM] * count,
    )


def blocks_dot(blocks, kernels_ref, k, owners):
    depth = blocks[0].shape[-1]
    lhs = jnp.concatenate(blocks, axis=-1)
    rhs = jnp.concatenate(
        [kernels_ref[k, pl.ds(pl.multiple_of(o * depth, depth), depth), :] for o in owners], axis=0
    )
    return jnp.dot(lhs, rhs, preferred_element_type=F32)


def along_y(core):
    return DIFFUSION * (pltpu.roll(core, 1, 0) + pltpu.roll(core, core.shape[0] - 1, 0)) - 2.0 * core


def before_first(ones, twos, lo, hi, growth, chunks):
    _, ycount, owned = ones[0].shape
    xcount = sum(len(cells) for cells in chunks)
    count = len(chunks)
    place = {x: (c, i) for c, cells in enumerate(chunks) for i, x in enumerate(cells)}

    def body(*refs):
        lo_ref, hi_ref, g_ref, *outs = refs[2 * count:]
        growth = g_ref[...]
        for f in range(2):

            def get(x):
                c, i = place[x]
                return refs[f * count + c][i]

            for x, (c, i) in place.items():
                core = get(x)
                before = get(x - 1) if x > 0 else lo_ref[f].astype(F32)
                behind = get(x + 1) if x < xcount - 1 else hi_ref[f].astype(F32)
                outs[c][f, i] = DIFFUSION * (before + behind) + along_y(core) + core * growth

    outs = [pltpu.VMEM((2, len(cells), ycount, owned), F32) for cells in chunks]
    return call(body, "before_first", [*ones, *twos, lo, hi, growth], outs)


def early_part(blocks, kernels, new=None, cells=(), xcount=0):
    rows, owned = blocks[0].shape[0] * blocks[0].shape[1], blocks[0].shape[2]
    count = len(blocks)

    def body(*refs):
        block_refs, k_ref = refs[:count], refs[count]
        copies = []
        if new is None:
            part_ref = refs[-1]
        else:
            new_ref, part_ref, whole_ref, sems = refs[count + 1:]
            copies = [
                pltpu.make_async_copy(new_ref.at[pl.ds(i, size)], whole_ref.at[pl.ds(x, size)], sems.at[r])
                for r, (i, x, size) in enumerate(runs_of(cells))
            ]
        for copy in copies:
            copy.start()
        me = lax.axis_index("trait")
        values = [r[...].reshape(rows, owned) for r in block_refs]
        for k in range(2):
            part_ref[k] = blocks_dot(values, k_ref, k, [me ^ j for j in range(count)])
        for copy in copies:
            copy.wait()

    args = [*blocks, kernels]
    outs = [pltpu.VMEM((2, rows, owned), F32)]
    if new is None:
        return call(body, "early_part", args, outs, gflop=20.0)[0]
    outs.append(jax.ShapeDtypeStruct((xcount, *new.shape[1:]), F32))
    return call(
        body, "early_part", [*args, new], outs, scratch=[pltpu.SemaphoreType.DMA((len(runs_of(cells)),))],
        out_specs=[SPEC, ANYWHERE], gflop=20.0,
    )


def first_node(part, last, base, one, two, initial, kernels, death, cells, with_faces):
    xcount, ycount, owned = initial.shape
    rows = len(cells) * ycount

    def body(part_ref, last_ref, base_ref, one_ref, two_ref, init_ref, k_ref, d_ref, *refs):
        new_ref, rounded_ref, rest_ref = refs[:3]
        sums = refs[-1]
        me = lax.axis_index("trait")
        for k in range(2):
            far_part = blocks_dot([last_ref[...].reshape(2 * rows, owned)], k_ref, k, [me ^ 3])
            sums[k] = (part_ref[k] + far_part).astype(BF16)
        death = d_ref[...]
        inv_one = 1.0 / (1.0 + FIRST * death)
        inv_two = 1.0 / (1.0 + SECOND * death)
        for i, x in enumerate(cells):
            cores = (one_ref[i], two_ref[i])
            e = []
            for f in range(2):
                at = pl.ds(f * rows + i * ycount, ycount)
                e.append(base_ref[f, i] - cores[f] * sums[0, at, :].astype(F32) + sums[1, at, :].astype(F32))
            full_one = e[0] - death * cores[0]
            full_two = e[1] - death * cores[1]
            new = (
                init_ref[x]
                + FIRST * death * cores[0]
                + STEP_SIZE * (5.0 / 12.0 * full_one - 1.0 / 12.0 * full_two)
            ) * inv_one
            new_ref[i] = new
            rounded = new.astype(BF16)
            rounded_ref[0, i * ycount:(i + 1) * ycount, :] = rounded
            if with_faces and x == 0:
                refs[3][0] = rounded
            if with_faces and x == xcount - 1:
                refs[4][0] = rounded
            rest_ref[i] = (
                new - SECOND * e[0] + SECOND * death * cores[1] + STEP_SIZE / 3.0 * (full_one + full_two)
            ) * inv_two

    outs = [
        pltpu.VMEM((len(cells), ycount, owned), F32),
        pltpu.VMEM((1, rows, owned), BF16),
        pltpu.VMEM((len(cells), ycount, owned), F32),
    ]
    if with_faces:
        outs += [pltpu.VMEM((1, ycount, owned), BF16)] * 2
    args = [part, last, base, one, two, initial, kernels, death]
    return call(
        body, "first_node", args, outs, scratch=[pltpu.VMEM((2, 2 * rows, owned), BF16)],
        gflop=0.0,
    )


def before_second(news, rests, growth, death, begun, blocks, kernels, chunks):
    _, ycount, owned = news[0].shape
    rows = blocks[0].shape[1]
    xcount = sum(len(cells) for cells in chunks)
    count = len(chunks)
    size = len(blocks)
    place = {x: (c, i) for c, cells in enumerate(chunks) for i, x in enumerate(cells)}

    def body(*refs):
        new_refs, rest_refs, block_refs = refs[:count], refs[count:2 * count], refs[2 * count:2 * count + size]
        k_ref, g_ref, d_ref, _, whole_ref, part_ref = refs[2 * count + size:2 * count + size + 6]
        base_refs, sems = refs[2 * count + size + 6:-1], refs[-1]
        copies = [
            pltpu.make_async_copy(new_refs[-1].at[pl.ds(i, size)], whole_ref.at[pl.ds(x, size)], sems.at[r])
            for r, (i, x, size) in enumerate(runs_of(chunks[-1]))
        ]
        for copy in copies:
            copy.start()
        me = lax.axis_index("trait")
        values = [r[...].reshape(rows, owned) for r in block_refs]
        for k in range(2):
            part_ref[k] = blocks_dot(values, k_ref, k, [me ^ j for j in range(size)])
        growth = g_ref[...]
        factor = SECOND / (1.0 + SECOND * d_ref[...])
        for x, (c, i) in place.items():
            core = new_refs[c][i]
            e = along_y(core) + core * growth
            for near in (x - 1, x + 1):
                if near in place:
                    e = e + DIFFUSION * new_refs[place[near][0]][place[near][1]]
            base_refs[c][i] = rest_refs[c][i] + factor * e
        for copy in copies:
            copy.wait()

    outs = [jax.ShapeDtypeStruct((xcount, ycount, owned), F32), pltpu.VMEM((2, rows, owned), F32)]
    outs += [pltpu.VMEM((len(cells), ycount, owned), F32) for cells in chunks]
    args = [*news, *rests, *blocks, kernels, growth, death, begun]
    return call(
        body, "before_second", args, outs, scratch=[pltpu.SemaphoreType.DMA((len(runs_of(chunks[-1])),))],
        specs=[SPEC] * (len(args) - 1) + [FROM_HBM], out_specs=[ANYWHERE] + [SPEC] * (len(outs) - 1), gflop=20.0,
        alias={len(args) - 1: 0},
    )


def whole_sums(part, last, kernels):
    rows, owned = last.shape[1:]

    def body(part_ref, last_ref, k_ref, sums_ref):
        me = lax.axis_index("trait")
        for k in range(2):
            last_part = blocks_dot([last_ref[...].reshape(rows, owned)], k_ref, k, [me ^ 3])
            sums_ref[k] = (part_ref[k] + last_part).astype(BF16)

    return call(body, "whole_sums", [part, last, kernels], [pltpu.VMEM((2, rows, owned), BF16)])[0]


def finish(cells, pieces, ycount, sums, base_ref, new_ref, factor, faces, held, out_ref, sems):
    copies = []
    size = ycount // pieces
    for i, x in enumerate(cells):
        for p in range(pieces):
            rows = pl.ds(p * size, size)
            at = pl.ds(i * ycount + p * size, size)
            e = sums[1, at, :].astype(F32) - new_ref[i, rows, :] * sums[0, at, :].astype(F32)
            if x in faces:
                e = e + DIFFUSION * faces[x][0, rows, :].astype(F32)
            held[i, rows, :] = base_ref[i, rows, :] + factor * e
            copies.append(
                pltpu.make_async_copy(held.at[i, rows], out_ref.at[x, rows], sems.at[i * pieces + p])
            )
            copies[-1].start()
    return copies


def second_first(sums, base, new, death, lo, hi, blocks, kernels, cells, xcount):
    _, ycount, owned = new.shape
    rows = blocks[0].shape[1]
    count = len(blocks)

    def body(sums_ref, base_ref, new_ref, d_ref, lo_ref, hi_ref, k_ref, *refs):
        block_refs = refs[:count]
        out_ref, part_ref, held, sems = refs[count:]
        factor = SECOND / (1.0 + SECOND * d_ref[...])
        faces = {0: lo_ref, xcount - 1: hi_ref}
        copies = finish(cells, 1, ycount, sums_ref, base_ref, new_ref, factor, faces, held, out_ref, sems)
        me = lax.axis_index("trait")
        values = [r[...].reshape(rows, owned) for r in block_refs]
        for k in range(2):
            part_ref[k] = blocks_dot(values, k_ref, k, [me ^ j for j in range(count)])
        for copy in copies:
            copy.wait()

    return call(
        body, "second_first", [sums, base, new, death, lo, hi, kernels, *blocks],
        [jax.ShapeDtypeStruct((xcount, ycount, owned), F32), pltpu.VMEM((2, rows, owned), F32)],
        scratch=[pltpu.VMEM((len(cells), ycount, owned), F32), pltpu.SemaphoreType.DMA((len(cells),))],
        out_specs=[ANYWHERE, SPEC],
    )


def second_last(part, last, base, new, death, kernels, begun, cells, xcount):
    _, ycount, owned = new.shape
    rows = len(cells) * ycount

    def body(part_ref, last_ref, base_ref, new_ref, d_ref, k_ref, begun_ref, out_ref, sums, held, sems):
        me = lax.axis_index("trait")
        for k in range(2):
            sums[k] = (part_ref[k] + blocks_dot([last_ref[...].reshape(rows, owned)], k_ref, k, [me ^ 3])).astype(BF16)
        factor = SECOND / (1.0 + SECOND * d_ref[...])
        for copy in finish(cells, 2, ycount, sums, base_ref, new_ref, factor, {}, held, out_ref, sems):
            copy.wait()

    return call(
        body, "second_last", [part, last, base, new, death, kernels, begun],
        [jax.ShapeDtypeStruct((xcount, ycount, owned), F32)],
        scratch=[
            pltpu.VMEM((2, rows, owned), BF16),
            pltpu.VMEM((len(cells), ycount, owned), F32),
            pltpu.SemaphoreType.DMA((2 * len(cells),)),
        ],
        specs=[SPEC] * 6 + [FROM_HBM], out_specs=[ANYWHERE], alias={6: 0},
    )[0]


def local(initial, section_one, section_two, kernels, growth, death_rate):
    xcount, ycount, owned = section_one.shape
    traits = lax.axis_size("trait")
    gcount = lax.axis_size("gx")
    growth = growth.reshape(1, owned)
    death = death_rate.reshape(1, owned)
    chunks = chunks_of(xcount)

    def to_sibling(v):
        return lax.ppermute(v, "trait", [(i, i ^ 1) for i in range(traits)])

    def to_far(v):
        return lax.ppermute(v, "trait", [(i, i ^ 2) for i in range(traits)])

    def from_below(tail):
        return lax.ppermute(tail, "gx", [(i, (i + 1) % gcount) for i in range(gcount)])

    def from_above(head):
        return lax.ppermute(head, "gx", [((i + 1) % gcount, i) for i in range(gcount)])

    one_a, two_a, own_a, head, tail = load_chunk((section_one, section_two), chunks[0], True)
    far_a = to_far(own_a)
    one_b, two_b, own_b = load_chunk((after(section_one, own_a), section_two), chunks[1], False)
    far_b = to_far(own_b)
    head, tail, kernels = lax.optimization_barrier((head, tail, kernels, own_b))[:3]
    lo, hi = from_below(tail), from_above(head)
    base_a, base_b = before_first((one_a, one_b), (two_a, two_b), lo, hi, growth, chunks)
    sib_a = to_sibling(after(own_a, own_b))
    sib_b = to_sibling(own_b)
    far_a = after(far_a, base_a)
    farsib_a = to_sibling(far_a)
    part_a = early_part([own_a, sib_a, far_a], kernels)
    new_a, rounded_a, rest_a, new_head, new_tail = first_node(
        part_a, farsib_a, base_a, one_a, two_a, initial, kernels, death, chunks[0], True
    )
    nfar_a = to_far(rounded_a)
    nsib_a = to_sibling(rounded_a)

    new_lo = from_below(new_tail)
    far_b = after(far_b, rounded_a)
    farsib_b = to_sibling(far_b)
    part_b, new_one = early_part([own_b, sib_b, far_b], after(kernels, new_lo), new_a, chunks[0], xcount)
    new_b, rounded_b, rest_b = first_node(
        part_b, farsib_b, base_b, one_b, two_b, initial, kernels, death, chunks[1], False
    )
    nfar_b = to_far(rounded_b)
    nsib_b = to_sibling(rounded_b)
    new_hi = from_above(after(new_head, rounded_b))
    nfar_a = after(nfar_a, rounded_b)
    nfarsib_a = to_sibling(nfar_a)
    new_one, npart_a, nbase_a, nbase_b = before_second(
        (new_a, new_b), (rest_a, rest_b), growth, death, new_one, [rounded_a, nsib_a, nfar_a], kernels, chunks
    )
    sums_a = whole_sums(npart_a, nfarsib_a, after(kernels, nbase_a))
    nfar_b = after(nfar_b, sums_a, new_hi)
    nfarsib_b = to_sibling(nfar_b)
    begun, npart_b = second_first(
        sums_a, nbase_a, new_a, death, new_lo, new_hi, [rounded_b, nsib_b, nfar_b], kernels, chunks[0], xcount
    )
    new_two = second_last(npart_b, nfarsib_b, nbase_b, new_b, death, kernels, begun, chunks[1], xcount)
    return new_one, new_two


def solution(mesh):
    in_specs = (
        P("gx", None, "trait"),
        P("gx", None, "trait"),
        P("gx", None, "trait"),
        P(None, None, "trait"),
        P("trait"),
        P("trait"),
    )
    out_specs = (P("gx", None, "trait"), P("gx", None, "trait"))
    return jax.shard_map(local, mesh=mesh, in_specs=in_specs, out_specs=out_specs, check_vma=False)
```

```python
import jax
import jax.numpy as jnp
from jax import lax
from jax.experimental import pallas as pl
from jax.experimental.pallas import tpu as pltpu
from jax.sharding import PartitionSpec as P

DIFFUSION = 0.25
STEP_SIZE = 0.5
FIRST = STEP_SIZE / 3.0
SECOND = 2.0 * STEP_SIZE / 3.0
F32 = jnp.float32
BF16 = jnp.bfloat16
VMEM_LIMIT = 20 * 1024 * 1024
SPEC = pl.BlockSpec(memory_space=pltpu.VMEM)
ANYWHERE = pl.BlockSpec(memory_space=pl.ANY)
FROM_HBM = pl.BlockSpec(memory_space=pltpu.HBM)


def chunks_of(xcount):
    last = max(1, 3 * xcount // 8)
    start = (xcount - last + 1) // 2
    middle = list(range(start, start + last))
    return [x for x in range(xcount) if x not in middle], middle


def after(value, *others):
    return lax.optimization_barrier((value, *others))[0]


def call(body, name, args, outs, scratch=(), specs=None, out_specs=None, gflop=0.0, alias=None):
    specs = specs or [SPEC] * len(args)
    space = {id(SPEC): pltpu.VMEM, id(FROM_HBM): pltpu.HBM}
    args = [
        pltpu.with_memory_space_constraint(a, space[id(s)]) if id(s) in space else a for a, s in zip(args, specs)
    ]
    return pl.pallas_call(
        body,
        out_shape=outs,
        in_specs=specs,
        out_specs=out_specs or [SPEC] * len(outs),
        scratch_shapes=list(scratch),
        compiler_params=pltpu.CompilerParams(vmem_limit_bytes=VMEM_LIMIT),
        cost_estimate=pl.CostEstimate(flops=int(gflop * 1e9), bytes_accessed=0, transcendentals=0),
        input_output_aliases=alias or {},
        name=name,
    )(*args)


def runs_of(cells):
    runs = []
    for i, x in enumerate(cells):
        if runs and x == sum(runs[-1][1:]):
            runs[-1][2] += 1
        else:
            runs.append([i, x, 1])
    return runs


def load_chunk(fields, cells, with_faces):
    xcount, ycount, owned = fields[0].shape
    count = len(fields)
    runs = runs_of(cells)

    def body(*refs):
        field_refs, held_refs, out_ref = refs[:count], refs[count:2 * count], refs[2 * count]
        sems = refs[-1]
        copies = {}
        for f in range(count):
            for r, (i, x, size) in enumerate(runs):
                copies[f, r] = pltpu.make_async_copy(
                    field_refs[f].at[pl.ds(x, size)], held_refs[f].at[pl.ds(i, size)], sems.at[f, r]
                )
                copies[f, r].start()
        for f in range(count):
            for r, (start, _, size) in enumerate(runs):
                copies[f, r].wait()
                for i in range(start, start + size):
                    value = held_refs[f][i].astype(BF16)
                    out_ref[f, i * ycount:(i + 1) * ycount, :] = value
                    if with_faces and cells[i] == 0:
                        refs[2 * count + 1][f] = value
                    if with_faces and cells[i] == xcount - 1:
                        refs[2 * count + 2][f] = value

    outs = [pltpu.VMEM((len(cells), ycount, owned), F32)] * count
    outs.append(pltpu.VMEM((count, len(cells) * ycount, owned), BF16))
    if with_faces:
        outs += [pltpu.VMEM((count, ycount, owned), BF16)] * 2
    return call(
        body, "load_chunk", fields, outs, scratch=[pltpu.SemaphoreType.DMA((count, len(runs)))],
        specs=[FROM_HBM] * count,
    )


def blocks_dot(blocks, kernels_ref, k, owners):
    depth = blocks[0].shape[-1]
    lhs = jnp.concatenate(blocks, axis=-1)
    rhs = jnp.concatenate(
        [kernels_ref[k, pl.ds(pl.multiple_of(o * depth, depth), depth), :] for o in owners], axis=0
    )
    return jnp.dot(lhs, rhs, preferred_element_type=F32)


def along_y(core):
    return DIFFUSION * (pltpu.roll(core, 1, 0) + pltpu.roll(core, core.shape[0] - 1, 0)) - 2.0 * core


def before_first(ones, twos, lo, hi, growth, chunks):
    _, ycount, owned = ones[0].shape
    xcount = sum(len(cells) for cells in chunks)
    count = len(chunks)
    place = {x: (c, i) for c, cells in enumerate(chunks) for i, x in enumerate(cells)}

    def body(*refs):
        lo_ref, hi_ref, g_ref, *outs = refs[2 * count:]
        growth = g_ref[...]
        for f in range(2):

            def get(x):
                c, i = place[x]
                return refs[f * count + c][i]

            for x, (c, i) in place.items():
                core = get(x)
                before = get(x - 1) if x > 0 else lo_ref[f].astype(F32)
                behind = get(x + 1) if x < xcount - 1 else hi_ref[f].astype(F32)
                outs[c][f, i] = DIFFUSION * (before + behind) + along_y(core) + core * growth

    outs = [pltpu.VMEM((2, len(cells), ycount, owned), F32) for cells in chunks]
    return call(body, "before_first", [*ones, *twos, lo, hi, growth], outs)


def early_part(blocks, base, one, two, initial, kernels, death, cells, new=None, new_cells=()):
    xcount, ycount, owned = initial.shape
    rows = len(cells) * ycount
    count = len(blocks)

    def body(*refs):
        block_refs = refs[:count]
        base_ref, one_ref, two_ref, init_ref, k_ref, d_ref, *refs = refs[count:]
        copies = []
        if new is not None:
            new_ref, whole_ref, sems = refs[0], refs[-2], refs[-1]
            copies = [
                pltpu.make_async_copy(new_ref.at[pl.ds(i, size)], whole_ref.at[pl.ds(x, size)], sems.at[r])
                for r, (i, x, size) in enumerate(runs_of(new_cells))
            ]
        for copy in copies:
            copy.start()
        first_ref, rest_ref = refs[:2] if new is None else refs[1:3]
        me = lax.axis_index("trait")
        values = [r[...].reshape(2 * rows, owned) for r in block_refs]
        compete, mutate = (blocks_dot(values, k_ref, k, [me ^ j for j in range(count)]) for k in range(2))
        death = d_ref[...]
        inv_one = 1.0 / (1.0 + FIRST * death)
        inv_two = 1.0 / (1.0 + SECOND * death)
        for i, x in enumerate(cells):
            cores = (one_ref[i], two_ref[i])
            e = []
            for f in range(2):
                at = slice(f * rows + i * ycount, f * rows + (i + 1) * ycount)
                e.append(base_ref[f, i] - cores[f] * compete[at] + mutate[at])
            full_one = e[0] - death * cores[0]
            full_two = e[1] - death * cores[1]
            first = (
                init_ref[x]
                + FIRST * death * cores[0]
                + STEP_SIZE * (5.0 / 12.0 * full_one - 1.0 / 12.0 * full_two)
            ) * inv_one
            first_ref[i] = first
            rest_ref[i] = (
                first - SECOND * e[0] + SECOND * death * cores[1] + STEP_SIZE / 3.0 * (full_one + full_two)
            ) * inv_two
        for copy in copies:
            copy.wait()

    args = [*blocks, base, one, two, initial, kernels, death]
    outs = [pltpu.VMEM((len(cells), ycount, owned), F32)] * 2
    if new is None:
        return call(body, "early_part", args, outs, gflop=20.0)
    outs.append(jax.ShapeDtypeStruct((xcount, ycount, owned), F32))
    return call(
        body, "early_part", [*args, new], outs, scratch=[pltpu.SemaphoreType.DMA((len(runs_of(new_cells)),))],
        out_specs=[SPEC, SPEC, ANYWHERE], gflop=20.0,
    )


def first_node(first, rest, last, one, two, kernels, death, cells, xcount, with_faces):
    _, ycount, owned = one.shape
    rows = len(cells) * ycount

    def body(first_ref, begun_ref, last_ref, one_ref, two_ref, k_ref, d_ref, new_ref, rounded_ref, rest_ref, *face_refs):
        me = lax.axis_index("trait")
        values = [last_ref[...].reshape(2 * rows, owned)]
        compete, mutate = (blocks_dot(values, k_ref, k, [me ^ 3]) for k in range(2))
        inv_one = STEP_SIZE / (1.0 + FIRST * d_ref[...])
        inv_two = 1.0 / (1.0 + SECOND * d_ref[...])
        for i, x in enumerate(cells):
            e = []
            for f, ref in enumerate((one_ref, two_ref)):
                at = slice(f * rows + i * ycount, f * rows + (i + 1) * ycount)
                e.append(mutate[at] - ref[i] * compete[at])
            more = (5.0 / 12.0 * e[0] - 1.0 / 12.0 * e[1]) * inv_one
            new = first_ref[i] + more
            new_ref[i] = new
            rounded = new.astype(BF16)
            rounded_ref[0, i * ycount:(i + 1) * ycount, :] = rounded
            if with_faces and x == 0:
                face_refs[0][0] = rounded
            if with_faces and x == xcount - 1:
                face_refs[1][0] = rounded
            rest_ref[i] = begun_ref[i] + (more - SECOND * e[0] + STEP_SIZE / 3.0 * (e[0] + e[1])) * inv_two

    outs = [
        pltpu.VMEM((len(cells), ycount, owned), F32),
        pltpu.VMEM((1, rows, owned), BF16),
        pltpu.VMEM((len(cells), ycount, owned), F32),
    ]
    if with_faces:
        outs += [pltpu.VMEM((1, ycount, owned), BF16)] * 2
    return call(body, "first_node", [first, rest, last, one, two, kernels, death], outs)


def before_second(news, rests, growth, death, begun, blocks, kernels, chunks):
    _, ycount, owned = news[0].shape
    rows = blocks[0].shape[1]
    xcount = sum(len(cells) for cells in chunks)
    count = len(chunks)
    size = len(blocks)
    place = {x: (c, i) for c, cells in enumerate(chunks) for i, x in enumerate(cells)}

    def body(*refs):
        new_refs, rest_refs, block_refs = refs[:count], refs[count:2 * count], refs[2 * count:2 * count + size]
        k_ref, g_ref, d_ref, _, whole_ref, part_ref = refs[2 * count + size:2 * count + size + 6]
        base_refs, sems = refs[2 * count + size + 6:-1], refs[-1]
        copies = [
            pltpu.make_async_copy(new_refs[-1].at[pl.ds(i, size)], whole_ref.at[pl.ds(x, size)], sems.at[r])
            for r, (i, x, size) in enumerate(runs_of(chunks[-1]))
        ]
        for copy in copies:
            copy.start()
        me = lax.axis_index("trait")
        values = [r[...].reshape(rows, owned) for r in block_refs]
        for k in range(2):
            part_ref[k] = blocks_dot(values, k_ref, k, [me ^ j for j in range(size)])
        growth = g_ref[...]
        factor = SECOND / (1.0 + SECOND * d_ref[...])
        for x, (c, i) in place.items():
            core = new_refs[c][i]
            e = along_y(core) + core * growth
            for near in (x - 1, x + 1):
                if near in place:
                    e = e + DIFFUSION * new_refs[place[near][0]][place[near][1]]
            base_refs[c][i] = rest_refs[c][i] + factor * e
        for copy in copies:
            copy.wait()

    outs = [jax.ShapeDtypeStruct((xcount, ycount, owned), F32), pltpu.VMEM((2, rows, owned), F32)]
    outs += [pltpu.VMEM((len(cells), ycount, owned), F32) for cells in chunks]
    args = [*news, *rests, *blocks, kernels, growth, death, begun]
    return call(
        body, "before_second", args, outs, scratch=[pltpu.SemaphoreType.DMA((len(runs_of(chunks[-1])),))],
        specs=[SPEC] * (len(args) - 1) + [FROM_HBM], out_specs=[ANYWHERE] + [SPEC] * (len(outs) - 1), gflop=20.0,
        alias={len(args) - 1: 0},
    )


def whole_sums(part, last, kernels):
    rows, owned = last.shape[1:]

    def body(part_ref, last_ref, k_ref, sums_ref):
        me = lax.axis_index("trait")
        for k in range(2):
            last_part = blocks_dot([last_ref[...].reshape(rows, owned)], k_ref, k, [me ^ 3])
            sums_ref[k] = (part_ref[k] + last_part).astype(BF16)

    return call(body, "whole_sums", [part, last, kernels], [pltpu.VMEM((2, rows, owned), BF16)])[0]


def finish(cells, pieces, ycount, sums, base_ref, new_ref, factor, faces, held, out_ref, sems):
    copies = []
    size = ycount // pieces
    for i, x in enumerate(cells):
        for p in range(pieces):
            rows = pl.ds(p * size, size)
            at = pl.ds(i * ycount + p * size, size)
            e = sums[1, at, :].astype(F32) - new_ref[i, rows, :] * sums[0, at, :].astype(F32)
            if x in faces:
                e = e + DIFFUSION * faces[x][0, rows, :].astype(F32)
            held[i, rows, :] = base_ref[i, rows, :] + factor * e
            copies.append(
                pltpu.make_async_copy(held.at[i, rows], out_ref.at[x, rows], sems.at[i * pieces + p])
            )
            copies[-1].start()
    return copies


def second_first(sums, base, new, death, lo, hi, blocks, kernels, cells, xcount):
    _, ycount, owned = new.shape
    rows = blocks[0].shape[1]
    count = len(blocks)

    def body(sums_ref, base_ref, new_ref, d_ref, lo_ref, hi_ref, k_ref, *refs):
        block_refs = refs[:count]
        out_ref, part_ref, held, sems = refs[count:]
        factor = SECOND / (1.0 + SECOND * d_ref[...])
        faces = {0: lo_ref, xcount - 1: hi_ref}
        copies = finish(cells, 1, ycount, sums_ref, base_ref, new_ref, factor, faces, held, out_ref, sems)
        me = lax.axis_index("trait")
        values = [r[...].reshape(rows, owned) for r in block_refs]
        for k in range(2):
            part_ref[k] = blocks_dot(values, k_ref, k, [me ^ j for j in range(count)])
        for copy in copies:
            copy.wait()

    return call(
        body, "second_first", [sums, base, new, death, lo, hi, kernels, *blocks],
        [jax.ShapeDtypeStruct((xcount, ycount, owned), F32), pltpu.VMEM((2, rows, owned), F32)],
        scratch=[pltpu.VMEM((len(cells), ycount, owned), F32), pltpu.SemaphoreType.DMA((len(cells),))],
        out_specs=[ANYWHERE, SPEC],
    )


def second_last(part, last, base, new, death, kernels, begun, cells, xcount):
    _, ycount, owned = new.shape
    rows = len(cells) * ycount

    def body(part_ref, last_ref, base_ref, new_ref, d_ref, k_ref, begun_ref, out_ref, sums, held, sems):
        me = lax.axis_index("trait")
        for k in range(2):
            sums[k] = (part_ref[k] + blocks_dot([last_ref[...].reshape(rows, owned)], k_ref, k, [me ^ 3])).astype(BF16)
        factor = SECOND / (1.0 + SECOND * d_ref[...])
        for copy in finish(cells, 2, ycount, sums, base_ref, new_ref, factor, {}, held, out_ref, sems):
            copy.wait()

    return call(
        body, "second_last", [part, last, base, new, death, kernels, begun],
        [jax.ShapeDtypeStruct((xcount, ycount, owned), F32)],
        scratch=[
            pltpu.VMEM((2, rows, owned), BF16),
            pltpu.VMEM((len(cells), ycount, owned), F32),
            pltpu.SemaphoreType.DMA((2 * len(cells),)),
        ],
        specs=[SPEC] * 6 + [FROM_HBM], out_specs=[ANYWHERE], alias={6: 0},
    )[0]


def local(initial, section_one, section_two, kernels, growth, death_rate):
    xcount, ycount, owned = section_one.shape
    traits = lax.axis_size("trait")
    gcount = lax.axis_size("gx")
    growth = growth.reshape(1, owned)
    death = death_rate.reshape(1, owned)
    chunks = chunks_of(xcount)

    def to_sibling(v):
        return lax.ppermute(v, "trait", [(i, i ^ 1) for i in range(traits)])

    def to_far(v):
        return lax.ppermute(v, "trait", [(i, i ^ 2) for i in range(traits)])

    def from_below(tail):
        return lax.ppermute(tail, "gx", [(i, (i + 1) % gcount) for i in range(gcount)])

    def from_above(head):
        return lax.ppermute(head, "gx", [((i + 1) % gcount, i) for i in range(gcount)])

    one_a, two_a, own_a, head, tail = load_chunk((section_one, section_two), chunks[0], True)
    far_a = to_far(own_a)
    one_b, two_b, own_b = load_chunk((after(section_one, own_a), section_two), chunks[1], False)
    far_b = to_far(own_b)
    head, tail, kernels = lax.optimization_barrier((head, tail, kernels, own_b))[:3]
    lo, hi = from_below(tail), from_above(head)
    base_a, base_b = before_first((one_a, one_b), (two_a, two_b), lo, hi, growth, chunks)
    sib_a = to_sibling(after(own_a, own_b))
    sib_b = to_sibling(own_b)
    far_a = after(far_a, base_a)
    farsib_a = to_sibling(far_a)
    first_a, rest_a = early_part([own_a, sib_a, far_a], base_a, one_a, two_a, initial, kernels, death, chunks[0])
    new_a, rounded_a, rest_a, new_head, new_tail = first_node(
        first_a, rest_a, farsib_a, one_a, two_a, kernels, death, chunks[0], xcount, True
    )
    nfar_a = to_far(rounded_a)
    nsib_a = to_sibling(rounded_a)

    new_lo = from_below(new_tail)
    far_b = after(far_b, rounded_a)
    farsib_b = to_sibling(far_b)
    first_b, rest_b, new_one = early_part(
        [own_b, sib_b, far_b], base_b, one_b, two_b, initial, after(kernels, new_lo), death, chunks[1], new_a, chunks[0]
    )
    new_b, rounded_b, rest_b = first_node(
        first_b, rest_b, farsib_b, one_b, two_b, kernels, death, chunks[1], xcount, False
    )
    nfar_b = to_far(rounded_b)
    nsib_b = to_sibling(rounded_b)
    new_hi = from_above(after(new_head, rounded_b))
    nfar_a = after(nfar_a, rounded_b)
    nfarsib_a = to_sibling(nfar_a)
    new_one, npart_a, nbase_a, nbase_b = before_second(
        (new_a, new_b), (rest_a, rest_b), growth, death, new_one, [rounded_a, nsib_a, nfar_a], kernels, chunks
    )
    sums_a = whole_sums(npart_a, nfarsib_a, after(kernels, nbase_a))
    nfar_b = after(nfar_b, sums_a, new_hi)
    nfarsib_b = to_sibling(nfar_b)
    begun, npart_b = second_first(
        sums_a, nbase_a, new_a, death, new_lo, new_hi, [rounded_b, nsib_b, nfar_b], kernels, chunks[0], xcount
    )
    new_two = second_last(npart_b, nfarsib_b, nbase_b, new_b, death, kernels, begun, chunks[1], xcount)
    return new_one, new_two


def solution(mesh):
    in_specs = (
        P("gx", None, "trait"),
        P("gx", None, "trait"),
        P("gx", None, "trait"),
        P(None, None, "trait"),
        P("trait"),
        P("trait"),
    )
    out_specs = (P("gx", None, "trait"), P("gx", None, "trait"))
    return jax.shard_map(local, mesh=mesh, in_specs=in_specs, out_specs=out_specs, check_vma=False)
```

```python
import jax
import jax.numpy as jnp
from jax import lax
from jax.experimental import pallas as pl
from jax.experimental.pallas import tpu as pltpu
from jax.sharding import PartitionSpec as P

DIFFUSION = 0.25
STEP_SIZE = 0.5
FIRST = STEP_SIZE / 3.0
SECOND = 2.0 * STEP_SIZE / 3.0
F32 = jnp.float32
BF16 = jnp.bfloat16
VMEM_LIMIT = 20 * 1024 * 1024
SPEC = pl.BlockSpec(memory_space=pltpu.VMEM)
ANYWHERE = pl.BlockSpec(memory_space=pl.ANY)
FROM_HBM = pl.BlockSpec(memory_space=pltpu.HBM)


def chunks_of(xcount):
    last = max(1, 3 * xcount // 8)
    start = (xcount - last + 1) // 2
    middle = list(range(start, start + last))
    return [x for x in range(xcount) if x not in middle], middle


def after(value, *others):
    return lax.optimization_barrier((value, *others))[0]


def call(body, name, args, outs, scratch=(), specs=None, out_specs=None, gflop=0.0, alias=None):
    specs = specs or [SPEC] * len(args)
    space = {id(SPEC): pltpu.VMEM, id(FROM_HBM): pltpu.HBM}
    args = [
        pltpu.with_memory_space_constraint(a, space[id(s)]) if id(s) in space else a for a, s in zip(args, specs)
    ]
    return pl.pallas_call(
        body,
        out_shape=outs,
        in_specs=specs,
        out_specs=out_specs or [SPEC] * len(outs),
        scratch_shapes=list(scratch),
        compiler_params=pltpu.CompilerParams(vmem_limit_bytes=VMEM_LIMIT),
        cost_estimate=pl.CostEstimate(flops=int(gflop * 1e9), bytes_accessed=0, transcendentals=0),
        input_output_aliases=alias or {},
        name=name,
    )(*args)


def runs_of(cells):
    runs = []
    for i, x in enumerate(cells):
        if runs and x == sum(runs[-1][1:]):
            runs[-1][2] += 1
        else:
            runs.append([i, x, 1])
    return runs


def load_chunk(fields, cells, with_faces):
    xcount, ycount, owned = fields[0].shape
    count = len(fields)
    runs = runs_of(cells)

    def body(*refs):
        field_refs, held_refs, out_ref = refs[:count], refs[count:2 * count], refs[2 * count]
        sems = refs[-1]
        copies = {}
        for f in range(count):
            for r, (i, x, size) in enumerate(runs):
                copies[f, r] = pltpu.make_async_copy(
                    field_refs[f].at[pl.ds(x, size)], held_refs[f].at[pl.ds(i, size)], sems.at[f, r]
                )
                copies[f, r].start()
        for f in range(count):
            for r, (start, _, size) in enumerate(runs):
                copies[f, r].wait()
                for i in range(start, start + size):
                    value = held_refs[f][i].astype(BF16)
                    out_ref[f, i * ycount:(i + 1) * ycount, :] = value
                    if with_faces and cells[i] == 0:
                        refs[2 * count + 1][f] = value
                    if with_faces and cells[i] == xcount - 1:
                        refs[2 * count + 2][f] = value

    outs = [pltpu.VMEM((len(cells), ycount, owned), F32)] * count
    outs.append(pltpu.VMEM((count, len(cells) * ycount, owned), BF16))
    if with_faces:
        outs += [pltpu.VMEM((count, ycount, owned), BF16)] * 2
    return call(
        body, "load_chunk", fields, outs, scratch=[pltpu.SemaphoreType.DMA((count, len(runs)))],
        specs=[FROM_HBM] * count,
    )


def blocks_dot(blocks, kernels_ref, k, owners):
    depth = blocks[0].shape[-1]
    lhs = jnp.concatenate(blocks, axis=-1)
    rhs = jnp.concatenate(
        [kernels_ref[k, pl.ds(pl.multiple_of(o * depth, depth), depth), :] for o in owners], axis=0
    )
    return jnp.dot(lhs, rhs, preferred_element_type=F32)


def along_y(core):
    return DIFFUSION * (pltpu.roll(core, 1, 0) + pltpu.roll(core, core.shape[0] - 1, 0)) - 2.0 * core


def before_first(ones, twos, lo, hi, growth, chunks):
    _, ycount, owned = ones[0].shape
    xcount = sum(len(cells) for cells in chunks)
    count = len(chunks)
    place = {x: (c, i) for c, cells in enumerate(chunks) for i, x in enumerate(cells)}

    def body(*refs):
        lo_ref, hi_ref, g_ref, *outs = refs[2 * count:]
        growth = g_ref[...]
        for f in range(2):

            def get(x):
                c, i = place[x]
                return refs[f * count + c][i]

            for x, (c, i) in place.items():
                core = get(x)
                before = get(x - 1) if x > 0 else lo_ref[f].astype(F32)
                behind = get(x + 1) if x < xcount - 1 else hi_ref[f].astype(F32)
                outs[c][f, i] = DIFFUSION * (before + behind) + along_y(core) + core * growth

    outs = [pltpu.VMEM((2, len(cells), ycount, owned), F32) for cells in chunks]
    return call(body, "before_first", [*ones, *twos, lo, hi, growth], outs)


def early_part(blocks, base, one, two, initial, kernels, death, cells, new=None, new_cells=()):
    xcount, ycount, owned = initial.shape
    rows = len(cells) * ycount
    count = len(blocks)

    def body(*refs):
        block_refs = refs[:count]
        base_ref, one_ref, two_ref, init_ref, k_ref, d_ref, *refs = refs[count:]
        copies = []
        if new is not None:
            new_ref, whole_ref, sems = refs[0], refs[-2], refs[-1]
            copies = [
                pltpu.make_async_copy(new_ref.at[pl.ds(i, size)], whole_ref.at[pl.ds(x, size)], sems.at[r])
                for r, (i, x, size) in enumerate(runs_of(new_cells))
            ]
        for copy in copies:
            copy.start()
        part_ref, first_ref, rest_ref = refs[:3] if new is None else refs[1:4]
        me = lax.axis_index("trait")
        values = [r[...].reshape(2 * rows, owned) for r in block_refs]
        for k in range(2):
            part_ref[k] = blocks_dot(values, k_ref, k, [me ^ j for j in range(count)])
        death = d_ref[...]
        inv_one = 1.0 / (1.0 + FIRST * death)
        inv_two = 1.0 / (1.0 + SECOND * death)
        for i, x in enumerate(cells):
            cores = (one_ref[i], two_ref[i])
            e = (base_ref[0, i], base_ref[1, i])
            full_one = e[0] - death * cores[0]
            full_two = e[1] - death * cores[1]
            first = (
                init_ref[x]
                + FIRST * death * cores[0]
                + STEP_SIZE * (5.0 / 12.0 * full_one - 1.0 / 12.0 * full_two)
            ) * inv_one
            first_ref[i] = first
            rest_ref[i] = (
                first - SECOND * e[0] + SECOND * death * cores[1] + STEP_SIZE / 3.0 * (full_one + full_two)
            ) * inv_two
        for copy in copies:
            copy.wait()

    args = [*blocks, base, one, two, initial, kernels, death]
    outs = [pltpu.VMEM((2, 2 * rows, owned), F32)] + [pltpu.VMEM((len(cells), ycount, owned), F32)] * 2
    if new is None:
        return call(body, "early_part", args, outs, gflop=20.0)
    outs.append(jax.ShapeDtypeStruct((xcount, ycount, owned), F32))
    return call(
        body, "early_part", [*args, new], outs, scratch=[pltpu.SemaphoreType.DMA((len(runs_of(new_cells)),))],
        out_specs=[SPEC, SPEC, SPEC, ANYWHERE], gflop=20.0,
    )


def first_node(part, first, rest, last, one, two, kernels, death, cells, xcount, with_faces):
    _, ycount, owned = one.shape
    rows = len(cells) * ycount

    def body(part_ref, first_ref, begun_ref, last_ref, one_ref, two_ref, k_ref, d_ref, *outs):
        new_ref, rounded_ref, rest_ref, *face_refs = outs
        me = lax.axis_index("trait")
        values = [last_ref[...].reshape(2 * rows, owned)]
        compete, mutate = ((part_ref[k] + blocks_dot(values, k_ref, k, [me ^ 3])).astype(BF16) for k in range(2))
        inv_one = STEP_SIZE / (1.0 + FIRST * d_ref[...])
        inv_two = 1.0 / (1.0 + SECOND * d_ref[...])
        for i, x in enumerate(cells):
            e = []
            for f, ref in enumerate((one_ref, two_ref)):
                at = slice(f * rows + i * ycount, f * rows + (i + 1) * ycount)
                e.append(mutate[at].astype(F32) - ref[i] * compete[at].astype(F32))
            more = (5.0 / 12.0 * e[0] - 1.0 / 12.0 * e[1]) * inv_one
            new = first_ref[i] + more
            new_ref[i] = new
            rounded = new.astype(BF16)
            rounded_ref[0, i * ycount:(i + 1) * ycount, :] = rounded
            if with_faces and x == 0:
                face_refs[0][0] = rounded
            if with_faces and x == xcount - 1:
                face_refs[1][0] = rounded
            rest_ref[i] = begun_ref[i] + (more - SECOND * e[0] + STEP_SIZE / 3.0 * (e[0] + e[1])) * inv_two

    outs = [
        pltpu.VMEM((len(cells), ycount, owned), F32),
        pltpu.VMEM((1, rows, owned), BF16),
        pltpu.VMEM((len(cells), ycount, owned), F32),
    ]
    if with_faces:
        outs += [pltpu.VMEM((1, ycount, owned), BF16)] * 2
    return call(body, "first_node", [part, first, rest, last, one, two, kernels, death], outs)


def before_second(news, rests, growth, death, begun, blocks, kernels, chunks):
    _, ycount, owned = news[0].shape
    rows = blocks[0].shape[1]
    xcount = sum(len(cells) for cells in chunks)
    count = len(chunks)
    size = len(blocks)
    place = {x: (c, i) for c, cells in enumerate(chunks) for i, x in enumerate(cells)}

    def body(*refs):
        new_refs, rest_refs, block_refs = refs[:count], refs[count:2 * count], refs[2 * count:2 * count + size]
        k_ref, g_ref, d_ref, _, whole_ref, part_ref = refs[2 * count + size:2 * count + size + 6]
        base_refs, sems = refs[2 * count + size + 6:-1], refs[-1]
        copies = [
            pltpu.make_async_copy(new_refs[-1].at[pl.ds(i, size)], whole_ref.at[pl.ds(x, size)], sems.at[r])
            for r, (i, x, size) in enumerate(runs_of(chunks[-1]))
        ]
        for copy in copies:
            copy.start()
        me = lax.axis_index("trait")
        values = [r[...].reshape(rows, owned) for r in block_refs]
        for k in range(2):
            part_ref[k] = blocks_dot(values, k_ref, k, [me ^ j for j in range(size)])
        growth = g_ref[...]
        factor = SECOND / (1.0 + SECOND * d_ref[...])
        for x, (c, i) in place.items():
            core = new_refs[c][i]
            e = along_y(core) + core * growth
            for near in (x - 1, x + 1):
                if near in place:
                    e = e + DIFFUSION * new_refs[place[near][0]][place[near][1]]
            base_refs[c][i] = rest_refs[c][i] + factor * e
        for copy in copies:
            copy.wait()

    outs = [jax.ShapeDtypeStruct((xcount, ycount, owned), F32), pltpu.VMEM((2, rows, owned), F32)]
    outs += [pltpu.VMEM((len(cells), ycount, owned), F32) for cells in chunks]
    args = [*news, *rests, *blocks, kernels, growth, death, begun]
    return call(
        body, "before_second", args, outs, scratch=[pltpu.SemaphoreType.DMA((len(runs_of(chunks[-1])),))],
        specs=[SPEC] * (len(args) - 1) + [FROM_HBM], out_specs=[ANYWHERE] + [SPEC] * (len(outs) - 1), gflop=20.0,
        alias={len(args) - 1: 0},
    )


def whole_sums(part, last, kernels):
    rows, owned = last.shape[1:]

    def body(part_ref, last_ref, k_ref, sums_ref):
        me = lax.axis_index("trait")
        for k in range(2):
            last_part = blocks_dot([last_ref[...].reshape(rows, owned)], k_ref, k, [me ^ 3])
            sums_ref[k] = (part_ref[k] + last_part).astype(BF16)

    return call(body, "whole_sums", [part, last, kernels], [pltpu.VMEM((2, rows, owned), BF16)])[0]


def finish(cells, pieces, ycount, sums, base_ref, new_ref, factor, faces, held, out_ref, sems):
    copies = []
    size = ycount // pieces
    for i, x in enumerate(cells):
        for p in range(pieces):
            rows = pl.ds(p * size, size)
            at = pl.ds(i * ycount + p * size, size)
            e = sums[1, at, :].astype(F32) - new_ref[i, rows, :] * sums[0, at, :].astype(F32)
            if x in faces:
                e = e + DIFFUSION * faces[x][0, rows, :].astype(F32)
            held[i, rows, :] = base_ref[i, rows, :] + factor * e
            copies.append(
                pltpu.make_async_copy(held.at[i, rows], out_ref.at[x, rows], sems.at[i * pieces + p])
            )
            copies[-1].start()
    return copies


def second_first(sums, base, new, death, lo, hi, blocks, kernels, cells, xcount):
    _, ycount, owned = new.shape
    rows = blocks[0].shape[1]
    count = len(blocks)

    def body(sums_ref, base_ref, new_ref, d_ref, lo_ref, hi_ref, k_ref, *refs):
        block_refs = refs[:count]
        out_ref, part_ref, held, sems = refs[count:]
        factor = SECOND / (1.0 + SECOND * d_ref[...])
        faces = {0: lo_ref, xcount - 1: hi_ref}
        copies = finish(cells, 1, ycount, sums_ref, base_ref, new_ref, factor, faces, held, out_ref, sems)
        me = lax.axis_index("trait")
        values = [r[...].reshape(rows, owned) for r in block_refs]
        for k in range(2):
            part_ref[k] = blocks_dot(values, k_ref, k, [me ^ j for j in range(count)])
        for copy in copies:
            copy.wait()

    return call(
        body, "second_first", [sums, base, new, death, lo, hi, kernels, *blocks],
        [jax.ShapeDtypeStruct((xcount, ycount, owned), F32), pltpu.VMEM((2, rows, owned), F32)],
        scratch=[pltpu.VMEM((len(cells), ycount, owned), F32), pltpu.SemaphoreType.DMA((len(cells),))],
        out_specs=[ANYWHERE, SPEC],
    )


def second_last(part, last, base, new, death, kernels, begun, cells, xcount):
    _, ycount, owned = new.shape
    rows = len(cells) * ycount

    def body(part_ref, last_ref, base_ref, new_ref, d_ref, k_ref, begun_ref, out_ref, sums, held, sems):
        me = lax.axis_index("trait")
        for k in range(2):
            sums[k] = (part_ref[k] + blocks_dot([last_ref[...].reshape(rows, owned)], k_ref, k, [me ^ 3])).astype(BF16)
        factor = SECOND / (1.0 + SECOND * d_ref[...])
        for copy in finish(cells, 2, ycount, sums, base_ref, new_ref, factor, {}, held, out_ref, sems):
            copy.wait()

    return call(
        body, "second_last", [part, last, base, new, death, kernels, begun],
        [jax.ShapeDtypeStruct((xcount, ycount, owned), F32)],
        scratch=[
            pltpu.VMEM((2, rows, owned), BF16),
            pltpu.VMEM((len(cells), ycount, owned), F32),
            pltpu.SemaphoreType.DMA((2 * len(cells),)),
        ],
        specs=[SPEC] * 6 + [FROM_HBM], out_specs=[ANYWHERE], alias={6: 0},
    )[0]


def local(initial, section_one, section_two, kernels, growth, death_rate):
    xcount, ycount, owned = section_one.shape
    traits = lax.axis_size("trait")
    gcount = lax.axis_size("gx")
    growth = growth.reshape(1, owned)
    death = death_rate.reshape(1, owned)
    chunks = chunks_of(xcount)

    def to_sibling(v):
        return lax.ppermute(v, "trait", [(i, i ^ 1) for i in range(traits)])

    def to_far(v):
        return lax.ppermute(v, "trait", [(i, i ^ 2) for i in range(traits)])

    def from_below(tail):
        return lax.ppermute(tail, "gx", [(i, (i + 1) % gcount) for i in range(gcount)])

    def from_above(head):
        return lax.ppermute(head, "gx", [((i + 1) % gcount, i) for i in range(gcount)])

    one_a, two_a, own_a, head, tail = load_chunk((section_one, section_two), chunks[0], True)
    far_a = to_far(own_a)
    one_b, two_b, own_b = load_chunk((after(section_one, own_a), section_two), chunks[1], False)
    far_b = to_far(own_b)
    head, tail, kernels = lax.optimization_barrier((head, tail, kernels, own_b))[:3]
    lo, hi = from_below(tail), from_above(head)
    base_a, base_b = before_first((one_a, one_b), (two_a, two_b), lo, hi, growth, chunks)
    sib_a = to_sibling(after(own_a, own_b))
    sib_b = to_sibling(own_b)
    far_a = after(far_a, base_a)
    farsib_a = to_sibling(far_a)
    part_a, first_a, rest_a = early_part([own_a, sib_a, far_a], base_a, one_a, two_a, initial, kernels, death, chunks[0])
    new_a, rounded_a, rest_a, new_head, new_tail = first_node(
        part_a, first_a, rest_a, farsib_a, one_a, two_a, kernels, death, chunks[0], xcount, True
    )
    nfar_a = to_far(rounded_a)
    nsib_a = to_sibling(rounded_a)

    new_lo = from_below(new_tail)
    far_b = after(far_b, rounded_a)
    farsib_b = to_sibling(far_b)
    part_b, first_b, rest_b, new_one = early_part(
        [own_b, sib_b, far_b], base_b, one_b, two_b, initial, after(kernels, new_lo), death, chunks[1], new_a, chunks[0]
    )
    new_b, rounded_b, rest_b = first_node(
        part_b, first_b, rest_b, farsib_b, one_b, two_b, kernels, death, chunks[1], xcount, False
    )
    nfar_b = to_far(rounded_b)
    nsib_b = to_sibling(rounded_b)
    new_hi = from_above(after(new_head, rounded_b))
    nfar_a = after(nfar_a, rounded_b)
    nfarsib_a = to_sibling(nfar_a)
    new_one, npart_a, nbase_a, nbase_b = before_second(
        (new_a, new_b), (rest_a, rest_b), growth, death, new_one, [rounded_a, nsib_a, nfar_a], kernels, chunks
    )
    sums_a = whole_sums(npart_a, nfarsib_a, after(kernels, nbase_a))
    nfar_b = after(nfar_b, sums_a, new_hi)
    nfarsib_b = to_sibling(nfar_b)
    begun, npart_b = second_first(
        sums_a, nbase_a, new_a, death, new_lo, new_hi, [rounded_b, nsib_b, nfar_b], kernels, chunks[0], xcount
    )
    new_two = second_last(npart_b, nfarsib_b, nbase_b, new_b, death, kernels, begun, chunks[1], xcount)
    return new_one, new_two


def solution(mesh):
    in_specs = (
        P("gx", None, "trait"),
        P("gx", None, "trait"),
        P("gx", None, "trait"),
        P(None, None, "trait"),
        P("trait"),
        P("trait"),
    )
    out_specs = (P("gx", None, "trait"), P("gx", None, "trait"))
    return jax.shard_map(local, mesh=mesh, in_specs=in_specs, out_specs=out_specs, check_vma=False)
```

```python
import jax
import jax.numpy as jnp
from jax import lax
from jax.experimental import pallas as pl
from jax.experimental.pallas import tpu as pltpu
from jax.sharding import PartitionSpec as P

DIFFUSION = 0.25
STEP_SIZE = 0.5
FIRST = STEP_SIZE / 3.0
SECOND = 2.0 * STEP_SIZE / 3.0
F32 = jnp.float32
BF16 = jnp.bfloat16
VMEM_LIMIT = 20 * 1024 * 1024
SPEC = pl.BlockSpec(memory_space=pltpu.VMEM)
ANYWHERE = pl.BlockSpec(memory_space=pl.ANY)
FROM_HBM = pl.BlockSpec(memory_space=pltpu.HBM)


def chunks_of(xcount):
    last = max(1, 3 * xcount // 8)
    start = (xcount - last + 1) // 2
    middle = list(range(start, start + last))
    return [x for x in range(xcount) if x not in middle], middle


def after(value, *others):
    return lax.optimization_barrier((value, *others))[0]


def call(body, name, args, outs, scratch=(), specs=None, out_specs=None, gflop=0.0, alias=None):
    specs = specs or [SPEC] * len(args)
    space = {id(SPEC): pltpu.VMEM, id(FROM_HBM): pltpu.HBM}
    args = [
        pltpu.with_memory_space_constraint(a, space[id(s)]) if id(s) in space else a for a, s in zip(args, specs)
    ]
    return pl.pallas_call(
        body,
        out_shape=outs,
        in_specs=specs,
        out_specs=out_specs or [SPEC] * len(outs),
        scratch_shapes=list(scratch),
        compiler_params=pltpu.CompilerParams(vmem_limit_bytes=VMEM_LIMIT),
        cost_estimate=pl.CostEstimate(flops=int(gflop * 1e9), bytes_accessed=0, transcendentals=0),
        input_output_aliases=alias or {},
        name=name,
    )(*args)


def runs_of(cells):
    runs = []
    for i, x in enumerate(cells):
        if runs and x == sum(runs[-1][1:]):
            runs[-1][2] += 1
        else:
            runs.append([i, x, 1])
    return runs


def load_chunk(fields, cells, with_faces):
    xcount, ycount, owned = fields[0].shape
    count = len(fields)
    runs = runs_of(cells)

    def body(*refs):
        field_refs, held_refs, out_ref = refs[:count], refs[count:2 * count], refs[2 * count]
        sems = refs[-1]
        copies = {}
        for f in range(count):
            for r, (i, x, size) in enumerate(runs):
                copies[f, r] = pltpu.make_async_copy(
                    field_refs[f].at[pl.ds(x, size)], held_refs[f].at[pl.ds(i, size)], sems.at[f, r]
                )
                copies[f, r].start()
        for f in range(count):
            for r, (start, _, size) in enumerate(runs):
                copies[f, r].wait()
                for i in range(start, start + size):
                    value = held_refs[f][i].astype(BF16)
                    out_ref[f, i * ycount:(i + 1) * ycount, :] = value
                    if with_faces and cells[i] == 0:
                        refs[2 * count + 1][f] = value
                    if with_faces and cells[i] == xcount - 1:
                        refs[2 * count + 2][f] = value

    outs = [pltpu.VMEM((len(cells), ycount, owned), F32)] * count
    outs.append(pltpu.VMEM((count, len(cells) * ycount, owned), BF16))
    if with_faces:
        outs += [pltpu.VMEM((count, ycount, owned), BF16)] * 2
    return call(
        body, "load_chunk", fields, outs, scratch=[pltpu.SemaphoreType.DMA((count, len(runs)))],
        specs=[FROM_HBM] * count,
    )


def blocks_dot(blocks, kernels_ref, k, owners):
    depth = blocks[0].shape[-1]
    lhs = jnp.concatenate(blocks, axis=-1)
    rhs = jnp.concatenate(
        [kernels_ref[k, pl.ds(pl.multiple_of(o * depth, depth), depth), :] for o in owners], axis=0
    )
    return jnp.dot(lhs, rhs, preferred_element_type=F32)


def along_y(core):
    return DIFFUSION * (pltpu.roll(core, 1, 0) + pltpu.roll(core, core.shape[0] - 1, 0)) - 2.0 * core


def before_first(ones, twos, lo, hi, growth, chunks):
    _, ycount, owned = ones[0].shape
    xcount = sum(len(cells) for cells in chunks)
    count = len(chunks)
    place = {x: (c, i) for c, cells in enumerate(chunks) for i, x in enumerate(cells)}

    def body(*refs):
        lo_ref, hi_ref, g_ref, *outs = refs[2 * count:]
        growth = g_ref[...]
        for f in range(2):

            def get(x):
                c, i = place[x]
                return refs[f * count + c][i]

            for x, (c, i) in place.items():
                core = get(x)
                before = get(x - 1) if x > 0 else lo_ref[f].astype(F32)
                behind = get(x + 1) if x < xcount - 1 else hi_ref[f].astype(F32)
                outs[c][f, i] = DIFFUSION * (before + behind) + along_y(core) + core * growth

    outs = [pltpu.VMEM((2, len(cells), ycount, owned), F32) for cells in chunks]
    return call(body, "before_first", [*ones, *twos, lo, hi, growth], outs)


def early_part(blocks, base, one, two, initial, kernels, death, cells, new=None, new_cells=()):
    xcount, ycount, owned = initial.shape
    rows = len(cells) * ycount
    count = len(blocks)

    def body(*refs):
        block_refs = refs[:count]
        base_ref, one_ref, two_ref, init_ref, k_ref, d_ref, *refs = refs[count:]
        copies = []
        if new is not None:
            new_ref, whole_ref, sems = refs[0], refs[-2], refs[-1]
            copies = [
                pltpu.make_async_copy(new_ref.at[pl.ds(i, size)], whole_ref.at[pl.ds(x, size)], sems.at[r])
                for r, (i, x, size) in enumerate(runs_of(new_cells))
            ]
        for copy in copies:
            copy.start()
        part_ref, first_ref, rest_ref = refs[:3] if new is None else refs[1:4]
        me = lax.axis_index("trait")
        values = [r[...].reshape(2 * rows, owned) for r in block_refs]
        for k in range(2):
            part_ref[k] = blocks_dot(values, k_ref, k, [me ^ j for j in range(count)])
        death = d_ref[...]
        inv_one = 1.0 / (1.0 + FIRST * death)
        inv_two = 1.0 / (1.0 + SECOND * death)
        for i, x in enumerate(cells):
            cores = (one_ref[i], two_ref[i])
            e = (base_ref[0, i], base_ref[1, i])
            full_one = e[0] - death * cores[0]
            full_two = e[1] - death * cores[1]
            first = (
                init_ref[x]
                + FIRST * death * cores[0]
                + STEP_SIZE * (5.0 / 12.0 * full_one - 1.0 / 12.0 * full_two)
            ) * inv_one
            first_ref[i] = first
            rest_ref[i] = (
                first - SECOND * e[0] + SECOND * death * cores[1] + STEP_SIZE / 3.0 * (full_one + full_two)
            ) * inv_two
        for copy in copies:
            copy.wait()

    args = [*blocks, base, one, two, initial, kernels, death]
    outs = [pltpu.VMEM((2, 2 * rows, owned), F32)] + [pltpu.VMEM((len(cells), ycount, owned), F32)] * 2
    if new is None:
        return call(body, "early_part", args, outs, gflop=20.0)
    outs.append(jax.ShapeDtypeStruct((xcount, ycount, owned), F32))
    return call(
        body, "early_part", [*args, new], outs, scratch=[pltpu.SemaphoreType.DMA((len(runs_of(new_cells)),))],
        out_specs=[SPEC, SPEC, SPEC, ANYWHERE], gflop=20.0,
    )


def first_node(part, first, rest, last, one, two, kernels, death, cells, xcount, with_faces):
    _, ycount, owned = one.shape
    rows = len(cells) * ycount

    def body(part_ref, first_ref, begun_ref, last_ref, one_ref, two_ref, k_ref, d_ref, *outs):
        new_ref, rounded_ref, rest_ref, *face_refs = outs
        me = lax.axis_index("trait")
        values = [last_ref[...].reshape(2 * rows, owned)]
        compete, mutate = ((part_ref[k] + blocks_dot(values, k_ref, k, [me ^ 3])).astype(BF16) for k in range(2))
        inv_one = STEP_SIZE / (1.0 + FIRST * d_ref[...])
        inv_two = 1.0 / (1.0 + SECOND * d_ref[...])
        for i, x in enumerate(cells):
            e = []
            for f, ref in enumerate((one_ref, two_ref)):
                at = slice(f * rows + i * ycount, f * rows + (i + 1) * ycount)
                e.append(mutate[at].astype(F32) - ref[i] * compete[at].astype(F32))
            more = (5.0 / 12.0 * e[0] - 1.0 / 12.0 * e[1]) * inv_one
            new = first_ref[i] + more
            new_ref[i] = new
            rounded = new.astype(BF16)
            rounded_ref[0, i * ycount:(i + 1) * ycount, :] = rounded
            if with_faces and x == 0:
                face_refs[0][0] = rounded
            if with_faces and x == xcount - 1:
                face_refs[1][0] = rounded
            rest_ref[i] = begun_ref[i] + (more - SECOND * e[0] + STEP_SIZE / 3.0 * (e[0] + e[1])) * inv_two

    outs = [
        pltpu.VMEM((len(cells), ycount, owned), F32),
        pltpu.VMEM((1, rows, owned), BF16),
        pltpu.VMEM((len(cells), ycount, owned), F32),
    ]
    if with_faces:
        outs += [pltpu.VMEM((1, ycount, owned), BF16)] * 2
    return call(body, "first_node", [part, first, rest, last, one, two, kernels, death], outs)


def before_second(news, rests, growth, death, begun, blocks, kernels, chunks):
    _, ycount, owned = news[0].shape
    rows = blocks[0].shape[1]
    xcount = sum(len(cells) for cells in chunks)
    count = len(chunks)
    size = len(blocks)
    place = {x: (c, i) for c, cells in enumerate(chunks) for i, x in enumerate(cells)}

    def body(*refs):
        new_refs, rest_refs, block_refs = refs[:count], refs[count:2 * count], refs[2 * count:2 * count + size]
        k_ref, g_ref, d_ref, _, whole_ref, part_ref = refs[2 * count + size:2 * count + size + 6]
        base_refs, sems = refs[2 * count + size + 6:-1], refs[-1]
        copies = [
            pltpu.make_async_copy(new_refs[-1].at[pl.ds(i, size)], whole_ref.at[pl.ds(x, size)], sems.at[r])
            for r, (i, x, size) in enumerate(runs_of(chunks[-1]))
        ]
        for copy in copies:
            copy.start()
        me = lax.axis_index("trait")
        values = [r[...].reshape(rows, owned) for r in block_refs]
        for k in range(2):
            part_ref[k] = blocks_dot(values, k_ref, k, [me ^ j for j in range(size)])
        growth = g_ref[...]
        factor = SECOND / (1.0 + SECOND * d_ref[...])
        for x, (c, i) in place.items():
            core = new_refs[c][i]
            e = along_y(core) + core * growth
            for near in (x - 1, x + 1):
                if near in place:
                    e = e + DIFFUSION * new_refs[place[near][0]][place[near][1]]
            base_refs[c][i] = rest_refs[c][i] + factor * e
        for copy in copies:
            copy.wait()

    outs = [jax.ShapeDtypeStruct((xcount, ycount, owned), F32), pltpu.VMEM((2, rows, owned), F32)]
    outs += [pltpu.VMEM((len(cells), ycount, owned), F32) for cells in chunks]
    args = [*news, *rests, *blocks, kernels, growth, death, begun]
    return call(
        body, "before_second", args, outs, scratch=[pltpu.SemaphoreType.DMA((len(runs_of(chunks[-1])),))],
        specs=[SPEC] * (len(args) - 1) + [FROM_HBM], out_specs=[ANYWHERE] + [SPEC] * (len(outs) - 1), gflop=20.0,
        alias={len(args) - 1: 0},
    )


def whole_sums(part, last, kernels):
    rows, owned = last.shape[1:]

    def body(part_ref, last_ref, k_ref, sums_ref):
        me = lax.axis_index("trait")
        for k in range(2):
            last_part = blocks_dot([last_ref[...].reshape(rows, owned)], k_ref, k, [me ^ 3])
            sums_ref[k] = (part_ref[k] + last_part).astype(BF16)

    return call(body, "whole_sums", [part, last, kernels], [pltpu.VMEM((2, rows, owned), BF16)])[0]


def finish(cells, sums_at, base_ref, new_ref, factor, faces, held, out_ref, sems, offset=0):
    copies = []
    for j, (i, x) in enumerate(cells, offset):
        e = sums_at(1, i) - new_ref[i] * sums_at(0, i)
        if x in faces:
            e = e + DIFFUSION * faces[x][0].astype(F32)
        held[j] = base_ref[i] + factor * e
        copies.append(pltpu.make_async_copy(held.at[j], out_ref.at[x], sems.at[j]))
        copies[-1].start()
    return copies


def rounded_at(sums, ycount):
    return lambda k, i: sums[k, pl.ds(i * ycount, ycount), :].astype(F32)


def second_first(sums, base, new, death, blocks, kernels, cells, xcount):
    _, ycount, owned = new.shape
    rows = blocks[0].shape[1]
    count = len(blocks)

    def body(sums_ref, base_ref, new_ref, d_ref, k_ref, *refs):
        block_refs = refs[:count]
        out_ref, part_ref, held, sems = refs[count:]
        factor = SECOND / (1.0 + SECOND * d_ref[...])
        copies = finish(
            cells, rounded_at(sums_ref, ycount), base_ref, new_ref, factor, {}, held, out_ref, sems
        )
        me = lax.axis_index("trait")
        values = [r[...].reshape(rows, owned) for r in block_refs]
        for k in range(2):
            part_ref[k] = blocks_dot(values, k_ref, k, [me ^ j for j in range(count)])
        for copy in copies:
            copy.wait()

    return call(
        body, "second_first", [sums, base, new, death, kernels, *blocks],
        [jax.ShapeDtypeStruct((xcount, ycount, owned), F32), pltpu.VMEM((2, rows, owned), F32)],
        scratch=[pltpu.VMEM((len(cells), ycount, owned), F32), pltpu.SemaphoreType.DMA((len(cells),))],
        out_specs=[ANYWHERE, SPEC],
    )


def second_last(sums_a, base_a, new_a, lo, hi, part, last, base, new, death, kernels, begun, ends, cells, xcount):
    _, ycount, owned = new.shape
    rows = len(cells) * ycount
    total = len(ends) + len(cells)

    def body(*refs):
        sums_a_ref, base_a_ref, new_a_ref, lo_ref, hi_ref, part_ref, last_ref, base_ref, new_ref, d_ref, k_ref = refs[:11]
        _, out_ref, sums, held, sems = refs[11:]
        factor = SECOND / (1.0 + SECOND * d_ref[...])
        faces = {0: lo_ref, xcount - 1: hi_ref}
        copies = finish(
            ends, rounded_at(sums_a_ref, ycount), base_a_ref, new_a_ref, factor, faces, held, out_ref, sems
        )
        me = lax.axis_index("trait")
        for k in range(2):
            sums[k] = (part_ref[k] + blocks_dot([last_ref[...].reshape(rows, owned)], k_ref, k, [me ^ 3])).astype(BF16)
        copies += finish(
            list(enumerate(cells)), rounded_at(sums, ycount), base_ref, new_ref, factor, {}, held, out_ref, sems,
            len(ends),
        )
        for copy in copies:
            copy.wait()

    args = [sums_a, base_a, new_a, lo, hi, part, last, base, new, death, kernels, begun]
    return call(
        body, "second_last", args, [jax.ShapeDtypeStruct((xcount, ycount, owned), F32)],
        scratch=[
            pltpu.VMEM((2, rows, owned), BF16),
            pltpu.VMEM((total, ycount, owned), F32),
            pltpu.SemaphoreType.DMA((total,)),
        ],
        specs=[SPEC] * 11 + [FROM_HBM], out_specs=[ANYWHERE], alias={11: 0},
    )[0]


def local(initial, section_one, section_two, kernels, growth, death_rate):
    xcount, ycount, owned = section_one.shape
    traits = lax.axis_size("trait")
    gcount = lax.axis_size("gx")
    growth = growth.reshape(1, owned)
    death = death_rate.reshape(1, owned)
    chunks = chunks_of(xcount)

    def to_sibling(v):
        return lax.ppermute(v, "trait", [(i, i ^ 1) for i in range(traits)])

    def to_far(v):
        return lax.ppermute(v, "trait", [(i, i ^ 2) for i in range(traits)])

    def from_below(tail):
        return lax.ppermute(tail, "gx", [(i, (i + 1) % gcount) for i in range(gcount)])

    def from_above(head):
        return lax.ppermute(head, "gx", [((i + 1) % gcount, i) for i in range(gcount)])

    one_a, two_a, own_a, head, tail = load_chunk((section_one, section_two), chunks[0], True)
    far_a = to_far(own_a)
    one_b, two_b, own_b = load_chunk((after(section_one, own_a), section_two), chunks[1], False)
    far_b = to_far(own_b)
    head, tail, kernels = lax.optimization_barrier((head, tail, kernels, own_b))[:3]
    lo, hi = from_below(tail), from_above(head)
    base_a, base_b = before_first((one_a, one_b), (two_a, two_b), lo, hi, growth, chunks)
    sib_a = to_sibling(after(own_a, own_b))
    sib_b = to_sibling(own_b)
    far_a = after(far_a, base_a)
    farsib_a = to_sibling(far_a)
    part_a, first_a, rest_a = early_part([own_a, sib_a, far_a], base_a, one_a, two_a, initial, kernels, death, chunks[0])
    new_a, rounded_a, rest_a, new_head, new_tail = first_node(
        part_a, first_a, rest_a, farsib_a, one_a, two_a, kernels, death, chunks[0], xcount, True
    )
    nfar_a = to_far(rounded_a)
    nsib_a = to_sibling(rounded_a)

    new_lo = from_below(new_tail)
    far_b = after(far_b, rounded_a)
    farsib_b = to_sibling(far_b)
    part_b, first_b, rest_b, new_one = early_part(
        [own_b, sib_b, far_b], base_b, one_b, two_b, initial, after(kernels, new_lo), death, chunks[1], new_a, chunks[0]
    )
    new_b, rounded_b, rest_b = first_node(
        part_b, first_b, rest_b, farsib_b, one_b, two_b, kernels, death, chunks[1], xcount, False
    )
    nfar_b = to_far(rounded_b)
    nsib_b = to_sibling(rounded_b)
    new_hi = from_above(after(new_head, rounded_b))
    nfar_a = after(nfar_a, rounded_b)
    nfarsib_a = to_sibling(nfar_a)
    new_one, npart_a, nbase_a, nbase_b = before_second(
        (new_a, new_b), (rest_a, rest_b), growth, death, new_one, [rounded_a, nsib_a, nfar_a], kernels, chunks
    )
    sums_a = whole_sums(npart_a, nfarsib_a, after(kernels, nbase_a))
    nfar_b = after(nfar_b, sums_a, new_hi)
    nfarsib_b = to_sibling(nfar_b)
    placed = list(enumerate(chunks[0]))
    ends = [p for p in placed if p[1] in (0, xcount - 1)]
    begun, npart_b = second_first(
        sums_a, nbase_a, new_a, death, [rounded_b, nsib_b, nfar_b], kernels, [p for p in placed if p not in ends], xcount
    )
    new_two = second_last(
        sums_a, nbase_a, new_a, new_lo, new_hi, npart_b, nfarsib_b, nbase_b, new_b, death, kernels, begun, ends,
        chunks[1], xcount,
    )
    return new_one, new_two


def solution(mesh):
    in_specs = (
        P("gx", None, "trait"),
        P("gx", None, "trait"),
        P("gx", None, "trait"),
        P(None, None, "trait"),
        P("trait"),
        P("trait"),
    )
    out_specs = (P("gx", None, "trait"), P("gx", None, "trait"))
    return jax.shard_map(local, mesh=mesh, in_specs=in_specs, out_specs=out_specs, check_vma=False)
```

```python
import jax
import jax.numpy as jnp
from jax import lax
from jax.experimental import pallas as pl
from jax.experimental.pallas import tpu as pltpu
from jax.sharding import PartitionSpec as P

DIFFUSION = 0.25
STEP_SIZE = 0.5
FIRST = STEP_SIZE / 3.0
SECOND = 2.0 * STEP_SIZE / 3.0
F32 = jnp.float32
BF16 = jnp.bfloat16
VMEM_LIMIT = 20 * 1024 * 1024
SPEC = pl.BlockSpec(memory_space=pltpu.VMEM)
ANYWHERE = pl.BlockSpec(memory_space=pl.ANY)
FROM_HBM = pl.BlockSpec(memory_space=pltpu.HBM)


def chunks_of(xcount):
    last = max(1, 3 * xcount // 8)
    start = (xcount - last + 1) // 2
    middle = list(range(start, start + last))
    return [x for x in range(xcount) if x not in middle], middle


def after(value, *others):
    return lax.optimization_barrier((value, *others))[0]


def call(body, name, args, outs, scratch=(), specs=None, out_specs=None, gflop=0.0, alias=None):
    specs = specs or [SPEC] * len(args)
    space = {id(SPEC): pltpu.VMEM, id(FROM_HBM): pltpu.HBM}
    args = [
        pltpu.with_memory_space_constraint(a, space[id(s)]) if id(s) in space else a for a, s in zip(args, specs)
    ]
    return pl.pallas_call(
        body,
        out_shape=outs,
        in_specs=specs,
        out_specs=out_specs or [SPEC] * len(outs),
        scratch_shapes=list(scratch),
        compiler_params=pltpu.CompilerParams(vmem_limit_bytes=VMEM_LIMIT),
        cost_estimate=pl.CostEstimate(flops=int(gflop * 1e9), bytes_accessed=0, transcendentals=0),
        input_output_aliases=alias or {},
        name=name,
    )(*args)


def runs_of(cells):
    runs = []
    for i, x in enumerate(cells):
        if runs and x == sum(runs[-1][1:]):
            runs[-1][2] += 1
        else:
            runs.append([i, x, 1])
    return runs


def load_chunk(fields, cells, with_faces, split=False):
    xcount, ycount, owned = fields[0].shape
    count = len(fields)
    runs = runs_of(cells)

    def body(*refs):
        field_refs, held_refs, out_ref = refs[:count], refs[count:2 * count], refs[2 * count]
        sems = refs[-1]
        copies = {}
        for f in range(count):
            for r, (i, x, size) in enumerate(runs):
                copies[f, r] = pltpu.make_async_copy(
                    field_refs[f].at[pl.ds(x, size)], held_refs[f].at[pl.ds(i, size)], sems.at[f, r]
                )
                copies[f, r].start()
        for f in range(count):
            for r, (start, _, size) in enumerate(runs):
                copies[f, r].wait()
                for i in range(start, start + size):
                    value = held_refs[f][i].astype(BF16)
                    out_ref[f, i * ycount:(i + 1) * ycount, :] = value
                    if split:
                        refs[2 * count + 1 + f][0, i * ycount:(i + 1) * ycount, :] = value
                    if with_faces and cells[i] == 0:
                        refs[2 * count + 1][f] = value
                    if with_faces and cells[i] == xcount - 1:
                        refs[2 * count + 2][f] = value

    outs = [pltpu.VMEM((len(cells), ycount, owned), F32)] * count
    outs.append(pltpu.VMEM((count, len(cells) * ycount, owned), BF16))
    if split:
        outs += [pltpu.VMEM((1, len(cells) * ycount, owned), BF16)] * count
    if with_faces:
        outs += [pltpu.VMEM((count, ycount, owned), BF16)] * 2
    return call(
        body, "load_chunk", fields, outs, scratch=[pltpu.SemaphoreType.DMA((count, len(runs)))],
        specs=[FROM_HBM] * count,
    )


def blocks_dot(blocks, kernels_ref, k, owners):
    depth = blocks[0].shape[-1]
    lhs = jnp.concatenate(blocks, axis=-1)
    rhs = jnp.concatenate(
        [kernels_ref[k, pl.ds(pl.multiple_of(o * depth, depth), depth), :] for o in owners], axis=0
    )
    return jnp.dot(lhs, rhs, preferred_element_type=F32)


def along_y(core):
    return DIFFUSION * (pltpu.roll(core, 1, 0) + pltpu.roll(core, core.shape[0] - 1, 0)) - 2.0 * core


def before_first(ones, twos, lo, hi, growth, chunks):
    _, ycount, owned = ones[0].shape
    xcount = sum(len(cells) for cells in chunks)
    count = len(chunks)
    place = {x: (c, i) for c, cells in enumerate(chunks) for i, x in enumerate(cells)}

    def body(*refs):
        lo_ref, hi_ref, g_ref, *outs = refs[2 * count:]
        growth = g_ref[...]
        for f in range(2):

            def get(x):
                c, i = place[x]
                return refs[f * count + c][i]

            for x, (c, i) in place.items():
                core = get(x)
                before = get(x - 1) if x > 0 else lo_ref[f].astype(F32)
                behind = get(x + 1) if x < xcount - 1 else hi_ref[f].astype(F32)
                outs[c][f, i] = DIFFUSION * (before + behind) + along_y(core) + core * growth

    outs = [pltpu.VMEM((2, len(cells), ycount, owned), F32) for cells in chunks]
    return call(body, "before_first", [*ones, *twos, lo, hi, growth], outs)


def rows_of(refs):
    return jnp.concatenate([r[...].reshape(-1, r.shape[-1]) for r in refs], axis=0)


def early_part(blocks, base, one, two, initial, kernels, death, cells, new=None, new_cells=()):
    xcount, ycount, owned = initial.shape
    rows = len(cells) * ycount
    owners = [j for j, block in enumerate(blocks) for _ in block]
    count = len(owners)

    def body(*refs):
        block_refs = refs[:count]
        base_ref, one_ref, two_ref, init_ref, k_ref, d_ref, *refs = refs[count:]
        copies = []
        if new is not None:
            new_ref, whole_ref, sems = refs[0], refs[-2], refs[-1]
            copies = [
                pltpu.make_async_copy(new_ref.at[pl.ds(i, size)], whole_ref.at[pl.ds(x, size)], sems.at[r])
                for r, (i, x, size) in enumerate(runs_of(new_cells))
            ]
        for copy in copies:
            copy.start()
        part_ref, first_ref, rest_ref = refs[:3] if new is None else refs[1:4]
        me = lax.axis_index("trait")
        values = [rows_of([r for j, r in zip(owners, block_refs) if j == n]) for n in range(len(blocks))]
        for k in range(2):
            part_ref[k] = blocks_dot(values, k_ref, k, [me ^ j for j in range(len(blocks))])
        death = d_ref[...]
        inv_one = 1.0 / (1.0 + FIRST * death)
        inv_two = 1.0 / (1.0 + SECOND * death)
        for i, x in enumerate(cells):
            cores = (one_ref[i], two_ref[i])
            e = (base_ref[0, i], base_ref[1, i])
            full_one = e[0] - death * cores[0]
            full_two = e[1] - death * cores[1]
            first = (
                init_ref[x]
                + FIRST * death * cores[0]
                + STEP_SIZE * (5.0 / 12.0 * full_one - 1.0 / 12.0 * full_two)
            ) * inv_one
            first_ref[i] = first
            rest_ref[i] = (
                first - SECOND * e[0] + SECOND * death * cores[1] + STEP_SIZE / 3.0 * (full_one + full_two)
            ) * inv_two
        for copy in copies:
            copy.wait()

    args = [*sum(blocks, []), base, one, two, initial, kernels, death]
    outs = [pltpu.VMEM((2, 2 * rows, owned), F32)] + [pltpu.VMEM((len(cells), ycount, owned), F32)] * 2
    if new is None:
        return call(body, "early_part", args, outs, gflop=20.0)
    outs.append(jax.ShapeDtypeStruct((xcount, ycount, owned), F32))
    return call(
        body, "early_part", [*args, new], outs, scratch=[pltpu.SemaphoreType.DMA((len(runs_of(new_cells)),))],
        out_specs=[SPEC, SPEC, SPEC, ANYWHERE], gflop=20.0,
    )


def first_node(part, first, rest, last, one, two, kernels, death, cells, xcount, with_faces):
    _, ycount, owned = one.shape
    rows = len(cells) * ycount

    count = len(last)

    def body(*refs):
        last_refs, (part_ref, first_ref, begun_ref, one_ref, two_ref, k_ref, d_ref, *outs) = refs[:count], refs[count:]
        new_ref, rounded_ref, rest_ref, *face_refs = outs
        me = lax.axis_index("trait")
        values = [rows_of(last_refs)]
        compete, mutate = ((part_ref[k] + blocks_dot(values, k_ref, k, [me ^ 3])).astype(BF16) for k in range(2))
        inv_one = STEP_SIZE / (1.0 + FIRST * d_ref[...])
        inv_two = 1.0 / (1.0 + SECOND * d_ref[...])
        for i, x in enumerate(cells):
            e = []
            for f, ref in enumerate((one_ref, two_ref)):
                at = slice(f * rows + i * ycount, f * rows + (i + 1) * ycount)
                e.append(mutate[at].astype(F32) - ref[i] * compete[at].astype(F32))
            more = (5.0 / 12.0 * e[0] - 1.0 / 12.0 * e[1]) * inv_one
            new = first_ref[i] + more
            new_ref[i] = new
            rounded = new.astype(BF16)
            rounded_ref[0, i * ycount:(i + 1) * ycount, :] = rounded
            if with_faces and x == 0:
                face_refs[0][0] = rounded
            if with_faces and x == xcount - 1:
                face_refs[1][0] = rounded
            rest_ref[i] = begun_ref[i] + (more - SECOND * e[0] + STEP_SIZE / 3.0 * (e[0] + e[1])) * inv_two

    outs = [
        pltpu.VMEM((len(cells), ycount, owned), F32),
        pltpu.VMEM((1, rows, owned), BF16),
        pltpu.VMEM((len(cells), ycount, owned), F32),
    ]
    if with_faces:
        outs += [pltpu.VMEM((1, ycount, owned), BF16)] * 2
    return call(body, "first_node", [*last, part, first, rest, one, two, kernels, death], outs)


def before_second(news, rests, growth, death, begun, blocks, kernels, chunks):
    _, ycount, owned = news[0].shape
    rows = blocks[0].shape[1]
    xcount = sum(len(cells) for cells in chunks)
    count = len(chunks)
    size = len(blocks)
    place = {x: (c, i) for c, cells in enumerate(chunks) for i, x in enumerate(cells)}

    def body(*refs):
        new_refs, rest_refs, block_refs = refs[:count], refs[count:2 * count], refs[2 * count:2 * count + size]
        k_ref, g_ref, d_ref, _, whole_ref, part_ref = refs[2 * count + size:2 * count + size + 6]
        base_refs, sems = refs[2 * count + size + 6:-1], refs[-1]
        copies = [
            pltpu.make_async_copy(new_refs[-1].at[pl.ds(i, size)], whole_ref.at[pl.ds(x, size)], sems.at[r])
            for r, (i, x, size) in enumerate(runs_of(chunks[-1]))
        ]
        for copy in copies:
            copy.start()
        me = lax.axis_index("trait")
        values = [r[...].reshape(rows, owned) for r in block_refs]
        for k in range(2):
            part_ref[k] = blocks_dot(values, k_ref, k, [me ^ j for j in range(size)])
        growth = g_ref[...]
        factor = SECOND / (1.0 + SECOND * d_ref[...])
        for x, (c, i) in place.items():
            core = new_refs[c][i]
            e = along_y(core) + core * growth
            for near in (x - 1, x + 1):
                if near in place:
                    e = e + DIFFUSION * new_refs[place[near][0]][place[near][1]]
            base_refs[c][i] = rest_refs[c][i] + factor * e
        for copy in copies:
            copy.wait()

    outs = [jax.ShapeDtypeStruct((xcount, ycount, owned), F32), pltpu.VMEM((2, rows, owned), F32)]
    outs += [pltpu.VMEM((len(cells), ycount, owned), F32) for cells in chunks]
    args = [*news, *rests, *blocks, kernels, growth, death, begun]
    return call(
        body, "before_second", args, outs, scratch=[pltpu.SemaphoreType.DMA((len(runs_of(chunks[-1])),))],
        specs=[SPEC] * (len(args) - 1) + [FROM_HBM], out_specs=[ANYWHERE] + [SPEC] * (len(outs) - 1), gflop=20.0,
        alias={len(args) - 1: 0},
    )


def whole_sums(part, last, kernels):
    rows, owned = last.shape[1:]

    def body(part_ref, last_ref, k_ref, sums_ref):
        me = lax.axis_index("trait")
        for k in range(2):
            last_part = blocks_dot([last_ref[...].reshape(rows, owned)], k_ref, k, [me ^ 3])
            sums_ref[k] = (part_ref[k] + last_part).astype(BF16)

    return call(body, "whole_sums", [part, last, kernels], [pltpu.VMEM((2, rows, owned), BF16)])[0]


def finish(cells, sums_at, base_ref, new_ref, factor, faces, held, out_ref, sems, offset=0):
    copies = []
    for j, (i, x) in enumerate(cells, offset):
        e = sums_at(1, i) - new_ref[i] * sums_at(0, i)
        if x in faces:
            e = e + DIFFUSION * faces[x][0].astype(F32)
        held[j] = base_ref[i] + factor * e
        copies.append(pltpu.make_async_copy(held.at[j], out_ref.at[x], sems.at[j]))
        copies[-1].start()
    return copies


def rounded_at(sums, ycount):
    return lambda k, i: sums[k, pl.ds(i * ycount, ycount), :].astype(F32)


def second_first(sums, base, new, death, blocks, kernels, cells, xcount):
    _, ycount, owned = new.shape
    rows = blocks[0].shape[1]
    count = len(blocks)

    def body(sums_ref, base_ref, new_ref, d_ref, k_ref, *refs):
        block_refs = refs[:count]
        out_ref, part_ref, held, sems = refs[count:]
        factor = SECOND / (1.0 + SECOND * d_ref[...])
        copies = finish(
            cells, rounded_at(sums_ref, ycount), base_ref, new_ref, factor, {}, held, out_ref, sems
        )
        me = lax.axis_index("trait")
        values = [r[...].reshape(rows, owned) for r in block_refs]
        for k in range(2):
            part_ref[k] = blocks_dot(values, k_ref, k, [me ^ j for j in range(count)])
        for copy in copies:
            copy.wait()

    return call(
        body, "second_first", [sums, base, new, death, kernels, *blocks],
        [jax.ShapeDtypeStruct((xcount, ycount, owned), F32), pltpu.VMEM((2, rows, owned), F32)],
        scratch=[pltpu.VMEM((len(cells), ycount, owned), F32), pltpu.SemaphoreType.DMA((len(cells),))],
        out_specs=[ANYWHERE, SPEC],
    )


def second_last(sums_a, base_a, new_a, lo, hi, part, last, base, new, death, kernels, begun, ends, cells, xcount):
    _, ycount, owned = new.shape
    rows = len(cells) * ycount
    total = len(ends) + len(cells)

    def body(*refs):
        sums_a_ref, base_a_ref, new_a_ref, lo_ref, hi_ref, part_ref, last_ref, base_ref, new_ref, d_ref, k_ref = refs[:11]
        _, out_ref, sums, held, sems = refs[11:]
        factor = SECOND / (1.0 + SECOND * d_ref[...])
        faces = {0: lo_ref, xcount - 1: hi_ref}
        copies = finish(
            ends, rounded_at(sums_a_ref, ycount), base_a_ref, new_a_ref, factor, faces, held, out_ref, sems
        )
        me = lax.axis_index("trait")
        for k in range(2):
            sums[k] = (part_ref[k] + blocks_dot([last_ref[...].reshape(rows, owned)], k_ref, k, [me ^ 3])).astype(BF16)
        copies += finish(
            list(enumerate(cells)), rounded_at(sums, ycount), base_ref, new_ref, factor, {}, held, out_ref, sems,
            len(ends),
        )
        for copy in copies:
            copy.wait()

    args = [sums_a, base_a, new_a, lo, hi, part, last, base, new, death, kernels, begun]
    return call(
        body, "second_last", args, [jax.ShapeDtypeStruct((xcount, ycount, owned), F32)],
        scratch=[
            pltpu.VMEM((2, rows, owned), BF16),
            pltpu.VMEM((total, ycount, owned), F32),
            pltpu.SemaphoreType.DMA((total,)),
        ],
        specs=[SPEC] * 11 + [FROM_HBM], out_specs=[ANYWHERE], alias={11: 0},
    )[0]


def local(initial, section_one, section_two, kernels, growth, death_rate):
    xcount, ycount, owned = section_one.shape
    traits = lax.axis_size("trait")
    gcount = lax.axis_size("gx")
    growth = growth.reshape(1, owned)
    death = death_rate.reshape(1, owned)
    chunks = chunks_of(xcount)

    def to_sibling(v):
        return lax.ppermute(v, "trait", [(i, i ^ 1) for i in range(traits)])

    def to_far(v):
        return lax.ppermute(v, "trait", [(i, i ^ 2) for i in range(traits)])

    def from_below(tail):
        return lax.ppermute(tail, "gx", [(i, (i + 1) % gcount) for i in range(gcount)])

    def from_above(head):
        return lax.ppermute(head, "gx", [((i + 1) % gcount, i) for i in range(gcount)])

    one_a, two_a, own_a, head, tail = load_chunk((section_one, section_two), chunks[0], True)
    far_a = to_far(own_a)
    one_b, two_b, own_b, *own_fields = load_chunk((after(section_one, own_a), section_two), chunks[1], False, True)
    far_b = [to_far(v) for v in own_fields]
    head, tail, kernels = lax.optimization_barrier((head, tail, kernels, own_b))[:3]
    lo, hi = from_below(tail), from_above(head)
    base_a, base_b = before_first((one_a, one_b), (two_a, two_b), lo, hi, growth, chunks)
    sib_a = to_sibling(after(own_a, own_b))
    sib_b = to_sibling(own_b)
    far_a = after(far_a, base_a)
    farsib_a = to_sibling(far_a)
    part_a, first_a, rest_a = early_part([[own_a], [sib_a], [far_a]], base_a, one_a, two_a, initial, kernels, death, chunks[0])
    new_a, rounded_a, rest_a, new_head, new_tail = first_node(
        part_a, first_a, rest_a, [farsib_a], one_a, two_a, kernels, death, chunks[0], xcount, True
    )
    nfar_a = to_far(rounded_a)
    nsib_a = to_sibling(rounded_a)

    new_lo = from_below(new_tail)
    far_b = [after(far_b[0], rounded_a), far_b[1]]
    farsib_b = [to_sibling(far_b[0])]
    far_b[1] = after(far_b[1], farsib_b[0])
    farsib_b.append(to_sibling(far_b[1]))
    part_b, first_b, rest_b, new_one = early_part(
        [[own_b], [sib_b], far_b], base_b, one_b, two_b, initial, after(kernels, new_lo), death, chunks[1], new_a, chunks[0]
    )
    new_b, rounded_b, rest_b = first_node(
        part_b, first_b, rest_b, farsib_b, one_b, two_b, kernels, death, chunks[1], xcount, False
    )
    nfar_b = to_far(rounded_b)
    nsib_b = to_sibling(rounded_b)
    new_hi = from_above(after(new_head, rounded_b))
    nfar_a = after(nfar_a, rounded_b)
    nfarsib_a = to_sibling(nfar_a)
    new_one, npart_a, nbase_a, nbase_b = before_second(
        (new_a, new_b), (rest_a, rest_b), growth, death, new_one, [rounded_a, nsib_a, nfar_a], kernels, chunks
    )
    sums_a = whole_sums(npart_a, nfarsib_a, after(kernels, nbase_a))
    nfar_b = after(nfar_b, sums_a, new_hi)
    nfarsib_b = to_sibling(nfar_b)
    placed = list(enumerate(chunks[0]))
    ends = [p for p in placed if p[1] in (0, xcount - 1)]
    begun, npart_b = second_first(
        sums_a, nbase_a, new_a, death, [rounded_b, nsib_b, nfar_b], kernels, [p for p in placed if p not in ends], xcount
    )
    new_two = second_last(
        sums_a, nbase_a, new_a, new_lo, new_hi, npart_b, nfarsib_b, nbase_b, new_b, death, kernels, begun, ends,
        chunks[1], xcount,
    )
    return new_one, new_two


def solution(mesh):
    in_specs = (
        P("gx", None, "trait"),
        P("gx", None, "trait"),
        P("gx", None, "trait"),
        P(None, None, "trait"),
        P("trait"),
        P("trait"),
    )
    out_specs = (P("gx", None, "trait"), P("gx", None, "trait"))
    return jax.shard_map(local, mesh=mesh, in_specs=in_specs, out_specs=out_specs, check_vma=False)
```

```python
import jax
import jax.numpy as jnp
from jax import lax
from jax.experimental import pallas as pl
from jax.experimental.pallas import tpu as pltpu
from jax.sharding import PartitionSpec as P

DIFFUSION = 0.25
STEP_SIZE = 0.5
FIRST = STEP_SIZE / 3.0
SECOND = 2.0 * STEP_SIZE / 3.0
F32 = jnp.float32
BF16 = jnp.bfloat16
VMEM_LIMIT = 20 * 1024 * 1024
SPEC = pl.BlockSpec(memory_space=pltpu.VMEM)
ANYWHERE = pl.BlockSpec(memory_space=pl.ANY)
FROM_HBM = pl.BlockSpec(memory_space=pltpu.HBM)


def chunks_of(xcount):
    last = max(1, 3 * xcount // 8)
    start = (xcount - last + 1) // 2
    middle = list(range(start, start + last))
    return [x for x in range(xcount) if x not in middle], middle


def after(value, *others):
    return lax.optimization_barrier((value, *others))[0]


def call(body, name, args, outs, scratch=(), specs=None, out_specs=None, gflop=0.0, alias=None):
    specs = specs or [SPEC] * len(args)
    space = {id(SPEC): pltpu.VMEM, id(FROM_HBM): pltpu.HBM}
    args = [
        pltpu.with_memory_space_constraint(a, space[id(s)]) if id(s) in space else a for a, s in zip(args, specs)
    ]
    return pl.pallas_call(
        body,
        out_shape=outs,
        in_specs=specs,
        out_specs=out_specs or [SPEC] * len(outs),
        scratch_shapes=list(scratch),
        compiler_params=pltpu.CompilerParams(vmem_limit_bytes=VMEM_LIMIT),
        cost_estimate=pl.CostEstimate(flops=int(gflop * 1e9), bytes_accessed=0, transcendentals=0),
        input_output_aliases=alias or {},
        name=name,
    )(*args)


def runs_of(cells):
    runs = []
    for i, x in enumerate(cells):
        if runs and x == sum(runs[-1][1:]):
            runs[-1][2] += 1
        else:
            runs.append([i, x, 1])
    return runs


def load_chunk(fields, cells, with_faces):
    xcount, ycount, owned = fields[0].shape
    count = len(fields)
    runs = runs_of(cells)

    def body(*refs):
        field_refs, held_refs, out_ref = refs[:count], refs[count:2 * count], refs[2 * count]
        sems = refs[-1]
        copies = {}
        for f in range(count):
            for r, (i, x, size) in enumerate(runs):
                copies[f, r] = pltpu.make_async_copy(
                    field_refs[f].at[pl.ds(x, size)], held_refs[f].at[pl.ds(i, size)], sems.at[f, r]
                )
                copies[f, r].start()
        for f in range(count):
            for r, (start, _, size) in enumerate(runs):
                copies[f, r].wait()
                for i in range(start, start + size):
                    value = held_refs[f][i].astype(BF16)
                    out_ref[f, i * ycount:(i + 1) * ycount, :] = value
                    if with_faces and cells[i] == 0:
                        refs[2 * count + 1][f] = value
                    if with_faces and cells[i] == xcount - 1:
                        refs[2 * count + 2][f] = value

    outs = [pltpu.VMEM((len(cells), ycount, owned), F32)] * count
    outs.append(pltpu.VMEM((count, len(cells) * ycount, owned), BF16))
    if with_faces:
        outs += [pltpu.VMEM((count, ycount, owned), BF16)] * 2
    return call(
        body, "load_chunk", fields, outs, scratch=[pltpu.SemaphoreType.DMA((count, len(runs)))],
        specs=[FROM_HBM] * count,
    )


def blocks_dot(blocks, kernels_ref, k, owners):
    depth = blocks[0].shape[-1]
    lhs = jnp.concatenate(blocks, axis=-1)
    rhs = jnp.concatenate(
        [kernels_ref[k, pl.ds(pl.multiple_of(o * depth, depth), depth), :] for o in owners], axis=0
    )
    return jnp.dot(lhs, rhs, preferred_element_type=F32)


def along_y(core):
    return DIFFUSION * (pltpu.roll(core, 1, 0) + pltpu.roll(core, core.shape[0] - 1, 0)) - 2.0 * core


def before_first(ones, twos, lo, hi, growth, chunks):
    _, ycount, owned = ones[0].shape
    xcount = sum(len(cells) for cells in chunks)
    count = len(chunks)
    place = {x: (c, i) for c, cells in enumerate(chunks) for i, x in enumerate(cells)}

    def body(*refs):
        lo_ref, hi_ref, g_ref, *outs = refs[2 * count:]
        growth = g_ref[...]
        for f in range(2):

            def get(x):
                c, i = place[x]
                return refs[f * count + c][i]

            for x, (c, i) in place.items():
                core = get(x)
                before = get(x - 1) if x > 0 else lo_ref[f].astype(F32)
                behind = get(x + 1) if x < xcount - 1 else hi_ref[f].astype(F32)
                outs[c][f, i] = DIFFUSION * (before + behind) + along_y(core) + core * growth

    outs = [pltpu.VMEM((2, len(cells), ycount, owned), F32) for cells in chunks]
    return call(body, "before_first", [*ones, *twos, lo, hi, growth], outs)


def early_part(blocks, base, one, two, initial, kernels, death, cells, new=None, new_cells=()):
    xcount, ycount, owned = initial.shape
    rows = len(cells) * ycount
    count = len(blocks)

    def body(*refs):
        block_refs = refs[:count]
        base_ref, one_ref, two_ref, init_ref, k_ref, d_ref, *refs = refs[count:]
        copies = []
        if new is not None:
            new_ref, whole_ref, sems = refs[0], refs[-2], refs[-1]
            copies = [
                pltpu.make_async_copy(new_ref.at[pl.ds(i, size)], whole_ref.at[pl.ds(x, size)], sems.at[r])
                for r, (i, x, size) in enumerate(runs_of(new_cells))
            ]
        for copy in copies:
            copy.start()
        part_ref, first_ref, rest_ref = refs[:3] if new is None else refs[1:4]
        me = lax.axis_index("trait")
        values = [r[...].reshape(2 * rows, owned) for r in block_refs]
        for k in range(2):
            part_ref[k] = blocks_dot(values, k_ref, k, [me ^ j for j in range(count)])
        death = d_ref[...]
        inv_one = 1.0 / (1.0 + FIRST * death)
        inv_two = 1.0 / (1.0 + SECOND * death)
        for i, x in enumerate(cells):
            cores = (one_ref[i], two_ref[i])
            e = (base_ref[0, i], base_ref[1, i])
            full_one = e[0] - death * cores[0]
            full_two = e[1] - death * cores[1]
            first = (
                init_ref[x]
                + FIRST * death * cores[0]
                + STEP_SIZE * (5.0 / 12.0 * full_one - 1.0 / 12.0 * full_two)
            ) * inv_one
            first_ref[i] = first
            rest_ref[i] = (
                first - SECOND * e[0] + SECOND * death * cores[1] + STEP_SIZE / 3.0 * (full_one + full_two)
            ) * inv_two
        for copy in copies:
            copy.wait()

    args = [*blocks, base, one, two, initial, kernels, death]
    outs = [pltpu.VMEM((2, 2 * rows, owned), F32)] + [pltpu.VMEM((len(cells), ycount, owned), F32)] * 2
    if new is None:
        return call(body, "early_part", args, outs, gflop=20.0)
    outs.append(jax.ShapeDtypeStruct((xcount, ycount, owned), F32))
    return call(
        body, "early_part", [*args, new], outs, scratch=[pltpu.SemaphoreType.DMA((len(runs_of(new_cells)),))],
        out_specs=[SPEC, SPEC, SPEC, ANYWHERE], gflop=20.0,
    )


def first_node(part, first, rest, last, one, two, kernels, death, cells, xcount, with_faces):
    _, ycount, owned = one.shape
    rows = len(cells) * ycount

    def body(part_ref, first_ref, begun_ref, last_ref, one_ref, two_ref, k_ref, d_ref, *outs):
        new_ref, rounded_ref, rest_ref, *face_refs = outs
        me = lax.axis_index("trait")
        values = [last_ref[...].reshape(2 * rows, owned)]
        compete, mutate = ((part_ref[k] + blocks_dot(values, k_ref, k, [me ^ 3])).astype(BF16) for k in range(2))
        inv_one = STEP_SIZE / (1.0 + FIRST * d_ref[...])
        inv_two = 1.0 / (1.0 + SECOND * d_ref[...])
        for i, x in enumerate(cells):
            e = []
            for f, ref in enumerate((one_ref, two_ref)):
                at = slice(f * rows + i * ycount, f * rows + (i + 1) * ycount)
                e.append(mutate[at].astype(F32) - ref[i] * compete[at].astype(F32))
            more = (5.0 / 12.0 * e[0] - 1.0 / 12.0 * e[1]) * inv_one
            new = first_ref[i] + more
            new_ref[i] = new
            rounded = new.astype(BF16)
            rounded_ref[0, i * ycount:(i + 1) * ycount, :] = rounded
            if with_faces and x == 0:
                face_refs[0][0] = rounded
            if with_faces and x == xcount - 1:
                face_refs[1][0] = rounded
            rest_ref[i] = begun_ref[i] + (more - SECOND * e[0] + STEP_SIZE / 3.0 * (e[0] + e[1])) * inv_two

    outs = [
        pltpu.VMEM((len(cells), ycount, owned), F32),
        pltpu.VMEM((1, rows, owned), BF16),
        pltpu.VMEM((len(cells), ycount, owned), F32),
    ]
    if with_faces:
        outs += [pltpu.VMEM((1, ycount, owned), BF16)] * 2
    return call(body, "first_node", [part, first, rest, last, one, two, kernels, death], outs)


def before_second(news, rests, growth, death, begun, blocks, own_b, kernels, chunks):
    _, ycount, owned = news[0].shape
    rows = blocks[0].shape[1]
    xcount = sum(len(cells) for cells in chunks)
    count = len(chunks)
    size = len(blocks)
    place = {x: (c, i) for c, cells in enumerate(chunks) for i, x in enumerate(cells)}

    def body(*refs):
        new_refs, rest_refs, block_refs = refs[:count], refs[count:2 * count], refs[2 * count:2 * count + size]
        own_b_ref, k_ref, g_ref, d_ref, _, whole_ref, part_ref, part_b_ref = refs[2 * count + size:2 * count + size + 8]
        base_refs, sems = refs[2 * count + size + 8:-1], refs[-1]
        copies = [
            pltpu.make_async_copy(new_refs[-1].at[pl.ds(i, size)], whole_ref.at[pl.ds(x, size)], sems.at[r])
            for r, (i, x, size) in enumerate(runs_of(chunks[-1]))
        ]
        for copy in copies:
            copy.start()
        me = lax.axis_index("trait")
        values = [r[...].reshape(rows, owned) for r in block_refs]
        for k in range(2):
            part_ref[k] = blocks_dot(values, k_ref, k, [me ^ j for j in range(size)])
            part_b_ref[k] = blocks_dot([own_b_ref[...].reshape(-1, owned)], k_ref, k, [me])
        growth = g_ref[...]
        factor = SECOND / (1.0 + SECOND * d_ref[...])
        for x, (c, i) in place.items():
            core = new_refs[c][i]
            e = along_y(core) + core * growth
            for near in (x - 1, x + 1):
                if near in place:
                    e = e + DIFFUSION * new_refs[place[near][0]][place[near][1]]
            base_refs[c][i] = rest_refs[c][i] + factor * e
        for copy in copies:
            copy.wait()

    outs = [jax.ShapeDtypeStruct((xcount, ycount, owned), F32), pltpu.VMEM((2, rows, owned), F32)]
    outs.append(pltpu.VMEM((2, own_b.shape[1], owned), F32))
    outs += [pltpu.VMEM((len(cells), ycount, owned), F32) for cells in chunks]
    args = [*news, *rests, *blocks, own_b, kernels, growth, death, begun]
    return call(
        body, "before_second", args, outs, scratch=[pltpu.SemaphoreType.DMA((len(runs_of(chunks[-1])),))],
        specs=[SPEC] * (len(args) - 1) + [FROM_HBM], out_specs=[ANYWHERE] + [SPEC] * (len(outs) - 1), gflop=20.0,
        alias={len(args) - 1: 0},
    )


def whole_sums(part, last, kernels):
    rows, owned = last.shape[1:]

    def body(part_ref, last_ref, k_ref, sums_ref):
        me = lax.axis_index("trait")
        for k in range(2):
            last_part = blocks_dot([last_ref[...].reshape(rows, owned)], k_ref, k, [me ^ 3])
            sums_ref[k] = (part_ref[k] + last_part).astype(BF16)

    return call(body, "whole_sums", [part, last, kernels], [pltpu.VMEM((2, rows, owned), BF16)])[0]


def finish(cells, sums_at, base_ref, new_ref, factor, faces, held, out_ref, sems, offset=0):
    copies = []
    for j, (i, x) in enumerate(cells, offset):
        e = sums_at(1, i) - new_ref[i] * sums_at(0, i)
        if x in faces:
            e = e + DIFFUSION * faces[x][0].astype(F32)
        held[j] = base_ref[i] + factor * e
        copies.append(pltpu.make_async_copy(held.at[j], out_ref.at[x], sems.at[j]))
        copies[-1].start()
    return copies


def rounded_at(sums, ycount):
    return lambda k, i: sums[k, pl.ds(i * ycount, ycount), :].astype(F32)


def second_first(sums, base, new, death, part, blocks, kernels, cells, xcount):
    _, ycount, owned = new.shape
    rows = blocks[0].shape[1]
    count = len(blocks)

    def body(sums_ref, base_ref, new_ref, d_ref, begun_ref, k_ref, *refs):
        block_refs = refs[:count]
        out_ref, part_ref, held, sems = refs[count:]
        factor = SECOND / (1.0 + SECOND * d_ref[...])
        copies = finish(
            cells, rounded_at(sums_ref, ycount), base_ref, new_ref, factor, {}, held, out_ref, sems
        )
        me = lax.axis_index("trait")
        values = [r[...].reshape(rows, owned) for r in block_refs]
        for k in range(2):
            part_ref[k] = begun_ref[k] + blocks_dot(values, k_ref, k, [me ^ (j + 1) for j in range(count)])
        for copy in copies:
            copy.wait()

    return call(
        body, "second_first", [sums, base, new, death, part, kernels, *blocks],
        [jax.ShapeDtypeStruct((xcount, ycount, owned), F32), pltpu.VMEM((2, rows, owned), F32)],
        scratch=[pltpu.VMEM((len(cells), ycount, owned), F32), pltpu.SemaphoreType.DMA((len(cells),))],
        out_specs=[ANYWHERE, SPEC],
    )


def second_last(sums_a, base_a, new_a, lo, hi, part, last, base, new, death, kernels, begun, ends, cells, xcount):
    _, ycount, owned = new.shape
    rows = len(cells) * ycount
    total = len(ends) + len(cells)

    def body(*refs):
        sums_a_ref, base_a_ref, new_a_ref, lo_ref, hi_ref, part_ref, last_ref, base_ref, new_ref, d_ref, k_ref = refs[:11]
        _, out_ref, sums, held, sems = refs[11:]
        factor = SECOND / (1.0 + SECOND * d_ref[...])
        faces = {0: lo_ref, xcount - 1: hi_ref}
        copies = finish(
            ends, rounded_at(sums_a_ref, ycount), base_a_ref, new_a_ref, factor, faces, held, out_ref, sems
        )
        me = lax.axis_index("trait")
        for k in range(2):
            sums[k] = (part_ref[k] + blocks_dot([last_ref[...].reshape(rows, owned)], k_ref, k, [me ^ 3])).astype(BF16)
        copies += finish(
            list(enumerate(cells)), rounded_at(sums, ycount), base_ref, new_ref, factor, {}, held, out_ref, sems,
            len(ends),
        )
        for copy in copies:
            copy.wait()

    args = [sums_a, base_a, new_a, lo, hi, part, last, base, new, death, kernels, begun]
    return call(
        body, "second_last", args, [jax.ShapeDtypeStruct((xcount, ycount, owned), F32)],
        scratch=[
            pltpu.VMEM((2, rows, owned), BF16),
            pltpu.VMEM((total, ycount, owned), F32),
            pltpu.SemaphoreType.DMA((total,)),
        ],
        specs=[SPEC] * 11 + [FROM_HBM], out_specs=[ANYWHERE], alias={11: 0},
    )[0]


def local(initial, section_one, section_two, kernels, growth, death_rate):
    xcount, ycount, owned = section_one.shape
    traits = lax.axis_size("trait")
    gcount = lax.axis_size("gx")
    growth = growth.reshape(1, owned)
    death = death_rate.reshape(1, owned)
    chunks = chunks_of(xcount)

    def to_sibling(v):
        return lax.ppermute(v, "trait", [(i, i ^ 1) for i in range(traits)])

    def to_far(v):
        return lax.ppermute(v, "trait", [(i, i ^ 2) for i in range(traits)])

    def from_below(tail):
        return lax.ppermute(tail, "gx", [(i, (i + 1) % gcount) for i in range(gcount)])

    def from_above(head):
        return lax.ppermute(head, "gx", [((i + 1) % gcount, i) for i in range(gcount)])

    one_a, two_a, own_a, head, tail = load_chunk((section_one, section_two), chunks[0], True)
    far_a = to_far(own_a)
    one_b, two_b, own_b = load_chunk((after(section_one, own_a), section_two), chunks[1], False)
    far_b = to_far(own_b)
    head, tail, kernels = lax.optimization_barrier((head, tail, kernels, own_b))[:3]
    lo, hi = from_below(tail), from_above(head)
    base_a, base_b = before_first((one_a, one_b), (two_a, two_b), lo, hi, growth, chunks)
    sib_a = to_sibling(after(own_a, own_b))
    sib_b = to_sibling(own_b)
    far_a = after(far_a, base_a)
    farsib_a = to_sibling(far_a)
    part_a, first_a, rest_a = early_part([own_a, sib_a, far_a], base_a, one_a, two_a, initial, kernels, death, chunks[0])
    new_a, rounded_a, rest_a, new_head, new_tail = first_node(
        part_a, first_a, rest_a, farsib_a, one_a, two_a, kernels, death, chunks[0], xcount, True
    )
    nfar_a = to_far(rounded_a)
    nsib_a = to_sibling(rounded_a)

    new_lo = from_below(new_tail)
    far_b = after(far_b, rounded_a)
    farsib_b = to_sibling(far_b)
    part_b, first_b, rest_b, new_one = early_part(
        [own_b, sib_b, far_b], base_b, one_b, two_b, initial, after(kernels, new_lo), death, chunks[1], new_a, chunks[0]
    )
    new_b, rounded_b, rest_b = first_node(
        part_b, first_b, rest_b, farsib_b, one_b, two_b, kernels, death, chunks[1], xcount, False
    )
    nfar_b = to_far(rounded_b)
    nsib_b = to_sibling(rounded_b)
    new_hi = from_above(after(new_head, rounded_b))
    nfar_a = after(nfar_a, rounded_b)
    nfarsib_a = to_sibling(nfar_a)
    new_one, npart_a, npart_b, nbase_a, nbase_b = before_second(
        (new_a, new_b), (rest_a, rest_b), growth, death, new_one, [rounded_a, nsib_a, nfar_a], rounded_b, kernels, chunks
    )
    sums_a = whole_sums(npart_a, nfarsib_a, after(kernels, nbase_a))
    nfar_b = after(nfar_b, sums_a, new_hi)
    nfarsib_b = to_sibling(nfar_b)
    placed = list(enumerate(chunks[0]))
    ends = [p for p in placed if p[1] in (0, xcount - 1)]
    begun, npart_b = second_first(
        sums_a, nbase_a, new_a, death, npart_b, [nsib_b, nfar_b], kernels, [p for p in placed if p not in ends], xcount
    )
    new_two = second_last(
        sums_a, nbase_a, new_a, new_lo, new_hi, npart_b, nfarsib_b, nbase_b, new_b, death, kernels, begun, ends,
        chunks[1], xcount,
    )
    return new_one, new_two


def solution(mesh):
    in_specs = (
        P("gx", None, "trait"),
        P("gx", None, "trait"),
        P("gx", None, "trait"),
        P(None, None, "trait"),
        P("trait"),
        P("trait"),
    )
    out_specs = (P("gx", None, "trait"), P("gx", None, "trait"))
    return jax.shard_map(local, mesh=mesh, in_specs=in_specs, out_specs=out_specs, check_vma=False)
```

```python
import jax
import jax.numpy as jnp
from jax import lax
from jax.experimental import pallas as pl
from jax.experimental.pallas import tpu as pltpu
from jax.sharding import PartitionSpec as P

DIFFUSION = 0.25
STEP_SIZE = 0.5
FIRST = STEP_SIZE / 3.0
SECOND = 2.0 * STEP_SIZE / 3.0
F32 = jnp.float32
BF16 = jnp.bfloat16
VMEM_LIMIT = 20 * 1024 * 1024
SPEC = pl.BlockSpec(memory_space=pltpu.VMEM)
ANYWHERE = pl.BlockSpec(memory_space=pl.ANY)
FROM_HBM = pl.BlockSpec(memory_space=pltpu.HBM)


def chunks_of(xcount):
    last = max(1, xcount // 2)
    start = (xcount - last + 1) // 2
    middle = list(range(start, start + last))
    return [x for x in range(xcount) if x not in middle], middle


def after(value, *others):
    return lax.optimization_barrier((value, *others))[0]


def call(body, name, args, outs, scratch=(), specs=None, out_specs=None, gflop=0.0, alias=None):
    specs = specs or [SPEC] * len(args)
    space = {id(SPEC): pltpu.VMEM, id(FROM_HBM): pltpu.HBM}
    args = [
        pltpu.with_memory_space_constraint(a, space[id(s)]) if id(s) in space else a for a, s in zip(args, specs)
    ]
    return pl.pallas_call(
        body,
        out_shape=outs,
        in_specs=specs,
        out_specs=out_specs or [SPEC] * len(outs),
        scratch_shapes=list(scratch),
        compiler_params=pltpu.CompilerParams(vmem_limit_bytes=VMEM_LIMIT),
        cost_estimate=pl.CostEstimate(flops=int(gflop * 1e9), bytes_accessed=0, transcendentals=0),
        input_output_aliases=alias or {},
        name=name,
    )(*args)


def runs_of(cells):
    runs = []
    for i, x in enumerate(cells):
        if runs and x == sum(runs[-1][1:]):
            runs[-1][2] += 1
        else:
            runs.append([i, x, 1])
    return runs


def load_chunk(fields, cells, with_faces):
    xcount, ycount, owned = fields[0].shape
    count = len(fields)
    runs = runs_of(cells)

    def body(*refs):
        field_refs, held_refs, out_ref = refs[:count], refs[count:2 * count], refs[2 * count]
        sems = refs[-1]
        copies = {}
        for f in range(count):
            for r, (i, x, size) in enumerate(runs):
                copies[f, r] = pltpu.make_async_copy(
                    field_refs[f].at[pl.ds(x, size)], held_refs[f].at[pl.ds(i, size)], sems.at[f, r]
                )
                copies[f, r].start()
        for f in range(count):
            for r, (start, _, size) in enumerate(runs):
                copies[f, r].wait()
                for i in range(start, start + size):
                    value = held_refs[f][i].astype(BF16)
                    out_ref[f, i * ycount:(i + 1) * ycount, :] = value
                    if with_faces and cells[i] == 0:
                        refs[2 * count + 1][f] = value
                    if with_faces and cells[i] == xcount - 1:
                        refs[2 * count + 2][f] = value

    outs = [pltpu.VMEM((len(cells), ycount, owned), F32)] * count
    outs.append(pltpu.VMEM((count, len(cells) * ycount, owned), BF16))
    if with_faces:
        outs += [pltpu.VMEM((count, ycount, owned), BF16)] * 2
    return call(
        body, "load_chunk", fields, outs, scratch=[pltpu.SemaphoreType.DMA((count, len(runs)))],
        specs=[FROM_HBM] * count,
    )


def blocks_dot(blocks, kernels_ref, k, owners):
    depth = blocks[0].shape[-1]
    lhs = jnp.concatenate(blocks, axis=-1)
    rhs = jnp.concatenate(
        [kernels_ref[k, pl.ds(pl.multiple_of(o * depth, depth), depth), :] for o in owners], axis=0
    )
    return jnp.dot(lhs, rhs, preferred_element_type=F32)


def along_y(core):
    return DIFFUSION * (pltpu.roll(core, 1, 0) + pltpu.roll(core, core.shape[0] - 1, 0)) - 2.0 * core


def before_first(ones, twos, lo, hi, growth, chunks):
    _, ycount, owned = ones[0].shape
    xcount = sum(len(cells) for cells in chunks)
    count = len(chunks)
    place = {x: (c, i) for c, cells in enumerate(chunks) for i, x in enumerate(cells)}

    def body(*refs):
        lo_ref, hi_ref, g_ref, *outs = refs[2 * count:]
        growth = g_ref[...]
        for f in range(2):

            def get(x):
                c, i = place[x]
                return refs[f * count + c][i]

            for x, (c, i) in place.items():
                core = get(x)
                before = get(x - 1) if x > 0 else lo_ref[f].astype(F32)
                behind = get(x + 1) if x < xcount - 1 else hi_ref[f].astype(F32)
                outs[c][f, i] = DIFFUSION * (before + behind) + along_y(core) + core * growth

    outs = [pltpu.VMEM((2, len(cells), ycount, owned), F32) for cells in chunks]
    return call(body, "before_first", [*ones, *twos, lo, hi, growth], outs)


def early_part(blocks, base, one, two, initial, kernels, death, cells, new=None, new_cells=()):
    xcount, ycount, owned = initial.shape
    rows = len(cells) * ycount
    count = len(blocks)

    def body(*refs):
        block_refs = refs[:count]
        base_ref, one_ref, two_ref, init_ref, k_ref, d_ref, *refs = refs[count:]
        copies = []
        if new is not None:
            new_ref, whole_ref, sems = refs[0], refs[-2], refs[-1]
            copies = [
                pltpu.make_async_copy(new_ref.at[pl.ds(i, size)], whole_ref.at[pl.ds(x, size)], sems.at[r])
                for r, (i, x, size) in enumerate(runs_of(new_cells))
            ]
        for copy in copies:
            copy.start()
        part_ref, first_ref, rest_ref = refs[:3] if new is None else refs[1:4]
        me = lax.axis_index("trait")
        values = [r[...].reshape(2 * rows, owned) for r in block_refs]
        for k in range(2):
            part_ref[k] = blocks_dot(values, k_ref, k, [me ^ j for j in range(count)])
        death = d_ref[...]
        inv_one = 1.0 / (1.0 + FIRST * death)
        inv_two = 1.0 / (1.0 + SECOND * death)
        for i, x in enumerate(cells):
            cores = (one_ref[i], two_ref[i])
            e = (base_ref[0, i], base_ref[1, i])
            full_one = e[0] - death * cores[0]
            full_two = e[1] - death * cores[1]
            first = (
                init_ref[x]
                + FIRST * death * cores[0]
                + STEP_SIZE * (5.0 / 12.0 * full_one - 1.0 / 12.0 * full_two)
            ) * inv_one
            first_ref[i] = first
            rest_ref[i] = (
                first - SECOND * e[0] + SECOND * death * cores[1] + STEP_SIZE / 3.0 * (full_one + full_two)
            ) * inv_two
        for copy in copies:
            copy.wait()

    args = [*blocks, base, one, two, initial, kernels, death]
    outs = [pltpu.VMEM((2, 2 * rows, owned), F32)] + [pltpu.VMEM((len(cells), ycount, owned), F32)] * 2
    if new is None:
        return call(body, "early_part", args, outs, gflop=20.0)
    outs.append(jax.ShapeDtypeStruct((xcount, ycount, owned), F32))
    return call(
        body, "early_part", [*args, new], outs, scratch=[pltpu.SemaphoreType.DMA((len(runs_of(new_cells)),))],
        out_specs=[SPEC, SPEC, SPEC, ANYWHERE], gflop=20.0,
    )


def first_node(part, first, rest, last, one, two, kernels, death, cells, xcount, with_faces):
    _, ycount, owned = one.shape
    rows = len(cells) * ycount

    def body(part_ref, first_ref, begun_ref, last_ref, one_ref, two_ref, k_ref, d_ref, *outs):
        new_ref, rounded_ref, rest_ref, *face_refs = outs
        me = lax.axis_index("trait")
        values = [last_ref[...].reshape(2 * rows, owned)]
        compete, mutate = ((part_ref[k] + blocks_dot(values, k_ref, k, [me ^ 3])).astype(BF16) for k in range(2))
        inv_one = STEP_SIZE / (1.0 + FIRST * d_ref[...])
        inv_two = 1.0 / (1.0 + SECOND * d_ref[...])
        for i, x in enumerate(cells):
            e = []
            for f, ref in enumerate((one_ref, two_ref)):
                at = slice(f * rows + i * ycount, f * rows + (i + 1) * ycount)
                e.append(mutate[at].astype(F32) - ref[i] * compete[at].astype(F32))
            more = (5.0 / 12.0 * e[0] - 1.0 / 12.0 * e[1]) * inv_one
            new = first_ref[i] + more
            new_ref[i] = new
            rounded = new.astype(BF16)
            rounded_ref[0, i * ycount:(i + 1) * ycount, :] = rounded
            if with_faces and x == 0:
                face_refs[0][0] = rounded
            if with_faces and x == xcount - 1:
                face_refs[1][0] = rounded
            rest_ref[i] = begun_ref[i] + (more - SECOND * e[0] + STEP_SIZE / 3.0 * (e[0] + e[1])) * inv_two

    outs = [
        pltpu.VMEM((len(cells), ycount, owned), F32),
        pltpu.VMEM((1, rows, owned), BF16),
        pltpu.VMEM((len(cells), ycount, owned), F32),
    ]
    if with_faces:
        outs += [pltpu.VMEM((1, ycount, owned), BF16)] * 2
    return call(body, "first_node", [part, first, rest, last, one, two, kernels, death], outs)


def before_second(news, rests, growth, death, begun, blocks, kernels, chunks):
    _, ycount, owned = news[0].shape
    rows = blocks[0].shape[1]
    xcount = sum(len(cells) for cells in chunks)
    count = len(chunks)
    size = len(blocks)
    place = {x: (c, i) for c, cells in enumerate(chunks) for i, x in enumerate(cells)}

    def body(*refs):
        new_refs, rest_refs, block_refs = refs[:count], refs[count:2 * count], refs[2 * count:2 * count + size]
        k_ref, g_ref, d_ref, _, whole_ref, part_ref = refs[2 * count + size:2 * count + size + 6]
        base_refs, sems = refs[2 * count + size + 6:-1], refs[-1]
        copies = [
            pltpu.make_async_copy(new_refs[-1].at[pl.ds(i, size)], whole_ref.at[pl.ds(x, size)], sems.at[r])
            for r, (i, x, size) in enumerate(runs_of(chunks[-1]))
        ]
        for copy in copies:
            copy.start()
        me = lax.axis_index("trait")
        values = [r[...].reshape(rows, owned) for r in block_refs]
        for k in range(2):
            part_ref[k] = blocks_dot(values, k_ref, k, [me ^ j for j in range(size)])
        growth = g_ref[...]
        factor = SECOND / (1.0 + SECOND * d_ref[...])
        for x, (c, i) in place.items():
            core = new_refs[c][i]
            e = along_y(core) + core * growth
            for near in (x - 1, x + 1):
                if near in place:
                    e = e + DIFFUSION * new_refs[place[near][0]][place[near][1]]
            base_refs[c][i] = rest_refs[c][i] + factor * e
        for copy in copies:
            copy.wait()

    outs = [jax.ShapeDtypeStruct((xcount, ycount, owned), F32), pltpu.VMEM((2, rows, owned), F32)]
    outs += [pltpu.VMEM((len(cells), ycount, owned), F32) for cells in chunks]
    args = [*news, *rests, *blocks, kernels, growth, death, begun]
    return call(
        body, "before_second", args, outs, scratch=[pltpu.SemaphoreType.DMA((len(runs_of(chunks[-1])),))],
        specs=[SPEC] * (len(args) - 1) + [FROM_HBM], out_specs=[ANYWHERE] + [SPEC] * (len(outs) - 1), gflop=20.0,
        alias={len(args) - 1: 0},
    )


def whole_sums(part, last, kernels):
    rows, owned = last.shape[1:]

    def body(part_ref, last_ref, k_ref, sums_ref):
        me = lax.axis_index("trait")
        for k in range(2):
            last_part = blocks_dot([last_ref[...].reshape(rows, owned)], k_ref, k, [me ^ 3])
            sums_ref[k] = (part_ref[k] + last_part).astype(BF16)

    return call(body, "whole_sums", [part, last, kernels], [pltpu.VMEM((2, rows, owned), BF16)])[0]


def finish(cells, sums_at, base_ref, new_ref, factor, faces, held, out_ref, sems, offset=0):
    copies = []
    for j, (i, x) in enumerate(cells, offset):
        e = sums_at(1, i) - new_ref[i] * sums_at(0, i)
        if x in faces:
            e = e + DIFFUSION * faces[x][0].astype(F32)
        held[j] = base_ref[i] + factor * e
        copies.append(pltpu.make_async_copy(held.at[j], out_ref.at[x], sems.at[j]))
        copies[-1].start()
    return copies


def rounded_at(sums, ycount):
    return lambda k, i: sums[k, pl.ds(i * ycount, ycount), :].astype(F32)


def second_first(sums, base, new, death, blocks, kernels, cells, xcount):
    _, ycount, owned = new.shape
    rows = blocks[0].shape[1]
    count = len(blocks)

    def body(sums_ref, base_ref, new_ref, d_ref, k_ref, *refs):
        block_refs = refs[:count]
        out_ref, part_ref, held, sems = refs[count:]
        factor = SECOND / (1.0 + SECOND * d_ref[...])
        copies = finish(
            cells, rounded_at(sums_ref, ycount), base_ref, new_ref, factor, {}, held, out_ref, sems
        )
        me = lax.axis_index("trait")
        values = [r[...].reshape(rows, owned) for r in block_refs]
        for k in range(2):
            part_ref[k] = blocks_dot(values, k_ref, k, [me ^ j for j in range(count)])
        for copy in copies:
            copy.wait()

    return call(
        body, "second_first", [sums, base, new, death, kernels, *blocks],
        [jax.ShapeDtypeStruct((xcount, ycount, owned), F32), pltpu.VMEM((2, rows, owned), F32)],
        scratch=[pltpu.VMEM((len(cells), ycount, owned), F32), pltpu.SemaphoreType.DMA((len(cells),))],
        out_specs=[ANYWHERE, SPEC],
    )


def second_last(sums_a, base_a, new_a, lo, hi, part, last, base, new, death, kernels, begun, ends, cells, xcount):
    _, ycount, owned = new.shape
    rows = len(cells) * ycount
    total = len(ends) + len(cells)

    def body(*refs):
        sums_a_ref, base_a_ref, new_a_ref, lo_ref, hi_ref, part_ref, last_ref, base_ref, new_ref, d_ref, k_ref = refs[:11]
        _, out_ref, sums, held, sems = refs[11:]
        factor = SECOND / (1.0 + SECOND * d_ref[...])
        faces = {0: lo_ref, xcount - 1: hi_ref}
        copies = finish(
            ends, rounded_at(sums_a_ref, ycount), base_a_ref, new_a_ref, factor, faces, held, out_ref, sems
        )
        me = lax.axis_index("trait")
        for k in range(2):
            sums[k] = (part_ref[k] + blocks_dot([last_ref[...].reshape(rows, owned)], k_ref, k, [me ^ 3])).astype(BF16)
        copies += finish(
            list(enumerate(cells)), rounded_at(sums, ycount), base_ref, new_ref, factor, {}, held, out_ref, sems,
            len(ends),
        )
        for copy in copies:
            copy.wait()

    args = [sums_a, base_a, new_a, lo, hi, part, last, base, new, death, kernels, begun]
    return call(
        body, "second_last", args, [jax.ShapeDtypeStruct((xcount, ycount, owned), F32)],
        scratch=[
            pltpu.VMEM((2, rows, owned), BF16),
            pltpu.VMEM((total, ycount, owned), F32),
            pltpu.SemaphoreType.DMA((total,)),
        ],
        specs=[SPEC] * 11 + [FROM_HBM], out_specs=[ANYWHERE], alias={11: 0},
    )[0]


def local(initial, section_one, section_two, kernels, growth, death_rate):
    xcount, ycount, owned = section_one.shape
    traits = lax.axis_size("trait")
    gcount = lax.axis_size("gx")
    growth = growth.reshape(1, owned)
    death = death_rate.reshape(1, owned)
    chunks = chunks_of(xcount)

    def to_sibling(v):
        return lax.ppermute(v, "trait", [(i, i ^ 1) for i in range(traits)])

    def to_far(v):
        return lax.ppermute(v, "trait", [(i, i ^ 2) for i in range(traits)])

    def from_below(tail):
        return lax.ppermute(tail, "gx", [(i, (i + 1) % gcount) for i in range(gcount)])

    def from_above(head):
        return lax.ppermute(head, "gx", [((i + 1) % gcount, i) for i in range(gcount)])

    one_a, two_a, own_a, head, tail = load_chunk((section_one, section_two), chunks[0], True)
    far_a = to_far(own_a)
    one_b, two_b, own_b = load_chunk((after(section_one, own_a), section_two), chunks[1], False)
    far_b = to_far(own_b)
    head, tail, kernels = lax.optimization_barrier((head, tail, kernels, own_b))[:3]
    lo, hi = from_below(tail), from_above(head)
    base_a, base_b = before_first((one_a, one_b), (two_a, two_b), lo, hi, growth, chunks)
    sib_a = to_sibling(after(own_a, own_b))
    sib_b = to_sibling(own_b)
    far_a = after(far_a, base_a)
    farsib_a = to_sibling(far_a)
    part_a, first_a, rest_a = early_part([own_a, sib_a, far_a], base_a, one_a, two_a, initial, kernels, death, chunks[0])
    new_a, rounded_a, rest_a, new_head, new_tail = first_node(
        part_a, first_a, rest_a, farsib_a, one_a, two_a, kernels, death, chunks[0], xcount, True
    )
    nfar_a = to_far(rounded_a)
    nsib_a = to_sibling(rounded_a)

    new_lo = from_below(new_tail)
    far_b = after(far_b, rounded_a)
    farsib_b = to_sibling(far_b)
    part_b, first_b, rest_b, new_one = early_part(
        [own_b, sib_b, far_b], base_b, one_b, two_b, initial, after(kernels, new_lo), death, chunks[1], new_a, chunks[0]
    )
    new_b, rounded_b, rest_b = first_node(
        part_b, first_b, rest_b, farsib_b, one_b, two_b, kernels, death, chunks[1], xcount, False
    )
    nfar_b = to_far(rounded_b)
    nsib_b = to_sibling(rounded_b)
    new_hi = from_above(after(new_head, rounded_b))
    nfar_a = after(nfar_a, rounded_b)
    nfarsib_a = to_sibling(nfar_a)
    new_one, npart_a, nbase_a, nbase_b = before_second(
        (new_a, new_b), (rest_a, rest_b), growth, death, new_one, [rounded_a, nsib_a, nfar_a], kernels, chunks
    )
    sums_a = whole_sums(npart_a, nfarsib_a, after(kernels, nbase_a))
    nfar_b = after(nfar_b, sums_a, new_hi)
    nfarsib_b = to_sibling(nfar_b)
    placed = list(enumerate(chunks[0]))
    ends = [p for p in placed if p[1] in (0, xcount - 1)]
    begun, npart_b = second_first(
        sums_a, nbase_a, new_a, death, [rounded_b, nsib_b, nfar_b], kernels, [p for p in placed if p not in ends], xcount
    )
    new_two = second_last(
        sums_a, nbase_a, new_a, new_lo, new_hi, npart_b, nfarsib_b, nbase_b, new_b, death, kernels, begun, ends,
        chunks[1], xcount,
    )
    return new_one, new_two


def solution(mesh):
    in_specs = (
        P("gx", None, "trait"),
        P("gx", None, "trait"),
        P("gx", None, "trait"),
        P(None, None, "trait"),
        P("trait"),
        P("trait"),
    )
    out_specs = (P("gx", None, "trait"), P("gx", None, "trait"))
    return jax.shard_map(local, mesh=mesh, in_specs=in_specs, out_specs=out_specs, check_vma=False)
```

```python
import jax
import jax.numpy as jnp
from jax import lax
from jax.experimental import pallas as pl
from jax.experimental.pallas import tpu as pltpu
from jax.sharding import PartitionSpec as P

DIFFUSION = 0.25
STEP_SIZE = 0.5
FIRST = STEP_SIZE / 3.0
SECOND = 2.0 * STEP_SIZE / 3.0
F32 = jnp.float32
BF16 = jnp.bfloat16
VMEM_LIMIT = 20 * 1024 * 1024
SPEC = pl.BlockSpec(memory_space=pltpu.VMEM)
ANYWHERE = pl.BlockSpec(memory_space=pl.ANY)
FROM_HBM = pl.BlockSpec(memory_space=pltpu.HBM)


def chunks_of(xcount):
    last = max(1, 3 * xcount // 8)
    start = (xcount - last + 1) // 2
    middle = list(range(start, start + last))
    return [x for x in range(xcount) if x not in middle], middle


def after(value, *others):
    return lax.optimization_barrier((value, *others))[0]


def call(body, name, args, outs, scratch=(), specs=None, out_specs=None, gflop=0.0, alias=None):
    specs = specs or [SPEC] * len(args)
    space = {id(SPEC): pltpu.VMEM, id(FROM_HBM): pltpu.HBM}
    args = [
        pltpu.with_memory_space_constraint(a, space[id(s)]) if id(s) in space else a for a, s in zip(args, specs)
    ]
    return pl.pallas_call(
        body,
        out_shape=outs,
        in_specs=specs,
        out_specs=out_specs or [SPEC] * len(outs),
        scratch_shapes=list(scratch),
        compiler_params=pltpu.CompilerParams(vmem_limit_bytes=VMEM_LIMIT),
        cost_estimate=pl.CostEstimate(flops=int(gflop * 1e9), bytes_accessed=0, transcendentals=0),
        input_output_aliases=alias or {},
        name=name,
    )(*args)


def runs_of(cells):
    runs = []
    for i, x in enumerate(cells):
        if runs and x == sum(runs[-1][1:]):
            runs[-1][2] += 1
        else:
            runs.append([i, x, 1])
    return runs


def load_chunk(fields, cells, with_faces):
    xcount, ycount, owned = fields[0].shape
    count = len(fields)
    runs = runs_of(cells)

    def body(*refs):
        field_refs, held_refs, out_ref = refs[:count], refs[count:2 * count], refs[2 * count]
        sems = refs[-1]
        copies = {}
        for f in range(count):
            for r, (i, x, size) in enumerate(runs):
                copies[f, r] = pltpu.make_async_copy(
                    field_refs[f].at[pl.ds(x, size)], held_refs[f].at[pl.ds(i, size)], sems.at[f, r]
                )
                copies[f, r].start()
        for f in range(count):
            for r, (start, _, size) in enumerate(runs):
                copies[f, r].wait()
                for i in range(start, start + size):
                    value = held_refs[f][i].astype(BF16)
                    out_ref[f, i * ycount:(i + 1) * ycount, :] = value
                    if with_faces and cells[i] == 0:
                        refs[2 * count + 1][f] = value
                    if with_faces and cells[i] == xcount - 1:
                        refs[2 * count + 2][f] = value

    outs = [pltpu.VMEM((len(cells), ycount, owned), F32)] * count
    outs.append(pltpu.VMEM((count, len(cells) * ycount, owned), BF16))
    if with_faces:
        outs += [pltpu.VMEM((count, ycount, owned), BF16)] * 2
    return call(
        body, "load_chunk", fields, outs, scratch=[pltpu.SemaphoreType.DMA((count, len(runs)))],
        specs=[FROM_HBM] * count,
    )


def blocks_dot(blocks, kernels_ref, k, owners):
    depth = blocks[0].shape[-1]
    lhs = jnp.concatenate(blocks, axis=-1)
    rhs = jnp.concatenate(
        [kernels_ref[k, pl.ds(pl.multiple_of(o * depth, depth), depth), :] for o in owners], axis=0
    )
    return jnp.dot(lhs, rhs, preferred_element_type=F32)


def along_y(core):
    return DIFFUSION * (pltpu.roll(core, 1, 0) + pltpu.roll(core, core.shape[0] - 1, 0)) - 2.0 * core


def before_first(ones, twos, lo, hi, growth, chunks):
    _, ycount, owned = ones[0].shape
    xcount = sum(len(cells) for cells in chunks)
    count = len(chunks)
    place = {x: (c, i) for c, cells in enumerate(chunks) for i, x in enumerate(cells)}

    def body(*refs):
        lo_ref, hi_ref, g_ref, *outs = refs[2 * count:]
        growth = g_ref[...]
        for f in range(2):

            def get(x):
                c, i = place[x]
                return refs[f * count + c][i]

            for x, (c, i) in place.items():
                core = get(x)
                before = get(x - 1) if x > 0 else lo_ref[f].astype(F32)
                behind = get(x + 1) if x < xcount - 1 else hi_ref[f].astype(F32)
                outs[c][f, i] = DIFFUSION * (before + behind) + along_y(core) + core * growth

    outs = [pltpu.VMEM((2, len(cells), ycount, owned), F32) for cells in chunks]
    return call(body, "before_first", [*ones, *twos, lo, hi, growth], outs)


def early_part(blocks, base, one, two, initial, kernels, death, cells, new=None, new_cells=()):
    xcount, ycount, owned = initial.shape
    rows = len(cells) * ycount
    count = len(blocks)

    def body(*refs):
        block_refs = refs[:count]
        base_ref, one_ref, two_ref, init_ref, k_ref, d_ref, *refs = refs[count:]
        copies = []
        if new is not None:
            new_ref, whole_ref, sems = refs[0], refs[-2], refs[-1]
            copies = [
                pltpu.make_async_copy(new_ref.at[pl.ds(i, size)], whole_ref.at[pl.ds(x, size)], sems.at[r])
                for r, (i, x, size) in enumerate(runs_of(new_cells))
            ]
        for copy in copies:
            copy.start()
        part_ref, first_ref, rest_ref = refs[:3] if new is None else refs[1:4]
        me = lax.axis_index("trait")
        values = [r[...].reshape(2 * rows, owned) for r in block_refs]
        for k in range(2):
            part_ref[k] = blocks_dot(values, k_ref, k, [me ^ j for j in range(count)])
        death = d_ref[...]
        inv_one = 1.0 / (1.0 + FIRST * death)
        inv_two = 1.0 / (1.0 + SECOND * death)
        for i, x in enumerate(cells):
            cores = (one_ref[i], two_ref[i])
            e = (base_ref[0, i], base_ref[1, i])
            full_one = e[0] - death * cores[0]
            full_two = e[1] - death * cores[1]
            first = (
                init_ref[x]
                + FIRST * death * cores[0]
                + STEP_SIZE * (5.0 / 12.0 * full_one - 1.0 / 12.0 * full_two)
            ) * inv_one
            first_ref[i] = first
            rest_ref[i] = (
                first - SECOND * e[0] + SECOND * death * cores[1] + STEP_SIZE / 3.0 * (full_one + full_two)
            ) * inv_two
        for copy in copies:
            copy.wait()

    args = [*blocks, base, one, two, initial, kernels, death]
    outs = [pltpu.VMEM((2, 2 * rows, owned), F32)] + [pltpu.VMEM((len(cells), ycount, owned), F32)] * 2
    if new is None:
        return call(body, "early_part", args, outs, gflop=20.0)
    outs.append(jax.ShapeDtypeStruct((xcount, ycount, owned), F32))
    return call(
        body, "early_part", [*args, new], outs, scratch=[pltpu.SemaphoreType.DMA((len(runs_of(new_cells)),))],
        out_specs=[SPEC, SPEC, SPEC, ANYWHERE], gflop=20.0,
    )


def first_node(part, first, rest, last, one, two, kernels, death, cells, xcount, with_faces):
    _, ycount, owned = one.shape
    rows = len(cells) * ycount

    def body(part_ref, first_ref, begun_ref, last_ref, one_ref, two_ref, k_ref, d_ref, *outs):
        new_ref, rounded_ref, rest_ref, *face_refs = outs
        me = lax.axis_index("trait")
        values = [last_ref[...].reshape(2 * rows, owned)]
        compete, mutate = ((part_ref[k] + blocks_dot(values, k_ref, k, [me ^ 3])).astype(BF16) for k in range(2))
        inv_one = STEP_SIZE / (1.0 + FIRST * d_ref[...])
        inv_two = 1.0 / (1.0 + SECOND * d_ref[...])
        for i, x in enumerate(cells):
            e = []
            for f, ref in enumerate((one_ref, two_ref)):
                at = slice(f * rows + i * ycount, f * rows + (i + 1) * ycount)
                e.append(mutate[at].astype(F32) - ref[i] * compete[at].astype(F32))
            more = (5.0 / 12.0 * e[0] - 1.0 / 12.0 * e[1]) * inv_one
            new = first_ref[i] + more
            new_ref[i] = new
            rounded = new.astype(BF16)
            rounded_ref[0, i * ycount:(i + 1) * ycount, :] = rounded
            if with_faces and x == 0:
                face_refs[0][0] = rounded
            if with_faces and x == xcount - 1:
                face_refs[1][0] = rounded
            rest_ref[i] = begun_ref[i] + (more - SECOND * e[0] + STEP_SIZE / 3.0 * (e[0] + e[1])) * inv_two

    outs = [
        pltpu.VMEM((len(cells), ycount, owned), F32),
        pltpu.VMEM((1, rows, owned), BF16),
        pltpu.VMEM((len(cells), ycount, owned), F32),
    ]
    if with_faces:
        outs += [pltpu.VMEM((1, ycount, owned), BF16)] * 2
    return call(body, "first_node", [part, first, rest, last, one, two, kernels, death], outs)


def before_second(news, rests, growth, death, begun, blocks, kernels, chunks):
    _, ycount, owned = news[0].shape
    rows = blocks[0].shape[1]
    xcount = sum(len(cells) for cells in chunks)
    count = len(chunks)
    size = len(blocks)
    place = {x: (c, i) for c, cells in enumerate(chunks) for i, x in enumerate(cells)}

    def body(*refs):
        new_refs, rest_refs, block_refs = refs[:count], refs[count:2 * count], refs[2 * count:2 * count + size]
        k_ref, g_ref, d_ref, _, whole_ref, part_ref = refs[2 * count + size:2 * count + size + 6]
        base_refs, sems = refs[2 * count + size + 6:-1], refs[-1]
        copies = [
            pltpu.make_async_copy(new_refs[-1].at[pl.ds(i, size)], whole_ref.at[pl.ds(x, size)], sems.at[r])
            for r, (i, x, size) in enumerate(runs_of(chunks[-1]))
        ]
        for copy in copies:
            copy.start()
        me = lax.axis_index("trait")
        values = [r[...].reshape(rows, owned) for r in block_refs]
        for k in range(2):
            part_ref[k] = blocks_dot(values, k_ref, k, [me ^ j for j in range(size)])
        growth = g_ref[...]
        factor = SECOND / (1.0 + SECOND * d_ref[...])
        for x, (c, i) in place.items():
            core = new_refs[c][i]
            e = along_y(core) + core * growth
            for near in (x - 1, x + 1):
                if near in place:
                    e = e + DIFFUSION * new_refs[place[near][0]][place[near][1]]
            base_refs[c][i] = rest_refs[c][i] + factor * e
        for copy in copies:
            copy.wait()

    outs = [jax.ShapeDtypeStruct((xcount, ycount, owned), F32), pltpu.VMEM((2, rows, owned), F32)]
    outs += [pltpu.VMEM((len(cells), ycount, owned), F32) for cells in chunks]
    args = [*news, *rests, *blocks, kernels, growth, death, begun]
    return call(
        body, "before_second", args, outs, scratch=[pltpu.SemaphoreType.DMA((len(runs_of(chunks[-1])),))],
        specs=[SPEC] * (len(args) - 1) + [FROM_HBM], out_specs=[ANYWHERE] + [SPEC] * (len(outs) - 1), gflop=20.0,
        alias={len(args) - 1: 0},
    )


def whole_sums(part, last, kernels):
    rows, owned = last.shape[1:]

    def body(part_ref, last_ref, k_ref, sums_ref):
        me = lax.axis_index("trait")
        for k in range(2):
            last_part = blocks_dot([last_ref[...].reshape(rows, owned)], k_ref, k, [me ^ 3])
            sums_ref[k] = (part_ref[k] + last_part).astype(BF16)

    return call(body, "whole_sums", [part, last, kernels], [pltpu.VMEM((2, rows, owned), BF16)])[0]


def finish(cells, sums_at, base_ref, new_ref, factor, faces, held, out_ref, sems, offset=0):
    copies = []
    for j, (i, x) in enumerate(cells, offset):
        e = sums_at(1, i) - new_ref[i] * sums_at(0, i)
        if x in faces:
            e = e + DIFFUSION * faces[x][0].astype(F32)
        held[j] = base_ref[i] + factor * e
        copies.append(pltpu.make_async_copy(held.at[j], out_ref.at[x], sems.at[j]))
        copies[-1].start()
    return copies


def rounded_at(sums, ycount):
    return lambda k, i: sums[k, pl.ds(i * ycount, ycount), :].astype(F32)


def second_first(sums, base, new, death, blocks, kernels, cells, xcount):
    _, ycount, owned = new.shape
    rows = blocks[0].shape[1]
    count = len(blocks)

    def body(sums_ref, base_ref, new_ref, d_ref, k_ref, *refs):
        block_refs = refs[:count]
        out_ref, part_ref, held, sems = refs[count:]
        factor = SECOND / (1.0 + SECOND * d_ref[...])
        copies = finish(
            cells, rounded_at(sums_ref, ycount), base_ref, new_ref, factor, {}, held, out_ref, sems
        )
        me = lax.axis_index("trait")
        values = [r[...].reshape(rows, owned) for r in block_refs]
        for k in range(2):
            part_ref[k] = blocks_dot(values, k_ref, k, [me ^ j for j in range(count)])
        for copy in copies:
            copy.wait()

    return call(
        body, "second_first", [sums, base, new, death, kernels, *blocks],
        [jax.ShapeDtypeStruct((xcount, ycount, owned), F32), pltpu.VMEM((2, rows, owned), F32)],
        scratch=[pltpu.VMEM((len(cells), ycount, owned), F32), pltpu.SemaphoreType.DMA((len(cells),))],
        out_specs=[ANYWHERE, SPEC],
    )


def second_last(sums_a, base_a, new_a, lo, hi, part, last, base, new, death, kernels, begun, ends, cells, xcount):
    _, ycount, owned = new.shape
    rows = len(cells) * ycount
    total = len(ends) + len(cells)

    def body(*refs):
        sums_a_ref, base_a_ref, new_a_ref, lo_ref, hi_ref, part_ref, last_ref, base_ref, new_ref, d_ref, k_ref = refs[:11]
        _, out_ref, sums, held, sems = refs[11:]
        factor = SECOND / (1.0 + SECOND * d_ref[...])
        faces = {0: lo_ref, xcount - 1: hi_ref}
        copies = finish(
            ends, rounded_at(sums_a_ref, ycount), base_a_ref, new_a_ref, factor, faces, held, out_ref, sems
        )
        me = lax.axis_index("trait")
        for k in range(2):
            sums[k] = (part_ref[k] + blocks_dot([last_ref[...].reshape(rows, owned)], k_ref, k, [me ^ 3])).astype(BF16)
        copies += finish(
            list(enumerate(cells)), rounded_at(sums, ycount), base_ref, new_ref, factor, {}, held, out_ref, sems,
            len(ends),
        )
        for copy in copies:
            copy.wait()

    args = [sums_a, base_a, new_a, lo, hi, part, last, base, new, death, kernels, begun]
    return call(
        body, "second_last", args, [jax.ShapeDtypeStruct((xcount, ycount, owned), F32)],
        scratch=[
            pltpu.VMEM((2, rows, owned), BF16),
            pltpu.VMEM((total, ycount, owned), F32),
            pltpu.SemaphoreType.DMA((total,)),
        ],
        specs=[SPEC] * 11 + [FROM_HBM], out_specs=[ANYWHERE], alias={11: 0},
    )[0]


def local(initial, section_one, section_two, kernels, growth, death_rate):
    xcount, ycount, owned = section_one.shape
    traits = lax.axis_size("trait")
    gcount = lax.axis_size("gx")
    growth = growth.reshape(1, owned)
    death = death_rate.reshape(1, owned)
    chunks = chunks_of(xcount)

    def to_sibling(v):
        return lax.ppermute(v, "trait", [(i, i ^ 1) for i in range(traits)])

    def to_far(v):
        return lax.ppermute(v, "trait", [(i, i ^ 2) for i in range(traits)])

    def from_below(tail):
        return lax.ppermute(tail, "gx", [(i, (i + 1) % gcount) for i in range(gcount)])

    def from_above(head):
        return lax.ppermute(head, "gx", [((i + 1) % gcount, i) for i in range(gcount)])

    one_a, two_a, own_a, head, tail = load_chunk((section_one, section_two), chunks[0], True)
    far_a = to_far(own_a)
    one_b, two_b, own_b = load_chunk((after(section_one, own_a), section_two), chunks[1], False)
    far_b = to_far(own_b)
    head, tail, kernels = lax.optimization_barrier((head, tail, kernels, own_b))[:3]
    lo, hi = from_below(tail), from_above(head)
    base_a, base_b = before_first((one_a, one_b), (two_a, two_b), lo, hi, growth, chunks)
    sib_a = to_sibling(after(own_a, own_b))
    sib_b = to_sibling(own_b)
    far_a = after(far_a, base_a)
    farsib_a = to_sibling(far_a)
    part_a, first_a, rest_a = early_part([own_a, sib_a, far_a], base_a, one_a, two_a, initial, kernels, death, chunks[0])
    new_a, rounded_a, rest_a, new_head, new_tail = first_node(
        part_a, first_a, rest_a, farsib_a, one_a, two_a, kernels, death, chunks[0], xcount, True
    )
    nfar_a = to_far(rounded_a)
    nsib_a = to_sibling(rounded_a)

    new_lo = from_below(new_tail)
    far_b = after(far_b, rounded_a)
    farsib_b = to_sibling(far_b)
    part_b, first_b, rest_b, new_one = early_part(
        [own_b, sib_b, far_b], base_b, one_b, two_b, initial, after(kernels, new_lo), death, chunks[1], new_a, chunks[0]
    )
    new_b, rounded_b, rest_b = first_node(
        part_b, first_b, rest_b, farsib_b, one_b, two_b, kernels, death, chunks[1], xcount, False
    )
    nfar_b = to_far(rounded_b)
    nsib_b = to_sibling(rounded_b)
    new_hi = from_above(after(new_head, rounded_b))
    nfar_a = after(nfar_a, rounded_b)
    nfarsib_a = to_sibling(nfar_a)
    new_one, npart_a, nbase_a, nbase_b = before_second(
        (new_a, new_b), (rest_a, rest_b), growth, death, new_one, [rounded_a, nsib_a, nfar_a], kernels, chunks
    )
    sums_a = whole_sums(npart_a, nfarsib_a, after(kernels, nbase_a))
    nfar_b = after(nfar_b, sums_a, new_hi)
    nfarsib_b = to_sibling(nfar_b)
    placed = list(enumerate(chunks[0]))
    ends = [p for p in placed if p[1] in (0, 1, xcount - 1)]
    begun, npart_b = second_first(
        sums_a, nbase_a, new_a, death, [rounded_b, nsib_b, nfar_b], kernels, [p for p in placed if p not in ends], xcount
    )
    new_two = second_last(
        sums_a, nbase_a, new_a, new_lo, new_hi, npart_b, nfarsib_b, nbase_b, new_b, death, kernels, begun, ends,
        chunks[1], xcount,
    )
    return new_one, new_two


def solution(mesh):
    in_specs = (
        P("gx", None, "trait"),
        P("gx", None, "trait"),
        P("gx", None, "trait"),
        P(None, None, "trait"),
        P("trait"),
        P("trait"),
    )
    out_specs = (P("gx", None, "trait"), P("gx", None, "trait"))
    return jax.shard_map(local, mesh=mesh, in_specs=in_specs, out_specs=out_specs, check_vma=False)
```

```python
import jax
import jax.numpy as jnp
from jax import lax
from jax.experimental import pallas as pl
from jax.experimental.pallas import tpu as pltpu
from jax.sharding import PartitionSpec as P

DIFFUSION = 0.25
STEP_SIZE = 0.5
FIRST = STEP_SIZE / 3.0
SECOND = 2.0 * STEP_SIZE / 3.0
F32 = jnp.float32
BF16 = jnp.bfloat16
VMEM_LIMIT = 20 * 1024 * 1024
SPEC = pl.BlockSpec(memory_space=pltpu.VMEM)
ANYWHERE = pl.BlockSpec(memory_space=pl.ANY)
FROM_HBM = pl.BlockSpec(memory_space=pltpu.HBM)


def chunks_of(xcount):
    last = max(1, 3 * xcount // 8)
    start = (xcount - last + 1) // 2
    middle = list(range(start, start + last))
    return [x for x in range(xcount) if x not in middle], middle


def after(value, *others):
    return lax.optimization_barrier((value, *others))[0]


def call(body, name, args, outs, scratch=(), specs=None, out_specs=None, gflop=0.0, alias=None):
    specs = specs or [SPEC] * len(args)
    space = {id(SPEC): pltpu.VMEM, id(FROM_HBM): pltpu.HBM}
    args = [
        pltpu.with_memory_space_constraint(a, space[id(s)]) if id(s) in space else a for a, s in zip(args, specs)
    ]
    return pl.pallas_call(
        body,
        out_shape=outs,
        in_specs=specs,
        out_specs=out_specs or [SPEC] * len(outs),
        scratch_shapes=list(scratch),
        compiler_params=pltpu.CompilerParams(vmem_limit_bytes=VMEM_LIMIT),
        cost_estimate=pl.CostEstimate(flops=int(gflop * 1e9), bytes_accessed=0, transcendentals=0),
        input_output_aliases=alias or {},
        name=name,
    )(*args)


def runs_of(cells):
    runs = []
    for i, x in enumerate(cells):
        if runs and x == sum(runs[-1][1:]):
            runs[-1][2] += 1
        else:
            runs.append([i, x, 1])
    return runs


def load_chunk(fields, cells, with_faces):
    xcount, ycount, owned = fields[0].shape
    count = len(fields)
    runs = runs_of(cells)

    def body(*refs):
        field_refs, held_refs, out_ref = refs[:count], refs[count:2 * count], refs[2 * count]
        sems = refs[-1]
        copies = {}
        for f in range(count):
            for r, (i, x, size) in enumerate(runs):
                copies[f, r] = pltpu.make_async_copy(
                    field_refs[f].at[pl.ds(x, size)], held_refs[f].at[pl.ds(i, size)], sems.at[f, r]
                )
                copies[f, r].start()
        for f in range(count):
            for r, (start, _, size) in enumerate(runs):
                copies[f, r].wait()
                for i in range(start, start + size):
                    value = held_refs[f][i].astype(BF16)
                    out_ref[f, i * ycount:(i + 1) * ycount, :] = value
                    if with_faces and cells[i] == 0:
                        refs[2 * count + 1][f] = value
                    if with_faces and cells[i] == xcount - 1:
                        refs[2 * count + 2][f] = value

    outs = [pltpu.VMEM((len(cells), ycount, owned), F32)] * count
    outs.append(pltpu.VMEM((count, len(cells) * ycount, owned), BF16))
    if with_faces:
        outs += [pltpu.VMEM((count, ycount, owned), BF16)] * 2
    return call(
        body, "load_chunk", fields, outs, scratch=[pltpu.SemaphoreType.DMA((count, len(runs)))],
        specs=[FROM_HBM] * count,
    )


def blocks_dot(blocks, kernels_ref, k, owners):
    depth = blocks[0].shape[-1]
    lhs = jnp.concatenate(blocks, axis=-1)
    rhs = jnp.concatenate(
        [kernels_ref[k, pl.ds(pl.multiple_of(o * depth, depth), depth), :] for o in owners], axis=0
    )
    return jnp.dot(lhs, rhs, preferred_element_type=F32)


def along_y(core):
    return DIFFUSION * (pltpu.roll(core, 1, 0) + pltpu.roll(core, core.shape[0] - 1, 0)) - 2.0 * core


def before_first(ones, twos, lo, hi, growth, chunks):
    _, ycount, owned = ones[0].shape
    xcount = sum(len(cells) for cells in chunks)
    count = len(chunks)
    place = {x: (c, i) for c, cells in enumerate(chunks) for i, x in enumerate(cells)}

    def body(*refs):
        lo_ref, hi_ref, g_ref, *outs = refs[2 * count:]
        growth = g_ref[...]
        for f in range(2):

            def get(x):
                c, i = place[x]
                return refs[f * count + c][i]

            for x, (c, i) in place.items():
                core = get(x)
                before = get(x - 1) if x > 0 else lo_ref[f].astype(F32)
                behind = get(x + 1) if x < xcount - 1 else hi_ref[f].astype(F32)
                outs[c][f, i] = DIFFUSION * (before + behind) + along_y(core) + core * growth

    outs = [pltpu.VMEM((2, len(cells), ycount, owned), F32) for cells in chunks]
    return call(body, "before_first", [*ones, *twos, lo, hi, growth], outs)


def early_part(blocks, base, one, two, initial, kernels, death, cells, new=None, new_cells=()):
    xcount, ycount, owned = initial.shape
    rows = len(cells) * ycount
    count = len(blocks)

    def body(*refs):
        block_refs = refs[:count]
        base_ref, one_ref, two_ref, init_ref, k_ref, d_ref, *refs = refs[count:]
        copies = []
        if new is not None:
            new_ref, whole_ref, sems = refs[0], refs[-2], refs[-1]
            copies = [
                pltpu.make_async_copy(new_ref.at[pl.ds(i, size)], whole_ref.at[pl.ds(x, size)], sems.at[r])
                for r, (i, x, size) in enumerate(runs_of(new_cells))
            ]
        for copy in copies:
            copy.start()
        part_ref, first_ref, rest_ref = refs[:3] if new is None else refs[1:4]
        me = lax.axis_index("trait")
        values = [r[...].reshape(2 * rows, owned) for r in block_refs]
        for k in range(2):
            part_ref[k] = blocks_dot(values, k_ref, k, [me ^ j for j in range(count)])
        death = d_ref[...]
        inv_one = 1.0 / (1.0 + FIRST * death)
        inv_two = 1.0 / (1.0 + SECOND * death)
        for i, x in enumerate(cells):
            cores = (one_ref[i], two_ref[i])
            e = (base_ref[0, i], base_ref[1, i])
            full_one = e[0] - death * cores[0]
            full_two = e[1] - death * cores[1]
            first = (
                init_ref[x]
                + FIRST * death * cores[0]
                + STEP_SIZE * (5.0 / 12.0 * full_one - 1.0 / 12.0 * full_two)
            ) * inv_one
            first_ref[i] = first
            rest_ref[i] = (
                first - SECOND * e[0] + SECOND * death * cores[1] + STEP_SIZE / 3.0 * (full_one + full_two)
            ) * inv_two
        for copy in copies:
            copy.wait()

    args = [*blocks, base, one, two, initial, kernels, death]
    outs = [pltpu.VMEM((2, 2 * rows, owned), F32)] + [pltpu.VMEM((len(cells), ycount, owned), F32)] * 2
    if new is None:
        return call(body, "early_part", args, outs, gflop=20.0)
    outs.append(jax.ShapeDtypeStruct((xcount, ycount, owned), F32))
    return call(
        body, "early_part", [*args, new], outs, scratch=[pltpu.SemaphoreType.DMA((len(runs_of(new_cells)),))],
        out_specs=[SPEC, SPEC, SPEC, ANYWHERE], gflop=20.0,
    )


def first_node(part, first, rest, last, one, two, kernels, death, cells, xcount, with_faces):
    _, ycount, owned = one.shape
    rows = len(cells) * ycount

    def body(part_ref, first_ref, begun_ref, last_ref, one_ref, two_ref, k_ref, d_ref, *outs):
        new_ref, rounded_ref, rest_ref, *face_refs = outs
        me = lax.axis_index("trait")
        values = [last_ref[...].reshape(2 * rows, owned)]
        compete, mutate = ((part_ref[k] + blocks_dot(values, k_ref, k, [me ^ 3])).astype(BF16) for k in range(2))
        inv_one = STEP_SIZE / (1.0 + FIRST * d_ref[...])
        inv_two = 1.0 / (1.0 + SECOND * d_ref[...])
        for i, x in enumerate(cells):
            e = []
            for f, ref in enumerate((one_ref, two_ref)):
                at = slice(f * rows + i * ycount, f * rows + (i + 1) * ycount)
                e.append(mutate[at].astype(F32) - ref[i] * compete[at].astype(F32))
            more = (5.0 / 12.0 * e[0] - 1.0 / 12.0 * e[1]) * inv_one
            new = first_ref[i] + more
            new_ref[i] = new
            rounded = new.astype(BF16)
            rounded_ref[0, i * ycount:(i + 1) * ycount, :] = rounded
            if with_faces and x == 0:
                face_refs[0][0] = rounded
            if with_faces and x == xcount - 1:
                face_refs[1][0] = rounded
            rest_ref[i] = begun_ref[i] + (more - SECOND * e[0] + STEP_SIZE / 3.0 * (e[0] + e[1])) * inv_two

    outs = [
        pltpu.VMEM((len(cells), ycount, owned), F32),
        pltpu.VMEM((1, rows, owned), BF16),
        pltpu.VMEM((len(cells), ycount, owned), F32),
    ]
    if with_faces:
        outs += [pltpu.VMEM((1, ycount, owned), BF16)] * 2
    return call(body, "first_node", [part, first, rest, last, one, two, kernels, death], outs)


def before_second(news, rests, growth, death, begun, blocks, kernels, chunks):
    _, ycount, owned = news[0].shape
    rows = blocks[0].shape[1]
    xcount = sum(len(cells) for cells in chunks)
    count = len(chunks)
    size = len(blocks)
    place = {x: (c, i) for c, cells in enumerate(chunks) for i, x in enumerate(cells)}

    def body(*refs):
        new_refs, rest_refs, block_refs = refs[:count], refs[count:2 * count], refs[2 * count:2 * count + size]
        k_ref, g_ref, d_ref, _, whole_ref, part_ref = refs[2 * count + size:2 * count + size + 6]
        base_refs, sems = refs[2 * count + size + 6:-1], refs[-1]
        copies = [
            pltpu.make_async_copy(new_refs[-1].at[pl.ds(i, size)], whole_ref.at[pl.ds(x, size)], sems.at[r])
            for r, (i, x, size) in enumerate(runs_of(chunks[-1]))
        ]
        for copy in copies:
            copy.start()
        me = lax.axis_index("trait")
        values = [r[...].reshape(rows, owned) for r in block_refs]
        for k in range(2):
            part_ref[k] = blocks_dot(values, k_ref, k, [me ^ j for j in range(size)])
        growth = g_ref[...]
        factor = SECOND / (1.0 + SECOND * d_ref[...])
        for x, (c, i) in place.items():
            core = new_refs[c][i]
            e = along_y(core) + core * growth
            for near in (x - 1, x + 1):
                if near in place:
                    e = e + DIFFUSION * new_refs[place[near][0]][place[near][1]]
            base_refs[c][i] = rest_refs[c][i] + factor * e
        for copy in copies:
            copy.wait()

    outs = [jax.ShapeDtypeStruct((xcount, ycount, owned), F32), pltpu.VMEM((2, rows, owned), F32)]
    outs += [pltpu.VMEM((len(cells), ycount, owned), F32) for cells in chunks]
    args = [*news, *rests, *blocks, kernels, growth, death, begun]
    return call(
        body, "before_second", args, outs, scratch=[pltpu.SemaphoreType.DMA((len(runs_of(chunks[-1])),))],
        specs=[SPEC] * (len(args) - 1) + [FROM_HBM], out_specs=[ANYWHERE] + [SPEC] * (len(outs) - 1), gflop=20.0,
        alias={len(args) - 1: 0},
    )


def whole_sums(part, last, kernels):
    rows, owned = last.shape[1:]

    def body(part_ref, last_ref, k_ref, sums_ref):
        me = lax.axis_index("trait")
        for k in range(2):
            last_part = blocks_dot([last_ref[...].reshape(rows, owned)], k_ref, k, [me ^ 3])
            sums_ref[k] = (part_ref[k] + last_part).astype(BF16)

    return call(body, "whole_sums", [part, last, kernels], [pltpu.VMEM((2, rows, owned), BF16)])[0]


def finish(cells, sums_at, base_ref, new_ref, factor, faces, held, out_ref, sems, offset=0):
    copies = []
    for j, (i, x) in enumerate(cells, offset):
        e = sums_at(1, i) - new_ref[i] * sums_at(0, i)
        if x in faces:
            e = e + DIFFUSION * faces[x][0].astype(F32)
        held[j] = base_ref[i] + factor * e
        copies.append(pltpu.make_async_copy(held.at[j], out_ref.at[x], sems.at[j]))
        copies[-1].start()
    return copies


def rounded_at(sums, ycount):
    return lambda k, i: sums[k, pl.ds(i * ycount, ycount), :].astype(F32)


def second_first(sums, base, new, death, blocks, kernels, cells, xcount):
    _, ycount, owned = new.shape
    rows = blocks[0].shape[1]
    count = len(blocks)

    def body(sums_ref, base_ref, new_ref, d_ref, k_ref, *refs):
        block_refs = refs[:count]
        out_ref, part_ref, held, sems = refs[count:]
        factor = SECOND / (1.0 + SECOND * d_ref[...])
        copies = finish(
            cells, rounded_at(sums_ref, ycount), base_ref, new_ref, factor, {}, held, out_ref, sems
        )
        me = lax.axis_index("trait")
        values = [r[...].reshape(rows, owned) for r in block_refs]
        for k in range(2):
            part_ref[k] = blocks_dot(values, k_ref, k, [me ^ j for j in range(count)])
        for copy in copies:
            copy.wait()

    return call(
        body, "second_first", [sums, base, new, death, kernels, *blocks],
        [jax.ShapeDtypeStruct((xcount, ycount, owned), F32), pltpu.VMEM((2, rows, owned), F32)],
        scratch=[pltpu.VMEM((len(cells), ycount, owned), F32), pltpu.SemaphoreType.DMA((len(cells),))],
        out_specs=[ANYWHERE, SPEC],
    )


def second_last(sums_a, base_a, new_a, lo, hi, part, last, base, new, death, kernels, begun, ends, cells, xcount):
    _, ycount, owned = new.shape
    rows = len(cells) * ycount
    total = len(ends) + len(cells)

    def body(*refs):
        sums_a_ref, base_a_ref, new_a_ref, lo_ref, hi_ref, part_ref, last_ref, base_ref, new_ref, d_ref, k_ref = refs[:11]
        _, out_ref, sums, held, sems = refs[11:]
        factor = SECOND / (1.0 + SECOND * d_ref[...])
        faces = {0: lo_ref, xcount - 1: hi_ref}
        copies = finish(
            ends, rounded_at(sums_a_ref, ycount), base_a_ref, new_a_ref, factor, faces, held, out_ref, sems
        )
        me = lax.axis_index("trait")
        for k in range(2):
            sums[k] = (part_ref[k] + blocks_dot([last_ref[...].reshape(rows, owned)], k_ref, k, [me ^ 3])).astype(BF16)
        copies += finish(
            list(enumerate(cells)), rounded_at(sums, ycount), base_ref, new_ref, factor, {}, held, out_ref, sems,
            len(ends),
        )
        for copy in copies:
            copy.wait()

    args = [sums_a, base_a, new_a, lo, hi, part, last, base, new, death, kernels, begun]
    return call(
        body, "second_last", args, [jax.ShapeDtypeStruct((xcount, ycount, owned), F32)],
        scratch=[
            pltpu.VMEM((2, rows, owned), BF16),
            pltpu.VMEM((total, ycount, owned), F32),
            pltpu.SemaphoreType.DMA((total,)),
        ],
        specs=[SPEC] * 11 + [FROM_HBM], out_specs=[ANYWHERE], alias={11: 0},
    )[0]


def local(initial, section_one, section_two, kernels, growth, death_rate):
    xcount, ycount, owned = section_one.shape
    traits = lax.axis_size("trait")
    gcount = lax.axis_size("gx")
    growth = growth.reshape(1, owned)
    death = death_rate.reshape(1, owned)
    chunks = chunks_of(xcount)

    def to_sibling(v):
        return lax.ppermute(v, "trait", [(i, i ^ 1) for i in range(traits)])

    def to_far(v):
        return lax.ppermute(v, "trait", [(i, i ^ 2) for i in range(traits)])

    def from_below(tail):
        return lax.ppermute(tail, "gx", [(i, (i + 1) % gcount) for i in range(gcount)])

    def from_above(head):
        return lax.ppermute(head, "gx", [((i + 1) % gcount, i) for i in range(gcount)])

    one_a, two_a, own_a, head, tail = load_chunk((section_one, section_two), chunks[0], True)
    far_a = to_far(own_a)
    one_b, two_b, own_b = load_chunk((after(section_one, own_a), section_two), chunks[1], False)
    far_b = to_far(own_b)
    kernels = after(kernels, own_b)
    lo, hi = from_below(tail), from_above(head)
    base_a, base_b = before_first((one_a, one_b), (two_a, two_b), lo, hi, growth, chunks)
    sib_a = to_sibling(after(own_a, own_b))
    sib_b = to_sibling(own_b)
    far_a = after(far_a, base_a)
    farsib_a = to_sibling(far_a)
    part_a, first_a, rest_a = early_part([own_a, sib_a, far_a], base_a, one_a, two_a, initial, kernels, death, chunks[0])
    new_a, rounded_a, rest_a, new_head, new_tail = first_node(
        part_a, first_a, rest_a, farsib_a, one_a, two_a, kernels, death, chunks[0], xcount, True
    )
    nfar_a = to_far(rounded_a)
    nsib_a = to_sibling(rounded_a)

    new_lo = from_below(new_tail)
    far_b = after(far_b, rounded_a)
    farsib_b = to_sibling(far_b)
    part_b, first_b, rest_b, new_one = early_part(
        [own_b, sib_b, far_b], base_b, one_b, two_b, initial, after(kernels, new_lo), death, chunks[1], new_a, chunks[0]
    )
    new_b, rounded_b, rest_b = first_node(
        part_b, first_b, rest_b, farsib_b, one_b, two_b, kernels, death, chunks[1], xcount, False
    )
    nfar_b = to_far(rounded_b)
    nsib_b = to_sibling(rounded_b)
    new_hi = from_above(after(new_head, rounded_b))
    nfar_a = after(nfar_a, rounded_b)
    nfarsib_a = to_sibling(nfar_a)
    new_one, npart_a, nbase_a, nbase_b = before_second(
        (new_a, new_b), (rest_a, rest_b), growth, death, new_one, [rounded_a, nsib_a, nfar_a], kernels, chunks
    )
    sums_a = whole_sums(npart_a, nfarsib_a, after(kernels, nbase_a))
    nfar_b = after(nfar_b, sums_a, new_hi)
    nfarsib_b = to_sibling(nfar_b)
    placed = list(enumerate(chunks[0]))
    ends = [p for p in placed if p[1] in (0, xcount - 1)]
    begun, npart_b = second_first(
        sums_a, nbase_a, new_a, death, [rounded_b, nsib_b, nfar_b], kernels, [p for p in placed if p not in ends], xcount
    )
    new_two = second_last(
        sums_a, nbase_a, new_a, new_lo, new_hi, npart_b, nfarsib_b, nbase_b, new_b, death, kernels, begun, ends,
        chunks[1], xcount,
    )
    return new_one, new_two


def solution(mesh):
    in_specs = (
        P("gx", None, "trait"),
        P("gx", None, "trait"),
        P("gx", None, "trait"),
        P(None, None, "trait"),
        P("trait"),
        P("trait"),
    )
    out_specs = (P("gx", None, "trait"), P("gx", None, "trait"))
    return jax.shard_map(local, mesh=mesh, in_specs=in_specs, out_specs=out_specs, check_vma=False)
```
